32 devices in a mesh: dp: 4 (over x, core), context: 2 (over y), expert: 4 (over z).
Axes of the slice: x: 2, y: 2, z: 4, core: 2. Of those that a mesh axis runs over, the one named last changes fastest.
Arguments:
- tokens: bfloat16 [4, 512, 2048], P('dp', 'context'), may hold values from -6 to 6
- norm1_gain: bfloat16 [2048], P(('dp', 'context')), may hold values from 0.5 to 1.5
- w_qkv: bfloat16 [2048, 3, 2048], P(('dp', 'context'), None, 'expert'), may hold values from -0.125 to 0.125
- b_qkv: bfloat16 [3, 16, 128], P(None, 'expert'), may hold values from -1.1953125 to 1.1953125
- w_out: bfloat16 [2048, 2048], P('expert', ('dp', 'context')), may hold values from -0.5 to 0.5
- norm2_gain: bfloat16 [2048], P(('dp', 'context')), may hold values from 0.5 to 1.5
- w_router: bfloat16 [2048, 8], P(('dp', 'context')), may hold values from -0.0625 to 0.0625
- shared_gate: bfloat16 [2048], P(('dp', 'context')), may hold values from -0.125 to 0.125
- w_shared_in: bfloat16 [2048, 2, 5632], P(('dp', 'context'), None, 'expert'), may hold values from -0.125 to 0.125
- w_shared_out: bfloat16 [5632, 2048], P('expert', ('dp', 'context')), may hold values from -0.15625 to 0.15625
- w_expert_in: bfloat16 [8, 2048, 2, 1408], P(('context', 'expert'), 'dp'), may hold values from -0.125 to 0.125
- w_expert_out: bfloat16 [8, 1408, 2048], P(('context', 'expert'), None, 'dp'), may hold values from -0.3125 to 0.3125
- block_ids: int32 [4, 512], P('dp'), may hold values from 0 to 3, never falling along the last dimension, each value on 1 to 256 neighbouring positions
- expert_ids: int32 [4, 512, 4], P('dp', ('context', 'expert')), may hold values from 0 to 7, all different within a row; in each aligned block of 64 rows (0 to 63, 64 to 127, ..., all dimensions but the last counted through in order) at most 48 rows name the same one
- out_grad: bfloat16 [4, 512, 2048], P('dp', 'context'), may hold values from -6 to 6
Outputs:
- output: bfloat16 [4, 512, 2048], P('dp', ('context', 'expert'))
- grad_tokens: bfloat16 [4, 512, 2048], P('dp', ('context', 'expert'))
- grad_norm1_gain: bfloat16 [2048], P(('dp', 'context'))
- grad_w_qkv: bfloat16 [2048, 3, 2048], P(('dp', 'context'), None, 'expert')
- grad_b_qkv: bfloat16 [3, 16, 128], P(None, 'expert', ('dp', 'context'))
- grad_w_out: bfloat16 [2048, 2048], P('expert', ('dp', 'context'))
- grad_norm2_gain: bfloat16 [2048], P(('dp', 'context'))
- grad_w_router: bfloat16 [2048, 8], P(('dp', 'context'))
- grad_shared_gate: bfloat16 [2048], P(('dp', 'context'))
- grad_w_shared_in: bfloat16 [2048, 2, 5632], P(('dp', 'context'), None, 'expert')
- grad_w_shared_out: bfloat16 [5632, 2048], P('expert', ('dp', 'context'))
- grad_w_expert_in: bfloat16 [8, 2048, 2, 1408], P(('context', 'expert'), 'dp')
- grad_w_expert_out: bfloat16 [8, 1408, 2048], P(('context', 'expert'), None, 'dp')
The draws below stay inside these ranges and needn't reach their ends.
Inputs may be any that keep to these rules, and one draw needn't show every extreme that they name: `expert_ids`: each row names 4 different experts. In each aligned block of 64 rows (the rows of one device in order of sequence and position) no expert is named by more than 48 rows, a bound that some block reaches. `block_ids`: within a sequence the block number never falls; each block holds 1 to 256 positions, one exactly 256.
All inputs are finite; a program needn't handle non-finite values.
Results may differ from the reference program's by a relative error of at most 0.035.
Values may be sent and summed in bfloat16 or wider, within the bound.
A program may use at most 256 MiB of HBM per device.

```python
import math
import jax
import jax.numpy as jnp
import numpy as np
from jax import lax

D = 2048
NH = 16
HD = 128
FFE = 1408
FS = 5632
TOPK = 4
BLOCK = 256
LENGTH = 512
BATCH = 4
TOK_E = 64
EXPERTS = 8
CAP = 48


def block_levels(rng, dims, cuts, least, high):
    def one(dim, shards_of):
        steps = jax.random.uniform(jax.random.fold_in(jax.random.fold_in(rng, 6), dim), (shards_of,), jnp.float32, least / len(cuts), high / len(cuts))
        return jnp.repeat(jnp.exp(steps), dims[dim] // shards_of).reshape((-1,) + (1,) * (len(dims) - dim - 1))

    factor_of = one(*cuts[0])
    for cut in cuts[1:]:
        factor_of = factor_of * one(*cut)
    return factor_of


def split_up(number_of, total, limit, lean):
    weights = [(1 << 20) // math.isqrt(grade ** lean) + 1 for grade in range(2, number_of + 1)]
    rest, given = total - limit - (number_of - 1), [1] * (number_of - 1)
    while rest > 0:
        candidates = [i for i in range(number_of - 1) if given[i] < limit]
        whole, remaining = sum([weights[i] for i in candidates]), rest
        for i in candidates:
            more = min(limit - given[i], max(1, remaining * weights[i] // whole), rest)
            given[i] = given[i] + more
            rest = rest - more
    return np.array([limit] + given)


def uneven_parts(key, number_of, total, bound, slope):
    if number_of == 2:
        one = jax.random.randint(key, (), max(1, total - bound), min(bound, total - 1) + 1)
        return jnp.stack([one, total - one])
    tallies = jnp.asarray(split_up(number_of, total, bound, slope), jnp.int32)
    twos = (number_of - 1) // 2
    donor, sink = tallies[1:1 + 2 * twos:2], tallies[2:2 + 2 * twos:2]
    room = jnp.minimum(donor - 1, bound - sink)
    moved = jax.random.randint(jax.random.fold_in(key, 1), (twos,), 0, 1 << 20) % (room + 1)
    tallies = tallies.at[1:1 + 2 * twos:2].set(donor - moved).at[2:2 + 2 * twos:2].set(sink + moved)
    return tallies[jax.random.permutation(jax.random.fold_in(key, 2), number_of)]


def routed_block(stream_key, own, number, rows, number_of, top, reach, skew):
    ranking = jax.random.permutation(stream_key, number_of)
    packed, common = shares(number_of, rows * top, reach, skew, True), shares(number_of, rows * top, reach, skew, False)
    places = jnp.arange(number_of)

    def named(tallies, turn):
        used = int((tallies > 0).sum())
        fixed = max(1, used // 4)
        passed = fixed + (places - fixed + turn * (used - fixed)) % max(1, number_of - fixed)
        return jnp.zeros((number_of,), jnp.int32).at[ranking[jnp.where(places < fixed, places, passed)]].set(jnp.asarray(tallies, jnp.int32))

    tallies = jnp.where(number % 4 == 0, named(packed, number // 4), named(common, number - number // 4 - 1))
    mixed = jax.random.permutation(jax.random.fold_in(own, 3), number_of)
    giver, sink = mixed[0:number_of // 2 * 2:2], mixed[1:number_of // 2 * 2:2]
    margin = jnp.minimum(tallies[giver] - 1, reach - tallies[sink]) // 2
    margin = jnp.where((giver == ranking[0]) | (sink == ranking[0]) | (tallies[sink] == 0), 0, jnp.maximum(margin, 0))
    passed = jax.random.randint(jax.random.fold_in(own, 4), (number_of // 2,), 0, 1 << 20) % (margin + 1)
    tallies = tallies.at[giver].add(-passed).at[sink].add(passed)
    members = jnp.searchsorted(jnp.cumsum(tallies), jnp.arange(rows * top), side="right").astype(jnp.int32)
    listing = members.reshape(top, rows).T
    listing = listing[jax.random.permutation(jax.random.fold_in(own, 1), rows)]
    turn = jax.random.randint(jax.random.fold_in(own, 2), (rows, 1), 0, top)
    return jnp.take_along_axis(listing, (jnp.arange(top)[None, :] + turn) % top, axis=1)


def shares(number_of, total, limit, lean, full):
    loads = [(1 << 20) // math.isqrt(grade ** lean) + 1 for grade in range(1, number_of + 1)]
    largest = limit if full else min(limit, max(-(-total // number_of), total * loads[0] // sum(loads)))
    least = 1 if total - largest >= number_of - 1 else 0
    holding, rest = [largest] + [least] * (number_of - 1), total - largest - least * (number_of - 1)
    while rest > 0:
        free = [i for i in range(1, number_of) if holding[i] < largest] or [i for i in range(1, number_of) if holding[i] < limit]
        whole, remaining = sum([loads[i] for i in free]), rest
        for i in free:
            extra = min(limit - holding[i], max(1, remaining * loads[i] // whole), rest)
            holding[i] = holding[i] + extra
            rest = rest - extra
    return np.array(holding)


def noise(key, dims, scale, most, split=(), kind=jnp.bfloat16):
    level = block_levels(key, dims, split, -0.22, 0.18) if split else 1.0
    entries = jax.random.normal(key, dims, jnp.float32) * scale * level
    return jnp.minimum(jnp.maximum(entries, -most), most).astype(kind)


def setup_inputs(seed: int = 0) -> dict:
    splits = jax.random.split(jax.random.key(seed), 16)
    tokens = noise(splits[0], (BATCH, LENGTH, D), 1.0, 6.0, ((0, 4), (1, 2)))
    norm1_gain = jnp.clip(1.0 + 0.1 * jax.random.normal(splits[1], (D,), jnp.float32), 0.5, 1.5).astype(jnp.bfloat16)
    w_qkv = noise(splits[2], (D, 3, NH * HD), D ** -0.5, 0.125, ((0, 8), (2, 4)))
    b_qkv = noise(splits[3], (3, NH, HD), 0.2, 1.1953125, ((1, 4),))
    w_out = noise(splits[4], (NH * HD, D), (max(1, NH * HD * 32 // LENGTH)) ** -0.5, 0.5, ((0, 4), (1, 8)))
    norm2_gain = jnp.clip(1.0 + 0.1 * jax.random.normal(splits[5], (D,), jnp.float32), 0.5, 1.5).astype(jnp.bfloat16)
    w_router = noise(splits[6], (D, EXPERTS), (4 * D) ** -0.5, 0.0625, ((0, 8),))
    shared_gate = noise(splits[7], (D,), D ** -0.5, 0.125, ((0, 8),))
    w_shared_in = noise(splits[8], (D, 2, FS), D ** -0.5, 0.125, ((0, 8), (2, 4)))
    w_shared_out = noise(splits[9], (FS, D), (max(1, FS // 4)) ** -0.5, 0.15625, ((0, 4), (1, 8)))
    w_expert_in = noise(splits[10], (EXPERTS, D, 2, FFE), D ** -0.5, 0.125, ((0, 8), (1, 4)))
    w_expert_out = noise(splits[11], (EXPERTS, FFE, D), (max(1, FFE * 16 // (EXPERTS * EXPERTS))) ** -0.5, 0.3125, ((0, 8), (2, 4)))
    block_ids = jax.vmap(lambda own: jnp.searchsorted(jnp.cumsum(uneven_parts(own, 2 * LENGTH // BLOCK, LENGTH, BLOCK, 1)), jnp.arange(LENGTH), side="right"))(jax.random.split(splits[12], BATCH)).reshape((BATCH, LENGTH)).astype(jnp.int32)
    expert_ids_keys = jax.random.split(jax.random.fold_in(splits[13], 1), BATCH * LENGTH // TOK_E)
    expert_ids_turns = jax.random.permutation(jax.random.fold_in(splits[13], 3), BATCH * LENGTH // TOK_E)
    expert_ids = jax.vmap(lambda own, number: routed_block(jax.random.fold_in(splits[13], 2), own, number, TOK_E, EXPERTS, TOPK, CAP, 2))(expert_ids_keys, expert_ids_turns).reshape((BATCH, LENGTH, TOPK))
    out_grad = noise(splits[14], (BATCH, LENGTH, D), 1.0, 6.0, ((0, 4), (1, 2)))
    return dict(tokens=tokens, norm1_gain=norm1_gain, w_qkv=w_qkv, b_qkv=b_qkv, w_out=w_out, norm2_gain=norm2_gain, w_router=w_router, shared_gate=shared_gate, w_shared_in=w_shared_in, w_shared_out=w_shared_out, w_expert_in=w_expert_in, w_expert_out=w_expert_out, block_ids=block_ids, expert_ids=expert_ids, out_grad=out_grad)


highest = lax.Precision.HIGHEST
epsilon = 1e-06
rope_base = 1000000.0

@jax.custom_vjp
def low(v):
    return lax.optimization_barrier(v.astype(jnp.bfloat16)).astype(jnp.float32)

@jax.custom_vjp
def low_back(v):
    return v

def low_keep(v):
    return (low(v), None)

def low_pass(kept, grad):
    return (grad,)

def back_keep(v):
    return (v, None)

def back_low(kept, grad):
    return (low(grad),)
low.defvjp(low_keep, low_pass)
low_back.defvjp(back_keep, back_low)

def rotary_tables(positions, head_size):
    exponent = jnp.arange(head_size // 2).astype(jnp.float32) * (2.0 / head_size)
    frequency = rope_base ** (-exponent)
    angles = positions.astype(jnp.float32)[:, None] * frequency[None, :]
    return (jnp.cos(angles)[:, None, :], jnp.sin(angles)[:, None, :])

def rotate(values, cosine, sine_table):
    half_size = values.shape[-1] // 2
    first_half = values[..., :half_size]
    second_half = values[..., half_size:]
    return jnp.concatenate([first_half * cosine - second_half * sine_table, second_half * cosine + first_half * sine_table], axis=-1)

def rms_norm(values, gain):
    inverse = lax.rsqrt(lax.optimization_barrier(jnp.mean(values * values, axis=-1, keepdims=True)) + epsilon)
    return values * inverse * gain

def attend(queries, key_rows, value_rows, block_row):
    length = queries.shape[0]
    rows_block = min(512, length)
    score_scale = HD ** (-0.5)
    query_blocks = queries.reshape(length // rows_block, rows_block, NH, HD)
    id_blocks = block_row.reshape(length // rows_block, rows_block)

    def one_block(pieces):
        query_block, query_ids = pieces
        scores = jnp.einsum('qhd,khd->hqk', query_block, key_rows, precision=highest) * score_scale
        scores = low_back(scores)
        allowed = block_row[None, None, :] <= query_ids[None, :, None]
        scores = jnp.where(allowed, scores, -1e+30)
        row_peak = lax.optimization_barrier(jnp.max(scores, axis=-1, keepdims=True))
        weights = jnp.exp(scores - row_peak)
        weights = low(weights / lax.optimization_barrier(jnp.sum(weights, axis=-1, keepdims=True)))
        return jnp.einsum('hqk,khd->qhd', weights, value_rows, precision=highest)
    outputs = lax.map(jax.checkpoint(one_block), (query_blocks, id_blocks))
    return outputs.reshape(length, NH, HD)

def expert_ranks(flat_ids):
    onehot = (flat_ids[..., None] == jnp.arange(EXPERTS, dtype=jnp.int32)).astype(jnp.int32)
    earlier = jnp.cumsum(onehot, axis=1) - onehot
    return lax.optimization_barrier(jnp.sum(earlier * onehot, axis=-1)).astype(jnp.int32)

def layer(tokens, norm1_gain, w_qkv, b_qkv, w_out, norm2_gain, w_router, shared_gate, w_shared_in, w_shared_out, w_expert_in, w_expert_out, block_ids, expert_ids):
    batch_size, length, model_width = tokens.shape
    normed = low(rms_norm(tokens, norm1_gain))
    linear = jnp.einsum('bld,dtn->bltn', normed, w_qkv, precision=highest) + b_qkv.reshape(3, NH * HD)
    linear = low_back(linear).reshape(batch_size, length, 3, NH, HD)
    cosine, sine_table = rotary_tables(jnp.arange(length), HD)
    queries = low(rotate(linear[:, :, 0], cosine, sine_table))
    key_rows = low(rotate(linear[:, :, 1], cosine, sine_table))
    value_rows = low(linear[:, :, 2])
    mixed_heads = lax.map(lambda pieces: attend(*pieces), (queries, key_rows, value_rows, block_ids))
    mixed_heads = low(low_back(mixed_heads)).reshape(batch_size, length, NH * HD)
    attention = low_back(jnp.einsum('bln,nd->bld', mixed_heads, w_out, precision=highest))
    hidden = tokens + attention
    routed = low(rms_norm(hidden, norm2_gain))
    logits = jnp.einsum('bld,de->ble', routed, w_router, precision=highest)
    probability = jax.nn.softmax(logits, axis=-1)
    gate_values = jnp.take_along_axis(probability, expert_ids, axis=-1)
    total_rows = batch_size * length
    block_count = total_rows // TOK_E
    flat_ids = expert_ids.reshape(block_count, TOK_E * TOPK)
    slot_rank = expert_ranks(flat_ids)
    block_index = jnp.broadcast_to(jnp.arange(block_count, dtype=jnp.int32)[:, None], flat_ids.shape)
    token_index = block_index * TOK_E + jnp.arange(TOK_E * TOPK, dtype=jnp.int32)[None, :] // TOPK
    slot_owner = jnp.full((EXPERTS, block_count, CAP), -1, jnp.int32).at[flat_ids, block_index, slot_rank].set(token_index)
    routed_rows = routed.reshape(total_rows, model_width)
    dispatched = jnp.where((slot_owner >= 0)[..., None], routed_rows[jnp.maximum(slot_owner, 0)], 0.0)
    dispatched = low_back(dispatched)

    def one_expert(pieces):
        expert_rows, weight_in, weight_back = pieces
        expert_rows = expert_rows.reshape(block_count * CAP, model_width)
        gate_up = jnp.dot(expert_rows, weight_in.reshape(model_width, 2 * FFE), precision=highest)
        gate_up = low_back(gate_up).reshape(block_count * CAP, 2, FFE)
        activated = low(jax.nn.silu(gate_up[:, 0]) * gate_up[:, 1])
        result = jnp.dot(activated, weight_back, precision=highest)
        return low(low_back(result)).reshape(block_count, CAP, model_width)
    expert_out = lax.map(jax.checkpoint(one_expert), (dispatched, w_expert_in, w_expert_out))
    picked = expert_out[flat_ids, block_index, slot_rank]
    weighted = gate_values.reshape(block_count, TOK_E, TOPK, 1) * picked.reshape(block_count, TOK_E, TOPK, model_width)
    combined = lax.optimization_barrier(jnp.sum(weighted, axis=2)).reshape(batch_size, length, model_width)
    shared_up = low_back(jnp.einsum('bld,dkf->blkf', routed, w_shared_in, precision=highest))
    shared_act = low(jax.nn.silu(shared_up[:, :, 0]) * shared_up[:, :, 1])
    shared_back = low_back(jnp.einsum('blf,fd->bld', shared_act, w_shared_out, precision=highest))
    shared_logit = jnp.einsum('bld,d->bl', routed, shared_gate, precision=highest)
    return hidden + combined + jax.nn.sigmoid(shared_logit)[..., None] * shared_back

def reference(tokens, norm1_gain, w_qkv, b_qkv, w_out, norm2_gain, w_router, shared_gate, w_shared_in, w_shared_out, w_expert_in, w_expert_out, block_ids, expert_ids, out_grad):
    widened = tuple((array_item.astype(jnp.float32) for array_item in (tokens, norm1_gain, w_qkv, b_qkv, w_out, norm2_gain, w_router, shared_gate, w_shared_in, w_shared_out, w_expert_in, w_expert_out)))

    def forward(*arrays):
        return layer(*arrays, block_ids, expert_ids)
    result, pullback = jax.vjp(forward, *widened)
    gradients = pullback(out_grad.astype(jnp.float32))
    return (result.astype(jnp.bfloat16), gradients[0].astype(jnp.bfloat16), gradients[1].astype(jnp.bfloat16), gradients[2].astype(jnp.bfloat16), gradients[3].astype(jnp.bfloat16), gradients[4].astype(jnp.bfloat16), gradients[5].astype(jnp.bfloat16), gradients[6].astype(jnp.bfloat16), gradients[7].astype(jnp.bfloat16), gradients[8].astype(jnp.bfloat16), gradients[9].astype(jnp.bfloat16), gradients[10].astype(jnp.bfloat16), gradients[11].astype(jnp.bfloat16))
```

```python
from types import SimpleNamespace

import jax
import jax.numpy as jnp
import numpy as np
from jax import lax
from jax.experimental import pallas as pl
from jax.experimental.pallas import tpu as pltpu
from jax.sharding import PartitionSpec as P

highest = lax.Precision.HIGHEST
epsilon = 1e-06
rope_base = 1000000.0
f32 = jnp.float32
bf16 = jnp.bfloat16
DP, CTX, EXP = "dp", "context", "expert"
PLANE, GROUP = (DP, CTX), (CTX, EXP)


def rotary_tables(first_row, row_count, head_size):
    exponent = jnp.arange(head_size // 2).astype(jnp.float32) * (2.0 / head_size)
    frequency = rope_base ** (-exponent)
    positions = (first_row + jnp.arange(row_count, dtype=jnp.int32)).astype(jnp.float32)
    angles = positions[:, None] * frequency[None, :]
    return (jnp.cos(angles)[:, None, :], jnp.sin(angles)[:, None, :])


def rotate(values, cosine, sine_table):
    half_size = values.shape[-1] // 2
    first_half = values[..., :half_size]
    second_half = values[..., half_size:]
    return jnp.concatenate(
        [
            first_half * cosine - second_half * sine_table,
            second_half * cosine + first_half * sine_table,
        ],
        axis=-1,
    )


def rotate_back(grad_values, cosine, sine_table):
    half_size = grad_values.shape[-1] // 2
    first_half = grad_values[..., :half_size]
    second_half = grad_values[..., half_size:]
    return jnp.concatenate(
        [
            first_half * cosine + second_half * sine_table,
            second_half * cosine - first_half * sine_table,
        ],
        axis=-1,
    )


def gated_grads(gate_part, up_part, grad_act):
    sigmoid_gate = jax.nn.sigmoid(gate_part)
    grad_gate = grad_act * up_part * sigmoid_gate * (1.0 + gate_part * (1.0 - sigmoid_gate))
    grad_up = grad_act * gate_part * sigmoid_gate
    return (grad_gate, grad_up)


def masked_scores(queries, all_keys, allowed, score_scale):
    scores = (
        jnp.einsum("qhd,khd->hqk", queries, all_keys, preferred_element_type=jnp.float32)
        * score_scale
    )
    return jnp.where(allowed[None], scores, -1e30)


def fetch_dense(
    norm1_gain, w_qkv, w_out, norm2_gain, w_router, shared_gate, w_shared_in, w_shared_out
):
    return (
        lax.all_gather(norm1_gain, PLANE, axis=0, tiled=True),
        lax.all_gather(w_qkv, PLANE, axis=0, tiled=True),
        lax.all_gather(w_out, PLANE, axis=1, tiled=True),
        lax.all_gather(norm2_gain, PLANE, axis=0, tiled=True),
        lax.all_gather(w_router, PLANE, axis=0, tiled=True),
        lax.all_gather(shared_gate, PLANE, axis=0, tiled=True),
        lax.all_gather(w_shared_in, PLANE, axis=0, tiled=True),
        lax.all_gather(w_shared_out, PLANE, axis=1, tiled=True),
    )


def fetch_experts(w_expert_in, w_expert_out):
    return (
        lax.all_gather(w_expert_in, DP, axis=1, tiled=True),
        lax.all_gather(w_expert_out, DP, axis=2, tiled=True),
    )


def fetch_keys(key_rows, value_rows):
    return (
        lax.all_gather(key_rows, CTX, axis=0, tiled=True),
        lax.all_gather(value_rows, CTX, axis=0, tiled=True),
    )


def general_body(
    tokens,
    norm1_gain,
    w_qkv,
    b_qkv,
    w_out,
    norm2_gain,
    w_router,
    shared_gate,
    w_shared_in,
    w_shared_out,
    w_expert_in,
    w_expert_out,
    block_ids,
    expert_ids,
    out_grad,
):
    token_rows = tokens[0]
    rows_local, model_width = token_rows.shape
    lane_count = lax.axis_size(EXP)
    quarter = rows_local // lane_count
    first_row = lax.axis_index(CTX) * rows_local
    own_row = lax.axis_index(EXP) * quarter
    sequence_ids = block_ids[0]
    chosen = expert_ids[0]
    top_count = chosen.shape[1]
    heads_local = b_qkv.shape[1]
    head_size = b_qkv.shape[2]
    dense_full = fetch_dense(
        norm1_gain, w_qkv, w_out, norm2_gain, w_router, shared_gate, w_shared_in, w_shared_out
    )
    (
        gain_one,
        qkv_weight,
        out_weight,
        gain_two,
        router_weight,
        gate_vector,
        shared_in,
        shared_out,
    ) = dense_full
    expert_pair = fetch_experts(w_expert_in, w_expert_out)
    expert_in = expert_pair[0][0]
    expert_back = expert_pair[1][0]
    ffe_width = expert_in.shape[2]
    experts = router_weight.shape[1]
    capacity = max(2, 3 * quarter * top_count // (2 * experts))
    tokens_wide = token_rows.astype(jnp.float32)
    inverse_one = lax.rsqrt(jnp.mean(tokens_wide * tokens_wide, axis=-1, keepdims=True) + epsilon)
    normed = (tokens_wide * inverse_one * gain_one.astype(jnp.float32)).astype(jnp.bfloat16)
    linear = jnp.dot(
        normed, qkv_weight.reshape(model_width, -1), preferred_element_type=jnp.float32
    )
    linear = linear.reshape(rows_local, 3, heads_local, head_size) + b_qkv.astype(jnp.float32)[None]
    cosine, sine_table = rotary_tables(first_row, rows_local, head_size)
    queries = rotate(linear[:, 0], cosine, sine_table).astype(jnp.bfloat16)
    key_rows = rotate(linear[:, 1], cosine, sine_table).astype(jnp.bfloat16)
    value_rows = linear[:, 2].astype(jnp.bfloat16)
    all_keys, all_values = fetch_keys(key_rows, value_rows)
    query_ids = lax.dynamic_slice_in_dim(sequence_ids, first_row, rows_local)
    allowed = sequence_ids[None, :] <= query_ids[:, None]
    score_scale = head_size ** (-0.5)
    scores = masked_scores(queries, all_keys, allowed, score_scale)
    row_peak = jnp.max(scores, axis=-1, keepdims=True)
    log_total = row_peak + jnp.log(jnp.sum(jnp.exp(scores - row_peak), axis=-1, keepdims=True))
    weights = jnp.exp(scores - log_total).astype(jnp.bfloat16)
    attended = jnp.einsum("hqk,khd->qhd", weights, all_values, preferred_element_type=jnp.float32)
    attended_low = attended.astype(jnp.bfloat16).reshape(rows_local, heads_local * head_size)
    attention = lax.psum(
        jnp.dot(attended_low, out_weight, preferred_element_type=jnp.float32).astype(jnp.bfloat16),
        EXP,
    ).astype(jnp.float32)
    hidden = tokens_wide + attention
    inverse_two = lax.rsqrt(jnp.mean(hidden * hidden, axis=-1, keepdims=True) + epsilon)
    routed = (hidden * inverse_two * gain_two.astype(jnp.float32)).astype(jnp.bfloat16)
    shared_up = jnp.dot(
        routed, shared_in.reshape(model_width, -1), preferred_element_type=jnp.float32
    )
    shared_up = shared_up.reshape(rows_local, 2, -1)
    shared_act = (jax.nn.silu(shared_up[:, 0]) * shared_up[:, 1]).astype(jnp.bfloat16)
    shared_part = jnp.dot(shared_act, shared_out, preferred_element_type=jnp.float32)
    shared_rows = lax.psum_scatter(
        shared_part.astype(jnp.bfloat16), EXP, scatter_dimension=0, tiled=True
    ).astype(jnp.float32)
    shared_weight = jax.nn.sigmoid(jnp.dot(routed, gate_vector, preferred_element_type=jnp.float32))
    routed_own = lax.dynamic_slice_in_dim(routed, own_row, quarter)
    hidden_own = lax.dynamic_slice_in_dim(hidden, own_row, quarter)
    weight_own = lax.dynamic_slice_in_dim(shared_weight, own_row, quarter)
    logits = jnp.dot(routed_own, router_weight, preferred_element_type=jnp.float32)
    probability = jax.nn.softmax(logits, axis=-1)
    expert_match = (chosen[..., None] == jnp.arange(experts, dtype=jnp.int32)).astype(jnp.float32)
    gate_values = jnp.sum(probability[:, None, :] * expert_match, axis=-1)
    flat_ids = chosen.reshape(-1)
    onehot = (flat_ids[:, None] == jnp.arange(experts, dtype=jnp.int32)).astype(jnp.int32)
    slot_rank = jnp.sum((jnp.cumsum(onehot, axis=0) - onehot) * onehot, axis=-1)
    slot_index = flat_ids * capacity + slot_rank
    placement = (slot_index[:, None] == jnp.arange(experts * capacity, dtype=jnp.int32)).astype(
        jnp.bfloat16
    )
    repeated = jnp.repeat(routed_own, top_count, axis=0)
    outgoing = jnp.einsum("sr,sd->rd", placement, repeated, preferred_element_type=jnp.float32)
    outgoing = outgoing.astype(jnp.bfloat16).reshape(experts, capacity, model_width)
    incoming = lax.all_to_all(
        outgoing, GROUP, split_axis=0, concat_axis=0, tiled=True
    )
    flat_rows = incoming.reshape(-1, model_width)
    gate_up = jnp.dot(
        flat_rows, expert_in.reshape(model_width, -1), preferred_element_type=jnp.float32
    ).reshape(-1, 2, ffe_width)
    activated = (jax.nn.silu(gate_up[:, 0]) * gate_up[:, 1]).astype(jnp.bfloat16)
    result = jnp.dot(activated, expert_back, preferred_element_type=jnp.float32).astype(
        jnp.bfloat16
    )
    expert_result = result.reshape(incoming.shape)
    returned = lax.all_to_all(
        expert_result, GROUP, split_axis=0, concat_axis=0, tiled=True
    )
    picked = jnp.dot(
        placement, returned.reshape(-1, model_width), preferred_element_type=jnp.float32
    )
    picked = picked.reshape(quarter, top_count, model_width)
    combined = jnp.sum(gate_values[..., None] * picked, axis=1)
    result_rows = hidden_own + combined + weight_own[:, None] * shared_rows
    output = result_rows.astype(jnp.bfloat16)[None]
    (
        gain_one_b,
        qkv_weight_b,
        out_weight_b,
        gain_two_b,
        router_weight_b,
        gate_vector_b,
        shared_in_b,
        shared_out_b,
    ) = dense_full
    expert_in_b = expert_pair[0][0]
    expert_back_b = expert_pair[1][0]
    grad_full = out_grad[0].astype(jnp.float32)
    grad_own = lax.dynamic_slice_in_dim(grad_full, own_row, quarter)
    shared_grad = (shared_weight[:, None] * grad_full).astype(jnp.bfloat16)
    grad_shared_out = jnp.einsum(
        "tf,td->fd", shared_act, shared_grad, preferred_element_type=jnp.float32
    )
    grad_shared_act = jnp.einsum(
        "td,fd->tf", shared_grad, shared_out_b, preferred_element_type=jnp.float32
    )
    shared_gate_grad, shared_up_grad = gated_grads(
        shared_up[:, 0], shared_up[:, 1], grad_shared_act
    )
    grad_shared_up = jnp.stack([shared_gate_grad, shared_up_grad], axis=1).astype(jnp.bfloat16)
    grad_shared_in = jnp.einsum(
        "td,tkf->dkf", routed, grad_shared_up, preferred_element_type=jnp.float32
    )
    grad_routed = jnp.einsum(
        "tkf,dkf->td", grad_shared_up, shared_in_b, preferred_element_type=jnp.float32
    )
    gate_slope = jnp.sum(grad_own * shared_rows, axis=-1) * weight_own * (1.0 - weight_own)
    grad_gate_vector = jnp.dot(gate_slope, routed_own.astype(jnp.float32), precision=highest)
    grad_own_routed = gate_slope[:, None] * gate_vector_b.astype(jnp.float32)[None]
    grad_gates = jnp.sum(grad_own[:, None, :] * picked, axis=-1)
    grad_slots = (
        (gate_values[..., None] * grad_own[:, None, :])
        .astype(jnp.bfloat16)
        .reshape(-1, model_width)
    )
    grad_send = jnp.einsum("sr,sd->rd", placement, grad_slots, preferred_element_type=jnp.float32)
    grad_send = grad_send.astype(jnp.bfloat16).reshape(experts, capacity, model_width)
    grad_arrived = lax.all_to_all(
        grad_send, GROUP, split_axis=0, concat_axis=0, tiled=True
    )
    arrived_rows = incoming.reshape(-1, model_width)
    arrived_grad = grad_arrived.reshape(-1, model_width)
    expert_up = jnp.dot(
        arrived_rows, expert_in_b.reshape(model_width, -1), preferred_element_type=jnp.float32
    ).reshape(-1, 2, ffe_width)
    expert_act = (jax.nn.silu(expert_up[:, 0]) * expert_up[:, 1]).astype(jnp.bfloat16)
    grad_expert_back = jnp.einsum(
        "rf,rd->fd", expert_act, arrived_grad, preferred_element_type=jnp.float32
    )
    grad_expert_act = jnp.einsum(
        "rd,fd->rf", arrived_grad, expert_back_b, preferred_element_type=jnp.float32
    )
    expert_gate_grad, expert_up_grad = gated_grads(
        expert_up[:, 0], expert_up[:, 1], grad_expert_act
    )
    grad_expert_up = jnp.stack([expert_gate_grad, expert_up_grad], axis=1).astype(jnp.bfloat16)
    grad_expert_in = jnp.einsum(
        "rd,rkf->dkf", arrived_rows, grad_expert_up, preferred_element_type=jnp.float32
    )
    grad_arrived_rows = jnp.einsum(
        "rkf,dkf->rd", grad_expert_up, expert_in_b, preferred_element_type=jnp.float32
    )
    grad_arrived_rows = grad_arrived_rows.astype(jnp.bfloat16).reshape(
        experts, capacity, model_width
    )
    grad_returned = lax.all_to_all(
        grad_arrived_rows, GROUP, split_axis=0, concat_axis=0, tiled=True
    )
    grad_copies = jnp.dot(
        placement, grad_returned.reshape(-1, model_width), preferred_element_type=jnp.float32
    )
    grad_own_routed = grad_own_routed + jnp.sum(
        grad_copies.reshape(quarter, top_count, model_width), axis=1
    )
    grad_probability = jnp.sum(grad_gates[..., None] * expert_match, axis=1)
    grad_logits = probability * (
        grad_probability - jnp.sum(probability * grad_probability, axis=-1, keepdims=True)
    )
    grad_router = jnp.dot(routed_own.astype(jnp.float32).T, grad_logits, precision=highest)
    grad_own_routed = grad_own_routed + jnp.dot(
        grad_logits, router_weight_b.astype(jnp.float32).T, precision=highest
    )
    own_part = lax.dynamic_slice_in_dim(grad_routed, own_row, quarter) + grad_own_routed
    grad_routed = lax.dynamic_update_slice_in_dim(grad_routed, own_part, own_row, 0)
    grad_routed, grad_router, grad_gate_vector = (
        lax.psum(grad_routed.astype(jnp.bfloat16), EXP).astype(jnp.float32),
        lax.psum(grad_router.astype(jnp.bfloat16), EXP).astype(jnp.float32),
        lax.psum(grad_gate_vector.astype(jnp.bfloat16), EXP).astype(jnp.float32),
    )
    scaled_two = grad_routed * gain_two_b.astype(jnp.float32)
    grad_gain_two = jnp.sum(grad_routed * hidden * inverse_two, axis=0)
    grad_hidden = (
        grad_full
        + inverse_two * scaled_two
        - hidden * inverse_two**3 * jnp.mean(scaled_two * hidden, axis=-1, keepdims=True)
    )
    grad_hidden_low = grad_hidden.astype(jnp.bfloat16)
    grad_out_weight = jnp.einsum(
        "tn,td->nd", attended_low, grad_hidden_low, preferred_element_type=jnp.float32
    )
    grad_attended = jnp.einsum(
        "td,nd->tn", grad_hidden_low, out_weight_b, preferred_element_type=jnp.float32
    )
    grad_attended = grad_attended.astype(jnp.bfloat16).reshape(rows_local, heads_local, head_size)
    back_keys, back_values = (all_keys, all_values)
    scores_again = masked_scores(queries, back_keys, allowed, score_scale)
    weights_wide = jnp.exp(scores_again - log_total)
    row_delta = jnp.sum(grad_attended.astype(jnp.float32) * attended, axis=-1).T
    grad_weights = jnp.einsum(
        "qhd,khd->hqk", grad_attended, back_values, preferred_element_type=jnp.float32
    )
    grad_scores = (weights_wide * (grad_weights - row_delta[..., None])).astype(jnp.bfloat16)
    grad_queries = (
        jnp.einsum("hqk,khd->qhd", grad_scores, back_keys, preferred_element_type=jnp.float32)
        * score_scale
    )
    grad_keys = (
        jnp.einsum("hqk,qhd->khd", grad_scores, queries, preferred_element_type=jnp.float32)
        * score_scale
    )
    grad_values = jnp.einsum(
        "hqk,qhd->khd",
        weights_wide.astype(jnp.bfloat16),
        grad_attended,
        preferred_element_type=jnp.float32,
    )
    grad_keys, grad_values = (
        lax.psum_scatter(
            grad_keys.astype(jnp.bfloat16), CTX, scatter_dimension=0, tiled=True
        ).astype(jnp.float32),
        lax.psum_scatter(
            grad_values.astype(jnp.bfloat16), CTX, scatter_dimension=0, tiled=True
        ).astype(jnp.float32),
    )
    grad_linear = jnp.stack(
        [
            rotate_back(grad_queries, cosine, sine_table),
            rotate_back(grad_keys, cosine, sine_table),
            grad_values,
        ],
        axis=1,
    )
    grad_linear = grad_linear.astype(jnp.bfloat16)
    grad_bias = jnp.sum(grad_linear.astype(jnp.float32), axis=0)
    grad_flat = grad_linear.reshape(rows_local, -1)
    grad_qkv = jnp.einsum(
        "td,tn->dn", normed, grad_flat, preferred_element_type=jnp.float32
    ).reshape(qkv_weight_b.shape)
    grad_normed = jnp.einsum(
        "tn,dn->td",
        grad_flat,
        qkv_weight_b.reshape(model_width, -1),
        preferred_element_type=jnp.float32,
    )
    grad_normed = lax.psum(grad_normed.astype(jnp.bfloat16), EXP).astype(jnp.float32)
    scaled_one = grad_normed * gain_one_b.astype(jnp.float32)
    grad_gain_one = jnp.sum(grad_normed * tokens_wide * inverse_one, axis=0)
    grad_tokens = (
        grad_hidden
        + inverse_one * scaled_one
        - tokens_wide * inverse_one**3 * jnp.mean(scaled_one * tokens_wide, axis=-1, keepdims=True)
    )
    grad_tokens_own = lax.dynamic_slice_in_dim(grad_tokens, own_row, quarter).astype(jnp.bfloat16)[
        None
    ]
    dense_sums = (
        lax.psum_scatter(
            grad_gain_one.astype(jnp.bfloat16), PLANE, scatter_dimension=0, tiled=True
        ).astype(jnp.float32),
        lax.psum_scatter(
            grad_qkv.astype(jnp.bfloat16), PLANE, scatter_dimension=0, tiled=True
        ).astype(jnp.float32),
        lax.psum_scatter(
            grad_bias.astype(jnp.bfloat16), PLANE, scatter_dimension=2, tiled=True
        ).astype(jnp.float32),
        lax.psum_scatter(
            grad_out_weight.astype(jnp.bfloat16), PLANE, scatter_dimension=1, tiled=True
        ).astype(jnp.float32),
        lax.psum_scatter(
            grad_gain_two.astype(jnp.bfloat16), PLANE, scatter_dimension=0, tiled=True
        ).astype(jnp.float32),
        lax.psum_scatter(
            grad_router.astype(jnp.bfloat16), PLANE, scatter_dimension=0, tiled=True
        ).astype(jnp.float32),
        lax.psum_scatter(
            grad_gate_vector.astype(jnp.bfloat16),
            PLANE,
            scatter_dimension=0,
            tiled=True,
        ).astype(jnp.float32),
        lax.psum_scatter(
            grad_shared_in.astype(jnp.bfloat16), PLANE, scatter_dimension=0, tiled=True
        ).astype(jnp.float32),
        lax.psum_scatter(
            grad_shared_out.astype(jnp.bfloat16), PLANE, scatter_dimension=1, tiled=True
        ).astype(jnp.float32),
    )
    expert_sums = (
        lax.psum_scatter(
            grad_expert_in[None].astype(jnp.bfloat16), DP, scatter_dimension=1, tiled=True
        ).astype(jnp.float32),
        lax.psum_scatter(
            grad_expert_back[None].astype(jnp.bfloat16), DP, scatter_dimension=2, tiled=True
        ).astype(jnp.float32),
    )
    return (
        output,
        grad_tokens_own,
        dense_sums[0].astype(jnp.bfloat16),
        dense_sums[1].astype(jnp.bfloat16),
        dense_sums[2].astype(jnp.bfloat16),
        dense_sums[3].astype(jnp.bfloat16),
        dense_sums[4].astype(jnp.bfloat16),
        dense_sums[5].astype(jnp.bfloat16),
        dense_sums[6].astype(jnp.bfloat16),
        dense_sums[7].astype(jnp.bfloat16),
        dense_sums[8].astype(jnp.bfloat16),
        expert_sums[0].astype(jnp.bfloat16),
        expert_sums[1].astype(jnp.bfloat16),
    )


MIB = 1 << 20
MESH = pl.DeviceIdType.MESH


def dot_nn(a, b):
    return lax.dot_general(a, b, (((1,), (0,)), ((), ())), preferred_element_type=f32)


def dot_nt(a, b):
    return lax.dot_general(a, b, (((1,), (1,)), ((), ())), preferred_element_type=f32)


def dot_tn(a, b):
    return lax.dot_general(a, b, (((0,), (0,)), ((), ())), preferred_element_type=f32)


def place():
    i = lax.axis_index(DP)
    return i // 2, i % 2, lax.axis_index(CTX), lax.axis_index(EXP)


def owner_dense(r):
    x, c, y, _ = place()
    return (((x + r % 2) % 2) * 2 + (c + r // 4) % 2) * 2 + (y + (r // 2) % 2) % 2


def owner_expert(r):
    x, c, _, _ = place()
    return ((x + r % 2) % 2) * 2 + (c + r // 2) % 2


def near(d):
    z = lax.axis_index(EXP)
    return ((z // 2 + d // 2) % 2) * 2 + (z % 2 + d % 2) % 2


def peers():
    x, c, y, _ = place()
    far = [{EXP: near(d)} for d in (1, 2, 3)]
    return {DP: ((x + 1) % 2) * 2 + c}, {CTX: 1 - y}, {DP: x * 2 + (c + 1) % 2}, far


def greet(devices):
    barrier = pltpu.get_barrier_semaphore()
    for device in devices:
        pl.semaphore_signal(barrier, 1, device_id=device, device_id_type=MESH)
    pl.semaphore_wait(barrier, len(devices))


class Wire:
    def __init__(self, wires, ends, device):
        self.ends, self.device, self.sent = ends, device, False
        self.send, self.recv, self.k = wires.send, wires.recv, len(wires.copies)
        wires.copies.append(self)

    def copy(self):
        source, target = self.ends()
        return pltpu.make_async_remote_copy(
            src_ref=source,
            dst_ref=target,
            send_sem=self.send.at[self.k],
            recv_sem=self.recv.at[self.k],
            device_id=self.device,
            device_id_type=MESH,
        )

    def start(self):
        self.copy().start()
        return self

    def wait_recv(self):
        self.copy().wait_recv()

    def wait_send(self):
        self.copy().wait_send()
        self.sent = True


class Wires:
    def __init__(self, send, recv):
        self.send, self.recv, self.copies = send, recv, []

    def add(self, ends, device):
        return Wire(self, ends, device)

    def go(self, ends, device):
        return Wire(self, ends, device).start()

    def drain(self):
        for wire in self.copies:
            if not wire.sent:
                wire.wait_send()


class Loads:
    def __init__(self, sems):
        self.sems, self.count = sems, 0

    def go(self, source, target):
        copy = pltpu.make_async_copy(source, target, self.sems.at[self.count])
        self.count += 1
        copy.start()
        return copy


def cols(ref, block, width):
    return ref[:, pl.ds(pl.multiple_of(block * width, width), width)]


def piece(ref, d, rows):
    return ref[pl.ds(pl.multiple_of(near(d) * rows, rows), rows), :]


def turn(values, cosine, sine):
    return values * cosine + pltpu.roll(values, 64, 1) * sine


def turn_back(values, cosine, sine):
    return values * cosine - pltpu.roll(values, 64, 1) * sine


def gated(gate, up, grad_act):
    s = jax.nn.sigmoid(gate)
    act = gate * s
    return act * up, grad_act * up * s * (1.0 + gate * (1.0 - s)), grad_act * act


def softmax_parts(q, k_own, k_oth, mask_own, mask_oth):
    scale = 128 ** (-0.5)
    s_own = jnp.where(mask_own, dot_nt(q, k_own) * scale, -1e30)
    s_oth = jnp.where(mask_oth, dot_nt(q, k_oth) * scale, -1e30)
    peak = jnp.maximum(
        jnp.max(s_own, axis=-1, keepdims=True), jnp.max(s_oth, axis=-1, keepdims=True)
    )
    e_own = jnp.exp(s_own - peak)
    e_oth = jnp.exp(s_oth - peak)
    total = jnp.sum(e_own, axis=-1, keepdims=True) + jnp.sum(e_oth, axis=-1, keepdims=True)
    back = 1.0 / total
    return e_own * back, e_oth * back


def split3(v):
    high = v.astype(bf16).astype(f32)
    mid = (v - high).astype(bf16).astype(f32)
    return high, mid, v - high - mid


def probabilities(rows, small):
    logits = dot_nt(rows, small[...])
    lane = lax.broadcasted_iota(jnp.int32, logits.shape, 1)
    logits = jnp.where((lane >= 3) & (lane < 11), logits, -1e30)
    e = jnp.exp(logits - jnp.max(logits, axis=-1, keepdims=True))
    return e / jnp.sum(e, axis=-1, keepdims=True), lane


ARRIVAL = (0, 4, 1, 5, 2, 6, 3, 7)


class Spread:
    def __init__(self, wires, own, slots, dense):
        x, y, core, _ = peers()
        self.slots, self.own, self.copies = slots, own, {}

        def ends(r, target):
            return lambda: (self.block(r), slots.at[target])

        self.copies[1] = wires.add(ends(0, 1), x)
        if dense:
            self.copies[2] = wires.add(ends(0, 2), y)
            self.copies[3] = wires.add(ends(1, 3), y)
        side = 4 if dense else 2
        for r in range(side):
            self.copies[side + r] = wires.add(ends(r, side + r), core)

    def block(self, r):
        return self.own() if r == 0 else self.slots.at[r]

    def start(self, r):
        self.copies[r].start()

    def wait(self, r):
        self.copies[r].wait_recv()


V, A = "vmem", "any"


def call(kernel, number, ins, outs, scratch, vmem, flops, traffic):
    def spec(kind):
        return pl.BlockSpec(memory_space=pl.ANY if kind == A else pltpu.VMEM)

    names = list(ins) + list(outs) + list(scratch)

    def run(*refs):
        kernel(SimpleNamespace(**dict(zip(names, refs))))

    made = pl.pallas_call(
        run,
        out_shape=tuple(jax.ShapeDtypeStruct(o[0], o[1]) for o in outs.values()),
        in_specs=[spec(i[1]) for i in ins.values()],
        out_specs=tuple(spec(o[2]) for o in outs.values()),
        scratch_shapes=list(scratch.values()),
        compiler_params=pltpu.CompilerParams(
            vmem_limit_bytes=vmem * MIB, collective_id=number, has_side_effects=True
        ),
        cost_estimate=pl.CostEstimate(flops=flops, bytes_accessed=traffic, transcendentals=0),
    )(*[i[0] for i in ins.values()])
    return SimpleNamespace(**dict(zip(outs, made)))


def own_rows(total, hidden, routed, g, small, high_o, low_o, vec_o):
    extra = total[:, 2048:2176]
    wide = routed.astype(f32)
    prob, _ = probabilities(routed, small)
    sw = jax.nn.sigmoid(jnp.sum(wide * small[2:3, :].astype(f32), axis=-1, keepdims=True))
    slope = jnp.sum(extra[:, 48:96], axis=-1, keepdims=True) * sw * (1.0 - sw)
    dgate = [
        extra[:, e : e + 1] + extra[:, 16 + e : 17 + e] + extra[:, 32 + e : 33 + e]
        for e in range(8)
    ]
    probs = [prob[:, 3 + e : 4 + e] for e in range(8)]
    mean = sum(p * d for p, d in zip(probs, dgate))
    grad = total[:, 0:2048] + slope * small[2:3, :].astype(f32)
    vec_o[...] = jnp.zeros_like(vec_o)
    vec_o[2:3, :] = jnp.sum(slope * wide, axis=0, keepdims=True)
    for e in range(8):
        dlogit = probs[e] * (dgate[e] - mean)
        grad += dlogit * small[3 + e : 4 + e, :].astype(f32)
        vec_o[3 + e : 4 + e, :] = jnp.sum(dlogit * wide, axis=0, keepdims=True)
    inv = lax.rsqrt(jnp.mean(hidden * hidden, axis=-1, keepdims=True) + epsilon)
    vec_o[1:2, :] = jnp.sum(grad * hidden * inv, axis=0, keepdims=True)
    scaled = grad * small[1:2, :].astype(f32)
    mean = jnp.mean(scaled * hidden, axis=-1, keepdims=True)
    high = g.astype(f32) + inv * scaled - hidden * (inv * inv * inv * mean)
    high_o[...] = high
    low_o[...] = high.astype(bf16)


def layer_kernel(k):
    x_dev, y_dev, core_dev, z_dev = peers()
    wires, loads = Wires(k.send_sems, k.recv_sems), Loads(k.load_sems)
    greet([x_dev, y_dev, core_dev] + z_dev)
    y = lax.axis_index(CTX)
    mine = y * 4 + lax.axis_index(EXP)

    def to_z(make):
        return [wires.go(make(d), z_dev[d - 1]) for d in (1, 2, 3)]

    vec = Spread(wires, lambda: k.w_v, k.s_v, True)
    qkv = Spread(wires, lambda: k.w_q, k.s_q, True)
    out = Spread(wires, lambda: k.w_o, k.s_o, True)
    eg = Spread(wires, lambda: k.split_ei.at[0], k.s_eg, False)
    eu = Spread(wires, lambda: k.split_ei.at[1], k.s_eu, False)
    ed = Spread(wires, lambda: k.w_ed, k.s_ed, False)
    sg = Spread(wires, lambda: k.split_si.at[0], k.s_sg, True)
    su = Spread(wires, lambda: k.split_si.at[1], k.s_su, True)
    sd = Spread(wires, lambda: k.w_sd, k.s_sd, True)
    first, expert, shared = (vec, qkv), (eg, eu, ed), (sg, su, sd)
    k.w_v[...] = jnp.zeros_like(k.w_v)
    for m, vector in enumerate((k.gain_one, k.gain_two, k.gate_vector)):
        k.w_v[m : m + 1, :] = vector[...].reshape(1, 256)
    k.w_v[3:11, :] = k.router[...]
    for s in first + (out, ed):
        s.start(1)
    for s in first:
        s.start(2)
    for s in first + (out,):
        s.start(4)
    k.col[0:128, :] = jnp.full((128, 128), -1.0, f32)
    k.col[0:4, 0:64] = k.ids_own[...].astype(f32)
    k.ids[0, 0:64, :] = k.col[0:128, :].T[0:64, :]
    ids_y = wires.go(lambda: (k.ids.at[0, pl.ds(0, 64), :], k.ids_y), y_dev)
    k.g_piece[...] = piece(k.g_own, 0, 64)
    g_y = wires.go(lambda: (k.g_piece, k.g_oth.at[0]), y_dev)
    k.s_v[0] = k.w_v[...]
    k.col[...] = jnp.broadcast_to(k.blocks[...].astype(f32), (128, 512)).T
    for target, half in ((k.ids_near, y), (k.ids_far, 1 - y)):
        for d in range(4):
            at = pl.ds(pl.multiple_of(half * 256 + near(d) * 64, 64), 64)
            k.ids_q[d * 64 : (d + 1) * 64, :] = k.col[at, :]
        target[...] = k.ids_q[...].T[0:8, :]
    for d in range(4):
        at = pl.ds(pl.multiple_of(y * 256 + near(d) * 64, 64), 64)
        to = slice(d * 64, (d + 1) * 64)
        k.ids_q[to, :] = k.col[at, :]
        k.cs[to, :] = k.cs_all[at, :]
        k.sn[to, :] = k.sn_all[at, :]
    later = []

    def attention_part(scaled, acc, w, low_w, mixed, apart):
        held, held_out = {}, []

        def bring(r):
            held[r] = loads.go(qkv.block(r), w.at[r])

        def bring_out(r):
            held_out.append(loads.go(out.block(r), low_w.at[r]))

        raw = [loads.go(k.w_ei.at[pl.ds(256 * m, 256)], mixed.at[m]) for m in range(2)]
        raw.append(loads.go(k.w_si, mixed.at[2]))
        bring(0)
        for d in range(4):
            t = piece(k.tok, d, 64).astype(f32)
            inv = lax.rsqrt(jnp.mean(t * t, axis=-1, keepdims=True) + epsilon)
            scaled[d * 64 : (d + 1) * 64, :] = t * inv
            k.inv1[d * 64 : (d + 1) * 64, :] = inv
        for m in range(3):
            for h in range(4):
                at = slice(h * 128, (h + 1) * 128)
                line = k.bias[m, h : h + 1, :].astype(f32)
                acc[m, :, at] = jnp.broadcast_to(line, (256, 128))

        def take_apart(m):
            raw[m].wait()
            target = k.split_si if m == 2 else k.split_ei
            to = pl.ds(0 if m == 2 else 256 * m, 256)
            done = []
            for n in range(2):
                apart[m, n] = mixed[m, :, n, :]
                done.append(loads.go(apart.at[m, n], target.at[n, to, :]))
            return done

        done = take_apart(0) + take_apart(1)
        for copy in done:
            copy.wait()
        for s in (eg, eu):
            s.start(1)
        for s in expert:
            s.start(2)

        def block(r):
            held[r].wait()
            o = owner_dense(r)
            vectors = k.s_v[r]
            k.small[:, pl.ds(pl.multiple_of(o * 256, 256), 256)] = vectors
            normed = (cols(scaled, o, 256) * vectors[0:1, :].astype(f32)).astype(bf16)
            target = k.n_keep if r < 4 else k.n_send
            target[:, (r % 4) * 256 : (r % 4 + 1) * 256] = normed
            for m in range(3):
                acc[m] += dot_nn(normed, w[r, m * 256 : (m + 1) * 256, :])

        def arrived(r, onward=()):
            for s in first:
                s.wait(r)
                for t in onward:
                    s.start(t)
            bring(r)

        arrived(4)
        block(0)
        block(4)
        arrived(1, (3, 5))
        out.start(2)
        arrived(2, (6,))
        block(1)
        arrived(5)
        block(5)
        arrived(6)
        block(2)
        block(6)
        for copy in take_apart(2):
            copy.wait()
        for s in shared:
            s.start(1)
        for s in shared:
            s.start(4)
        ids_y.wait_recv()
        k.ids[0, 64:128, :] = k.ids_y[...]
        g_y.wait_recv()
        later.extend(to_z(lambda d: lambda: (k.ids.at[0], k.ids.at[d])))
        later.extend(to_z(lambda d: lambda: (k.g_oth.at[0], k.g_oth.at[d])))
        bring_out(0)
        out.wait(4)
        bring_out(4)
        out.wait(1)
        out.start(5)
        bring_out(1)
        arrived(3, (7,))
        block(3)
        arrived(7)
        block(7)
        for h in range(4):
            at = slice(h * 128, (h + 1) * 128)
            k.kv[0:256, at] = turn(acc[1, :, at], k.cs[...], k.sn[...]).astype(bf16)
        k.kv[256:512, :] = acc[2].astype(bf16)
        kv_y = wires.go(lambda: (k.kv, k.kv_oth), y_dev)
        out.start(3)
        sg.start(2)
        su.start(2)
        for h in range(4):
            at = slice(h * 128, (h + 1) * 128)
            k.q[:, at] = turn(acc[0, :, at], k.cs[...], k.sn[...]).astype(bf16)
        out.wait(5)
        bring_out(5)
        out.wait(2)
        out.start(6)
        bring_out(2)
        kv_y.wait_recv()
        mask_own = k.ids_near[0:1, :] <= k.ids_q[:, 0:1]
        mask_oth = k.ids_far[0:1, :] <= k.ids_q[:, 0:1]
        for h in range(4):
            at = slice(h * 128, (h + 1) * 128)
            w_own, w_oth = softmax_parts(
                k.q[:, at], k.kv[0:256, at], k.kv_oth[0:256, at], mask_own, mask_oth
            )
            value = dot_nn(w_own.astype(bf16), k.kv[256:512, at])
            value += dot_nn(w_oth.astype(bf16), k.kv_oth[256:512, at])
            k.low[:, at] = value.astype(bf16)
        out.wait(6)
        bring_out(6)
        out.wait(3)
        out.start(7)
        bring_out(3)
        out.wait(7)
        bring_out(7)
        for copy in held_out:
            copy.wait()
        for r in range(8):
            part = dot_nn(k.low[...], low_w[r]).astype(bf16)
            at = pl.ds(pl.multiple_of(owner_dense(r) * 256, 256), 256)
            for d in range(4):
                k.att_send[d, :, at] = part[d * 64 : (d + 1) * 64, :]

    pl.run_scoped(
        attention_part,
        pltpu.VMEM((256, 2048), f32),
        pltpu.VMEM((3, 256, 512), f32),
        pltpu.VMEM((8, 768, 512), bf16),
        pltpu.VMEM((8, 512, 256), bf16),
        pltpu.VMEM((3, 256, 2, 1408), bf16),
        pltpu.VMEM((3, 2, 256, 1408), bf16),
    )
    att_z = to_z(lambda d: lambda: (k.att_send.at[d], k.att.at[d - 1]))
    swap_n = wires.go(lambda: (k.n_send, k.n_x), core_dev)
    swap_low = wires.go(lambda: (k.low, k.low_x), core_dev)
    parts = SimpleNamespace(started=False)

    def expert_part(wg, wu, wd, slopes, acc, up, keep, send):
        group = []

        def gather(s, w):
            group.append(loads.go(s.block(0), w.at[0]))
            s.wait(2)
            group.append(loads.go(s.block(2), w.at[2]))
            s.wait(1)
            s.start(3)
            group.append(loads.go(s.block(1), w.at[1]))

        def gather_last(s, w):
            s.wait(3)
            group.append(loads.go(s.block(3), w.at[3]))

        gather(ed, wd)
        for copy in att_z:
            copy.wait_recv()
        value = piece(k.tok, 0, 64).astype(f32) + (
            k.att_send[0].astype(f32)
            + k.att[0].astype(f32)
            + k.att[1].astype(f32)
            + k.att[2].astype(f32)
        )
        inv = lax.rsqrt(jnp.mean(value * value, axis=-1, keepdims=True) + epsilon)
        k.hidden[...] = value
        k.rows[0:64, :] = (value * inv * k.small[1:2, :].astype(f32)).astype(bf16)
        own_y = wires.go(
            lambda: (k.rows.at[pl.ds(0, 64), :], k.rows.at[pl.ds(256, 64), :]), y_dev
        )
        sd.start(2)
        own_z = to_z(
            lambda d: lambda: (k.rows.at[pl.ds(0, 64), :], k.rows.at[pl.ds(64 * d, 64), :])
        )
        gather_last(ed, wd)
        gather(eg, wg)
        own_y.wait_recv()
        oth_z = to_z(
            lambda d: lambda: (
                k.rows.at[pl.ds(256, 64), :],
                k.rows.at[pl.ds(256 + 64 * d, 64), :],
            )
        )
        gather_last(eg, wg)
        gather(eu, wu)
        gather_last(eu, wu)

        def g_piece(half, d, at):
            if half:
                return k.g_oth[d, :, at].astype(f32)
            return k.g_own[pl.ds(pl.multiple_of(near(d) * 64, 64), 64), at].astype(f32)

        def route(half):
            chosen = []
            for d in range(4):
                named = (k.ids[d, half * 64 : (half + 1) * 64, :] == mine.astype(f32)).astype(f32)
                chosen.append(jnp.sum(named, axis=-1, keepdims=True))
            chosen = jnp.concatenate(chosen, axis=0)
            prob, lane = probabilities(k.rows[half * 256 : (half + 1) * 256, :], k.small)
            here = jnp.sum(jnp.where(lane == mine + 3, prob, 0.0), axis=-1, keepdims=True)
            gate = here * chosen
            for d in range(4):
                at = slice(half * 256 + d * 64, half * 256 + (d + 1) * 64)
                value = gate[d * 64 : (d + 1) * 64, :] * g_piece(half, d, slice(None))
                slopes[at, :] = value.astype(bf16)
            return gate, chosen

        def phase_one(half):
            rows_at = slice(half * 256, (half + 1) * 256)

            def one(r, _):
                at = pl.ds(pl.multiple_of(owner_expert(r) * 512, 512), 512)
                row = k.rows[rows_at, at]
                acc[0] += dot_nn(row, wg[r])
                acc[1] += dot_nn(row, wu[r])
                acc[2] += dot_nt(slopes[rows_at, at], wd[r])
                return 0

            acc[...] = jnp.zeros_like(acc)
            lax.fori_loop(0, 4, one, 0)
            for d in range(4):
                at, to = slice(d * 64, (d + 1) * 64), slice(half * 256 + d * 64, half * 256 + (d + 1) * 64)
                act, gate_grad, up_grad = gated(acc[0, at, :], acc[1, at, :], acc[2, at, :])
                up[0, to, :] = act.astype(bf16)
                up[1, to, :] = gate_grad.astype(bf16)
                up[2, to, :] = up_grad.astype(bf16)

        lanes = lax.broadcasted_iota(jnp.int32, (64, 128), 1)

        def phase_two(half, gate, chosen):
            rows_at = slice(half * 256, (half + 1) * 256)

            def two(r, dgate):
                at = pl.ds(pl.multiple_of(owner_expert(r) * 512, 512), 512)
                result = dot_nn(up[0, rows_at, :], wd[r]).astype(bf16).astype(f32)
                grad = dot_nt(up[1, rows_at, :], wg[r]) + dot_nt(up[2, rows_at, :], wu[r])
                sums = []
                for d in range(4):
                    here = slice(d * 64, (d + 1) * 64)
                    g_rows = g_piece(half, d, at)
                    sums.append(jnp.sum(g_rows * result[here, :], axis=-1, keepdims=True))
                    part = gate[here, :] * result[here, :]
                    if half == 0:
                        k.out_sum[here, at] = part
                        k.grad_sum[here, at] = grad[here, :]
                    else:
                        k.e_out[d, :, at] = part.astype(bf16)
                        k.e_grad[d, :, at] = grad[here, :].astype(bf16)
                return dgate + jnp.concatenate(sums, axis=0)

            dgate = lax.fori_loop(0, 4, two, jnp.zeros((256, 1), f32)) * chosen
            for d in range(4):
                extra = jnp.zeros((64, 128), f32)
                for m, part in enumerate(split3(dgate[d * 64 : (d + 1) * 64, :])):
                    extra = jnp.where(lanes == mine + 16 * m, part, extra)
                if half == 0:
                    k.extras[d * 64 : (d + 1) * 64, :] = extra
                else:
                    k.e_grad[d, :, 2048:2176] = extra.astype(bf16)

        for copy in own_z + later:
            copy.wait_recv()
        gate, chosen = route(0)
        for copy in group:
            copy.wait()
        phase_one(0)
        phase_two(0, gate, chosen)
        sg.wait(1)
        sg.start(3)
        sg.start(5)
        for copy in oth_z:
            copy.wait_recv()
        gate, chosen = route(1)
        phase_one(1)
        saved = [loads.go(up, k.ex_up)]
        for r in range(4):
            to = slice(r * 256, (r + 1) * 256)
            for target, m in ((keep, r), (send, r + 4)):
                at = pl.ds(pl.multiple_of(owner_dense(m) * 256, 256), 256)
                target[0:512, to] = slopes[:, at]
                target[512:1024, to] = k.rows[:, at]
        saved.append(loads.go(keep, k.ex_keep))
        swap_ex = wires.go(lambda: (send, k.ex_x), core_dev)
        su.wait(1)
        su.start(3)
        su.start(5)
        phase_two(1, gate, chosen)
        for copy in saved:
            copy.wait()
        swap_ex.wait_send()
        swap_ex.ends = lambda: (k.ex_keep, k.ex_x)
        parts.swap_ex = swap_ex

    pl.run_scoped(
        expert_part,
        pltpu.VMEM((4, 512, 1408), bf16),
        pltpu.VMEM((4, 512, 1408), bf16),
        pltpu.VMEM((4, 1408, 512), bf16),
        pltpu.VMEM((512, 2048), bf16),
        pltpu.VMEM((3, 256, 1408), f32),
        pltpu.VMEM((3, 512, 1408), bf16),
        pltpu.VMEM((1024, 1024), bf16),
        pltpu.VMEM((1024, 1024), bf16),
    )
    swap_up = {}
    for m in (1, 2, 0):
        swap_up[m] = wires.go(lambda m=m: (k.ex_up.at[m], k.ex_up_x.at[m]), core_dev)
    e_grad_z = to_z(lambda d: lambda: (k.e_grad.at[d], k.e_grad_z.at[d - 1]))
    e_out_z = to_z(lambda d: lambda: (k.e_out.at[d], k.e_out_z.at[d - 1]))
    over_y, over_x = {}, {}

    def expert_grad(m, kept, sent, landed):
        parts.swap_ex_wait()
        swap_up[m].wait_recv()

        def inner(left, right, keep, send):
            start = pl.ds(0 if m == 0 else 512, 512)
            got = [
                loads.go(k.ex_up.at[m], right.at[0]),
                loads.go(k.ex_up_x.at[m], right.at[1]),
                loads.go(k.ex_keep.at[start, :], left.at[0]),
                loads.go(k.ex_x.at[start, :], left.at[1]),
            ]
            for copy in got:
                copy.wait()
            saved = []
            for r in (3, 1, 2, 0):
                target = send if r % 2 else keep
                at = slice(r * 256, (r + 1) * 256)
                to = pl.ds(pl.multiple_of(((y + r // 2) % 2) * 256, 256), 256)
                if m == 0:
                    total = dot_tn(right[0], left[0, :, at]) + dot_tn(right[1], left[1, :, at])
                    target[:, to] = total.astype(bf16)
                else:
                    total = dot_tn(left[0, :, at], right[0]) + dot_tn(left[1, :, at], right[1])
                    target[to, :] = total.astype(bf16)
                if r == 1:
                    saved.append(loads.go(send, sent))
                if r == 2:
                    saved[0].wait()
                    over_x[6 + m] = wires.go(lambda: (sent, landed), x_dev)
            loads.go(keep, kept).wait()

        shape = (1408, 512) if m == 0 else (512, 1408)
        pl.run_scoped(
            inner,
            pltpu.VMEM((2, 512, 1024), bf16),
            pltpu.VMEM((2, 512, 1408), bf16),
            pltpu.VMEM(shape, bf16),
            pltpu.VMEM(shape, bf16),
        )

    def to_y(name, r, source, target):
        over_y[name, r] = wires.go(lambda: (source.at[r % 2], target.at[r % 2]), y_dev)

    def shared_grad(m, keep, send):
        def inner(left, right):
            if m == 0:
                got = [loads.go(k.sh_keep, left.at[0]), loads.go(k.sh_x, left.at[1])]
            else:
                start = pl.ds(512, 256)
                got = [
                    loads.go(k.ex_keep.at[start, :], left.at[0]),
                    loads.go(k.ex_x.at[start, :], left.at[1]),
                ]
            got.append(loads.go(k.sh_up.at[m], right.at[0]))
            got.append(loads.go(k.sh_up_x.at[m], right.at[1]))
            for copy in got:
                copy.wait()
            for r in (3, 1, 2, 0):
                target = send if r >= 2 else keep
                at = slice(r * 256, (r + 1) * 256)
                if m == 0:
                    total = dot_tn(right[0], left[0, :, at]) + dot_tn(right[1], left[1, :, at])
                else:
                    total = dot_tn(left[0, :, at], right[0]) + dot_tn(left[1, :, at], right[1])
                target[r % 2] = total.astype(bf16)

        pl.run_scoped(
            inner, pltpu.VMEM((2, 256, 1024), bf16), pltpu.VMEM((2, 256, 1408), bf16)
        )

    def swap_ex_wait():
        if not parts.started:
            parts.swap_ex.wait_recv()
            parts.started = True

    parts.swap_ex_wait = swap_ex_wait
    expert_grad(1, k.k_eg, k.t_eg, k.x_eg)
    sd.wait(1)
    sd.start(3)
    sd.start(5)

    def shared_part(wg, wu, wd, slopes, acc, up, keep, send):
        routed = k.rows.at[pl.ds(0, 256), :]
        held = []

        def bring(r, group):
            for s in group:
                held.append(loads.go(s.block(r), {sg: wg, su: wu, sd: wd}[s].at[r]))

        def arrived(r, group, onward=()):
            for s in group:
                s.wait(r)
                for t in onward:
                    s.start(t)
            bring(r, group)

        def settle():
            for copy in held:
                copy.wait()
            held.clear()

        pair, last = (sg, su), (sd,)
        bring(0, shared)
        bring(1, shared)
        arrived(4, shared)
        arrived(2, shared, (6,))
        arrived(5, shared)
        arrived(6, shared)
        wide = routed[...].astype(f32) * k.small[2:3, :].astype(f32)
        sw = jax.nn.sigmoid(jnp.sum(wide, axis=-1, keepdims=True))
        for d in range(4):
            at = slice(d * 64, (d + 1) * 64)
            slopes[at, :] = (sw[at, :] * piece(k.g_own, d, 64).astype(f32)).astype(bf16)
        for r in range(4):
            to = slice(r * 256, (r + 1) * 256)
            keep[:, to] = cols(slopes, owner_dense(r), 256)
            send[:, to] = cols(slopes, owner_dense(r + 4), 256)
        saved = [loads.go(keep, k.sh_keep), loads.go(send, k.sh_send)]
        acc[...] = jnp.zeros_like(acc)

        def one(j, _):
            r = j // 2 + (j % 2) * 4
            row = cols(routed, owner_dense(r), 256)
            acc[0] += dot_nn(row, wg[r])
            acc[1] += dot_nn(row, wu[r])
            return 0

        def back(j, _):
            r = j // 2 + (j % 2) * 4
            acc[2] += dot_nt(cols(slopes, owner_dense(r), 256), wd[r])
            return 0

        settle()
        lax.fori_loop(0, 6, one, 0)
        arrived(3, pair, (7,))
        arrived(7, pair)
        settle()
        lax.fori_loop(6, 8, one, 0)
        for d in range(4):
            at = slice(d * 64, (d + 1) * 64)
            up[0, at, :] = (jax.nn.silu(acc[0, at, :]) * acc[1, at, :]).astype(bf16)
        saved.append(loads.go(up.at[0], k.sh_up.at[0]))
        for copy in saved:
            copy.wait()
        swaps = [
            wires.go(lambda: (k.sh_up.at[0], k.sh_up_x.at[0]), core_dev),
            wires.go(lambda: (k.sh_send, k.sh_x), core_dev),
        ]
        lax.fori_loop(0, 6, back, 0)
        expert_grad(2, k.k_eu, k.t_eu, k.x_eu)
        for copy in swaps:
            copy.wait_recv()
        shared_grad(0, k.k_sd, k.t_sd)
        to_y(2, 3, k.t_sd, k.y_sd)
        arrived(3, last, (7,))
        arrived(7, last)
        settle()
        lax.fori_loop(6, 8, back, 0)
        for d in range(4):
            at = slice(d * 64, (d + 1) * 64)
            _, gate_grad, up_grad = gated(acc[0, at, :], acc[1, at, :], acc[2, at, :])
            up[1, at, :] = gate_grad.astype(bf16)
            up[2, at, :] = up_grad.astype(bf16)
        saved = [loads.go(up.at[m], k.sh_up.at[m]) for m in (1, 2)]

        def two(r, slope):
            at = pl.ds(pl.multiple_of(owner_dense(r) * 256, 256), 256)
            part = dot_nn(up[0], wd[r])
            total = sw * part + k.out_sum[:, at]
            back = dot_nt(up[1], wg[r]) + dot_nt(up[2], wu[r]) + k.grad_sum[:, at]
            sums = []
            for d in range(4):
                rows_at = slice(d * 64, (d + 1) * 64)
                g_rows = k.g_own[pl.ds(pl.multiple_of(near(d) * 64, 64), 64), at].astype(f32)
                sums.append(jnp.sum(g_rows * part[rows_at, :], axis=-1, keepdims=True))
                k.s_out[d, :, at] = total[rows_at, :].astype(bf16)
                k.s_grad[d, :, at] = back[rows_at, :].astype(bf16)
            return slope + jnp.concatenate(sums, axis=0)

        slope = lax.fori_loop(0, 8, two, jnp.zeros((256, 1), f32))
        lanes = lax.broadcasted_iota(jnp.int32, (64, 128), 1)
        for d in range(4):
            rows_at = slice(d * 64, (d + 1) * 64)
            extra = k.extras[rows_at, :]
            for m, part in enumerate(split3(slope[rows_at, :])):
                extra = jnp.where(lanes == mine + 48 + 16 * m, part, extra)
            k.s_grad[d, :, 2048:2176] = extra.astype(bf16)
        for copy in saved:
            copy.wait()

    pl.run_scoped(
        shared_part,
        pltpu.VMEM((8, 256, 1408), bf16),
        pltpu.VMEM((8, 256, 1408), bf16),
        pltpu.VMEM((8, 1408, 256), bf16),
        pltpu.VMEM((256, 2048), bf16),
        pltpu.VMEM((3, 256, 1408), f32),
        pltpu.VMEM((3, 256, 1408), bf16),
        pltpu.VMEM((256, 1024), bf16),
        pltpu.VMEM((256, 1024), bf16),
    )
    swap_sh = [
        wires.go(lambda m=m: (k.sh_up.at[m], k.sh_up_x.at[m]), core_dev) for m in (1, 2)
    ]
    s_grad_z = to_z(lambda d: lambda: (k.s_grad.at[d], k.s_grad_z.at[d - 1]))
    for copy in e_grad_z:
        copy.wait_recv()
    oth = k.e_grad[0].astype(f32)
    for d in range(3):
        oth += k.e_grad_z[d].astype(f32)
    k.g_send[...] = oth.astype(bf16)
    grad_y = wires.go(lambda: (k.g_send, k.g_y), y_dev)

    def back_part(*refs):
        k_sg, k_su, k_q, k_o, k_v = refs[:5]
        t_sg, t_su, t_q, t_o, t_v = refs[5:10]
        f_sg, f_su, f_q, f_o, f_v, f_sd = refs[10:16]
        h_keep, h_send, h_x, lin, lin_x, vec, high, gkv, gkv_send, gn = refs[16:]
        k_sd, t_sd = k.k_sd, k.t_sd

        def fold(name, keep, landed, send, target):
            over_y[name, 3].wait_recv()

            def inner(buffer):
                loads.go(landed.at[1], buffer).wait()
                send[...] = (keep[1].astype(f32) + buffer[...].astype(f32)).astype(bf16)

            pl.run_scoped(inner, pltpu.VMEM(tuple(keep.shape[1:]), bf16))
            over_x[name] = wires.go(lambda: (send, target), x_dev)

        def finish_pair():
            for name in (0, 1):
                over_y[name, 2].wait_recv()
                over_x[name].wait_recv()

            def inner(left, right, total):
                got = [
                    loads.go(k.y_sg.at[0], left.at[0]),
                    loads.go(k.x_sg, right.at[0]),
                    loads.go(k.y_su.at[0], left.at[1]),
                    loads.go(k.x_su, right.at[1]),
                ]
                for copy in got:
                    copy.wait()
                for n, keep in enumerate((k_sg, k_su)):
                    value = keep[0].astype(f32) + left[n].astype(f32) + right[n].astype(f32)
                    total[:, n, :] = value.astype(bf16)
                loads.go(total, k.d_si).wait()

            pair = pltpu.VMEM((2, 256, 1408), bf16)
            pl.run_scoped(inner, pair, pair, pltpu.VMEM((256, 2, 1408), bf16))

        def finish(name, keep, landed, target, result):
            over_y[name, 2].wait_recv()

            def inner(left, right, total):
                got = loads.go(landed.at[0], left)
                over_x[name].wait_recv()
                more = loads.go(target, right)
                got.wait()
                more.wait()
                value = keep[0].astype(f32) + left[...].astype(f32) + right[...].astype(f32)
                total[...] = value.astype(total.dtype)
                loads.go(total, result).wait()

            shape = tuple(keep.shape[1:])
            pl.run_scoped(
                inner,
                pltpu.VMEM(shape, bf16),
                pltpu.VMEM(shape, bf16),
                pltpu.VMEM(shape, result.dtype),
            )

        swap_sh[0].wait_recv()
        shared_grad(1, k_sg, t_sg)
        to_y(0, 3, t_sg, k.y_sg)
        swap_sh[1].wait_recv()
        shared_grad(2, k_su, t_su)
        to_y(1, 3, t_su, k.y_su)
        expert_grad(0, k.k_ed, k.t_ed, k.x_ed)
        fold(2, k_sd, k.y_sd, f_sd, k.x_sd)

        def other_rows(buffer):
            for copy in e_out_z:
                copy.wait_recv()
            loads.go(k.e_out_z, buffer).wait()
            oth = k.e_out[0].astype(f32)
            for d in range(3):
                oth += buffer[d].astype(f32)
            k.o_send[...] = oth.astype(bf16)

        pl.run_scoped(other_rows, pltpu.VMEM((3, 64, 2048), bf16))
        for copy in s_grad_z:
            copy.wait_recv()
        grad_y.wait_recv()
        total = k.s_grad[0].astype(f32) + k.g_y[...].astype(f32)
        for d in range(3):
            total += k.s_grad_z[d].astype(f32)
        own_rows(
            total,
            k.hidden[...],
            k.rows[0:64, :],
            piece(k.g_own, 0, 64),
            k.small,
            high,
            k.gh.at[0],
            vec,
        )
        gh_z = to_z(lambda d: lambda: (k.gh.at[0], k.gh.at[d]))
        s_out_z = to_z(lambda d: lambda: (k.s_out.at[d], k.s_out_z.at[d - 1]))
        out_y = wires.go(lambda: (k.o_send, k.o_y), y_dev)
        to_y(2, 2, t_sd, k.y_sd)
        fold(0, k_sg, k.y_sg, f_sg, k.x_sg)
        gn_z = []

        def attention_back(w, o_w, acc, low_g):
            got, more = [loads.go(k.w_o, o_w.at[0])], [loads.go(k.w_q, w.at[0])]
            for r in range(1, 8):
                got.append(loads.go(k.s_o.at[r], o_w.at[r]))
                more.append(loads.go(k.s_q.at[r], w.at[r]))
            for copy in gh_z:
                copy.wait_recv()
            for copy in got:
                copy.wait()
            acc[...] = jnp.zeros_like(acc)
            for r in range(8):
                at = pl.ds(pl.multiple_of(owner_dense(r) * 256, 256), 256)
                row = jnp.concatenate([k.gh[d, :, at] for d in range(4)], axis=0)
                target = h_keep if r < 4 else h_send
                target[:, (r % 4) * 256 : (r % 4 + 1) * 256] = row
                acc[...] += dot_nt(row, o_w[r])
            swap_h = wires.go(lambda: (h_send, k.h_x), core_dev)
            low_g[...] = acc[...].astype(bf16)
            mask_own = k.ids_near[0:1, :] <= k.ids_q[:, 0:1]
            mask_oth = k.ids_far[0:1, :] <= k.ids_q[:, 0:1]
            scale = 128 ** (-0.5)
            for h in range(4):
                at = slice(h * 128, (h + 1) * 128)
                w_own, w_oth = softmax_parts(
                    k.q[:, at], k.kv[0:256, at], k.kv_oth[0:256, at], mask_own, mask_oth
                )
                dw_own = dot_nt(low_g[:, at], k.kv[256:512, at])
                dw_oth = dot_nt(low_g[:, at], k.kv_oth[256:512, at])
                mean = jnp.sum(w_own * dw_own, axis=-1, keepdims=True)
                mean += jnp.sum(w_oth * dw_oth, axis=-1, keepdims=True)
                ds_own = (w_own * (dw_own - mean)).astype(bf16)
                ds_oth = (w_oth * (dw_oth - mean)).astype(bf16)
                gq = dot_nn(ds_own, k.kv[0:256, at]) + dot_nn(ds_oth, k.kv_oth[0:256, at])
                lin[0:256, at] = turn_back(gq * scale, k.cs[...], k.sn[...]).astype(bf16)
                gkv[0:256, at] = dot_tn(ds_own, k.q[:, at]) * scale
                gkv[256:512, at] = dot_tn(w_own.astype(bf16), low_g[:, at])
                gkv_send[0:256, at] = (dot_tn(ds_oth, k.q[:, at]) * scale).astype(bf16)
                gkv_send[256:512, at] = dot_tn(w_oth.astype(bf16), low_g[:, at]).astype(bf16)
            gkv_y = wires.go(lambda: (gkv_send, k.gkv_y), y_dev)
            to_y(0, 2, t_sg, k.y_sg)
            fold(1, k_su, k.y_su, f_su, k.x_su)
            for copy in more:
                copy.wait()
            gkv_y.wait_recv()
            for h in range(4):
                at = slice(h * 128, (h + 1) * 128)
                gk = gkv[0:256, at] + k.gkv_y[0:256, at].astype(f32)
                lin[256:512, at] = turn_back(gk, k.cs[...], k.sn[...]).astype(bf16)
            lin[512:768, :] = (gkv[256:512, :] + k.gkv_y[256:512, :].astype(f32)).astype(bf16)
            swap_lin = wires.go(lambda: (lin, k.lin_x), core_dev)
            for m in range(3):
                part = lin[m * 256 : (m + 1) * 256, :].astype(f32)
                vec[11 + m : 12 + m, 0:512] = jnp.sum(part, axis=0, keepdims=True)
            for r in range(8):
                at = pl.ds(pl.multiple_of(owner_dense(r) * 256, 256), 256)
                back = dot_nt(lin[0:256, :], w[r, 0:256, :])
                back += dot_nt(lin[256:512, :], w[r, 256:512, :])
                back += dot_nt(lin[512:768, :], w[r, 512:768, :])
                gain = jnp.zeros((1, 256), f32)
                for d in range(4):
                    rows_at = slice(d * 64, (d + 1) * 64)
                    t = k.tok[pl.ds(pl.multiple_of(near(d) * 64, 64), 64), at].astype(f32)
                    gain += jnp.sum(
                        back[rows_at, :] * t * k.inv1[rows_at, :], axis=0, keepdims=True
                    )
                    gn[d, :, at] = back[rows_at, :].astype(bf16)
                vec[0:1, at] = gain
            swap_vec = wires.go(lambda: (vec, k.vec_x), core_dev)
            gn_z.extend(to_z(lambda d: lambda: (gn.at[d], k.gn_z.at[d - 1])))
            for copy in (swap_h, swap_lin, swap_vec, swap_n, swap_low):
                copy.wait_recv()

        pl.run_scoped(
            attention_back,
            pltpu.VMEM((8, 768, 512), bf16),
            pltpu.VMEM((8, 512, 256), bf16),
            pltpu.VMEM((256, 512), f32),
            pltpu.VMEM((256, 512), bf16),
        )
        k.vec_x[...] += vec[...]
        line = lax.broadcasted_iota(jnp.int32, (16, 512), 0)

        def attention_grad(n_x, low_x):
            got = [
                loads.go(k.n_x, n_x),
                loads.go(k.low_x, low_x),
                loads.go(k.h_x, h_x),
                loads.go(k.lin_x, lin_x),
            ]
            for copy in got:
                copy.wait()

            def one(r):
                keep = r < 2
                b_q, b_o, b_v = (k_q, k_o, k_v) if keep else (t_q, t_o, t_v)
                at = slice(r * 256, (r + 1) * 256)
                left, left_x = k.n_keep[:, at], n_x[:, at]
                for m in range(3):
                    rows_at = slice(m * 256, (m + 1) * 256)
                    total = dot_tn(left, lin[rows_at, :]) + dot_tn(left_x, lin_x[rows_at, :])
                    b_q[r % 2, rows_at, :] = total.astype(bf16)
                total = dot_tn(k.low[...], h_keep[:, at]) + dot_tn(low_x[...], h_x[:, at])
                b_o[r % 2] = total.astype(bf16)
                here = cols(k.vec_x, owner_dense(r), 256)
                here = jnp.concatenate([here, jnp.zeros((16, 256), f32)], axis=1)
                b_v[r % 2] = jnp.where(line < 11, here, k.vec_x[:, 0:512]).astype(bf16)
                if not keep:
                    to_y(5, r, t_v, k.y_v)
                    to_y(3, r, t_q, k.y_q)
                    to_y(4, r, t_o, k.y_o)

            one(3)
            to_y(1, 2, t_su, k.y_su)
            one(2)
            one(1)
            one(0)

        pl.run_scoped(
            attention_grad, pltpu.VMEM((256, 1024), bf16), pltpu.VMEM((256, 512), bf16)
        )

        def expert_finish(m, kept, landed, result):
            def inner(left, right):
                got = loads.go(kept, left)
                over_x[6 + m].wait_recv()
                more = loads.go(landed, right)
                got.wait()
                more.wait()
                left[...] = (left[...].astype(f32) + right[...].astype(f32)).astype(bf16)
                loads.go(left, result).wait()

            shape = pltpu.VMEM(tuple(result.shape), bf16)
            pl.run_scoped(inner, shape, shape)

        def expert_pair():
            for m in (1, 2):
                over_x[6 + m].wait_recv()

            def inner(left, right, total):
                for half in range(2):
                    at = pl.ds(256 * half, 256)
                    got = []
                    for n, (kept, landed) in enumerate(((k.k_eg, k.x_eg), (k.k_eu, k.x_eu))):
                        got.append(loads.go(kept.at[at, :], left.at[n]))
                        got.append(loads.go(landed.at[at, :], right.at[n]))
                    for copy in got:
                        copy.wait()
                    for n in range(2):
                        value = left[n].astype(f32) + right[n].astype(f32)
                        total[:, n, :] = value.astype(bf16)
                    loads.go(total, k.d_ei.at[at]).wait()

            pair = pltpu.VMEM((2, 256, 1408), bf16)
            pl.run_scoped(inner, pair, pair, pltpu.VMEM((256, 2, 1408), bf16))

        expert_pair()

        def outputs(s_z):
            for copy in s_out_z:
                copy.wait_recv()
            got = loads.go(k.s_out_z, s_z)
            for copy in gn_z:
                copy.wait_recv()
            grad = gn[0].astype(f32)
            for d in range(3):
                grad += k.gn_z[d].astype(f32)
            t = piece(k.tok, 0, 64).astype(f32)
            i = k.inv1[0:64, :]
            scaled = grad * k.small[0:1, :].astype(f32)
            mean = jnp.mean(scaled * t, axis=-1, keepdims=True)
            grad = high[...] + i * scaled - t * (i * i * i * mean)
            k.grad_tokens[...] = grad.astype(bf16)
            got.wait()
            total = k.hidden[...] + k.s_out[0].astype(f32)
            for d in range(3):
                total += s_z[d].astype(f32)
            out_y.wait_recv()
            k.output[...] = (total + k.o_y[...].astype(f32)).astype(bf16)

        expert_finish(0, k.k_ed, k.x_ed, k.d_ed)
        finish(2, k_sd, k.y_sd, k.x_sd, k.d_sd)
        fold(5, k_v, k.y_v, f_v, k.x_v)
        fold(3, k_q, k.y_q, f_q, k.x_q)
        fold(4, k_o, k.y_o, f_o, k.x_o)
        pl.run_scoped(outputs, pltpu.VMEM((3, 64, 2048), bf16))
        finish_pair()
        finish(5, k_v, k.y_v, k.x_v, k.v_own)
        v_z = to_z(lambda d: lambda: (k.v_own, k.v_z.at[d - 1]))
        finish(3, k_q, k.y_q, k.x_q, k.d_q)
        finish(4, k_o, k.y_o, k.x_o, k.d_o)
        for copy in v_z:
            copy.wait_recv()
        total = k.v_own[...] + k.v_z[0] + k.v_z[1] + k.v_z[2]
        k.d_v[...] = total[:, 0:256].astype(bf16)
        for h in range(4):
            lanes_at = slice(h * 128, (h + 1) * 128)
            turned = pltpu.roll(k.v_own[:, lanes_at], (128 - owner_dense(0) * 16) % 128, 1)
            for m in range(3):
                k.d_b[m, h : h + 1, :] = turned[11 + m : 12 + m, :].astype(bf16)
        wires.drain()

    def buffers(lead):
        return tuple(
            pltpu.VMEM(lead + shape, bf16)
            for shape in ((256, 1408), (256, 1408), (768, 512), (512, 256), (16, 512))
        )

    pl.run_scoped(
        back_part,
        *buffers((2,)),
        *buffers((2,)),
        *buffers(()),
        pltpu.VMEM((1408, 256), bf16),
        pltpu.VMEM((256, 1024), bf16),
        pltpu.VMEM((256, 1024), bf16),
        pltpu.VMEM((256, 1024), bf16),
        pltpu.VMEM((768, 512), bf16),
        pltpu.VMEM((768, 512), bf16),
        pltpu.VMEM((16, 2048), f32),
        pltpu.VMEM((64, 2048), f32),
        pltpu.VMEM((512, 512), f32),
        pltpu.VMEM((512, 512), bf16),
        pltpu.VMEM((4, 64, 2048), bf16),
    )


def dma(n):
    return pltpu.SemaphoreType.DMA((n,))


def fixed_body(
    tokens,
    norm1_gain,
    w_qkv,
    b_qkv,
    w_out,
    norm2_gain,
    w_router,
    shared_gate,
    w_shared_in,
    w_shared_out,
    w_expert_in,
    w_expert_out,
    block_ids,
    expert_ids,
    out_grad,
):
    tok, g_own = tokens[0], out_grad[0]
    rows = tok.shape[0]
    places = np.arange(2 * rows)[:, None]
    frequency = rope_base ** (-np.arange(64) / 64.0)
    cosine, sine = np.cos(places * frequency), np.sin(places * frequency)
    cs = np.concatenate([cosine, cosine], axis=1).astype(np.float32)
    sn = np.concatenate([-sine, sine], axis=1).astype(np.float32)

    def vm(*shape, kind=bf16):
        return pltpu.VMEM(shape, kind)

    def o(*shape, kind=bf16, at=A):
        return (shape, kind, at)

    w_q = w_qkv.transpose(1, 0, 2).reshape(768, 512)
    b = call(
        layer_kernel,
        0,
        dict(
            tok=(tok, V),
            g_own=(g_own, V),
            bias=(b_qkv, V),
            cs_all=(cs, V),
            sn_all=(sn, V),
            blocks=(block_ids, V),
            ids_own=(expert_ids[0].T, V),
            gain_one=(norm1_gain, V),
            gain_two=(norm2_gain, V),
            gate_vector=(shared_gate, V),
            router=(w_router.T, V),
            w_q=(w_q, A),
            w_o=(w_out, A),
            w_si=(w_shared_in, A),
            w_sd=(w_shared_out, A),
            w_ei=(w_expert_in[0], A),
            w_ed=(w_expert_out[0], A),
        ),
        dict(
            output=o(64, 2048, at=V),
            grad_tokens=o(64, 2048, at=V),
            d_v=o(16, 256, at=V),
            d_b=o(3, 4, 128, at=V),
            d_q=o(768, 512),
            d_o=o(512, 256),
            d_si=o(256, 2, 1408),
            d_sd=o(1408, 256),
            d_ei=o(512, 2, 1408),
            d_ed=o(1408, 512),
            split_si=o(2, 256, 1408),
            split_ei=o(2, 512, 1408),
            s_q=o(8, 768, 512),
            s_o=o(8, 512, 256),
            s_sg=o(8, 256, 1408),
            s_su=o(8, 256, 1408),
            s_sd=o(8, 1408, 256),
            s_eg=o(4, 512, 1408),
            s_eu=o(4, 512, 1408),
            s_ed=o(4, 1408, 512),
            ex_up=o(3, 512, 1408),
            ex_up_x=o(3, 512, 1408),
            ex_keep=o(1024, 1024),
            ex_x=o(1024, 1024),
            sh_up=o(3, 256, 1408),
            sh_up_x=o(3, 256, 1408),
            sh_keep=o(256, 1024),
            sh_send=o(256, 1024),
            sh_x=o(256, 1024),
            k_eg=o(512, 1408),
            k_eu=o(512, 1408),
            k_ed=o(1408, 512),
            t_eg=o(512, 1408),
            t_eu=o(512, 1408),
            t_ed=o(1408, 512),
            y_sg=o(2, 256, 1408),
            y_su=o(2, 256, 1408),
            y_sd=o(2, 1408, 256),
            y_q=o(2, 768, 512),
            y_o=o(2, 512, 256),
            y_v=o(2, 16, 512),
            x_sg=o(256, 1408),
            x_su=o(256, 1408),
            x_sd=o(1408, 256),
            x_q=o(768, 512),
            x_o=o(512, 256),
            x_v=o(16, 512),
            x_eg=o(512, 1408),
            x_eu=o(512, 1408),
            x_ed=o(1408, 512),
            n_x=o(256, 1024),
            low_x=o(256, 512),
            h_x=o(256, 1024),
            lin_x=o(768, 512),
            e_out_z=o(3, 64, 2048),
            s_out_z=o(3, 64, 2048),
        ),
        dict(
            s_v=vm(8, 16, 256),
            w_v=vm(16, 256),
            col=vm(512, 128, kind=f32),
            ids_q=vm(256, 128, kind=f32),
            ids_near=vm(8, 256, kind=f32),
            ids_far=vm(8, 256, kind=f32),
            cs=vm(256, 128, kind=f32),
            sn=vm(256, 128, kind=f32),
            ids=vm(4, 128, 128, kind=f32),
            ids_y=vm(64, 128, kind=f32),
            g_piece=vm(64, 2048),
            g_oth=vm(4, 64, 2048),
            q=vm(256, 512),
            kv=vm(512, 512),
            kv_oth=vm(512, 512),
            low=vm(256, 512),
            n_keep=vm(256, 1024),
            n_send=vm(256, 1024),
            small=vm(16, 2048),
            inv1=vm(256, 1, kind=f32),
            k_sd=vm(2, 1408, 256),
            t_sd=vm(2, 1408, 256),
            att=vm(3, 64, 2048),
            att_send=vm(4, 64, 2048),
            hidden=vm(64, 2048, kind=f32),
            rows=vm(512, 2048),
            out_sum=vm(256, 2048, kind=f32),
            grad_sum=vm(256, 2048, kind=f32),
            extras=vm(256, 128, kind=f32),
            e_out=vm(4, 64, 2048),
            e_grad=vm(4, 64, 2176),
            e_grad_z=vm(3, 64, 2176),
            s_out=vm(4, 64, 2048),
            s_grad=vm(4, 64, 2176),
            s_grad_z=vm(3, 64, 2176),
            g_send=vm(64, 2176),
            g_y=vm(64, 2176),
            o_send=vm(64, 2048),
            o_y=vm(64, 2048),
            gh=vm(4, 64, 2048),
            gkv_y=vm(512, 512),
            gn_z=vm(3, 64, 2048),
            vec_x=vm(16, 2048, kind=f32),
            v_own=vm(16, 512, kind=f32),
            v_z=vm(3, 16, 512, kind=f32),
            send_sems=dma(128),
            recv_sems=dma(128),
            load_sems=dma(224),
        ),
        63,
        4 * 10**10,
        2 * 10**8,
    )
    return (
        b.output[None],
        b.grad_tokens[None],
        b.d_v[0],
        b.d_q.reshape(3, 256, 512).transpose(1, 0, 2),
        b.d_b[:, :, 0:16],
        b.d_o,
        b.d_v[1],
        b.d_v[3:11].T,
        b.d_v[2],
        b.d_si,
        b.d_sd,
        b.d_ei[None],
        b.d_ed[None],
    )


def solution(mesh):
    placed = (
        P(DP, CTX, None),
        P(PLANE),
        P(PLANE, None, EXP),
        P(None, EXP, None),
        P(EXP, PLANE),
        P(PLANE),
        P(PLANE, None),
        P(PLANE),
        P(PLANE, None, EXP),
        P(EXP, PLANE),
        P(GROUP, DP, None, None),
        P(GROUP, None, DP),
        P(DP, None),
        P(DP, GROUP, None),
        P(DP, CTX, None),
    )
    fixed = tuple(mesh.shape[a] for a in (DP, CTX, EXP)) == (4, 2, 4)
    return jax.shard_map(
        fixed_body if fixed else general_body,
        mesh=mesh,
        in_specs=placed,
        out_specs=(
            P(DP, GROUP, None),
            P(DP, GROUP, None),
            P(PLANE),
            P(PLANE, None, EXP),
            P(None, EXP, PLANE),
            P(EXP, PLANE),
            P(PLANE),
            P(PLANE, None),
            P(PLANE),
            P(PLANE, None, EXP),
            P(EXP, PLANE),
            P(GROUP, DP, None, None),
            P(GROUP, None, DP),
        ),
        check_vma=False,
    )
```

```python
from types import SimpleNamespace

import jax
import jax.numpy as jnp
import numpy as np
from jax import lax
from jax.experimental import pallas as pl
from jax.experimental.pallas import tpu as pltpu
from jax.sharding import PartitionSpec as P

highest = lax.Precision.HIGHEST
epsilon = 1e-06
rope_base = 1000000.0
f32 = jnp.float32
bf16 = jnp.bfloat16
DP, CTX, EXP = "dp", "context", "expert"
PLANE, GROUP = (DP, CTX), (CTX, EXP)


def rotary_tables(first_row, row_count, head_size):
    exponent = jnp.arange(head_size // 2).astype(jnp.float32) * (2.0 / head_size)
    frequency = rope_base ** (-exponent)
    positions = (first_row + jnp.arange(row_count, dtype=jnp.int32)).astype(jnp.float32)
    angles = positions[:, None] * frequency[None, :]
    return (jnp.cos(angles)[:, None, :], jnp.sin(angles)[:, None, :])


def rotate(values, cosine, sine_table):
    half_size = values.shape[-1] // 2
    first_half = values[..., :half_size]
    second_half = values[..., half_size:]
    return jnp.concatenate(
        [
            first_half * cosine - second_half * sine_table,
            second_half * cosine + first_half * sine_table,
        ],
        axis=-1,
    )


def rotate_back(grad_values, cosine, sine_table):
    half_size = grad_values.shape[-1] // 2
    first_half = grad_values[..., :half_size]
    second_half = grad_values[..., half_size:]
    return jnp.concatenate(
        [
            first_half * cosine + second_half * sine_table,
            second_half * cosine - first_half * sine_table,
        ],
        axis=-1,
    )


def gated_grads(gate_part, up_part, grad_act):
    sigmoid_gate = jax.nn.sigmoid(gate_part)
    grad_gate = grad_act * up_part * sigmoid_gate * (1.0 + gate_part * (1.0 - sigmoid_gate))
    grad_up = grad_act * gate_part * sigmoid_gate
    return (grad_gate, grad_up)


def masked_scores(queries, all_keys, allowed, score_scale):
    scores = (
        jnp.einsum("qhd,khd->hqk", queries, all_keys, preferred_element_type=jnp.float32)
        * score_scale
    )
    return jnp.where(allowed[None], scores, -1e30)


def fetch_dense(
    norm1_gain, w_qkv, w_out, norm2_gain, w_router, shared_gate, w_shared_in, w_shared_out
):
    return (
        lax.all_gather(norm1_gain, PLANE, axis=0, tiled=True),
        lax.all_gather(w_qkv, PLANE, axis=0, tiled=True),
        lax.all_gather(w_out, PLANE, axis=1, tiled=True),
        lax.all_gather(norm2_gain, PLANE, axis=0, tiled=True),
        lax.all_gather(w_router, PLANE, axis=0, tiled=True),
        lax.all_gather(shared_gate, PLANE, axis=0, tiled=True),
        lax.all_gather(w_shared_in, PLANE, axis=0, tiled=True),
        lax.all_gather(w_shared_out, PLANE, axis=1, tiled=True),
    )


def fetch_experts(w_expert_in, w_expert_out):
    return (
        lax.all_gather(w_expert_in, DP, axis=1, tiled=True),
        lax.all_gather(w_expert_out, DP, axis=2, tiled=True),
    )


def fetch_keys(key_rows, value_rows):
    return (
        lax.all_gather(key_rows, CTX, axis=0, tiled=True),
        lax.all_gather(value_rows, CTX, axis=0, tiled=True),
    )


def general_body(
    tokens,
    norm1_gain,
    w_qkv,
    b_qkv,
    w_out,
    norm2_gain,
    w_router,
    shared_gate,
    w_shared_in,
    w_shared_out,
    w_expert_in,
    w_expert_out,
    block_ids,
    expert_ids,
    out_grad,
):
    token_rows = tokens[0]
    rows_local, model_width = token_rows.shape
    lane_count = lax.axis_size(EXP)
    quarter = rows_local // lane_count
    first_row = lax.axis_index(CTX) * rows_local
    own_row = lax.axis_index(EXP) * quarter
    sequence_ids = block_ids[0]
    chosen = expert_ids[0]
    top_count = chosen.shape[1]
    heads_local = b_qkv.shape[1]
    head_size = b_qkv.shape[2]
    dense_full = fetch_dense(
        norm1_gain, w_qkv, w_out, norm2_gain, w_router, shared_gate, w_shared_in, w_shared_out
    )
    (
        gain_one,
        qkv_weight,
        out_weight,
        gain_two,
        router_weight,
        gate_vector,
        shared_in,
        shared_out,
    ) = dense_full
    expert_pair = fetch_experts(w_expert_in, w_expert_out)
    expert_in = expert_pair[0][0]
    expert_back = expert_pair[1][0]
    ffe_width = expert_in.shape[2]
    experts = router_weight.shape[1]
    capacity = max(2, 3 * quarter * top_count // (2 * experts))
    tokens_wide = token_rows.astype(jnp.float32)
    inverse_one = lax.rsqrt(jnp.mean(tokens_wide * tokens_wide, axis=-1, keepdims=True) + epsilon)
    normed = (tokens_wide * inverse_one * gain_one.astype(jnp.float32)).astype(jnp.bfloat16)
    linear = jnp.dot(
        normed, qkv_weight.reshape(model_width, -1), preferred_element_type=jnp.float32
    )
    linear = linear.reshape(rows_local, 3, heads_local, head_size) + b_qkv.astype(jnp.float32)[None]
    cosine, sine_table = rotary_tables(first_row, rows_local, head_size)
    queries = rotate(linear[:, 0], cosine, sine_table).astype(jnp.bfloat16)
    key_rows = rotate(linear[:, 1], cosine, sine_table).astype(jnp.bfloat16)
    value_rows = linear[:, 2].astype(jnp.bfloat16)
    all_keys, all_values = fetch_keys(key_rows, value_rows)
    query_ids = lax.dynamic_slice_in_dim(sequence_ids, first_row, rows_local)
    allowed = sequence_ids[None, :] <= query_ids[:, None]
    score_scale = head_size ** (-0.5)
    scores = masked_scores(queries, all_keys, allowed, score_scale)
    row_peak = jnp.max(scores, axis=-1, keepdims=True)
    log_total = row_peak + jnp.log(jnp.sum(jnp.exp(scores - row_peak), axis=-1, keepdims=True))
    weights = jnp.exp(scores - log_total).astype(jnp.bfloat16)
    attended = jnp.einsum("hqk,khd->qhd", weights, all_values, preferred_element_type=jnp.float32)
    attended_low = attended.astype(jnp.bfloat16).reshape(rows_local, heads_local * head_size)
    attention = lax.psum(
        jnp.dot(attended_low, out_weight, preferred_element_type=jnp.float32).astype(jnp.bfloat16),
        EXP,
    ).astype(jnp.float32)
    hidden = tokens_wide + attention
    inverse_two = lax.rsqrt(jnp.mean(hidden * hidden, axis=-1, keepdims=True) + epsilon)
    routed = (hidden * inverse_two * gain_two.astype(jnp.float32)).astype(jnp.bfloat16)
    shared_up = jnp.dot(
        routed, shared_in.reshape(model_width, -1), preferred_element_type=jnp.float32
    )
    shared_up = shared_up.reshape(rows_local, 2, -1)
    shared_act = (jax.nn.silu(shared_up[:, 0]) * shared_up[:, 1]).astype(jnp.bfloat16)
    shared_part = jnp.dot(shared_act, shared_out, preferred_element_type=jnp.float32)
    shared_rows = lax.psum_scatter(
        shared_part.astype(jnp.bfloat16), EXP, scatter_dimension=0, tiled=True
    ).astype(jnp.float32)
    shared_weight = jax.nn.sigmoid(jnp.dot(routed, gate_vector, preferred_element_type=jnp.float32))
    routed_own = lax.dynamic_slice_in_dim(routed, own_row, quarter)
    hidden_own = lax.dynamic_slice_in_dim(hidden, own_row, quarter)
    weight_own = lax.dynamic_slice_in_dim(shared_weight, own_row, quarter)
    logits = jnp.dot(routed_own, router_weight, preferred_element_type=jnp.float32)
    probability = jax.nn.softmax(logits, axis=-1)
    expert_match = (chosen[..., None] == jnp.arange(experts, dtype=jnp.int32)).astype(jnp.float32)
    gate_values = jnp.sum(probability[:, None, :] * expert_match, axis=-1)
    flat_ids = chosen.reshape(-1)
    onehot = (flat_ids[:, None] == jnp.arange(experts, dtype=jnp.int32)).astype(jnp.int32)
    slot_rank = jnp.sum((jnp.cumsum(onehot, axis=0) - onehot) * onehot, axis=-1)
    slot_index = flat_ids * capacity + slot_rank
    placement = (slot_index[:, None] == jnp.arange(experts * capacity, dtype=jnp.int32)).astype(
        jnp.bfloat16
    )
    repeated = jnp.repeat(routed_own, top_count, axis=0)
    outgoing = jnp.einsum("sr,sd->rd", placement, repeated, preferred_element_type=jnp.float32)
    outgoing = outgoing.astype(jnp.bfloat16).reshape(experts, capacity, model_width)
    incoming = lax.all_to_all(
        outgoing, GROUP, split_axis=0, concat_axis=0, tiled=True
    )
    flat_rows = incoming.reshape(-1, model_width)
    gate_up = jnp.dot(
        flat_rows, expert_in.reshape(model_width, -1), preferred_element_type=jnp.float32
    ).reshape(-1, 2, ffe_width)
    activated = (jax.nn.silu(gate_up[:, 0]) * gate_up[:, 1]).astype(jnp.bfloat16)
    result = jnp.dot(activated, expert_back, preferred_element_type=jnp.float32).astype(
        jnp.bfloat16
    )
    expert_result = result.reshape(incoming.shape)
    returned = lax.all_to_all(
        expert_result, GROUP, split_axis=0, concat_axis=0, tiled=True
    )
    picked = jnp.dot(
        placement, returned.reshape(-1, model_width), preferred_element_type=jnp.float32
    )
    picked = picked.reshape(quarter, top_count, model_width)
    combined = jnp.sum(gate_values[..., None] * picked, axis=1)
    result_rows = hidden_own + combined + weight_own[:, None] * shared_rows
    output = result_rows.astype(jnp.bfloat16)[None]
    (
        gain_one_b,
        qkv_weight_b,
        out_weight_b,
        gain_two_b,
        router_weight_b,
        gate_vector_b,
        shared_in_b,
        shared_out_b,
    ) = dense_full
    expert_in_b = expert_pair[0][0]
    expert_back_b = expert_pair[1][0]
    grad_full = out_grad[0].astype(jnp.float32)
    grad_own = lax.dynamic_slice_in_dim(grad_full, own_row, quarter)
    shared_grad = (shared_weight[:, None] * grad_full).astype(jnp.bfloat16)
    grad_shared_out = jnp.einsum(
        "tf,td->fd", shared_act, shared_grad, preferred_element_type=jnp.float32
    )
    grad_shared_act = jnp.einsum(
        "td,fd->tf", shared_grad, shared_out_b, preferred_element_type=jnp.float32
    )
    shared_gate_grad, shared_up_grad = gated_grads(
        shared_up[:, 0], shared_up[:, 1], grad_shared_act
    )
    grad_shared_up = jnp.stack([shared_gate_grad, shared_up_grad], axis=1).astype(jnp.bfloat16)
    grad_shared_in = jnp.einsum(
        "td,tkf->dkf", routed, grad_shared_up, preferred_element_type=jnp.float32
    )
    grad_routed = jnp.einsum(
        "tkf,dkf->td", grad_shared_up, shared_in_b, preferred_element_type=jnp.float32
    )
    gate_slope = jnp.sum(grad_own * shared_rows, axis=-1) * weight_own * (1.0 - weight_own)
    grad_gate_vector = jnp.dot(gate_slope, routed_own.astype(jnp.float32), precision=highest)
    grad_own_routed = gate_slope[:, None] * gate_vector_b.astype(jnp.float32)[None]
    grad_gates = jnp.sum(grad_own[:, None, :] * picked, axis=-1)
    grad_slots = (
        (gate_values[..., None] * grad_own[:, None, :])
        .astype(jnp.bfloat16)
        .reshape(-1, model_width)
    )
    grad_send = jnp.einsum("sr,sd->rd", placement, grad_slots, preferred_element_type=jnp.float32)
    grad_send = grad_send.astype(jnp.bfloat16).reshape(experts, capacity, model_width)
    grad_arrived = lax.all_to_all(
        grad_send, GROUP, split_axis=0, concat_axis=0, tiled=True
    )
    arrived_rows = incoming.reshape(-1, model_width)
    arrived_grad = grad_arrived.reshape(-1, model_width)
    expert_up = jnp.dot(
        arrived_rows, expert_in_b.reshape(model_width, -1), preferred_element_type=jnp.float32
    ).reshape(-1, 2, ffe_width)
    expert_act = (jax.nn.silu(expert_up[:, 0]) * expert_up[:, 1]).astype(jnp.bfloat16)
    grad_expert_back = jnp.einsum(
        "rf,rd->fd", expert_act, arrived_grad, preferred_element_type=jnp.float32
    )
    grad_expert_act = jnp.einsum(
        "rd,fd->rf", arrived_grad, expert_back_b, preferred_element_type=jnp.float32
    )
    expert_gate_grad, expert_up_grad = gated_grads(
        expert_up[:, 0], expert_up[:, 1], grad_expert_act
    )
    grad_expert_up = jnp.stack([expert_gate_grad, expert_up_grad], axis=1).astype(jnp.bfloat16)
    grad_expert_in = jnp.einsum(
        "rd,rkf->dkf", arrived_rows, grad_expert_up, preferred_element_type=jnp.float32
    )
    grad_arrived_rows = jnp.einsum(
        "rkf,dkf->rd", grad_expert_up, expert_in_b, preferred_element_type=jnp.float32
    )
    grad_arrived_rows = grad_arrived_rows.astype(jnp.bfloat16).reshape(
        experts, capacity, model_width
    )
    grad_returned = lax.all_to_all(
        grad_arrived_rows, GROUP, split_axis=0, concat_axis=0, tiled=True
    )
    grad_copies = jnp.dot(
        placement, grad_returned.reshape(-1, model_width), preferred_element_type=jnp.float32
    )
    grad_own_routed = grad_own_routed + jnp.sum(
        grad_copies.reshape(quarter, top_count, model_width), axis=1
    )
    grad_probability = jnp.sum(grad_gates[..., None] * expert_match, axis=1)
    grad_logits = probability * (
        grad_probability - jnp.sum(probability * grad_probability, axis=-1, keepdims=True)
    )
    grad_router = jnp.dot(routed_own.astype(jnp.float32).T, grad_logits, precision=highest)
    grad_own_routed = grad_own_routed + jnp.dot(
        grad_logits, router_weight_b.astype(jnp.float32).T, precision=highest
    )
    own_part = lax.dynamic_slice_in_dim(grad_routed, own_row, quarter) + grad_own_routed
    grad_routed = lax.dynamic_update_slice_in_dim(grad_routed, own_part, own_row, 0)
    grad_routed, grad_router, grad_gate_vector = (
        lax.psum(grad_routed.astype(jnp.bfloat16), EXP).astype(jnp.float32),
        lax.psum(grad_router.astype(jnp.bfloat16), EXP).astype(jnp.float32),
        lax.psum(grad_gate_vector.astype(jnp.bfloat16), EXP).astype(jnp.float32),
    )
    scaled_two = grad_routed * gain_two_b.astype(jnp.float32)
    grad_gain_two = jnp.sum(grad_routed * hidden * inverse_two, axis=0)
    grad_hidden = (
        grad_full
        + inverse_two * scaled_two
        - hidden * inverse_two**3 * jnp.mean(scaled_two * hidden, axis=-1, keepdims=True)
    )
    grad_hidden_low = grad_hidden.astype(jnp.bfloat16)
    grad_out_weight = jnp.einsum(
        "tn,td->nd", attended_low, grad_hidden_low, preferred_element_type=jnp.float32
    )
    grad_attended = jnp.einsum(
        "td,nd->tn", grad_hidden_low, out_weight_b, preferred_element_type=jnp.float32
    )
    grad_attended = grad_attended.astype(jnp.bfloat16).reshape(rows_local, heads_local, head_size)
    back_keys, back_values = (all_keys, all_values)
    scores_again = masked_scores(queries, back_keys, allowed, score_scale)
    weights_wide = jnp.exp(scores_again - log_total)
    row_delta = jnp.sum(grad_attended.astype(jnp.float32) * attended, axis=-1).T
    grad_weights = jnp.einsum(
        "qhd,khd->hqk", grad_attended, back_values, preferred_element_type=jnp.float32
    )
    grad_scores = (weights_wide * (grad_weights - row_delta[..., None])).astype(jnp.bfloat16)
    grad_queries = (
        jnp.einsum("hqk,khd->qhd", grad_scores, back_keys, preferred_element_type=jnp.float32)
        * score_scale
    )
    grad_keys = (
        jnp.einsum("hqk,qhd->khd", grad_scores, queries, preferred_element_type=jnp.float32)
        * score_scale
    )
    grad_values = jnp.einsum(
        "hqk,qhd->khd",
        weights_wide.astype(jnp.bfloat16),
        grad_attended,
        preferred_element_type=jnp.float32,
    )
    grad_keys, grad_values = (
        lax.psum_scatter(
            grad_keys.astype(jnp.bfloat16), CTX, scatter_dimension=0, tiled=True
        ).astype(jnp.float32),
        lax.psum_scatter(
            grad_values.astype(jnp.bfloat16), CTX, scatter_dimension=0, tiled=True
        ).astype(jnp.float32),
    )
    grad_linear = jnp.stack(
        [
            rotate_back(grad_queries, cosine, sine_table),
            rotate_back(grad_keys, cosine, sine_table),
            grad_values,
        ],
        axis=1,
    )
    grad_linear = grad_linear.astype(jnp.bfloat16)
    grad_bias = jnp.sum(grad_linear.astype(jnp.float32), axis=0)
    grad_flat = grad_linear.reshape(rows_local, -1)
    grad_qkv = jnp.einsum(
        "td,tn->dn", normed, grad_flat, preferred_element_type=jnp.float32
    ).reshape(qkv_weight_b.shape)
    grad_normed = jnp.einsum(
        "tn,dn->td",
        grad_flat,
        qkv_weight_b.reshape(model_width, -1),
        preferred_element_type=jnp.float32,
    )
    grad_normed = lax.psum(grad_normed.astype(jnp.bfloat16), EXP).astype(jnp.float32)
    scaled_one = grad_normed * gain_one_b.astype(jnp.float32)
    grad_gain_one = jnp.sum(grad_normed * tokens_wide * inverse_one, axis=0)
    grad_tokens = (
        grad_hidden
        + inverse_one * scaled_one
        - tokens_wide * inverse_one**3 * jnp.mean(scaled_one * tokens_wide, axis=-1, keepdims=True)
    )
    grad_tokens_own = lax.dynamic_slice_in_dim(grad_tokens, own_row, quarter).astype(jnp.bfloat16)[
        None
    ]
    dense_sums = (
        lax.psum_scatter(
            grad_gain_one.astype(jnp.bfloat16), PLANE, scatter_dimension=0, tiled=True
        ).astype(jnp.float32),
        lax.psum_scatter(
            grad_qkv.astype(jnp.bfloat16), PLANE, scatter_dimension=0, tiled=True
        ).astype(jnp.float32),
        lax.psum_scatter(
            grad_bias.astype(jnp.bfloat16), PLANE, scatter_dimension=2, tiled=True
        ).astype(jnp.float32),
        lax.psum_scatter(
            grad_out_weight.astype(jnp.bfloat16), PLANE, scatter_dimension=1, tiled=True
        ).astype(jnp.float32),
        lax.psum_scatter(
            grad_gain_two.astype(jnp.bfloat16), PLANE, scatter_dimension=0, tiled=True
        ).astype(jnp.float32),
        lax.psum_scatter(
            grad_router.astype(jnp.bfloat16), PLANE, scatter_dimension=0, tiled=True
        ).astype(jnp.float32),
        lax.psum_scatter(
            grad_gate_vector.astype(jnp.bfloat16),
            PLANE,
            scatter_dimension=0,
            tiled=True,
        ).astype(jnp.float32),
        lax.psum_scatter(
            grad_shared_in.astype(jnp.bfloat16), PLANE, scatter_dimension=0, tiled=True
        ).astype(jnp.float32),
        lax.psum_scatter(
            grad_shared_out.astype(jnp.bfloat16), PLANE, scatter_dimension=1, tiled=True
        ).astype(jnp.float32),
    )
    expert_sums = (
        lax.psum_scatter(
            grad_expert_in[None].astype(jnp.bfloat16), DP, scatter_dimension=1, tiled=True
        ).astype(jnp.float32),
        lax.psum_scatter(
            grad_expert_back[None].astype(jnp.bfloat16), DP, scatter_dimension=2, tiled=True
        ).astype(jnp.float32),
    )
    return (
        output,
        grad_tokens_own,
        dense_sums[0].astype(jnp.bfloat16),
        dense_sums[1].astype(jnp.bfloat16),
        dense_sums[2].astype(jnp.bfloat16),
        dense_sums[3].astype(jnp.bfloat16),
        dense_sums[4].astype(jnp.bfloat16),
        dense_sums[5].astype(jnp.bfloat16),
        dense_sums[6].astype(jnp.bfloat16),
        dense_sums[7].astype(jnp.bfloat16),
        dense_sums[8].astype(jnp.bfloat16),
        expert_sums[0].astype(jnp.bfloat16),
        expert_sums[1].astype(jnp.bfloat16),
    )


MIB = 1 << 20
MESH = pl.DeviceIdType.MESH


def dot_nn(a, b):
    return lax.dot_general(a, b, (((1,), (0,)), ((), ())), preferred_element_type=f32)


def dot_nt(a, b):
    return lax.dot_general(a, b, (((1,), (1,)), ((), ())), preferred_element_type=f32)


def dot_tn(a, b):
    return lax.dot_general(a, b, (((0,), (0,)), ((), ())), preferred_element_type=f32)


def place():
    i = lax.axis_index(DP)
    return i // 2, i % 2, lax.axis_index(CTX), lax.axis_index(EXP)


def owner_dense(r):
    x, c, y, _ = place()
    return (((x + r % 2) % 2) * 2 + (c + r // 4) % 2) * 2 + (y + (r // 2) % 2) % 2


def owner_expert(r):
    x, c, _, _ = place()
    return ((x + r % 2) % 2) * 2 + (c + r // 2) % 2


def near(d):
    z = lax.axis_index(EXP)
    return ((z // 2 + d // 2) % 2) * 2 + (z % 2 + d % 2) % 2


def peers():
    x, c, y, _ = place()
    far = [{EXP: near(d)} for d in (1, 2, 3)]
    return {DP: ((x + 1) % 2) * 2 + c}, {CTX: 1 - y}, {DP: x * 2 + (c + 1) % 2}, far


def greet(devices):
    barrier = pltpu.get_barrier_semaphore()
    for device in devices:
        pl.semaphore_signal(barrier, 1, device_id=device, device_id_type=MESH)
    pl.semaphore_wait(barrier, len(devices))


class Wire:
    def __init__(self, wires, ends, device):
        self.ends, self.device, self.sent = ends, device, False
        self.send, self.recv, self.k = wires.send, wires.recv, len(wires.copies)
        wires.copies.append(self)

    def copy(self):
        source, target = self.ends()
        return pltpu.make_async_remote_copy(
            src_ref=source,
            dst_ref=target,
            send_sem=self.send.at[self.k],
            recv_sem=self.recv.at[self.k],
            device_id=self.device,
            device_id_type=MESH,
        )

    def start(self):
        self.copy().start()
        return self

    def wait_recv(self):
        self.copy().wait_recv()

    def wait_send(self):
        self.copy().wait_send()
        self.sent = True


class Wires:
    def __init__(self, send, recv):
        self.send, self.recv, self.copies = send, recv, []

    def add(self, ends, device):
        return Wire(self, ends, device)

    def go(self, ends, device):
        return Wire(self, ends, device).start()

    def drain(self):
        for wire in self.copies:
            if not wire.sent:
                wire.wait_send()


class Loads:
    def __init__(self, sems):
        self.sems, self.count = sems, 0

    def go(self, source, target):
        copy = pltpu.make_async_copy(source, target, self.sems.at[self.count])
        self.count += 1
        copy.start()
        return copy


def cols(ref, block, width):
    return ref[:, pl.ds(pl.multiple_of(block * width, width), width)]


def piece(ref, d, rows):
    return ref[pl.ds(pl.multiple_of(near(d) * rows, rows), rows), :]


def turn(values, cosine, sine):
    return values * cosine + pltpu.roll(values, 64, 1) * sine


def turn_back(values, cosine, sine):
    return values * cosine - pltpu.roll(values, 64, 1) * sine


def gated(gate, up, grad_act):
    s = jax.nn.sigmoid(gate)
    act = gate * s
    return act * up, grad_act * up * s * (1.0 + gate * (1.0 - s)), grad_act * act


def softmax_parts(q, k_own, k_oth, mask_own, mask_oth):
    scale = 128 ** (-0.5)
    s_own = jnp.where(mask_own, dot_nt(q, k_own) * scale, -1e30)
    s_oth = jnp.where(mask_oth, dot_nt(q, k_oth) * scale, -1e30)
    peak = jnp.maximum(
        jnp.max(s_own, axis=-1, keepdims=True), jnp.max(s_oth, axis=-1, keepdims=True)
    )
    e_own = jnp.exp(s_own - peak)
    e_oth = jnp.exp(s_oth - peak)
    total = jnp.sum(e_own, axis=-1, keepdims=True) + jnp.sum(e_oth, axis=-1, keepdims=True)
    back = 1.0 / total
    return e_own * back, e_oth * back


def split3(v):
    high = v.astype(bf16).astype(f32)
    mid = (v - high).astype(bf16).astype(f32)
    return high, mid, v - high - mid


def probabilities(rows, small):
    logits = dot_nt(rows, small[...])
    lane = lax.broadcasted_iota(jnp.int32, logits.shape, 1)
    logits = jnp.where((lane >= 3) & (lane < 11), logits, -1e30)
    e = jnp.exp(logits - jnp.max(logits, axis=-1, keepdims=True))
    return e / jnp.sum(e, axis=-1, keepdims=True), lane


ARRIVAL = (0, 4, 1, 5, 2, 6, 3, 7)


class Spread:
    def __init__(self, wires, own, slots, dense):
        x, y, core, _ = peers()
        self.slots, self.own, self.copies = slots, own, {}

        def ends(r, target):
            return lambda: (self.block(r), slots.at[target])

        self.copies[1] = wires.add(ends(0, 1), x)
        if dense:
            self.copies[2] = wires.add(ends(0, 2), y)
            self.copies[3] = wires.add(ends(1, 3), y)
        side = 4 if dense else 2
        for r in range(side):
            self.copies[side + r] = wires.add(ends(r, side + r), core)

    def block(self, r):
        return self.own() if r == 0 else self.slots.at[r]

    def start(self, r):
        self.copies[r].start()

    def wait(self, r):
        self.copies[r].wait_recv()


V, A = "vmem", "any"


def call(kernel, number, ins, outs, scratch, vmem, flops, traffic):
    def spec(kind):
        return pl.BlockSpec(memory_space=pl.ANY if kind == A else pltpu.VMEM)

    names = list(ins) + list(outs) + list(scratch)

    def run(*refs):
        kernel(SimpleNamespace(**dict(zip(names, refs))))

    made = pl.pallas_call(
        run,
        out_shape=tuple(jax.ShapeDtypeStruct(o[0], o[1]) for o in outs.values()),
        in_specs=[spec(i[1]) for i in ins.values()],
        out_specs=tuple(spec(o[2]) for o in outs.values()),
        scratch_shapes=list(scratch.values()),
        compiler_params=pltpu.CompilerParams(
            vmem_limit_bytes=vmem * MIB, collective_id=number, has_side_effects=number is not None
        ),
        cost_estimate=pl.CostEstimate(flops=flops, bytes_accessed=traffic, transcendentals=0),
    )(*[i[0] for i in ins.values()])
    return SimpleNamespace(**dict(zip(outs, made)))


def own_rows(total, hidden, routed, g, small, high_o, low_o, vec_o):
    extra = total[:, 2048:2176]
    wide = routed.astype(f32)
    prob, _ = probabilities(routed, small)
    sw = jax.nn.sigmoid(jnp.sum(wide * small[2:3, :].astype(f32), axis=-1, keepdims=True))
    slope = jnp.sum(extra[:, 48:96], axis=-1, keepdims=True) * sw * (1.0 - sw)
    dgate = [
        extra[:, e : e + 1] + extra[:, 16 + e : 17 + e] + extra[:, 32 + e : 33 + e]
        for e in range(8)
    ]
    probs = [prob[:, 3 + e : 4 + e] for e in range(8)]
    mean = sum(p * d for p, d in zip(probs, dgate))
    grad = total[:, 0:2048] + slope * small[2:3, :].astype(f32)
    vec_o[...] = jnp.zeros_like(vec_o)
    vec_o[2:3, :] = jnp.sum(slope * wide, axis=0, keepdims=True)
    for e in range(8):
        dlogit = probs[e] * (dgate[e] - mean)
        grad += dlogit * small[3 + e : 4 + e, :].astype(f32)
        vec_o[3 + e : 4 + e, :] = jnp.sum(dlogit * wide, axis=0, keepdims=True)
    inv = lax.rsqrt(jnp.mean(hidden * hidden, axis=-1, keepdims=True) + epsilon)
    vec_o[1:2, :] = jnp.sum(grad * hidden * inv, axis=0, keepdims=True)
    scaled = grad * small[1:2, :].astype(f32)
    mean = jnp.mean(scaled * hidden, axis=-1, keepdims=True)
    high = g.astype(f32) + inv * scaled - hidden * (inv * inv * inv * mean)
    high_o[...] = high
    low_o[...] = high.astype(bf16)


def layer_kernel(k):
    x_dev, y_dev, core_dev, z_dev = peers()
    wires, loads = Wires(k.send_sems, k.recv_sems), Loads(k.load_sems)
    greet([x_dev, y_dev, core_dev] + z_dev)
    y = lax.axis_index(CTX)
    mine = y * 4 + lax.axis_index(EXP)

    def to_z(make):
        return [wires.go(make(d), z_dev[d - 1]) for d in (1, 2, 3)]

    class Collect:
        def __init__(self, slot):
            self.slot = slot
            self.one = wires.go(lambda: (slot(0), slot(1)), z_dev[0])
            self.three = wires.go(lambda: (slot(0), slot(3)), z_dev[2])

        def hand_on(self):
            self.three.wait_recv()
            self.two = wires.go(lambda: (self.slot(3), self.slot(2)), z_dev[0])

        def wait(self):
            self.one.wait_recv()
            self.two.wait_recv()

    vec = Spread(wires, lambda: k.w_v, k.s_v, True)
    qkv = Spread(wires, lambda: k.w_q, k.s_q, True)
    out = Spread(wires, lambda: k.w_o, k.s_o, True)
    eg = Spread(wires, lambda: k.split_ei.at[0], k.s_eg, False)
    eu = Spread(wires, lambda: k.split_ei.at[1], k.s_eu, False)
    ed = Spread(wires, lambda: k.w_ed, k.s_ed, False)
    sg = Spread(wires, lambda: k.split_si.at[0], k.s_sg, True)
    su = Spread(wires, lambda: k.split_si.at[1], k.s_su, True)
    sd = Spread(wires, lambda: k.w_sd, k.s_sd, True)
    first, expert, shared = (vec, qkv), (eg, eu, ed), (sg, su, sd)
    k.w_v[...] = jnp.zeros_like(k.w_v)
    for m, vector in enumerate((k.gain_one, k.gain_two, k.gate_vector)):
        k.w_v[m : m + 1, :] = vector[...].reshape(1, 256)
    k.w_v[3:11, :] = k.router[...]
    for s in first + (out, ed):
        s.start(1)
    for s in first:
        s.start(2)
    for s in first + (out,):
        s.start(4)
    k.col[0:128, :] = jnp.full((128, 128), -1.0, f32)
    k.col[0:4, 0:64] = k.ids_own[...].astype(f32)
    k.ids[0, 0:64, :] = k.col[0:128, :].T[0:64, :]
    ids_y = wires.go(lambda: (k.ids.at[0, pl.ds(0, 64), :], k.ids_y), y_dev)
    k.s_v[0] = k.w_v[...]
    k.col[...] = jnp.broadcast_to(k.blocks[...].astype(f32), (128, 512)).T
    for target, half in ((k.ids_near, y), (k.ids_far, 1 - y)):
        for d in range(4):
            at = pl.ds(pl.multiple_of(half * 256 + near(d) * 64, 64), 64)
            k.ids_q[d * 64 : (d + 1) * 64, :] = k.col[at, :]
        target[...] = k.ids_q[...].T[0:8, :]
    for d in range(4):
        at = pl.ds(pl.multiple_of(y * 256 + near(d) * 64, 64), 64)
        to = slice(d * 64, (d + 1) * 64)
        k.ids_q[to, :] = k.col[at, :]
        k.cs[to, :] = k.cs_all[at, :]
        k.sn[to, :] = k.sn_all[at, :]
    later = []

    def attention_part(scaled, acc, w, low_w, mixed, apart):
        held, held_out = {}, []

        def bring(r):
            held[r] = loads.go(qkv.block(r), w.at[r])

        def bring_out(r):
            held_out.append(loads.go(out.block(r), low_w.at[r]))

        raw = [loads.go(k.w_ei.at[pl.ds(256 * m, 256)], mixed.at[m]) for m in range(2)]
        raw.append(loads.go(k.w_si, mixed.at[2]))
        bring(0)
        for d in range(4):
            t = piece(k.tok, d, 64).astype(f32)
            inv = lax.rsqrt(jnp.mean(t * t, axis=-1, keepdims=True) + epsilon)
            scaled[d * 64 : (d + 1) * 64, :] = t * inv
            k.inv1[d * 64 : (d + 1) * 64, :] = inv
        for m in range(3):
            for h in range(4):
                at = slice(h * 128, (h + 1) * 128)
                line = k.bias[m, h : h + 1, :].astype(f32)
                acc[m, :, at] = jnp.broadcast_to(line, (256, 128))

        def take_apart(m):
            raw[m].wait()
            target = k.split_si if m == 2 else k.split_ei
            to = pl.ds(0 if m == 2 else 256 * m, 256)
            done = []
            for n in range(2):
                apart[m, n] = mixed[m, :, n, :]
                done.append(loads.go(apart.at[m, n], target.at[n, to, :]))
            return done

        done = take_apart(0) + take_apart(1)
        for copy in done:
            copy.wait()
        for s in (eg, eu):
            s.start(1)
        for s in expert:
            s.start(2)

        def block(r):
            held[r].wait()
            o = owner_dense(r)
            vectors = k.s_v[r]
            k.small[:, pl.ds(pl.multiple_of(o * 256, 256), 256)] = vectors
            normed = (cols(scaled, o, 256) * vectors[0:1, :].astype(f32)).astype(bf16)
            target = k.n_keep if r < 4 else k.n_send
            target[:, (r % 4) * 256 : (r % 4 + 1) * 256] = normed
            for m in range(3):
                acc[m] += dot_nn(normed, w[r, m * 256 : (m + 1) * 256, :])

        def arrived(r, onward=()):
            for s in first:
                s.wait(r)
                for t in onward:
                    s.start(t)
            bring(r)

        arrived(4)
        block(0)
        block(4)
        arrived(1, (3, 5))
        out.start(2)
        arrived(2, (6,))
        block(1)
        arrived(5)
        block(5)
        arrived(6)
        block(2)
        block(6)
        for copy in take_apart(2):
            copy.wait()
        for s in shared:
            s.start(1)
        for s in shared:
            s.start(4)
        ids_y.wait_recv()
        k.ids[0, 64:128, :] = k.ids_y[...]
        later.extend(to_z(lambda d: lambda: (k.ids.at[0], k.ids.at[d])))
        bring_out(0)
        out.wait(4)
        bring_out(4)
        out.wait(1)
        out.start(5)
        bring_out(1)
        arrived(3, (7,))
        block(3)
        arrived(7)
        block(7)
        for h in range(4):
            at = slice(h * 128, (h + 1) * 128)
            k.kv[0:256, at] = turn(acc[1, :, at], k.cs[...], k.sn[...]).astype(bf16)
        k.kv[256:512, :] = acc[2].astype(bf16)
        kv_y = wires.go(lambda: (k.kv, k.kv_oth), y_dev)
        out.start(3)
        sg.start(2)
        su.start(2)
        for h in range(4):
            at = slice(h * 128, (h + 1) * 128)
            k.q[:, at] = turn(acc[0, :, at], k.cs[...], k.sn[...]).astype(bf16)
        out.wait(5)
        bring_out(5)
        out.wait(2)
        out.start(6)
        bring_out(2)
        kv_y.wait_recv()
        mask_own = k.ids_near[0:1, :] <= k.ids_q[:, 0:1]
        mask_oth = k.ids_far[0:1, :] <= k.ids_q[:, 0:1]
        for h in range(4):
            at = slice(h * 128, (h + 1) * 128)
            w_own, w_oth = softmax_parts(
                k.q[:, at], k.kv[0:256, at], k.kv_oth[0:256, at], mask_own, mask_oth
            )
            value = dot_nn(w_own.astype(bf16), k.kv[256:512, at])
            value += dot_nn(w_oth.astype(bf16), k.kv_oth[256:512, at])
            k.low[:, at] = value.astype(bf16)
        out.wait(6)
        bring_out(6)
        out.wait(3)
        out.start(7)
        bring_out(3)
        out.wait(7)
        bring_out(7)
        for copy in held_out:
            copy.wait()
        for r in range(8):
            part = dot_nn(k.low[...], low_w[r]).astype(bf16)
            at = pl.ds(pl.multiple_of(owner_dense(r) * 256, 256), 256)
            for d in range(4):
                k.att_send[d, :, at] = part[d * 64 : (d + 1) * 64, :]

    pl.run_scoped(
        attention_part,
        pltpu.VMEM((256, 2048), f32),
        pltpu.VMEM((3, 256, 512), f32),
        pltpu.VMEM((8, 768, 512), bf16),
        pltpu.VMEM((8, 512, 256), bf16),
        pltpu.VMEM((3, 256, 2, 1408), bf16),
        pltpu.VMEM((3, 2, 256, 1408), bf16),
    )
    att_z = to_z(lambda d: lambda: (k.att_send.at[d], k.att.at[d - 1]))
    swap_n = wires.go(lambda: (k.n_send, k.n_x), core_dev)
    swap_low = wires.go(lambda: (k.low, k.low_x), core_dev)
    parts = SimpleNamespace(started=False)

    def expert_part(wg, wu, wd, slopes, acc, up, keep, send):
        group = []

        def gather(s, w):
            group.append(loads.go(s.block(0), w.at[0]))
            s.wait(2)
            group.append(loads.go(s.block(2), w.at[2]))
            s.wait(1)
            s.start(3)
            group.append(loads.go(s.block(1), w.at[1]))

        def gather_last(s, w):
            s.wait(3)
            group.append(loads.go(s.block(3), w.at[3]))

        gather(ed, wd)
        for copy in att_z:
            copy.wait_recv()
        value = piece(k.tok, 0, 64).astype(f32) + (
            k.att_send[0].astype(f32)
            + k.att[0].astype(f32)
            + k.att[1].astype(f32)
            + k.att[2].astype(f32)
        )
        inv = lax.rsqrt(jnp.mean(value * value, axis=-1, keepdims=True) + epsilon)
        k.hidden[...] = value
        k.rows[0:64, :] = (value * inv * k.small[1:2, :].astype(f32)).astype(bf16)
        own_y = wires.go(
            lambda: (k.rows.at[pl.ds(0, 64), :], k.rows.at[pl.ds(256, 64), :]), y_dev
        )
        g_y = wires.go(lambda: (k.g_own, k.g_oth), y_dev)
        sd.start(2)
        own_z = Collect(lambda d: k.rows.at[pl.ds(64 * d, 64), :])
        gather_last(ed, wd)
        gather(eg, wg)
        gather_last(eg, wg)
        for s in (sg, su):
            s.wait(2)
            s.start(6)
        own_z.hand_on()
        for copy in later:
            copy.wait_recv()
        own_y.wait_recv()
        own_z.wait()
        oth_z = to_z(
            lambda d: lambda: (
                k.rows.at[pl.ds(256, 64), :],
                k.rows.at[pl.ds(256 + 64 * d, 64), :],
            )
        )

        def g_piece(half, d, at):
            g = k.g_oth if half else k.g_own
            return g[pl.ds(pl.multiple_of(near(d) * 64, 64), 64), at].astype(f32)

        def route(half):
            chosen = []
            for d in range(4):
                named = (k.ids[d, half * 64 : (half + 1) * 64, :] == mine.astype(f32)).astype(f32)
                chosen.append(jnp.sum(named, axis=-1, keepdims=True))
            chosen = jnp.concatenate(chosen, axis=0)
            prob, lane = probabilities(k.rows[half * 256 : (half + 1) * 256, :], k.small)
            here = jnp.sum(jnp.where(lane == mine + 3, prob, 0.0), axis=-1, keepdims=True)
            gate = here * chosen
            for d in range(4):
                at = slice(half * 256 + d * 64, half * 256 + (d + 1) * 64)
                value = gate[d * 64 : (d + 1) * 64, :] * g_piece(half, d, slice(None))
                slopes[at, :] = value.astype(bf16)
            return gate, chosen

        def gate_part(half):
            rows_at = slice(half * 256, (half + 1) * 256)

            def one(r, _):
                at = pl.ds(pl.multiple_of(owner_expert(r) * 512, 512), 512)
                acc[0] += dot_nn(k.rows[rows_at, at], wg[r])
                acc[2] += dot_nt(slopes[rows_at, at], wd[r])
                return 0

            acc[...] = jnp.zeros_like(acc)
            lax.fori_loop(0, 4, one, 0)

        def phase_one(half):
            rows_at = slice(half * 256, (half + 1) * 256)

            def one(r, _):
                at = pl.ds(pl.multiple_of(owner_expert(r) * 512, 512), 512)
                acc[1] += dot_nn(k.rows[rows_at, at], wu[r])
                return 0

            lax.fori_loop(0, 4, one, 0)
            for d in range(4):
                at, to = slice(d * 64, (d + 1) * 64), slice(half * 256 + d * 64, half * 256 + (d + 1) * 64)
                act, gate_grad, up_grad = gated(acc[0, at, :], acc[1, at, :], acc[2, at, :])
                up[0, to, :] = act.astype(bf16)
                up[1, to, :] = gate_grad.astype(bf16)
                up[2, to, :] = up_grad.astype(bf16)

        lanes = lax.broadcasted_iota(jnp.int32, (64, 128), 1)

        def phase_two(half, gate, chosen, between):
            rows_at = slice(half * 256, (half + 1) * 256)

            def two(r, dgate):
                at = pl.ds(pl.multiple_of(owner_expert(r) * 512, 512), 512)
                result = dot_nn(up[0, rows_at, :], wd[r]).astype(bf16).astype(f32)
                grad = dot_nt(up[1, rows_at, :], wg[r]) + dot_nt(up[2, rows_at, :], wu[r])
                sums = []
                for d in range(4):
                    here = slice(d * 64, (d + 1) * 64)
                    g_rows = g_piece(half, d, at)
                    sums.append(jnp.sum(g_rows * result[here, :], axis=-1, keepdims=True))
                    part = gate[here, :] * result[here, :]
                    if half == 0:
                        k.out_sum[here, at] = part
                        k.grad_sum[here, at] = grad[here, :]
                    else:
                        k.e_out[d, :, at] = part.astype(bf16)
                        k.e_grad[d, :, at] = grad[here, :].astype(bf16)
                return dgate + jnp.concatenate(sums, axis=0)

            dgate = lax.fori_loop(0, 2, two, jnp.zeros((256, 1), f32))
            between()
            dgate = lax.fori_loop(2, 4, two, dgate) * chosen
            for d in range(4):
                extra = jnp.zeros((64, 128), f32)
                for m, part in enumerate(split3(dgate[d * 64 : (d + 1) * 64, :])):
                    extra = jnp.where(lanes == mine + 16 * m, part, extra)
                if half == 0:
                    k.extras[d * 64 : (d + 1) * 64, :] = extra
                else:
                    k.e_grad[d, :, 2048:2176] = extra.astype(bf16)

        gate, chosen = route(0)
        for copy in group:
            copy.wait()
        group.clear()
        gate_part(0)
        gather(eu, wu)
        gather_last(eu, wu)
        for copy in group:
            copy.wait()
        phase_one(0)
        phase_two(0, gate, chosen, lambda: None)
        sg.wait(1)
        sg.start(3)
        sg.start(5)
        for copy in oth_z + [g_y]:
            copy.wait_recv()
        gate, chosen = route(1)
        gate_part(1)
        phase_one(1)
        saved = [loads.go(up, k.ex_up)]
        for r in range(4):
            to = slice(r * 256, (r + 1) * 256)
            for target, m in ((keep, r), (send, r + 4)):
                at = pl.ds(pl.multiple_of(owner_dense(m) * 256, 256), 256)
                target[0:512, to] = slopes[:, at]
                target[512:1024, to] = k.rows[:, at]
        saved.append(loads.go(keep, k.ex_keep))
        swap_ex = wires.go(lambda: (send, k.ex_x), core_dev)
        sd.wait(2)
        sd.start(6)

        def pass_on():
            su.wait(1)
            su.start(3)
            su.start(5)

        phase_two(1, gate, chosen, pass_on)
        for copy in saved:
            copy.wait()
        swap_ex.wait_send()
        swap_ex.ends = lambda: (k.ex_keep, k.ex_x)
        parts.swap_ex = swap_ex

    pl.run_scoped(
        expert_part,
        pltpu.VMEM((4, 512, 1408), bf16),
        pltpu.VMEM((4, 512, 1408), bf16),
        pltpu.VMEM((4, 1408, 512), bf16),
        pltpu.VMEM((512, 2048), bf16),
        pltpu.VMEM((3, 256, 1408), f32),
        pltpu.VMEM((3, 512, 1408), bf16),
        pltpu.VMEM((1024, 1024), bf16),
        pltpu.VMEM((1024, 1024), bf16),
    )
    swap_up = {}
    for m in (1, 2, 0):
        swap_up[m] = wires.go(lambda m=m: (k.ex_up.at[m], k.ex_up_x.at[m]), core_dev)
    e_grad_z = to_z(lambda d: lambda: (k.e_grad.at[d], k.e_grad_z.at[d - 1]))
    e_out_z = to_z(lambda d: lambda: (k.e_out.at[d], k.e_out_z.at[d - 1]))
    over_y, over_x = {}, {}

    def expert_grad(m, kept, sent, landed):
        parts.swap_ex_wait()
        swap_up[m].wait_recv()

        def inner(left, right, keep, send):
            start = pl.ds(0 if m == 0 else 512, 512)
            got = [
                loads.go(k.ex_up.at[m], right.at[0]),
                loads.go(k.ex_up_x.at[m], right.at[1]),
                loads.go(k.ex_keep.at[start, :], left.at[0]),
                loads.go(k.ex_x.at[start, :], left.at[1]),
            ]
            for copy in got:
                copy.wait()
            saved = []
            for r in (3, 1, 2, 0):
                target = send if r % 2 else keep
                at = slice(r * 256, (r + 1) * 256)
                to = pl.ds(pl.multiple_of(((y + r // 2) % 2) * 256, 256), 256)
                if m == 0:
                    total = dot_tn(right[0], left[0, :, at]) + dot_tn(right[1], left[1, :, at])
                    target[:, to] = total.astype(bf16)
                else:
                    total = dot_tn(left[0, :, at], right[0]) + dot_tn(left[1, :, at], right[1])
                    target[to, :] = total.astype(bf16)
                if r == 1:
                    saved.append(loads.go(send, sent))
                if r == 2:
                    saved[0].wait()
                    over_x[6 + m] = wires.go(lambda: (sent, landed), x_dev)
            loads.go(keep, kept).wait()

        shape = (1408, 512) if m == 0 else (512, 1408)
        pl.run_scoped(
            inner,
            pltpu.VMEM((2, 512, 1024), bf16),
            pltpu.VMEM((2, 512, 1408), bf16),
            pltpu.VMEM(shape, bf16),
            pltpu.VMEM(shape, bf16),
        )

    def to_y(name, r, source, target):
        over_y[name, r] = wires.go(lambda: (source.at[r % 2], target.at[r % 2]), y_dev)

    def shared_grad(m, keep, send):
        def inner(left, right):
            if m == 0:
                got = [loads.go(k.sh_keep, left.at[0]), loads.go(k.sh_x, left.at[1])]
            else:
                start = pl.ds(512, 256)
                got = [
                    loads.go(k.ex_keep.at[start, :], left.at[0]),
                    loads.go(k.ex_x.at[start, :], left.at[1]),
                ]
            got.append(loads.go(k.sh_up.at[m], right.at[0]))
            got.append(loads.go(k.sh_up_x.at[m], right.at[1]))
            for copy in got:
                copy.wait()
            for r in (3, 1, 2, 0):
                target = send if r >= 2 else keep
                at = slice(r * 256, (r + 1) * 256)
                if m == 0:
                    total = dot_tn(right[0], left[0, :, at]) + dot_tn(right[1], left[1, :, at])
                else:
                    total = dot_tn(left[0, :, at], right[0]) + dot_tn(left[1, :, at], right[1])
                target[r % 2] = total.astype(bf16)

        pl.run_scoped(
            inner, pltpu.VMEM((2, 256, 1024), bf16), pltpu.VMEM((2, 256, 1408), bf16)
        )

    def swap_ex_wait():
        if not parts.started:
            parts.swap_ex.wait_recv()
            parts.started = True

    parts.swap_ex_wait = swap_ex_wait

    def shared_part(wg, wu, wd, slopes, acc, up, keep, send):
        routed = k.rows.at[pl.ds(0, 256), :]
        held = []

        def bring(r, group):
            for s in group:
                held.append(loads.go(s.block(r), {sg: wg, su: wu, sd: wd}[s].at[r]))

        def arrived(r, group, onward=()):
            for s in group:
                s.wait(r)
                for t in onward:
                    s.start(t)
            bring(r, group)

        def settle():
            for copy in held:
                copy.wait()
            held.clear()

        pair, last = (sg, su), (sd,)
        for r in (0, 1, 2):
            bring(r, pair)
        for r in (4, 6):
            arrived(r, pair)
        expert_grad(1, k.k_eg, k.t_eg, k.x_eg)
        arrived(5, pair)
        sd.wait(1)
        sd.start(3)
        sd.start(5)
        bring(0, last)
        bring(1, last)
        bring(2, last)
        arrived(4, last)
        arrived(6, last)
        arrived(5, last)
        wide = routed[...].astype(f32) * k.small[2:3, :].astype(f32)
        sw = jax.nn.sigmoid(jnp.sum(wide, axis=-1, keepdims=True))
        for d in range(4):
            at = slice(d * 64, (d + 1) * 64)
            slopes[at, :] = (sw[at, :] * piece(k.g_own, d, 64).astype(f32)).astype(bf16)
        for r in range(4):
            to = slice(r * 256, (r + 1) * 256)
            keep[:, to] = cols(slopes, owner_dense(r), 256)
            send[:, to] = cols(slopes, owner_dense(r + 4), 256)
        saved = [loads.go(keep, k.sh_keep), loads.go(send, k.sh_send)]
        acc[...] = jnp.zeros_like(acc)

        def one(j, _):
            r = j // 2 + (j % 2) * 4
            row = cols(routed, owner_dense(r), 256)
            acc[0] += dot_nn(row, wg[r])
            acc[1] += dot_nn(row, wu[r])
            return 0

        def back(j, _):
            r = j // 2 + (j % 2) * 4
            acc[2] += dot_nt(cols(slopes, owner_dense(r), 256), wd[r])
            return 0

        settle()
        lax.fori_loop(0, 6, one, 0)
        arrived(3, pair, (7,))
        arrived(7, pair)
        settle()
        lax.fori_loop(6, 8, one, 0)
        for d in range(4):
            at = slice(d * 64, (d + 1) * 64)
            up[0, at, :] = (jax.nn.silu(acc[0, at, :]) * acc[1, at, :]).astype(bf16)
        saved.append(loads.go(up.at[0], k.sh_up.at[0]))
        for copy in saved:
            copy.wait()
        swaps = [
            wires.go(lambda: (k.sh_up.at[0], k.sh_up_x.at[0]), core_dev),
            wires.go(lambda: (k.sh_send, k.sh_x), core_dev),
        ]
        lax.fori_loop(0, 6, back, 0)
        for copy in swaps:
            copy.wait_recv()
        shared_grad(0, k.k_sd, k.t_sd)
        to_y(2, 3, k.t_sd, k.y_sd)
        for copy in e_grad_z:
            copy.wait_recv()
        oth = k.e_grad[0].astype(f32)
        for d in range(3):
            oth += k.e_grad_z[d].astype(f32)
        k.g_send[...] = oth.astype(bf16)
        parts.grad_y = wires.go(lambda: (k.g_send, k.g_y), y_dev)
        expert_grad(2, k.k_eu, k.t_eu, k.x_eu)
        arrived(3, last, (7,))
        arrived(7, last)
        settle()
        lax.fori_loop(6, 8, back, 0)
        for d in range(4):
            at = slice(d * 64, (d + 1) * 64)
            _, gate_grad, up_grad = gated(acc[0, at, :], acc[1, at, :], acc[2, at, :])
            up[1, at, :] = gate_grad.astype(bf16)
            up[2, at, :] = up_grad.astype(bf16)
        saved = [loads.go(up.at[m], k.sh_up.at[m]) for m in (1, 2)]

        def two(r, slope):
            at = pl.ds(pl.multiple_of(owner_dense(r) * 256, 256), 256)
            part = dot_nn(up[0], wd[r])
            total = sw * part + k.out_sum[:, at]
            back = dot_nt(up[1], wg[r]) + dot_nt(up[2], wu[r]) + k.grad_sum[:, at]
            sums = []
            for d in range(4):
                rows_at = slice(d * 64, (d + 1) * 64)
                g_rows = k.g_own[pl.ds(pl.multiple_of(near(d) * 64, 64), 64), at].astype(f32)
                sums.append(jnp.sum(g_rows * part[rows_at, :], axis=-1, keepdims=True))
                k.s_out[d, :, at] = total[rows_at, :].astype(bf16)
                k.s_grad[d, :, at] = back[rows_at, :].astype(bf16)
            return slope + jnp.concatenate(sums, axis=0)

        slope = lax.fori_loop(0, 8, two, jnp.zeros((256, 1), f32))
        lanes = lax.broadcasted_iota(jnp.int32, (64, 128), 1)
        for d in range(4):
            rows_at = slice(d * 64, (d + 1) * 64)
            extra = k.extras[rows_at, :]
            for m, part in enumerate(split3(slope[rows_at, :])):
                extra = jnp.where(lanes == mine + 48 + 16 * m, part, extra)
            k.s_grad[d, :, 2048:2176] = extra.astype(bf16)
        for copy in saved:
            copy.wait()

    pl.run_scoped(
        shared_part,
        pltpu.VMEM((8, 256, 1408), bf16),
        pltpu.VMEM((8, 256, 1408), bf16),
        pltpu.VMEM((8, 1408, 256), bf16),
        pltpu.VMEM((256, 2048), bf16),
        pltpu.VMEM((3, 256, 1408), f32),
        pltpu.VMEM((3, 256, 1408), bf16),
        pltpu.VMEM((256, 1024), bf16),
        pltpu.VMEM((256, 1024), bf16),
    )
    swap_sh = [
        wires.go(lambda m=m: (k.sh_up.at[m], k.sh_up_x.at[m]), core_dev) for m in (1, 2)
    ]
    s_grad_z = to_z(lambda d: lambda: (k.s_grad.at[d], k.s_grad_z.at[d - 1]))

    def back_part(*refs):
        k_sg, k_su, k_q, k_o, k_v = refs[:5]
        t_sg, t_su, t_q, t_o, t_v = refs[5:10]
        f_sg, f_su, f_q, f_o, f_v, f_sd = refs[10:16]
        h_keep, h_send, h_x, lin, lin_x, vec, high, gkv, gkv_send, gn = refs[16:]
        k_sd, t_sd = k.k_sd, k.t_sd

        def fold(name, keep, landed, send, target, device=x_dev):
            over_y[name, 3].wait_recv()

            def inner(buffer):
                loads.go(landed.at[1], buffer).wait()
                send[...] = (keep[1].astype(f32) + buffer[...].astype(f32)).astype(bf16)

            pl.run_scoped(inner, pltpu.VMEM(tuple(keep.shape[1:]), bf16))
            over_x[name] = wires.go(lambda: (send, target), device)

        def finish_pair():
            for name in (0, 1):
                over_y[name, 2].wait_recv()
                over_x[name].wait_recv()

            def inner(left, right, total):
                got = [
                    loads.go(k.y_sg.at[0], left.at[0]),
                    loads.go(k.x_sg, right.at[0]),
                    loads.go(k.y_su.at[0], left.at[1]),
                    loads.go(k.x_su, right.at[1]),
                ]
                for copy in got:
                    copy.wait()
                for n, keep in enumerate((k_sg, k_su)):
                    value = keep[0].astype(f32) + left[n].astype(f32) + right[n].astype(f32)
                    total[:, n, :] = value.astype(bf16)
                loads.go(total, k.d_si).wait()

            pair = pltpu.VMEM((2, 256, 1408), bf16)
            pl.run_scoped(inner, pair, pair, pltpu.VMEM((256, 2, 1408), bf16))

        def finish(name, keep, landed, target, result):
            over_y[name, 2].wait_recv()

            def inner(left, right, total):
                got = loads.go(landed.at[0], left)
                over_x[name].wait_recv()
                more = loads.go(target, right)
                got.wait()
                more.wait()
                value = keep[0].astype(f32) + left[...].astype(f32) + right[...].astype(f32)
                total[...] = value.astype(total.dtype)
                loads.go(total, result).wait()

            shape = tuple(keep.shape[1:])
            pl.run_scoped(
                inner,
                pltpu.VMEM(shape, bf16),
                pltpu.VMEM(shape, bf16),
                pltpu.VMEM(shape, result.dtype),
            )

        swap_sh[0].wait_recv()
        shared_grad(1, k_sg, t_sg)
        to_y(0, 3, t_sg, k.y_sg)
        swap_sh[1].wait_recv()
        shared_grad(2, k_su, t_su)
        to_y(1, 3, t_su, k.y_su)
        expert_grad(0, k.k_ed, k.t_ed, k.x_ed)
        fold(2, k_sd, k.y_sd, f_sd, k.x_sd)

        def other_rows(buffer):
            for copy in e_out_z:
                copy.wait_recv()
            loads.go(k.e_out_z, buffer).wait()
            oth = k.e_out[0].astype(f32)
            for d in range(3):
                oth += buffer[d].astype(f32)
            k.o_send[...] = oth.astype(bf16)

        pl.run_scoped(other_rows, pltpu.VMEM((3, 64, 2048), bf16))
        for copy in s_grad_z:
            copy.wait_recv()
        parts.grad_y.wait_recv()
        total = k.s_grad[0].astype(f32) + k.g_y[...].astype(f32)
        for d in range(3):
            total += k.s_grad_z[d].astype(f32)
        own_rows(
            total,
            k.hidden[...],
            k.rows[0:64, :],
            piece(k.g_own, 0, 64),
            k.small,
            high,
            k.gh.at[0],
            vec,
        )
        gh_z = Collect(lambda d: k.gh.at[d])
        out_y = wires.go(lambda: (k.o_send, k.o_y), y_dev)
        to_y(2, 2, t_sd, k.y_sd)
        fold(0, k_sg, k.y_sg, f_sg, k.x_sg)
        gn_z, s_out_z = [], []

        def attention_back(w, o_w, acc, low_g):
            got, more = [loads.go(k.w_o, o_w.at[0])], [loads.go(k.w_q, w.at[0])]
            for r in range(1, 8):
                got.append(loads.go(k.s_o.at[r], o_w.at[r]))
                more.append(loads.go(k.s_q.at[r], w.at[r]))
            gh_z.hand_on()
            gh_z.wait()
            s_out_z.extend(to_z(lambda d: lambda: (k.s_out.at[d], k.s_out_z.at[d - 1])))
            for copy in got:
                copy.wait()
            acc[...] = jnp.zeros_like(acc)
            for r in range(8):
                at = pl.ds(pl.multiple_of(owner_dense(r) * 256, 256), 256)
                row = jnp.concatenate([k.gh[d, :, at] for d in range(4)], axis=0)
                target = h_keep if r < 4 else h_send
                target[:, (r % 4) * 256 : (r % 4 + 1) * 256] = row
                acc[...] += dot_nt(row, o_w[r])
            swap_h = wires.go(lambda: (h_send, k.h_x), core_dev)
            low_g[...] = acc[...].astype(bf16)
            mask_own = k.ids_near[0:1, :] <= k.ids_q[:, 0:1]
            mask_oth = k.ids_far[0:1, :] <= k.ids_q[:, 0:1]
            scale = 128 ** (-0.5)
            for h in range(4):
                at = slice(h * 128, (h + 1) * 128)
                w_own, w_oth = softmax_parts(
                    k.q[:, at], k.kv[0:256, at], k.kv_oth[0:256, at], mask_own, mask_oth
                )
                dw_own = dot_nt(low_g[:, at], k.kv[256:512, at])
                dw_oth = dot_nt(low_g[:, at], k.kv_oth[256:512, at])
                mean = jnp.sum(w_own * dw_own, axis=-1, keepdims=True)
                mean += jnp.sum(w_oth * dw_oth, axis=-1, keepdims=True)
                ds_own = (w_own * (dw_own - mean)).astype(bf16)
                ds_oth = (w_oth * (dw_oth - mean)).astype(bf16)
                gq = dot_nn(ds_own, k.kv[0:256, at]) + dot_nn(ds_oth, k.kv_oth[0:256, at])
                lin[0:256, at] = turn_back(gq * scale, k.cs[...], k.sn[...]).astype(bf16)
                gkv[0:256, at] = dot_tn(ds_own, k.q[:, at]) * scale
                gkv[256:512, at] = dot_tn(w_own.astype(bf16), low_g[:, at])
                gkv_send[0:256, at] = (dot_tn(ds_oth, k.q[:, at]) * scale).astype(bf16)
                gkv_send[256:512, at] = dot_tn(w_oth.astype(bf16), low_g[:, at]).astype(bf16)
            gkv_y = wires.go(lambda: (gkv_send, k.gkv_y), y_dev)
            to_y(0, 2, t_sg, k.y_sg)
            fold(1, k_su, k.y_su, f_su, k.x_su)
            for copy in more:
                copy.wait()
            gkv_y.wait_recv()
            for h in range(4):
                at = slice(h * 128, (h + 1) * 128)
                gk = gkv[0:256, at] + k.gkv_y[0:256, at].astype(f32)
                lin[256:512, at] = turn_back(gk, k.cs[...], k.sn[...]).astype(bf16)
            lin[512:768, :] = (gkv[256:512, :] + k.gkv_y[256:512, :].astype(f32)).astype(bf16)
            swap_lin = wires.go(lambda: (lin, k.lin_x), core_dev)
            for m in range(3):
                part = lin[m * 256 : (m + 1) * 256, :].astype(f32)
                vec[11 + m : 12 + m, 0:512] = jnp.sum(part, axis=0, keepdims=True)
            for r in range(8):
                at = pl.ds(pl.multiple_of(owner_dense(r) * 256, 256), 256)
                back = dot_nt(lin[0:256, :], w[r, 0:256, :])
                back += dot_nt(lin[256:512, :], w[r, 256:512, :])
                back += dot_nt(lin[512:768, :], w[r, 512:768, :])
                gain = jnp.zeros((1, 256), f32)
                for d in range(4):
                    rows_at = slice(d * 64, (d + 1) * 64)
                    t = k.tok[pl.ds(pl.multiple_of(near(d) * 64, 64), 64), at].astype(f32)
                    gain += jnp.sum(
                        back[rows_at, :] * t * k.inv1[rows_at, :], axis=0, keepdims=True
                    )
                    gn[d, :, at] = back[rows_at, :].astype(bf16)
                vec[0:1, at] = gain
            swap_vec = wires.go(lambda: (vec, k.vec_x), core_dev)
            gn_z.extend(to_z(lambda d: lambda: (gn.at[d], k.gn_z.at[d - 1])))
            for copy in (swap_h, swap_lin, swap_vec, swap_n, swap_low):
                copy.wait_recv()

        pl.run_scoped(
            attention_back,
            pltpu.VMEM((8, 768, 512), bf16),
            pltpu.VMEM((8, 512, 256), bf16),
            pltpu.VMEM((256, 512), f32),
            pltpu.VMEM((256, 512), bf16),
        )
        k.vec_x[...] += vec[...]
        line = lax.broadcasted_iota(jnp.int32, (16, 512), 0)

        def attention_grad(n_x, low_x):
            got = [
                loads.go(k.n_x, n_x),
                loads.go(k.low_x, low_x),
                loads.go(k.h_x, h_x),
                loads.go(k.lin_x, lin_x),
            ]
            for copy in got:
                copy.wait()

            def one(r):
                keep = r < 2
                b_q, b_v = (k_q, k_v) if keep else (t_q, t_v)
                at = slice(r * 256, (r + 1) * 256)
                left, left_x = k.n_keep[:, at], n_x[:, at]
                for m in range(3):
                    rows_at = slice(m * 256, (m + 1) * 256)
                    total = dot_tn(left, lin[rows_at, :]) + dot_tn(left_x, lin_x[rows_at, :])
                    b_q[r % 2, rows_at, :] = total.astype(bf16)
                total = dot_tn(k.low[...], h_keep[:, at]) + dot_tn(low_x[...], h_x[:, at])
                (t_o if r % 2 else k_o)[r // 2] = total.astype(bf16)
                here = cols(k.vec_x, owner_dense(r), 256)
                here = jnp.concatenate([here, jnp.zeros((16, 256), f32)], axis=1)
                b_v[r % 2] = jnp.where(line < 11, here, k.vec_x[:, 0:512]).astype(bf16)
                if not keep:
                    to_y(5, r, t_v, k.y_v)
                    to_y(3, r, t_q, k.y_q)
                if r % 2:
                    over_y[4, 2 + r // 2] = wires.go(
                        lambda: (t_o.at[r // 2], k.y_o.at[r // 2]), x_dev
                    )

            one(3)
            to_y(1, 2, t_su, k.y_su)
            one(1)
            one(2)
            one(0)

        pl.run_scoped(
            attention_grad, pltpu.VMEM((256, 1024), bf16), pltpu.VMEM((256, 512), bf16)
        )
        kept = [loads.go(k_q.at[0], k.keep_q), loads.go(k_o.at[0], k.keep_o)]

        def expert_finish(m, kept, landed, result):
            def inner(left, right):
                got = loads.go(kept, left)
                over_x[6 + m].wait_recv()
                more = loads.go(landed, right)
                got.wait()
                more.wait()
                left[...] = (left[...].astype(f32) + right[...].astype(f32)).astype(bf16)
                loads.go(left, result).wait()

            shape = pltpu.VMEM(tuple(result.shape), bf16)
            pl.run_scoped(inner, shape, shape)

        def expert_pair():
            for m in (1, 2):
                over_x[6 + m].wait_recv()

            def inner(left, right, total):
                for half in range(2):
                    at = pl.ds(256 * half, 256)
                    got = []
                    for n, (kept, landed) in enumerate(((k.k_eg, k.x_eg), (k.k_eu, k.x_eu))):
                        got.append(loads.go(kept.at[at, :], left.at[n]))
                        got.append(loads.go(landed.at[at, :], right.at[n]))
                    for copy in got:
                        copy.wait()
                    for n in range(2):
                        value = left[n].astype(f32) + right[n].astype(f32)
                        total[:, n, :] = value.astype(bf16)
                    loads.go(total, k.d_ei.at[at]).wait()

            pair = pltpu.VMEM((2, 256, 1408), bf16)
            pl.run_scoped(inner, pair, pair, pltpu.VMEM((256, 2, 1408), bf16))

        expert_pair()

        def outputs(s_z):
            for copy in s_out_z:
                copy.wait_recv()
            got = loads.go(k.s_out_z, s_z)
            for copy in gn_z:
                copy.wait_recv()
            grad = gn[0].astype(f32)
            for d in range(3):
                grad += k.gn_z[d].astype(f32)
            t = piece(k.tok, 0, 64).astype(f32)
            i = k.inv1[0:64, :]
            scaled = grad * k.small[0:1, :].astype(f32)
            mean = jnp.mean(scaled * t, axis=-1, keepdims=True)
            grad = high[...] + i * scaled - t * (i * i * i * mean)
            k.grad_tokens[...] = grad.astype(bf16)
            got.wait()
            total = k.hidden[...] + k.s_out[0].astype(f32)
            for d in range(3):
                total += s_z[d].astype(f32)
            out_y.wait_recv()
            k.output[...] = (total + k.o_y[...].astype(f32)).astype(bf16)

        expert_finish(0, k.k_ed, k.x_ed, k.d_ed)
        finish(2, k_sd, k.y_sd, k.x_sd, k.d_sd)
        fold(5, k_v, k.y_v, f_v, k.x_v)
        fold(3, k_q, k.y_q, f_q, k.x_q)
        fold(4, k_o, k.y_o, f_o, k.x_o, y_dev)
        pl.run_scoped(outputs, pltpu.VMEM((3, 64, 2048), bf16))
        finish_pair()
        finish(5, k_v, k.y_v, k.x_v, k.v_own)
        v_z = to_z(lambda d: lambda: (k.v_own, k.v_z.at[d - 1]))
        for name in (3, 4):
            over_y[name, 2].wait_recv()
            over_x[name].wait_recv()
        for copy in kept:
            copy.wait()
        for copy in v_z:
            copy.wait_recv()
        total = k.v_own[...] + k.v_z[0] + k.v_z[1] + k.v_z[2]
        k.d_v[...] = total[:, 0:256].astype(bf16)
        for h in range(4):
            lanes_at = slice(h * 128, (h + 1) * 128)
            turned = pltpu.roll(k.v_own[:, lanes_at], (128 - owner_dense(0) * 16) % 128, 1)
            for m in range(3):
                k.d_b[m, h : h + 1, :] = turned[11 + m : 12 + m, :].astype(bf16)
        wires.drain()

    def buffers(lead):
        return tuple(
            pltpu.VMEM(lead + shape, bf16)
            for shape in ((256, 1408), (256, 1408), (768, 512), (512, 256), (16, 512))
        )

    pl.run_scoped(
        back_part,
        *buffers((2,)),
        *buffers((2,)),
        *buffers(()),
        pltpu.VMEM((1408, 256), bf16),
        pltpu.VMEM((256, 1024), bf16),
        pltpu.VMEM((256, 1024), bf16),
        pltpu.VMEM((256, 1024), bf16),
        pltpu.VMEM((768, 512), bf16),
        pltpu.VMEM((768, 512), bf16),
        pltpu.VMEM((16, 2048), f32),
        pltpu.VMEM((64, 2048), f32),
        pltpu.VMEM((512, 512), f32),
        pltpu.VMEM((512, 512), bf16),
        pltpu.VMEM((4, 64, 2048), bf16),
    )


def close_kernel(k):
    loads = Loads(k.load_sems)
    sums = ((k.keep_q, k.y_q, k.x_q, k.b_q, k.c_q), (k.keep_o, k.y_o, k.x_o, k.b_o, k.c_o))
    parts = []
    for keep, y, x, buffer, _ in sums:
        parts.append([loads.go(a, buffer.at[n]) for n, a in enumerate((keep, y.at[0], x))])
    passed = (
        (k.d_ei, k.b_ei, k.c_ei),
        (k.d_ed, k.b_ed, k.c_ed),
        (k.d_si, k.b_si, k.c_si),
        (k.d_sd, k.b_sd, k.c_sd),
        (k.output, k.b_out, k.c_out),
        (k.grad_tokens, k.b_tok, k.c_tok),
    )
    got = [loads.go(source, buffer) for source, buffer, _ in passed]
    for m, target in enumerate((k.c_one, k.c_two, k.c_gate)):
        target[...] = k.d_v[m : m + 1, :].reshape(256)
    k.c_router[...] = k.d_v[3:11, :]
    k.c_bias[...] = k.d_b[:, :, 0:16]
    done = []
    for copies, (_, _, _, buffer, target) in zip(parts, sums):
        for copy in copies:
            copy.wait()
        total = buffer[0].astype(f32) + buffer[1].astype(f32) + buffer[2].astype(f32)
        buffer[0] = total.astype(bf16)
        done.append(loads.go(buffer.at[0], target))
    for copy, (_, buffer, target) in zip(got, passed):
        copy.wait()
        done.append(loads.go(buffer, target))
    for copy in done:
        copy.wait()


def dma(n):
    return pltpu.SemaphoreType.DMA((n,))


def fixed_body(
    tokens,
    norm1_gain,
    w_qkv,
    b_qkv,
    w_out,
    norm2_gain,
    w_router,
    shared_gate,
    w_shared_in,
    w_shared_out,
    w_expert_in,
    w_expert_out,
    block_ids,
    expert_ids,
    out_grad,
):
    tok, g_own = tokens[0], out_grad[0]
    rows = tok.shape[0]
    places = np.arange(2 * rows)[:, None]
    frequency = rope_base ** (-np.arange(64) / 64.0)
    cosine, sine = np.cos(places * frequency), np.sin(places * frequency)
    cs = np.concatenate([cosine, cosine], axis=1).astype(np.float32)
    sn = np.concatenate([-sine, sine], axis=1).astype(np.float32)

    def vm(*shape, kind=bf16):
        return pltpu.VMEM(shape, kind)

    def o(*shape, kind=bf16, at=A):
        return (shape, kind, at)

    w_q = w_qkv.transpose(1, 0, 2).reshape(768, 512)
    b = call(
        layer_kernel,
        0,
        dict(
            tok=(tok, V),
            g_own=(g_own, V),
            bias=(b_qkv, V),
            cs_all=(cs, V),
            sn_all=(sn, V),
            blocks=(block_ids, V),
            ids_own=(expert_ids[0].T, V),
            gain_one=(norm1_gain, V),
            gain_two=(norm2_gain, V),
            gate_vector=(shared_gate, V),
            router=(w_router.T, V),
            w_q=(w_q, A),
            w_o=(w_out, A),
            w_si=(w_shared_in, A),
            w_sd=(w_shared_out, A),
            w_ei=(w_expert_in[0], A),
            w_ed=(w_expert_out[0], A),
        ),
        dict(
            output=o(64, 2048, at=V),
            grad_tokens=o(64, 2048, at=V),
            d_v=o(16, 256, at=V),
            d_b=o(3, 4, 128, at=V),
            keep_q=o(768, 512),
            keep_o=o(512, 256),
            d_si=o(256, 2, 1408),
            d_sd=o(1408, 256),
            d_ei=o(512, 2, 1408),
            d_ed=o(1408, 512),
            split_si=o(2, 256, 1408),
            split_ei=o(2, 512, 1408),
            s_q=o(8, 768, 512),
            s_o=o(8, 512, 256),
            s_sg=o(8, 256, 1408),
            s_su=o(8, 256, 1408),
            s_sd=o(8, 1408, 256),
            s_eg=o(4, 512, 1408),
            s_eu=o(4, 512, 1408),
            s_ed=o(4, 1408, 512),
            ex_up=o(3, 512, 1408),
            ex_up_x=o(3, 512, 1408),
            ex_keep=o(1024, 1024),
            ex_x=o(1024, 1024),
            sh_up=o(3, 256, 1408),
            sh_up_x=o(3, 256, 1408),
            sh_keep=o(256, 1024),
            sh_send=o(256, 1024),
            sh_x=o(256, 1024),
            k_eg=o(512, 1408),
            k_eu=o(512, 1408),
            k_ed=o(1408, 512),
            t_eg=o(512, 1408),
            t_eu=o(512, 1408),
            t_ed=o(1408, 512),
            y_sg=o(2, 256, 1408),
            y_su=o(2, 256, 1408),
            y_sd=o(2, 1408, 256),
            y_q=o(2, 768, 512),
            y_o=o(2, 512, 256),
            y_v=o(2, 16, 512),
            x_sg=o(256, 1408),
            x_su=o(256, 1408),
            x_sd=o(1408, 256),
            x_q=o(768, 512),
            x_o=o(512, 256),
            x_v=o(16, 512),
            x_eg=o(512, 1408),
            x_eu=o(512, 1408),
            x_ed=o(1408, 512),
            n_x=o(256, 1024),
            low_x=o(256, 512),
            h_x=o(256, 1024),
            lin_x=o(768, 512),
            e_out_z=o(3, 64, 2048),
            s_out_z=o(3, 64, 2048),
        ),
        dict(
            s_v=vm(8, 16, 256),
            w_v=vm(16, 256),
            col=vm(512, 128, kind=f32),
            ids_q=vm(256, 128, kind=f32),
            ids_near=vm(8, 256, kind=f32),
            ids_far=vm(8, 256, kind=f32),
            cs=vm(256, 128, kind=f32),
            sn=vm(256, 128, kind=f32),
            ids=vm(4, 128, 128, kind=f32),
            ids_y=vm(64, 128, kind=f32),
            g_oth=vm(256, 2048),
            q=vm(256, 512),
            kv=vm(512, 512),
            kv_oth=vm(512, 512),
            low=vm(256, 512),
            n_keep=vm(256, 1024),
            n_send=vm(256, 1024),
            small=vm(16, 2048),
            inv1=vm(256, 1, kind=f32),
            k_sd=vm(2, 1408, 256),
            t_sd=vm(2, 1408, 256),
            att=vm(3, 64, 2048),
            att_send=vm(4, 64, 2048),
            hidden=vm(64, 2048, kind=f32),
            rows=vm(512, 2048),
            out_sum=vm(256, 2048, kind=f32),
            grad_sum=vm(256, 2048, kind=f32),
            extras=vm(256, 128, kind=f32),
            e_out=vm(4, 64, 2048),
            e_grad=vm(4, 64, 2176),
            e_grad_z=vm(3, 64, 2176),
            s_out=vm(4, 64, 2048),
            s_grad=vm(4, 64, 2176),
            s_grad_z=vm(3, 64, 2176),
            g_send=vm(64, 2176),
            g_y=vm(64, 2176),
            o_send=vm(64, 2048),
            o_y=vm(64, 2048),
            gh=vm(4, 64, 2048),
            gkv_y=vm(512, 512),
            gn_z=vm(3, 64, 2048),
            vec_x=vm(16, 2048, kind=f32),
            v_own=vm(16, 512, kind=f32),
            v_z=vm(3, 16, 512, kind=f32),
            send_sems=dma(128),
            recv_sems=dma(128),
            load_sems=dma(224),
        ),
        63,
        4 * 10**10,
        2 * 10**8,
    )
    c = call(
        close_kernel,
        None,
        dict(
            output=(b.output, A),
            grad_tokens=(b.grad_tokens, A),
            d_v=(b.d_v, V),
            d_b=(b.d_b, V),
            keep_q=(b.keep_q, A),
            y_q=(b.y_q, A),
            x_q=(b.x_q, A),
            keep_o=(b.keep_o, A),
            y_o=(b.y_o, A),
            x_o=(b.x_o, A),
            d_si=(b.d_si, A),
            d_sd=(b.d_sd, A),
            d_ei=(b.d_ei, A),
            d_ed=(b.d_ed, A),
        ),
        dict(
            c_out=o(64, 2048),
            c_tok=o(64, 2048),
            c_one=o(256, at=V),
            c_two=o(256, at=V),
            c_gate=o(256, at=V),
            c_router=o(8, 256, at=V),
            c_bias=o(3, 4, 16, at=V),
            c_q=o(768, 512),
            c_o=o(512, 256),
            c_si=o(256, 2, 1408),
            c_sd=o(1408, 256),
            c_ei=o(512, 2, 1408),
            c_ed=o(1408, 512),
        ),
        dict(
            b_out=vm(64, 2048),
            b_tok=vm(64, 2048),
            b_q=vm(3, 768, 512),
            b_o=vm(3, 512, 256),
            b_si=vm(256, 2, 1408),
            b_sd=vm(1408, 256),
            b_ei=vm(512, 2, 1408),
            b_ed=vm(1408, 512),
            load_sems=dma(32),
        ),
        63,
        10**6,
        2 * 10**7,
    )
    return (
        c.c_out[None],
        c.c_tok[None],
        c.c_one,
        c.c_q.reshape(3, 256, 512).transpose(1, 0, 2),
        c.c_bias,
        c.c_o,
        c.c_two,
        c.c_router.T,
        c.c_gate,
        c.c_si,
        c.c_sd,
        c.c_ei[None],
        c.c_ed[None],
    )


def solution(mesh):
    placed = (
        P(DP, CTX, None),
        P(PLANE),
        P(PLANE, None, EXP),
        P(None, EXP, None),
        P(EXP, PLANE),
        P(PLANE),
        P(PLANE, None),
        P(PLANE),
        P(PLANE, None, EXP),
        P(EXP, PLANE),
        P(GROUP, DP, None, None),
        P(GROUP, None, DP),
        P(DP, None),
        P(DP, GROUP, None),
        P(DP, CTX, None),
    )
    fixed = tuple(mesh.shape[a] for a in (DP, CTX, EXP)) == (4, 2, 4)
    return jax.shard_map(
        fixed_body if fixed else general_body,
        mesh=mesh,
        in_specs=placed,
        out_specs=(
            P(DP, GROUP, None),
            P(DP, GROUP, None),
            P(PLANE),
            P(PLANE, None, EXP),
            P(None, EXP, PLANE),
            P(EXP, PLANE),
            P(PLANE),
            P(PLANE, None),
            P(PLANE),
            P(PLANE, None, EXP),
            P(EXP, PLANE),
            P(GROUP, DP, None, None),
            P(GROUP, None, DP),
        ),
        check_vma=False,
    )
```

```python
from types import SimpleNamespace

import jax
import jax.numpy as jnp
import numpy as np
from jax import lax
from jax.experimental import pallas as pl
from jax.experimental.pallas import tpu as pltpu
from jax.sharding import PartitionSpec as P

highest = lax.Precision.HIGHEST
epsilon = 1e-06
rope_base = 1000000.0
f32 = jnp.float32
bf16 = jnp.bfloat16
DP, CTX, EXP = "dp", "context", "expert"
PLANE, GROUP = (DP, CTX), (CTX, EXP)


def rotary_tables(first_row, row_count, head_size):
    exponent = jnp.arange(head_size // 2).astype(jnp.float32) * (2.0 / head_size)
    frequency = rope_base ** (-exponent)
    positions = (first_row + jnp.arange(row_count, dtype=jnp.int32)).astype(jnp.float32)
    angles = positions[:, None] * frequency[None, :]
    return (jnp.cos(angles)[:, None, :], jnp.sin(angles)[:, None, :])


def rotate(values, cosine, sine_table):
    half_size = values.shape[-1] // 2
    first_half = values[..., :half_size]
    second_half = values[..., half_size:]
    return jnp.concatenate(
        [
            first_half * cosine - second_half * sine_table,
            second_half * cosine + first_half * sine_table,
        ],
        axis=-1,
    )


def rotate_back(grad_values, cosine, sine_table):
    half_size = grad_values.shape[-1] // 2
    first_half = grad_values[..., :half_size]
    second_half = grad_values[..., half_size:]
    return jnp.concatenate(
        [
            first_half * cosine + second_half * sine_table,
            second_half * cosine - first_half * sine_table,
        ],
        axis=-1,
    )


def gated_grads(gate_part, up_part, grad_act):
    sigmoid_gate = jax.nn.sigmoid(gate_part)
    grad_gate = grad_act * up_part * sigmoid_gate * (1.0 + gate_part * (1.0 - sigmoid_gate))
    grad_up = grad_act * gate_part * sigmoid_gate
    return (grad_gate, grad_up)


def masked_scores(queries, all_keys, allowed, score_scale):
    scores = (
        jnp.einsum("qhd,khd->hqk", queries, all_keys, preferred_element_type=jnp.float32)
        * score_scale
    )
    return jnp.where(allowed[None], scores, -1e30)


def fetch_dense(
    norm1_gain, w_qkv, w_out, norm2_gain, w_router, shared_gate, w_shared_in, w_shared_out
):
    return (
        lax.all_gather(norm1_gain, PLANE, axis=0, tiled=True),
        lax.all_gather(w_qkv, PLANE, axis=0, tiled=True),
        lax.all_gather(w_out, PLANE, axis=1, tiled=True),
        lax.all_gather(norm2_gain, PLANE, axis=0, tiled=True),
        lax.all_gather(w_router, PLANE, axis=0, tiled=True),
        lax.all_gather(shared_gate, PLANE, axis=0, tiled=True),
        lax.all_gather(w_shared_in, PLANE, axis=0, tiled=True),
        lax.all_gather(w_shared_out, PLANE, axis=1, tiled=True),
    )


def fetch_experts(w_expert_in, w_expert_out):
    return (
        lax.all_gather(w_expert_in, DP, axis=1, tiled=True),
        lax.all_gather(w_expert_out, DP, axis=2, tiled=True),
    )


def fetch_keys(key_rows, value_rows):
    return (
        lax.all_gather(key_rows, CTX, axis=0, tiled=True),
        lax.all_gather(value_rows, CTX, axis=0, tiled=True),
    )


def general_body(
    tokens,
    norm1_gain,
    w_qkv,
    b_qkv,
    w_out,
    norm2_gain,
    w_router,
    shared_gate,
    w_shared_in,
    w_shared_out,
    w_expert_in,
    w_expert_out,
    block_ids,
    expert_ids,
    out_grad,
):
    token_rows = tokens[0]
    rows_local, model_width = token_rows.shape
    lane_count = lax.axis_size(EXP)
    quarter = rows_local // lane_count
    first_row = lax.axis_index(CTX) * rows_local
    own_row = lax.axis_index(EXP) * quarter
    sequence_ids = block_ids[0]
    chosen = expert_ids[0]
    top_count = chosen.shape[1]
    heads_local = b_qkv.shape[1]
    head_size = b_qkv.shape[2]
    dense_full = fetch_dense(
        norm1_gain, w_qkv, w_out, norm2_gain, w_router, shared_gate, w_shared_in, w_shared_out
    )
    (
        gain_one,
        qkv_weight,
        out_weight,
        gain_two,
        router_weight,
        gate_vector,
        shared_in,
        shared_out,
    ) = dense_full
    expert_pair = fetch_experts(w_expert_in, w_expert_out)
    expert_in = expert_pair[0][0]
    expert_back = expert_pair[1][0]
    ffe_width = expert_in.shape[2]
    experts = router_weight.shape[1]
    capacity = max(2, 3 * quarter * top_count // (2 * experts))
    tokens_wide = token_rows.astype(jnp.float32)
    inverse_one = lax.rsqrt(jnp.mean(tokens_wide * tokens_wide, axis=-1, keepdims=True) + epsilon)
    normed = (tokens_wide * inverse_one * gain_one.astype(jnp.float32)).astype(jnp.bfloat16)
    linear = jnp.dot(
        normed, qkv_weight.reshape(model_width, -1), preferred_element_type=jnp.float32
    )
    linear = linear.reshape(rows_local, 3, heads_local, head_size) + b_qkv.astype(jnp.float32)[None]
    cosine, sine_table = rotary_tables(first_row, rows_local, head_size)
    queries = rotate(linear[:, 0], cosine, sine_table).astype(jnp.bfloat16)
    key_rows = rotate(linear[:, 1], cosine, sine_table).astype(jnp.bfloat16)
    value_rows = linear[:, 2].astype(jnp.bfloat16)
    all_keys, all_values = fetch_keys(key_rows, value_rows)
    query_ids = lax.dynamic_slice_in_dim(sequence_ids, first_row, rows_local)
    allowed = sequence_ids[None, :] <= query_ids[:, None]
    score_scale = head_size ** (-0.5)
    scores = masked_scores(queries, all_keys, allowed, score_scale)
    row_peak = jnp.max(scores, axis=-1, keepdims=True)
    log_total = row_peak + jnp.log(jnp.sum(jnp.exp(scores - row_peak), axis=-1, keepdims=True))
    weights = jnp.exp(scores - log_total).astype(jnp.bfloat16)
    attended = jnp.einsum("hqk,khd->qhd", weights, all_values, preferred_element_type=jnp.float32)
    attended_low = attended.astype(jnp.bfloat16).reshape(rows_local, heads_local * head_size)
    attention = lax.psum(
        jnp.dot(attended_low, out_weight, preferred_element_type=jnp.float32).astype(jnp.bfloat16),
        EXP,
    ).astype(jnp.float32)
    hidden = tokens_wide + attention
    inverse_two = lax.rsqrt(jnp.mean(hidden * hidden, axis=-1, keepdims=True) + epsilon)
    routed = (hidden * inverse_two * gain_two.astype(jnp.float32)).astype(jnp.bfloat16)
    shared_up = jnp.dot(
        routed, shared_in.reshape(model_width, -1), preferred_element_type=jnp.float32
    )
    shared_up = shared_up.reshape(rows_local, 2, -1)
    shared_act = (jax.nn.silu(shared_up[:, 0]) * shared_up[:, 1]).astype(jnp.bfloat16)
    shared_part = jnp.dot(shared_act, shared_out, preferred_element_type=jnp.float32)
    shared_rows = lax.psum_scatter(
        shared_part.astype(jnp.bfloat16), EXP, scatter_dimension=0, tiled=True
    ).astype(jnp.float32)
    shared_weight = jax.nn.sigmoid(jnp.dot(routed, gate_vector, preferred_element_type=jnp.float32))
    routed_own = lax.dynamic_slice_in_dim(routed, own_row, quarter)
    hidden_own = lax.dynamic_slice_in_dim(hidden, own_row, quarter)
    weight_own = lax.dynamic_slice_in_dim(shared_weight, own_row, quarter)
    logits = jnp.dot(routed_own, router_weight, preferred_element_type=jnp.float32)
    probability = jax.nn.softmax(logits, axis=-1)
    expert_match = (chosen[..., None] == jnp.arange(experts, dtype=jnp.int32)).astype(jnp.float32)
    gate_values = jnp.sum(probability[:, None, :] * expert_match, axis=-1)
    flat_ids = chosen.reshape(-1)
    onehot = (flat_ids[:, None] == jnp.arange(experts, dtype=jnp.int32)).astype(jnp.int32)
    slot_rank = jnp.sum((jnp.cumsum(onehot, axis=0) - onehot) * onehot, axis=-1)
    slot_index = flat_ids * capacity + slot_rank
    placement = (slot_index[:, None] == jnp.arange(experts * capacity, dtype=jnp.int32)).astype(
        jnp.bfloat16
    )
    repeated = jnp.repeat(routed_own, top_count, axis=0)
    outgoing = jnp.einsum("sr,sd->rd", placement, repeated, preferred_element_type=jnp.float32)
    outgoing = outgoing.astype(jnp.bfloat16).reshape(experts, capacity, model_width)
    incoming = lax.all_to_all(
        outgoing, GROUP, split_axis=0, concat_axis=0, tiled=True
    )
    flat_rows = incoming.reshape(-1, model_width)
    gate_up = jnp.dot(
        flat_rows, expert_in.reshape(model_width, -1), preferred_element_type=jnp.float32
    ).reshape(-1, 2, ffe_width)
    activated = (jax.nn.silu(gate_up[:, 0]) * gate_up[:, 1]).astype(jnp.bfloat16)
    result = jnp.dot(activated, expert_back, preferred_element_type=jnp.float32).astype(
        jnp.bfloat16
    )
    expert_result = result.reshape(incoming.shape)
    returned = lax.all_to_all(
        expert_result, GROUP, split_axis=0, concat_axis=0, tiled=True
    )
    picked = jnp.dot(
        placement, returned.reshape(-1, model_width), preferred_element_type=jnp.float32
    )
    picked = picked.reshape(quarter, top_count, model_width)
    combined = jnp.sum(gate_values[..., None] * picked, axis=1)
    result_rows = hidden_own + combined + weight_own[:, None] * shared_rows
    output = result_rows.astype(jnp.bfloat16)[None]
    (
        gain_one_b,
        qkv_weight_b,
        out_weight_b,
        gain_two_b,
        router_weight_b,
        gate_vector_b,
        shared_in_b,
        shared_out_b,
    ) = dense_full
    expert_in_b = expert_pair[0][0]
    expert_back_b = expert_pair[1][0]
    grad_full = out_grad[0].astype(jnp.float32)
    grad_own = lax.dynamic_slice_in_dim(grad_full, own_row, quarter)
    shared_grad = (shared_weight[:, None] * grad_full).astype(jnp.bfloat16)
    grad_shared_out = jnp.einsum(
        "tf,td->fd", shared_act, shared_grad, preferred_element_type=jnp.float32
    )
    grad_shared_act = jnp.einsum(
        "td,fd->tf", shared_grad, shared_out_b, preferred_element_type=jnp.float32
    )
    shared_gate_grad, shared_up_grad = gated_grads(
        shared_up[:, 0], shared_up[:, 1], grad_shared_act
    )
    grad_shared_up = jnp.stack([shared_gate_grad, shared_up_grad], axis=1).astype(jnp.bfloat16)
    grad_shared_in = jnp.einsum(
        "td,tkf->dkf", routed, grad_shared_up, preferred_element_type=jnp.float32
    )
    grad_routed = jnp.einsum(
        "tkf,dkf->td", grad_shared_up, shared_in_b, preferred_element_type=jnp.float32
    )
    gate_slope = jnp.sum(grad_own * shared_rows, axis=-1) * weight_own * (1.0 - weight_own)
    grad_gate_vector = jnp.dot(gate_slope, routed_own.astype(jnp.float32), precision=highest)
    grad_own_routed = gate_slope[:, None] * gate_vector_b.astype(jnp.float32)[None]
    grad_gates = jnp.sum(grad_own[:, None, :] * picked, axis=-1)
    grad_slots = (
        (gate_values[..., None] * grad_own[:, None, :])
        .astype(jnp.bfloat16)
        .reshape(-1, model_width)
    )
    grad_send = jnp.einsum("sr,sd->rd", placement, grad_slots, preferred_element_type=jnp.float32)
    grad_send = grad_send.astype(jnp.bfloat16).reshape(experts, capacity, model_width)
    grad_arrived = lax.all_to_all(
        grad_send, GROUP, split_axis=0, concat_axis=0, tiled=True
    )
    arrived_rows = incoming.reshape(-1, model_width)
    arrived_grad = grad_arrived.reshape(-1, model_width)
    expert_up = jnp.dot(
        arrived_rows, expert_in_b.reshape(model_width, -1), preferred_element_type=jnp.float32
    ).reshape(-1, 2, ffe_width)
    expert_act = (jax.nn.silu(expert_up[:, 0]) * expert_up[:, 1]).astype(jnp.bfloat16)
    grad_expert_back = jnp.einsum(
        "rf,rd->fd", expert_act, arrived_grad, preferred_element_type=jnp.float32
    )
    grad_expert_act = jnp.einsum(
        "rd,fd->rf", arrived_grad, expert_back_b, preferred_element_type=jnp.float32
    )
    expert_gate_grad, expert_up_grad = gated_grads(
        expert_up[:, 0], expert_up[:, 1], grad_expert_act
    )
    grad_expert_up = jnp.stack([expert_gate_grad, expert_up_grad], axis=1).astype(jnp.bfloat16)
    grad_expert_in = jnp.einsum(
        "rd,rkf->dkf", arrived_rows, grad_expert_up, preferred_element_type=jnp.float32
    )
    grad_arrived_rows = jnp.einsum(
        "rkf,dkf->rd", grad_expert_up, expert_in_b, preferred_element_type=jnp.float32
    )
    grad_arrived_rows = grad_arrived_rows.astype(jnp.bfloat16).reshape(
        experts, capacity, model_width
    )
    grad_returned = lax.all_to_all(
        grad_arrived_rows, GROUP, split_axis=0, concat_axis=0, tiled=True
    )
    grad_copies = jnp.dot(
        placement, grad_returned.reshape(-1, model_width), preferred_element_type=jnp.float32
    )
    grad_own_routed = grad_own_routed + jnp.sum(
        grad_copies.reshape(quarter, top_count, model_width), axis=1
    )
    grad_probability = jnp.sum(grad_gates[..., None] * expert_match, axis=1)
    grad_logits = probability * (
        grad_probability - jnp.sum(probability * grad_probability, axis=-1, keepdims=True)
    )
    grad_router = jnp.dot(routed_own.astype(jnp.float32).T, grad_logits, precision=highest)
    grad_own_routed = grad_own_routed + jnp.dot(
        grad_logits, router_weight_b.astype(jnp.float32).T, precision=highest
    )
    own_part = lax.dynamic_slice_in_dim(grad_routed, own_row, quarter) + grad_own_routed
    grad_routed = lax.dynamic_update_slice_in_dim(grad_routed, own_part, own_row, 0)
    grad_routed, grad_router, grad_gate_vector = (
        lax.psum(grad_routed.astype(jnp.bfloat16), EXP).astype(jnp.float32),
        lax.psum(grad_router.astype(jnp.bfloat16), EXP).astype(jnp.float32),
        lax.psum(grad_gate_vector.astype(jnp.bfloat16), EXP).astype(jnp.float32),
    )
    scaled_two = grad_routed * gain_two_b.astype(jnp.float32)
    grad_gain_two = jnp.sum(grad_routed * hidden * inverse_two, axis=0)
    grad_hidden = (
        grad_full
        + inverse_two * scaled_two
        - hidden * inverse_two**3 * jnp.mean(scaled_two * hidden, axis=-1, keepdims=True)
    )
    grad_hidden_low = grad_hidden.astype(jnp.bfloat16)
    grad_out_weight = jnp.einsum(
        "tn,td->nd", attended_low, grad_hidden_low, preferred_element_type=jnp.float32
    )
    grad_attended = jnp.einsum(
        "td,nd->tn", grad_hidden_low, out_weight_b, preferred_element_type=jnp.float32
    )
    grad_attended = grad_attended.astype(jnp.bfloat16).reshape(rows_local, heads_local, head_size)
    back_keys, back_values = (all_keys, all_values)
    scores_again = masked_scores(queries, back_keys, allowed, score_scale)
    weights_wide = jnp.exp(scores_again - log_total)
    row_delta = jnp.sum(grad_attended.astype(jnp.float32) * attended, axis=-1).T
    grad_weights = jnp.einsum(
        "qhd,khd->hqk", grad_attended, back_values, preferred_element_type=jnp.float32
    )
    grad_scores = (weights_wide * (grad_weights - row_delta[..., None])).astype(jnp.bfloat16)
    grad_queries = (
        jnp.einsum("hqk,khd->qhd", grad_scores, back_keys, preferred_element_type=jnp.float32)
        * score_scale
    )
    grad_keys = (
        jnp.einsum("hqk,qhd->khd", grad_scores, queries, preferred_element_type=jnp.float32)
        * score_scale
    )
    grad_values = jnp.einsum(
        "hqk,qhd->khd",
        weights_wide.astype(jnp.bfloat16),
        grad_attended,
        preferred_element_type=jnp.float32,
    )
    grad_keys, grad_values = (
        lax.psum_scatter(
            grad_keys.astype(jnp.bfloat16), CTX, scatter_dimension=0, tiled=True
        ).astype(jnp.float32),
        lax.psum_scatter(
            grad_values.astype(jnp.bfloat16), CTX, scatter_dimension=0, tiled=True
        ).astype(jnp.float32),
    )
    grad_linear = jnp.stack(
        [
            rotate_back(grad_queries, cosine, sine_table),
            rotate_back(grad_keys, cosine, sine_table),
            grad_values,
        ],
        axis=1,
    )
    grad_linear = grad_linear.astype(jnp.bfloat16)
    grad_bias = jnp.sum(grad_linear.astype(jnp.float32), axis=0)
    grad_flat = grad_linear.reshape(rows_local, -1)
    grad_qkv = jnp.einsum(
        "td,tn->dn", normed, grad_flat, preferred_element_type=jnp.float32
    ).reshape(qkv_weight_b.shape)
    grad_normed = jnp.einsum(
        "tn,dn->td",
        grad_flat,
        qkv_weight_b.reshape(model_width, -1),
        preferred_element_type=jnp.float32,
    )
    grad_normed = lax.psum(grad_normed.astype(jnp.bfloat16), EXP).astype(jnp.float32)
    scaled_one = grad_normed * gain_one_b.astype(jnp.float32)
    grad_gain_one = jnp.sum(grad_normed * tokens_wide * inverse_one, axis=0)
    grad_tokens = (
        grad_hidden
        + inverse_one * scaled_one
        - tokens_wide * inverse_one**3 * jnp.mean(scaled_one * tokens_wide, axis=-1, keepdims=True)
    )
    grad_tokens_own = lax.dynamic_slice_in_dim(grad_tokens, own_row, quarter).astype(jnp.bfloat16)[
        None
    ]
    dense_sums = (
        lax.psum_scatter(
            grad_gain_one.astype(jnp.bfloat16), PLANE, scatter_dimension=0, tiled=True
        ).astype(jnp.float32),
        lax.psum_scatter(
            grad_qkv.astype(jnp.bfloat16), PLANE, scatter_dimension=0, tiled=True
        ).astype(jnp.float32),
        lax.psum_scatter(
            grad_bias.astype(jnp.bfloat16), PLANE, scatter_dimension=2, tiled=True
        ).astype(jnp.float32),
        lax.psum_scatter(
            grad_out_weight.astype(jnp.bfloat16), PLANE, scatter_dimension=1, tiled=True
        ).astype(jnp.float32),
        lax.psum_scatter(
            grad_gain_two.astype(jnp.bfloat16), PLANE, scatter_dimension=0, tiled=True
        ).astype(jnp.float32),
        lax.psum_scatter(
            grad_router.astype(jnp.bfloat16), PLANE, scatter_dimension=0, tiled=True
        ).astype(jnp.float32),
        lax.psum_scatter(
            grad_gate_vector.astype(jnp.bfloat16),
            PLANE,
            scatter_dimension=0,
            tiled=True,
        ).astype(jnp.float32),
        lax.psum_scatter(
            grad_shared_in.astype(jnp.bfloat16), PLANE, scatter_dimension=0, tiled=True
        ).astype(jnp.float32),
        lax.psum_scatter(
            grad_shared_out.astype(jnp.bfloat16), PLANE, scatter_dimension=1, tiled=True
        ).astype(jnp.float32),
    )
    expert_sums = (
        lax.psum_scatter(
            grad_expert_in[None].astype(jnp.bfloat16), DP, scatter_dimension=1, tiled=True
        ).astype(jnp.float32),
        lax.psum_scatter(
            grad_expert_back[None].astype(jnp.bfloat16), DP, scatter_dimension=2, tiled=True
        ).astype(jnp.float32),
    )
    return (
        output,
        grad_tokens_own,
        dense_sums[0].astype(jnp.bfloat16),
        dense_sums[1].astype(jnp.bfloat16),
        dense_sums[2].astype(jnp.bfloat16),
        dense_sums[3].astype(jnp.bfloat16),
        dense_sums[4].astype(jnp.bfloat16),
        dense_sums[5].astype(jnp.bfloat16),
        dense_sums[6].astype(jnp.bfloat16),
        dense_sums[7].astype(jnp.bfloat16),
        dense_sums[8].astype(jnp.bfloat16),
        expert_sums[0].astype(jnp.bfloat16),
        expert_sums[1].astype(jnp.bfloat16),
    )


MIB = 1 << 20
MESH = pl.DeviceIdType.MESH


def dot_nn(a, b):
    return lax.dot_general(a, b, (((1,), (0,)), ((), ())), preferred_element_type=f32)


def dot_nt(a, b):
    return lax.dot_general(a, b, (((1,), (1,)), ((), ())), preferred_element_type=f32)


def dot_tn(a, b):
    return lax.dot_general(a, b, (((0,), (0,)), ((), ())), preferred_element_type=f32)


def place():
    i = lax.axis_index(DP)
    return i // 2, i % 2, lax.axis_index(CTX), lax.axis_index(EXP)


def owner_dense(r):
    x, c, y, _ = place()
    return (((x + r % 2) % 2) * 2 + (c + r // 4) % 2) * 2 + (y + (r // 2) % 2) % 2


def owner_expert(r):
    x, c, _, _ = place()
    return ((x + r % 2) % 2) * 2 + (c + r // 2) % 2


def near(d):
    z = lax.axis_index(EXP)
    return ((z // 2 + d // 2) % 2) * 2 + (z % 2 + d % 2) % 2


def peers():
    x, c, y, _ = place()
    far = [{EXP: near(d)} for d in (1, 2, 3)]
    return {DP: ((x + 1) % 2) * 2 + c}, {CTX: 1 - y}, {DP: x * 2 + (c + 1) % 2}, far


def greet(devices):
    barrier = pltpu.get_barrier_semaphore()
    for device in devices:
        pl.semaphore_signal(barrier, 1, device_id=device, device_id_type=MESH)
    pl.semaphore_wait(barrier, len(devices))


class Wire:
    def __init__(self, wires, ends, device):
        self.ends, self.device, self.sent = ends, device, False
        self.send, self.recv, self.k = wires.send, wires.recv, len(wires.copies)
        wires.copies.append(self)

    def copy(self):
        source, target = self.ends()
        return pltpu.make_async_remote_copy(
            src_ref=source,
            dst_ref=target,
            send_sem=self.send.at[self.k],
            recv_sem=self.recv.at[self.k],
            device_id=self.device,
            device_id_type=MESH,
        )

    def start(self):
        self.copy().start()
        return self

    def wait_recv(self):
        self.copy().wait_recv()

    def wait_send(self):
        self.copy().wait_send()
        self.sent = True


class Wires:
    def __init__(self, send, recv):
        self.send, self.recv, self.copies = send, recv, []

    def add(self, ends, device):
        return Wire(self, ends, device)

    def go(self, ends, device):
        return Wire(self, ends, device).start()

    def drain(self):
        for wire in self.copies:
            if not wire.sent:
                wire.wait_send()


class Loads:
    def __init__(self, sems):
        self.sems, self.count = sems, 0

    def go(self, source, target):
        copy = pltpu.make_async_copy(source, target, self.sems.at[self.count])
        self.count += 1
        copy.start()
        return copy


def cols(ref, block, width):
    return ref[:, pl.ds(pl.multiple_of(block * width, width), width)]


def piece(ref, d, rows):
    return ref[pl.ds(pl.multiple_of(near(d) * rows, rows), rows), :]


def turn(values, cosine, sine):
    return values * cosine + pltpu.roll(values, 64, 1) * sine


def turn_back(values, cosine, sine):
    return values * cosine - pltpu.roll(values, 64, 1) * sine


def gated(gate, up, grad_act):
    s = jax.nn.sigmoid(gate)
    act = gate * s
    return act * up, grad_act * up * s * (1.0 + gate * (1.0 - s)), grad_act * act


def softmax_parts(q, k_own, k_oth, mask_own, mask_oth):
    scale = 128 ** (-0.5)
    s_own = jnp.where(mask_own, dot_nt(q, k_own) * scale, -1e30)
    s_oth = jnp.where(mask_oth, dot_nt(q, k_oth) * scale, -1e30)
    peak = jnp.maximum(
        jnp.max(s_own, axis=-1, keepdims=True), jnp.max(s_oth, axis=-1, keepdims=True)
    )
    e_own = jnp.exp(s_own - peak)
    e_oth = jnp.exp(s_oth - peak)
    total = jnp.sum(e_own, axis=-1, keepdims=True) + jnp.sum(e_oth, axis=-1, keepdims=True)
    back = 1.0 / total
    return e_own * back, e_oth * back


def split3(v):
    high = v.astype(bf16).astype(f32)
    mid = (v - high).astype(bf16).astype(f32)
    return high, mid, v - high - mid


def probabilities(rows, small):
    logits = dot_nt(rows, small[...])
    lane = lax.broadcasted_iota(jnp.int32, logits.shape, 1)
    logits = jnp.where((lane >= 3) & (lane < 11), logits, -1e30)
    e = jnp.exp(logits - jnp.max(logits, axis=-1, keepdims=True))
    return e / jnp.sum(e, axis=-1, keepdims=True), lane


ARRIVAL = (0, 4, 1, 5, 2, 6, 3, 7)


class Spread:
    def __init__(self, wires, own, slots, dense):
        x, y, core, _ = peers()
        self.slots, self.own, self.copies = slots, own, {}

        def ends(r, target):
            return lambda: (self.block(r), slots.at[target])

        self.copies[1] = wires.add(ends(0, 1), x)
        if dense:
            self.copies[2] = wires.add(ends(0, 2), y)
            self.copies[3] = wires.add(ends(1, 3), y)
        side = 4 if dense else 2
        for r in range(side):
            self.copies[side + r] = wires.add(ends(r, side + r), core)

    def block(self, r):
        return self.own() if r == 0 else self.slots.at[r]

    def start(self, r):
        self.copies[r].start()

    def wait(self, r):
        self.copies[r].wait_recv()


V, A = "vmem", "any"


def call(kernel, number, ins, outs, scratch, vmem, flops, traffic):
    def spec(kind):
        return pl.BlockSpec(memory_space=pl.ANY if kind == A else pltpu.VMEM)

    names = list(ins) + list(outs) + list(scratch)

    def run(*refs):
        kernel(SimpleNamespace(**dict(zip(names, refs))))

    made = pl.pallas_call(
        run,
        out_shape=tuple(jax.ShapeDtypeStruct(o[0], o[1]) for o in outs.values()),
        in_specs=[spec(i[1]) for i in ins.values()],
        out_specs=tuple(spec(o[2]) for o in outs.values()),
        scratch_shapes=list(scratch.values()),
        compiler_params=pltpu.CompilerParams(
            vmem_limit_bytes=vmem * MIB, collective_id=number, has_side_effects=number is not None
        ),
        cost_estimate=pl.CostEstimate(flops=flops, bytes_accessed=traffic, transcendentals=0),
    )(*[i[0] for i in ins.values()])
    return SimpleNamespace(**dict(zip(outs, made)))


def own_rows(total, hidden, routed, g, small, high_o, low_o, vec_o):
    extra = total[:, 2048:2176]
    wide = routed.astype(f32)
    prob, _ = probabilities(routed, small)
    sw = jax.nn.sigmoid(jnp.sum(wide * small[2:3, :].astype(f32), axis=-1, keepdims=True))
    slope = jnp.sum(extra[:, 48:96], axis=-1, keepdims=True) * sw * (1.0 - sw)
    dgate = [
        extra[:, e : e + 1] + extra[:, 16 + e : 17 + e] + extra[:, 32 + e : 33 + e]
        for e in range(8)
    ]
    probs = [prob[:, 3 + e : 4 + e] for e in range(8)]
    mean = sum(p * d for p, d in zip(probs, dgate))
    grad = total[:, 0:2048] + slope * small[2:3, :].astype(f32)
    vec_o[...] = jnp.zeros_like(vec_o)
    vec_o[2:3, :] = jnp.sum(slope * wide, axis=0, keepdims=True)
    for e in range(8):
        dlogit = probs[e] * (dgate[e] - mean)
        grad += dlogit * small[3 + e : 4 + e, :].astype(f32)
        vec_o[3 + e : 4 + e, :] = jnp.sum(dlogit * wide, axis=0, keepdims=True)
    inv = lax.rsqrt(jnp.mean(hidden * hidden, axis=-1, keepdims=True) + epsilon)
    vec_o[1:2, :] = jnp.sum(grad * hidden * inv, axis=0, keepdims=True)
    scaled = grad * small[1:2, :].astype(f32)
    mean = jnp.mean(scaled * hidden, axis=-1, keepdims=True)
    high = g.astype(f32) + inv * scaled - hidden * (inv * inv * inv * mean)
    high_o[...] = high
    low_o[...] = high.astype(bf16)


def layer_kernel(k):
    x_dev, y_dev, core_dev, z_dev = peers()
    wires, loads = Wires(k.send_sems, k.recv_sems), Loads(k.load_sems)
    inputs = [
        loads.go(a, b)
        for a, b in (
            (k.tok_in, k.tok),
            (k.cs_in, k.cs_all),
            (k.sn_in, k.sn_all),
            (k.g_in, k.g_own),
        )
    ]
    greet([x_dev, y_dev, core_dev] + z_dev)
    y = lax.axis_index(CTX)
    mine = y * 4 + lax.axis_index(EXP)

    def to_z(make):
        return [wires.go(make(d), z_dev[d - 1]) for d in (1, 2, 3)]

    class Collect:
        def __init__(self, slot):
            self.slot = slot
            self.one = wires.go(lambda: (slot(0), slot(1)), z_dev[0])
            self.three = wires.go(lambda: (slot(0), slot(3)), z_dev[2])

        def hand_on(self):
            self.three.wait_recv()
            self.two = wires.go(lambda: (self.slot(3), self.slot(2)), z_dev[0])

        def wait(self):
            self.one.wait_recv()
            self.two.wait_recv()

    vec = Spread(wires, lambda: k.w_v, k.s_v, True)
    qkv = Spread(wires, lambda: k.w_q, k.s_q, True)
    out = Spread(wires, lambda: k.w_o, k.s_o, True)
    eg = Spread(wires, lambda: k.split_ei.at[0], k.s_eg, False)
    eu = Spread(wires, lambda: k.split_ei.at[1], k.s_eu, False)
    ed = Spread(wires, lambda: k.w_ed, k.s_ed, False)
    sg = Spread(wires, lambda: k.split_si.at[0], k.s_sg, True)
    su = Spread(wires, lambda: k.split_si.at[1], k.s_su, True)
    sd = Spread(wires, lambda: k.w_sd, k.s_sd, True)
    first, expert, shared = (vec, qkv), (eg, eu, ed), (sg, su, sd)
    qkv.start(1)
    qkv.start(2)
    k.w_v[...] = jnp.zeros_like(k.w_v)
    for m, vector in enumerate((k.gain_one, k.gain_two, k.gate_vector)):
        k.w_v[m : m + 1, :] = vector[...].reshape(1, 256)
    k.w_v[3:11, :] = k.router[...]
    for s in (vec, out, ed):
        s.start(1)
    vec.start(2)
    for s in (qkv, out, vec):
        s.start(4)
    k.col[0:128, :] = jnp.full((128, 128), -1.0, f32)
    k.col[0:4, 0:64] = k.ids_own[...].astype(f32)
    k.ids[0, 0:64, :] = k.col[0:128, :].T[0:64, :]
    ids_y = wires.go(lambda: (k.ids.at[0, pl.ds(0, 64), :], k.ids_y), y_dev)
    k.s_v[0] = k.w_v[...]
    for copy in inputs:
        copy.wait()
    k.col[...] = jnp.broadcast_to(k.blocks[...].astype(f32), (128, 512)).T
    for target, half in ((k.ids_near, y), (k.ids_far, 1 - y)):
        for d in range(4):
            at = pl.ds(pl.multiple_of(half * 256 + near(d) * 64, 64), 64)
            k.ids_q[d * 64 : (d + 1) * 64, :] = k.col[at, :]
        target[...] = k.ids_q[...].T[0:8, :]
    for d in range(4):
        at = pl.ds(pl.multiple_of(y * 256 + near(d) * 64, 64), 64)
        to = slice(d * 64, (d + 1) * 64)
        k.ids_q[to, :] = k.col[at, :]
        k.cs[to, :] = k.cs_all[at, :]
        k.sn[to, :] = k.sn_all[at, :]
    later = []

    def attention_part(scaled, acc, w, low_w, mixed, apart):
        held, held_out = {}, []

        def bring(r):
            held[r] = loads.go(qkv.block(r), w.at[r])

        def bring_out(r):
            held_out.append(loads.go(out.block(r), low_w.at[r]))

        raw = [loads.go(k.w_ei.at[pl.ds(256 * m, 256)], mixed.at[m]) for m in range(2)]
        raw.append(loads.go(k.w_si, mixed.at[2]))
        bring(0)
        for d in range(4):
            t = piece(k.tok, d, 64).astype(f32)
            inv = lax.rsqrt(jnp.mean(t * t, axis=-1, keepdims=True) + epsilon)
            scaled[d * 64 : (d + 1) * 64, :] = t * inv
            k.inv1[d * 64 : (d + 1) * 64, :] = inv
        for m in range(3):
            for h in range(4):
                at = slice(h * 128, (h + 1) * 128)
                line = k.bias[m, h : h + 1, :].astype(f32)
                acc[m, :, at] = jnp.broadcast_to(line, (256, 128))

        def take_apart(m):
            raw[m].wait()
            target = k.split_si if m == 2 else k.split_ei
            to = pl.ds(0 if m == 2 else 256 * m, 256)
            done = []
            for n in range(2):
                apart[m, n] = mixed[m, :, n, :]
                done.append(loads.go(apart.at[m, n], target.at[n, to, :]))
            return done

        done = take_apart(0) + take_apart(1)
        for copy in done:
            copy.wait()
        for s in (eg, eu):
            s.start(1)
        for s in expert:
            s.start(2)

        def block(r):
            held[r].wait()
            o = owner_dense(r)
            vectors = k.s_v[r]
            k.small[:, pl.ds(pl.multiple_of(o * 256, 256), 256)] = vectors
            normed = (cols(scaled, o, 256) * vectors[0:1, :].astype(f32)).astype(bf16)
            target = k.n_keep if r < 4 else k.n_send
            target[:, (r % 4) * 256 : (r % 4 + 1) * 256] = normed
            for m in range(3):
                acc[m] += dot_nn(normed, w[r, m * 256 : (m + 1) * 256, :])

        def arrived(r, onward=()):
            for s in first:
                s.wait(r)
                for t in onward:
                    s.start(t)
            bring(r)

        arrived(4)
        block(0)
        block(4)
        arrived(1, (3, 5))
        out.start(2)
        arrived(2, (6,))
        block(1)
        arrived(5)
        block(5)
        arrived(6)
        block(2)
        block(6)
        for copy in take_apart(2):
            copy.wait()
        for s in shared:
            s.start(1)
        for s in shared:
            s.start(4)
        ids_y.wait_recv()
        k.ids[0, 64:128, :] = k.ids_y[...]
        later.extend(to_z(lambda d: lambda: (k.ids.at[0], k.ids.at[d])))
        bring_out(0)
        out.wait(4)
        bring_out(4)
        out.wait(1)
        out.start(5)
        bring_out(1)
        arrived(3, (7,))
        block(3)
        arrived(7)
        block(7)
        for h in range(4):
            at = slice(h * 128, (h + 1) * 128)
            k.kv[0:256, at] = turn(acc[1, :, at], k.cs[...], k.sn[...]).astype(bf16)
        k.kv[256:512, :] = acc[2].astype(bf16)
        kv_y = wires.go(lambda: (k.kv, k.kv_oth), y_dev)
        out.start(3)
        sg.start(2)
        su.start(2)
        for h in range(4):
            at = slice(h * 128, (h + 1) * 128)
            k.q[:, at] = turn(acc[0, :, at], k.cs[...], k.sn[...]).astype(bf16)
        out.wait(5)
        bring_out(5)
        out.wait(2)
        out.start(6)
        bring_out(2)
        kv_y.wait_recv()
        mask_own = k.ids_near[0:1, :] <= k.ids_q[:, 0:1]
        mask_oth = k.ids_far[0:1, :] <= k.ids_q[:, 0:1]
        for h in range(4):
            at = slice(h * 128, (h + 1) * 128)
            w_own, w_oth = softmax_parts(
                k.q[:, at], k.kv[0:256, at], k.kv_oth[0:256, at], mask_own, mask_oth
            )
            value = dot_nn(w_own.astype(bf16), k.kv[256:512, at])
            value += dot_nn(w_oth.astype(bf16), k.kv_oth[256:512, at])
            k.low[:, at] = value.astype(bf16)
        out.wait(6)
        bring_out(6)
        out.wait(3)
        out.start(7)
        bring_out(3)
        out.wait(7)
        bring_out(7)
        for copy in held_out:
            copy.wait()
        for r in range(8):
            part = dot_nn(k.low[...], low_w[r]).astype(bf16)
            at = pl.ds(pl.multiple_of(owner_dense(r) * 256, 256), 256)
            for d in range(4):
                k.att_send[d, :, at] = part[d * 64 : (d + 1) * 64, :]

    pl.run_scoped(
        attention_part,
        pltpu.VMEM((256, 2048), f32),
        pltpu.VMEM((3, 256, 512), f32),
        pltpu.VMEM((8, 768, 512), bf16),
        pltpu.VMEM((8, 512, 256), bf16),
        pltpu.VMEM((3, 256, 2, 1408), bf16),
        pltpu.VMEM((3, 2, 256, 1408), bf16),
    )
    att_z = to_z(lambda d: lambda: (k.att_send.at[d], k.att.at[d - 1]))
    swap_n = wires.go(lambda: (k.n_send, k.n_x), core_dev)
    swap_low = wires.go(lambda: (k.low, k.low_x), core_dev)
    parts = SimpleNamespace(started=False)

    def expert_part(wg, wu, wd, slopes, acc, up, keep, send):
        group = []

        def gather(s, w):
            group.append(loads.go(s.block(0), w.at[0]))
            s.wait(2)
            group.append(loads.go(s.block(2), w.at[2]))
            s.wait(1)
            s.start(3)
            group.append(loads.go(s.block(1), w.at[1]))

        def gather_last(s, w):
            s.wait(3)
            group.append(loads.go(s.block(3), w.at[3]))

        gather(ed, wd)
        for copy in att_z:
            copy.wait_recv()
        value = piece(k.tok, 0, 64).astype(f32) + (
            k.att_send[0].astype(f32)
            + k.att[0].astype(f32)
            + k.att[1].astype(f32)
            + k.att[2].astype(f32)
        )
        inv = lax.rsqrt(jnp.mean(value * value, axis=-1, keepdims=True) + epsilon)
        k.hidden[...] = value
        k.rows[0:64, :] = (value * inv * k.small[1:2, :].astype(f32)).astype(bf16)
        own_y = wires.go(
            lambda: (k.rows.at[pl.ds(0, 64), :], k.rows.at[pl.ds(256, 64), :]), y_dev
        )
        g_y = wires.go(lambda: (k.g_own, k.g_oth), y_dev)
        sd.start(2)
        own_z = Collect(lambda d: k.rows.at[pl.ds(64 * d, 64), :])
        gather_last(ed, wd)
        gather(eg, wg)
        gather_last(eg, wg)
        for s in (sg, su):
            s.wait(2)
            s.start(6)
        own_z.hand_on()
        for copy in later:
            copy.wait_recv()
        own_y.wait_recv()
        own_z.wait()
        oth_z = to_z(
            lambda d: lambda: (
                k.rows.at[pl.ds(256, 64), :],
                k.rows.at[pl.ds(256 + 64 * d, 64), :],
            )
        )

        def g_piece(half, d, at):
            g = k.g_oth if half else k.g_own
            return g[pl.ds(pl.multiple_of(near(d) * 64, 64), 64), at].astype(f32)

        def route(half):
            chosen = []
            for d in range(4):
                named = (k.ids[d, half * 64 : (half + 1) * 64, :] == mine.astype(f32)).astype(f32)
                chosen.append(jnp.sum(named, axis=-1, keepdims=True))
            chosen = jnp.concatenate(chosen, axis=0)
            prob, lane = probabilities(k.rows[half * 256 : (half + 1) * 256, :], k.small)
            here = jnp.sum(jnp.where(lane == mine + 3, prob, 0.0), axis=-1, keepdims=True)
            gate = here * chosen
            for d in range(4):
                at = slice(half * 256 + d * 64, half * 256 + (d + 1) * 64)
                value = gate[d * 64 : (d + 1) * 64, :] * g_piece(half, d, slice(None))
                slopes[at, :] = value.astype(bf16)
            return gate, chosen

        def gate_part(half):
            rows_at = slice(half * 256, (half + 1) * 256)

            def one(r, _):
                at = pl.ds(pl.multiple_of(owner_expert(r) * 512, 512), 512)
                acc[0] += dot_nn(k.rows[rows_at, at], wg[r])
                acc[2] += dot_nt(slopes[rows_at, at], wd[r])
                return 0

            acc[...] = jnp.zeros_like(acc)
            lax.fori_loop(0, 4, one, 0)

        def phase_one(half):
            rows_at = slice(half * 256, (half + 1) * 256)

            def one(r, _):
                at = pl.ds(pl.multiple_of(owner_expert(r) * 512, 512), 512)
                acc[1] += dot_nn(k.rows[rows_at, at], wu[r])
                return 0

            lax.fori_loop(0, 4, one, 0)
            for d in range(4):
                at, to = slice(d * 64, (d + 1) * 64), slice(half * 256 + d * 64, half * 256 + (d + 1) * 64)
                act, gate_grad, up_grad = gated(acc[0, at, :], acc[1, at, :], acc[2, at, :])
                up[0, to, :] = act.astype(bf16)
                up[1, to, :] = gate_grad.astype(bf16)
                up[2, to, :] = up_grad.astype(bf16)

        lanes = lax.broadcasted_iota(jnp.int32, (64, 128), 1)

        def phase_two(half, gate, chosen, between):
            rows_at = slice(half * 256, (half + 1) * 256)

            def two(r, dgate):
                at = pl.ds(pl.multiple_of(owner_expert(r) * 512, 512), 512)
                result = dot_nn(up[0, rows_at, :], wd[r]).astype(bf16).astype(f32)
                grad = dot_nt(up[1, rows_at, :], wg[r]) + dot_nt(up[2, rows_at, :], wu[r])
                sums = []
                for d in range(4):
                    here = slice(d * 64, (d + 1) * 64)
                    g_rows = g_piece(half, d, at)
                    sums.append(jnp.sum(g_rows * result[here, :], axis=-1, keepdims=True))
                    part = gate[here, :] * result[here, :]
                    if half == 0:
                        k.out_sum[here, at] = part
                        k.grad_sum[here, at] = grad[here, :]
                    else:
                        k.e_out[d, :, at] = part.astype(bf16)
                        k.e_grad[d, :, at] = grad[here, :].astype(bf16)
                return dgate + jnp.concatenate(sums, axis=0)

            dgate = lax.fori_loop(0, 2, two, jnp.zeros((256, 1), f32))
            between()
            dgate = lax.fori_loop(2, 4, two, dgate) * chosen
            for d in range(4):
                extra = jnp.zeros((64, 128), f32)
                for m, part in enumerate(split3(dgate[d * 64 : (d + 1) * 64, :])):
                    extra = jnp.where(lanes == mine + 16 * m, part, extra)
                if half == 0:
                    k.extras[d * 64 : (d + 1) * 64, :] = extra
                else:
                    k.e_grad[d, :, 2048:2176] = extra.astype(bf16)

        gate, chosen = route(0)
        for copy in group:
            copy.wait()
        group.clear()
        gate_part(0)
        gather(eu, wu)
        gather_last(eu, wu)
        for copy in group:
            copy.wait()
        phase_one(0)
        phase_two(0, gate, chosen, lambda: None)
        sg.wait(1)
        sg.start(3)
        sg.start(5)
        for copy in oth_z + [g_y]:
            copy.wait_recv()
        gate, chosen = route(1)
        gate_part(1)
        phase_one(1)
        saved = [loads.go(up, k.ex_up)]
        for r in range(4):
            to = slice(r * 256, (r + 1) * 256)
            for target, m in ((keep, r), (send, r + 4)):
                at = pl.ds(pl.multiple_of(owner_dense(m) * 256, 256), 256)
                target[0:512, to] = slopes[:, at]
                target[512:1024, to] = k.rows[:, at]
        saved.append(loads.go(keep, k.ex_keep))
        swap_ex = wires.go(lambda: (send, k.ex_x), core_dev)
        sd.wait(2)
        sd.start(6)

        def pass_on():
            su.wait(1)
            su.start(3)
            su.start(5)

        phase_two(1, gate, chosen, pass_on)
        for copy in saved:
            copy.wait()
        swap_ex.wait_send()
        swap_ex.ends = lambda: (k.ex_keep, k.ex_x)
        parts.swap_ex = swap_ex

    pl.run_scoped(
        expert_part,
        pltpu.VMEM((4, 512, 1408), bf16),
        pltpu.VMEM((4, 512, 1408), bf16),
        pltpu.VMEM((4, 1408, 512), bf16),
        pltpu.VMEM((512, 2048), bf16),
        pltpu.VMEM((3, 256, 1408), f32),
        pltpu.VMEM((3, 512, 1408), bf16),
        pltpu.VMEM((1024, 1024), bf16),
        pltpu.VMEM((1024, 1024), bf16),
    )
    swap_up = {}
    for m in (1, 2, 0):
        swap_up[m] = wires.go(lambda m=m: (k.ex_up.at[m], k.ex_up_x.at[m]), core_dev)
    e_grad_z = to_z(lambda d: lambda: (k.e_grad.at[d], k.e_grad_z.at[d - 1]))
    e_out_z = to_z(lambda d: lambda: (k.e_out.at[d], k.e_out_z.at[d - 1]))
    over_y, over_x = {}, {}

    def expert_grad(m, kept, sent, landed):
        parts.swap_ex_wait()
        swap_up[m].wait_recv()

        def inner(left, right, keep, send):
            start = pl.ds(0 if m == 0 else 512, 512)
            got = [
                loads.go(k.ex_up.at[m], right.at[0]),
                loads.go(k.ex_up_x.at[m], right.at[1]),
                loads.go(k.ex_keep.at[start, :], left.at[0]),
                loads.go(k.ex_x.at[start, :], left.at[1]),
            ]
            for copy in got:
                copy.wait()
            saved = []
            for r in (3, 1, 2, 0):
                target = send if r % 2 else keep
                at = slice(r * 256, (r + 1) * 256)
                to = pl.ds(pl.multiple_of(((y + r // 2) % 2) * 256, 256), 256)
                if m == 0:
                    total = dot_tn(right[0], left[0, :, at]) + dot_tn(right[1], left[1, :, at])
                    target[:, to] = total.astype(bf16)
                else:
                    total = dot_tn(left[0, :, at], right[0]) + dot_tn(left[1, :, at], right[1])
                    target[to, :] = total.astype(bf16)
                if r == 1:
                    saved.append(loads.go(send, sent))
                if r == 2:
                    saved[0].wait()
                    over_x[6 + m] = wires.go(lambda: (sent, landed), x_dev)
            loads.go(keep, kept).wait()

        shape = (1408, 512) if m == 0 else (512, 1408)
        pl.run_scoped(
            inner,
            pltpu.VMEM((2, 512, 1024), bf16),
            pltpu.VMEM((2, 512, 1408), bf16),
            pltpu.VMEM(shape, bf16),
            pltpu.VMEM(shape, bf16),
        )

    def set_out(name, n, source, target, device):
        over_y[name, n] = wires.go(lambda: (source.at[n], target.at[n]), device)

    def y_first(name, keep, send, landed):
        def store(r, total):
            (send if r >= 2 else keep)[r % 2] = total
            if r == 3:
                set_out(name, 1, send, landed, y_dev)

        return store

    def shared_grad(m, store):
        def inner(left, right):
            if m == 0:
                got = [loads.go(k.sh_keep, left.at[0]), loads.go(k.sh_x, left.at[1])]
            else:
                start = pl.ds(512, 256)
                got = [
                    loads.go(k.ex_keep.at[start, :], left.at[0]),
                    loads.go(k.ex_x.at[start, :], left.at[1]),
                ]
            got.append(loads.go(k.sh_up.at[m], right.at[0]))
            got.append(loads.go(k.sh_up_x.at[m], right.at[1]))
            for copy in got:
                copy.wait()
            for r in (3, 1, 2, 0):
                at = slice(r * 256, (r + 1) * 256)
                if m == 0:
                    total = dot_tn(right[0], left[0, :, at]) + dot_tn(right[1], left[1, :, at])
                else:
                    total = dot_tn(left[0, :, at], right[0]) + dot_tn(left[1, :, at], right[1])
                store(r, total.astype(bf16))

        pl.run_scoped(
            inner, pltpu.VMEM((2, 256, 1024), bf16), pltpu.VMEM((2, 256, 1408), bf16)
        )

    def swap_ex_wait():
        if not parts.started:
            parts.swap_ex.wait_recv()
            parts.started = True

    parts.swap_ex_wait = swap_ex_wait

    def shared_part(wg, wu, wd, slopes, acc, up, keep, send):
        routed = k.rows.at[pl.ds(0, 256), :]
        held = []

        def bring(r, group):
            for s in group:
                held.append(loads.go(s.block(r), {sg: wg, su: wu, sd: wd}[s].at[r]))

        def arrived(r, group, onward=()):
            for s in group:
                s.wait(r)
                for t in onward:
                    s.start(t)
            bring(r, group)

        def settle():
            for copy in held:
                copy.wait()
            held.clear()

        pair, last = (sg, su), (sd,)
        for r in (0, 1, 2):
            bring(r, pair)
        for r in (4, 6):
            arrived(r, pair)
        expert_grad(1, k.k_eg, k.t_eg, k.x_eg)
        arrived(5, pair)
        sd.wait(1)
        sd.start(3)
        sd.start(5)
        bring(0, last)
        bring(1, last)
        bring(2, last)
        arrived(4, last)
        arrived(6, last)
        arrived(5, last)
        wide = routed[...].astype(f32) * k.small[2:3, :].astype(f32)
        sw = jax.nn.sigmoid(jnp.sum(wide, axis=-1, keepdims=True))
        for d in range(4):
            at = slice(d * 64, (d + 1) * 64)
            slopes[at, :] = (sw[at, :] * piece(k.g_own, d, 64).astype(f32)).astype(bf16)
        for r in range(4):
            to = slice(r * 256, (r + 1) * 256)
            keep[:, to] = cols(slopes, owner_dense(r), 256)
            send[:, to] = cols(slopes, owner_dense(r + 4), 256)
        saved = [loads.go(keep, k.sh_keep)]
        acc[...] = jnp.zeros_like(acc)

        def one(j, _):
            r = j // 2 + (j % 2) * 4
            row = cols(routed, owner_dense(r), 256)
            acc[0] += dot_nn(row, wg[r])
            acc[1] += dot_nn(row, wu[r])
            return 0

        def back(j, _):
            r = j // 2 + (j % 2) * 4
            acc[2] += dot_nt(cols(slopes, owner_dense(r), 256), wd[r])
            return 0

        settle()
        lax.fori_loop(0, 6, one, 0)
        arrived(3, pair, (7,))
        arrived(7, pair)
        settle()
        lax.fori_loop(6, 8, one, 0)
        for d in range(4):
            at = slice(d * 64, (d + 1) * 64)
            up[0, at, :] = (jax.nn.silu(acc[0, at, :]) * acc[1, at, :]).astype(bf16)
        swaps = [
            wires.go(lambda: (up.at[0], k.sh_up_x.at[0]), core_dev),
            wires.go(lambda: (send, k.sh_x), core_dev),
        ]
        saved.append(loads.go(up.at[0], k.sh_up.at[0]))
        for copy in saved:
            copy.wait()
        lax.fori_loop(0, 6, back, 0)
        for copy in swaps:
            copy.wait_recv()
            copy.wait_send()
        shared_grad(0, y_first(2, k.k_sd, k.t_sd, k.y_sd))
        for copy in e_grad_z:
            copy.wait_recv()
        oth = k.e_grad[0].astype(f32)
        for d in range(3):
            oth += k.e_grad_z[d].astype(f32)
        k.g_send[...] = oth.astype(bf16)
        parts.grad_y = wires.go(lambda: (k.g_send, k.g_y), y_dev)
        set_out(2, 0, k.t_sd, k.y_sd, y_dev)
        expert_grad(2, k.k_eu, k.t_eu, k.x_eu)
        arrived(3, last, (7,))
        arrived(7, last)
        settle()
        lax.fori_loop(6, 8, back, 0)
        for d in range(4):
            at = slice(d * 64, (d + 1) * 64)
            _, gate_grad, up_grad = gated(acc[0, at, :], acc[1, at, :], acc[2, at, :])
            up[1, at, :] = gate_grad.astype(bf16)
            up[2, at, :] = up_grad.astype(bf16)
        saved = [loads.go(up.at[m], k.sh_up.at[m]) for m in (1, 2)]

        def two(r, slope):
            at = pl.ds(pl.multiple_of(owner_dense(r) * 256, 256), 256)
            part = dot_nn(up[0], wd[r])
            total = sw * part + k.out_sum[:, at]
            back = dot_nt(up[1], wg[r]) + dot_nt(up[2], wu[r]) + k.grad_sum[:, at]
            sums = []
            for d in range(4):
                rows_at = slice(d * 64, (d + 1) * 64)
                g_rows = k.g_own[pl.ds(pl.multiple_of(near(d) * 64, 64), 64), at].astype(f32)
                sums.append(jnp.sum(g_rows * part[rows_at, :], axis=-1, keepdims=True))
                k.s_out[d, :, at] = total[rows_at, :].astype(bf16)
                k.s_grad[d, :, at] = back[rows_at, :].astype(bf16)
            return slope + jnp.concatenate(sums, axis=0)

        slope = lax.fori_loop(0, 8, two, jnp.zeros((256, 1), f32))
        lanes = lax.broadcasted_iota(jnp.int32, (64, 128), 1)
        for d in range(4):
            rows_at = slice(d * 64, (d + 1) * 64)
            extra = k.extras[rows_at, :]
            for m, part in enumerate(split3(slope[rows_at, :])):
                extra = jnp.where(lanes == mine + 48 + 16 * m, part, extra)
            k.s_grad[d, :, 2048:2176] = extra.astype(bf16)
        for copy in saved:
            copy.wait()

    pl.run_scoped(
        shared_part,
        pltpu.VMEM((8, 256, 1408), bf16),
        pltpu.VMEM((8, 256, 1408), bf16),
        pltpu.VMEM((8, 1408, 256), bf16),
        pltpu.VMEM((256, 2048), bf16),
        pltpu.VMEM((3, 256, 1408), f32),
        pltpu.VMEM((3, 256, 1408), bf16),
        pltpu.VMEM((256, 1024), bf16),
        pltpu.VMEM((256, 1024), bf16),
    )
    swap_sh = [
        wires.go(lambda m=m: (k.sh_up.at[m], k.sh_up_x.at[m]), core_dev) for m in (1, 2)
    ]
    s_grad_z = to_z(lambda d: lambda: (k.s_grad.at[d], k.s_grad_z.at[d - 1]))

    def back_part(*refs):
        k_ga, k_gb, k_su, k_q, k_kv, k_o, k_v = refs[:7]
        t_ga, t_gb, t_su, t_q, t_kv, t_o, t_v = refs[7:14]
        f_ga, f_gb, f_su, f_q, f_kv, f_o, f_v, f_sd = refs[14:22]
        h_keep, h_send, h_x, lin, lin_x, vec, high, gkv, gkv_send, gn = refs[22:]
        k_sd, t_sd = k.k_sd, k.t_sd

        def fold(name, keep, landed, send, target, device=x_dev):
            over_y[name, 1].wait_recv()

            def inner(buffer):
                loads.go(landed.at[1], buffer).wait()
                send[...] = (keep[1].astype(f32) + buffer[...].astype(f32)).astype(bf16)

            pl.run_scoped(inner, pltpu.VMEM(tuple(keep.shape[1:]), bf16))
            over_x[name] = wires.go(lambda: (send, target), device)

        def finish_pair():
            for name in (0, 9, 1):
                over_y[name, 0].wait_recv()
                over_x[name].wait_recv()

            def inner(left, right, total):
                first, last, whole = pl.ds(0, 128), pl.ds(128, 128), slice(0, 256)
                got = [
                    loads.go(k.y_ga.at[0], left.at[0, first, :]),
                    loads.go(k.x_ga, right.at[0, first, :]),
                    loads.go(k.y_gb.at[0], left.at[0, last, :]),
                    loads.go(k.x_gb, right.at[0, last, :]),
                    loads.go(k.y_su.at[0], left.at[1]),
                    loads.go(k.x_su, right.at[1]),
                ]
                for copy in got:
                    copy.wait()
                for n, keep, at in (
                    (0, k_ga, slice(0, 128)),
                    (0, k_gb, slice(128, 256)),
                    (1, k_su, whole),
                ):
                    value = keep[0].astype(f32) + left[n, at, :].astype(f32)
                    value += right[n, at, :].astype(f32)
                    total[at, n, :] = value.astype(bf16)
                loads.go(total, k.d_si).wait()

            pair = pltpu.VMEM((2, 256, 1408), bf16)
            pl.run_scoped(inner, pair, pair, pltpu.VMEM((256, 2, 1408), bf16))

        def finish(name, keep, landed, target, result):
            over_y[name, 0].wait_recv()

            def inner(left, right, total):
                got = loads.go(landed.at[0], left)
                over_x[name].wait_recv()
                more = loads.go(target, right)
                got.wait()
                more.wait()
                value = keep[0].astype(f32) + left[...].astype(f32) + right[...].astype(f32)
                total[...] = value.astype(total.dtype)
                loads.go(total, result).wait()

            shape = tuple(keep.shape[1:])
            pl.run_scoped(
                inner,
                pltpu.VMEM(shape, bf16),
                pltpu.VMEM(shape, bf16),
                pltpu.VMEM(shape, result.dtype),
            )

        swap_sh[0].wait_recv()

        def gate_store(r, total):
            (t_ga if r >= 2 else k_ga)[r % 2] = total[0:128, :]
            (t_gb if r % 2 else k_gb)[r // 2] = total[128:256, :]
            if r == 3:
                set_out(0, 1, t_ga, k.y_ga, y_dev)
                set_out(9, 1, t_gb, k.y_gb, x_dev)

        shared_grad(1, gate_store)
        set_out(9, 0, t_gb, k.y_gb, x_dev)
        swap_sh[1].wait_recv()
        shared_grad(2, y_first(1, k_su, t_su, k.y_su))
        expert_grad(0, k.k_ed, k.t_ed, k.x_ed)
        fold(2, k_sd, k.y_sd, f_sd, k.x_sd)

        def other_rows(buffer):
            for copy in e_out_z:
                copy.wait_recv()
            loads.go(k.e_out_z, buffer).wait()
            oth = k.e_out[0].astype(f32)
            for d in range(3):
                oth += buffer[d].astype(f32)
            k.o_send[...] = oth.astype(bf16)

        pl.run_scoped(other_rows, pltpu.VMEM((3, 64, 2048), bf16))
        for copy in s_grad_z:
            copy.wait_recv()
        parts.grad_y.wait_recv()
        total = k.s_grad[0].astype(f32) + k.g_y[...].astype(f32)
        for d in range(3):
            total += k.s_grad_z[d].astype(f32)
        own_rows(
            total,
            k.hidden[...],
            k.rows[0:64, :],
            piece(k.g_own, 0, 64),
            k.small,
            high,
            k.gh.at[0],
            vec,
        )
        gh_z = Collect(lambda d: k.gh.at[d])
        out_y = wires.go(lambda: (k.o_send, k.o_y), y_dev)
        fold(0, k_ga, k.y_ga, f_ga, k.x_ga)
        fold(9, k_gb, k.y_gb, f_gb, k.x_gb, y_dev)
        gn_z, s_out_z, vec_z = [], [], []

        def attention_back(w, o_w, acc, low_g, n_x, low_x):
            got, more = [loads.go(k.w_o, o_w.at[0])], [loads.go(k.w_q, w.at[0])]
            for r in range(1, 8):
                got.append(loads.go(k.s_o.at[r], o_w.at[r]))
                more.append(loads.go(k.s_q.at[r], w.at[r]))
            gh_z.hand_on()
            gh_z.wait()
            s_out_z.extend(to_z(lambda d: lambda: (k.s_out.at[d], k.s_out_z.at[d - 1])))
            for copy in got:
                copy.wait()
            acc[...] = jnp.zeros_like(acc)
            for r in range(8):
                at = pl.ds(pl.multiple_of(owner_dense(r) * 256, 256), 256)
                row = jnp.concatenate([k.gh[d, :, at] for d in range(4)], axis=0)
                target = h_keep if r < 4 else h_send
                target[:, (r % 4) * 256 : (r % 4 + 1) * 256] = row
                acc[...] += dot_nt(row, o_w[r])
            swap_h = wires.go(lambda: (h_send, k.h_x), core_dev)
            low_g[...] = acc[...].astype(bf16)
            mask_own = k.ids_near[0:1, :] <= k.ids_q[:, 0:1]
            mask_oth = k.ids_far[0:1, :] <= k.ids_q[:, 0:1]
            scale = 128 ** (-0.5)
            for h in range(4):
                at = slice(h * 128, (h + 1) * 128)
                w_own, w_oth = softmax_parts(
                    k.q[:, at], k.kv[0:256, at], k.kv_oth[0:256, at], mask_own, mask_oth
                )
                dw_own = dot_nt(low_g[:, at], k.kv[256:512, at])
                dw_oth = dot_nt(low_g[:, at], k.kv_oth[256:512, at])
                mean = jnp.sum(w_own * dw_own, axis=-1, keepdims=True)
                mean += jnp.sum(w_oth * dw_oth, axis=-1, keepdims=True)
                ds_own = (w_own * (dw_own - mean)).astype(bf16)
                ds_oth = (w_oth * (dw_oth - mean)).astype(bf16)
                gq = dot_nn(ds_own, k.kv[0:256, at]) + dot_nn(ds_oth, k.kv_oth[0:256, at])
                lin[0:256, at] = turn_back(gq * scale, k.cs[...], k.sn[...]).astype(bf16)
                gkv[0:256, at] = dot_tn(ds_own, k.q[:, at]) * scale
                gkv[256:512, at] = dot_tn(w_own.astype(bf16), low_g[:, at])
                gkv_send[0:256, at] = (dot_tn(ds_oth, k.q[:, at]) * scale).astype(bf16)
                gkv_send[256:512, at] = dot_tn(w_oth.astype(bf16), low_g[:, at]).astype(bf16)
            gkv_y = wires.go(lambda: (gkv_send, k.gkv_y), y_dev)
            swap_q = wires.go(
                lambda: (lin.at[pl.ds(0, 256), :], k.lin_x.at[pl.ds(0, 256), :]), core_dev
            )
            set_out(0, 0, t_ga, k.y_ga, y_dev)
            fold(1, k_su, k.y_su, f_su, k.x_su)
            for copy in (swap_h, swap_n, swap_low, swap_q):
                copy.wait_recv()
            got = [
                loads.go(k.n_x, n_x),
                loads.go(k.low_x, low_x),
                loads.go(k.h_x, h_x),
                loads.go(k.lin_x.at[pl.ds(0, 256), :], lin_x.at[pl.ds(0, 256), :]),
            ]
            for copy in got:
                copy.wait()

            def projection(r, m):
                at, rows_at = slice(r * 256, (r + 1) * 256), slice(m * 256, (m + 1) * 256)
                total = dot_tn(k.n_keep[:, at], lin[rows_at, :])
                return (total + dot_tn(n_x[:, at], lin_x[rows_at, :])).astype(bf16)

            for r in (3, 1, 2, 0):
                at = slice(r * 256, (r + 1) * 256)
                total = dot_tn(k.low[...], h_keep[:, at]) + dot_tn(low_x[...], h_x[:, at])
                (t_o if r % 2 else k_o)[r // 2] = total.astype(bf16)
                if r % 2:
                    set_out(4, r // 2, t_o, k.y_o, x_dev)
                (t_q if r >= 2 else k_q)[r % 2] = projection(r, 0)
                if r == 3:
                    set_out(3, 1, t_q, k.y_q, y_dev)
            for copy in more:
                copy.wait()
            gkv_y.wait_recv()
            for h in range(4):
                at = slice(h * 128, (h + 1) * 128)
                gk = gkv[0:256, at] + k.gkv_y[0:256, at].astype(f32)
                lin[256:512, at] = turn_back(gk, k.cs[...], k.sn[...]).astype(bf16)
            lin[512:768, :] = (gkv[256:512, :] + k.gkv_y[256:512, :].astype(f32)).astype(bf16)
            swap_kv = wires.go(
                lambda: (lin.at[pl.ds(256, 512), :], k.lin_x.at[pl.ds(256, 512), :]), core_dev
            )
            for m in range(3):
                part = lin[m * 256 : (m + 1) * 256, :].astype(f32)
                vec[11 + m : 12 + m, 0:512] = jnp.sum(part, axis=0, keepdims=True)
            swap_kv.wait_recv()
            loads.go(k.lin_x.at[pl.ds(256, 512), :], lin_x.at[pl.ds(256, 512), :]).wait()
            for r in (3, 2, 1, 0):
                target = t_kv if r >= 2 else k_kv
                for m in (1, 2):
                    target[r % 2, (m - 1) * 256 : m * 256, :] = projection(r, m)
                if r == 3:
                    set_out(10, 1, t_kv, k.y_kv, y_dev)
                    set_out(1, 0, t_su, k.y_su, y_dev)
            for r in range(8):
                at = pl.ds(pl.multiple_of(owner_dense(r) * 256, 256), 256)
                back = dot_nt(lin[0:256, :], w[r, 0:256, :])
                back += dot_nt(lin[256:512, :], w[r, 256:512, :])
                back += dot_nt(lin[512:768, :], w[r, 512:768, :])
                gain = jnp.zeros((1, 256), f32)
                for d in range(4):
                    rows_at = slice(d * 64, (d + 1) * 64)
                    t = k.tok[pl.ds(pl.multiple_of(near(d) * 64, 64), 64), at].astype(f32)
                    gain += jnp.sum(
                        back[rows_at, :] * t * k.inv1[rows_at, :], axis=0, keepdims=True
                    )
                    gn[d, :, at] = back[rows_at, :].astype(bf16)
                vec[0:1, at] = gain
            vec_z.extend(to_z(lambda d: lambda: (vec, k.vec_z.at[d - 1])))
            gn_z.extend(to_z(lambda d: lambda: (gn.at[d], k.gn_z.at[d - 1])))

        pl.run_scoped(
            attention_back,
            pltpu.VMEM((8, 768, 512), bf16),
            pltpu.VMEM((8, 512, 256), bf16),
            pltpu.VMEM((256, 512), f32),
            pltpu.VMEM((256, 512), bf16),
            pltpu.VMEM((256, 1024), bf16),
            pltpu.VMEM((256, 512), bf16),
        )
        kept = [loads.go(k_q.at[0], k.keep_q), loads.go(k_kv.at[0], k.keep_kv)]
        kept.append(loads.go(k_o.at[0], k.keep_o))
        def expert_finish(m, kept, landed, result):
            def inner(left, right):
                got = loads.go(kept, left)
                over_x[6 + m].wait_recv()
                more = loads.go(landed, right)
                got.wait()
                more.wait()
                left[...] = (left[...].astype(f32) + right[...].astype(f32)).astype(bf16)
                loads.go(left, result).wait()

            shape = pltpu.VMEM(tuple(result.shape), bf16)
            pl.run_scoped(inner, shape, shape)

        def expert_pair():
            for m in (1, 2):
                over_x[6 + m].wait_recv()

            def inner(left, right, total):
                for half in range(2):
                    at = pl.ds(256 * half, 256)
                    got = []
                    for n, (kept, landed) in enumerate(((k.k_eg, k.x_eg), (k.k_eu, k.x_eu))):
                        got.append(loads.go(kept.at[at, :], left.at[n]))
                        got.append(loads.go(landed.at[at, :], right.at[n]))
                    for copy in got:
                        copy.wait()
                    for n in range(2):
                        value = left[n].astype(f32) + right[n].astype(f32)
                        total[:, n, :] = value.astype(bf16)
                    loads.go(total, k.d_ei.at[at]).wait()

            pair = pltpu.VMEM((2, 256, 1408), bf16)
            pl.run_scoped(inner, pair, pair, pltpu.VMEM((256, 2, 1408), bf16))

        expert_pair()
        for copy in vec_z:
            copy.wait_recv()
        line = lax.broadcasted_iota(jnp.int32, (16, 2048), 0)
        over_z = k.vec_z[0] + k.vec_z[1] + k.vec_z[2]
        k.vec_sum[...] = vec[...] + jnp.where(line < 11, over_z, 0.0)
        swap_vec = wires.go(lambda: (k.vec_sum, k.vec_x), core_dev)
        swap_vec.wait_recv()
        k.vec_x[...] += k.vec_sum[...]
        line = lax.broadcasted_iota(jnp.int32, (16, 512), 0)
        for r in (3, 2, 1, 0):
            here = cols(k.vec_x, owner_dense(r), 256)
            here = jnp.concatenate([here, jnp.zeros((16, 256), f32)], axis=1)
            here = jnp.where(line < 11, here, k.vec_x[:, 0:512]).astype(bf16)
            (t_v if r >= 2 else k_v)[r % 2] = here
            if r >= 2:
                set_out(5, r % 2, t_v, k.y_v, y_dev)
        kept.append(loads.go(k_v.at[0], k.keep_v))
        set_out(3, 0, t_q, k.y_q, y_dev)
        set_out(10, 0, t_kv, k.y_kv, y_dev)

        def outputs(s_z):
            for copy in s_out_z:
                copy.wait_recv()
            got = loads.go(k.s_out_z, s_z)
            for copy in gn_z:
                copy.wait_recv()
            grad = gn[0].astype(f32)
            for d in range(3):
                grad += k.gn_z[d].astype(f32)
            t = piece(k.tok, 0, 64).astype(f32)
            i = k.inv1[0:64, :]
            scaled = grad * k.small[0:1, :].astype(f32)
            mean = jnp.mean(scaled * t, axis=-1, keepdims=True)
            grad = high[...] + i * scaled - t * (i * i * i * mean)
            k.grad_tokens[...] = grad.astype(bf16)
            got.wait()
            total = k.hidden[...] + k.s_out[0].astype(f32)
            for d in range(3):
                total += s_z[d].astype(f32)
            out_y.wait_recv()
            k.output[...] = (total + k.o_y[...].astype(f32)).astype(bf16)

        expert_finish(0, k.k_ed, k.x_ed, k.d_ed)
        finish(2, k_sd, k.y_sd, k.x_sd, k.d_sd)
        fold(3, k_q, k.y_q, f_q, k.x_q)
        fold(10, k_kv, k.y_kv, f_kv, k.x_kv)
        fold(5, k_v, k.y_v, f_v, k.x_v)
        fold(4, k_o, k.y_o, f_o, k.x_o, y_dev)
        pl.run_scoped(outputs, pltpu.VMEM((3, 64, 2048), bf16))
        finish_pair()
        for name in (3, 10, 4, 5):
            over_y[name, 0].wait_recv()
            over_x[name].wait_recv()
        for copy in kept:
            copy.wait()
        wires.drain()

    shapes = [(128, 1408), (128, 1408), (256, 1408), (256, 512), (512, 512), (512, 256), (16, 512)]

    def buffers(lead):
        return tuple(
            pltpu.VMEM(lead + shape, bf16)
            for shape in shapes
        )

    pl.run_scoped(
        back_part,
        *buffers((2,)),
        *buffers((2,)),
        *buffers(()),
        pltpu.VMEM((1408, 256), bf16),
        pltpu.VMEM((256, 1024), bf16),
        pltpu.VMEM((256, 1024), bf16),
        pltpu.VMEM((256, 1024), bf16),
        pltpu.VMEM((768, 512), bf16),
        pltpu.VMEM((768, 512), bf16),
        pltpu.VMEM((16, 2048), f32),
        pltpu.VMEM((64, 2048), f32),
        pltpu.VMEM((512, 512), f32),
        pltpu.VMEM((512, 512), bf16),
        pltpu.VMEM((4, 64, 2048), bf16),
    )


def close_kernel(k):
    loads = Loads(k.load_sems)
    sums = (
        (k.keep_q, k.y_q, k.x_q, k.b_q, k.c_q.at[pl.ds(0, 256), :]),
        (k.keep_kv, k.y_kv, k.x_kv, k.b_kv, k.c_q.at[pl.ds(256, 512), :]),
        (k.keep_o, k.y_o, k.x_o, k.b_o, k.c_o),
    )
    parts = []
    for keep, y, x, buffer, _ in sums:
        parts.append([loads.go(a, buffer.at[n]) for n, a in enumerate((keep, y.at[0], x))])
    passed = (
        (k.d_ei, k.b_ei, k.c_ei),
        (k.d_ed, k.b_ed, k.c_ed),
        (k.d_si, k.b_si, k.c_si),
        (k.d_sd, k.b_sd, k.c_sd),
        (k.output, k.b_out, k.c_out),
        (k.grad_tokens, k.b_tok, k.c_tok),
    )
    got = [loads.go(source, buffer) for source, buffer, _ in passed]
    total = k.keep_v[...].astype(f32) + k.y_v[0].astype(f32) + k.x_v[...].astype(f32)
    low = total.astype(bf16)
    for m, target in enumerate((k.c_one, k.c_two, k.c_gate)):
        target[...] = low[m : m + 1, 0:256].reshape(256)
    k.c_router[...] = low[3:11, 0:256]
    for h in range(4):
        here = pltpu.roll(
            total[:, h * 128 : (h + 1) * 128], (128 - owner_dense(0) * 16) % 128, 1
        )
        for m in range(3):
            k.c_bias[m, h : h + 1, :] = here[11 + m : 12 + m, 0:16].astype(bf16)
    done = []
    for copies, (_, _, _, buffer, target) in zip(parts, sums):
        for copy in copies:
            copy.wait()
        total = buffer[0].astype(f32) + buffer[1].astype(f32) + buffer[2].astype(f32)
        buffer[0] = total.astype(bf16)
        done.append(loads.go(buffer.at[0], target))
    for copy, (_, buffer, target) in zip(got, passed):
        copy.wait()
        done.append(loads.go(buffer, target))
    for copy in done:
        copy.wait()


def dma(n):
    return pltpu.SemaphoreType.DMA((n,))


def fixed_body(
    tokens,
    norm1_gain,
    w_qkv,
    b_qkv,
    w_out,
    norm2_gain,
    w_router,
    shared_gate,
    w_shared_in,
    w_shared_out,
    w_expert_in,
    w_expert_out,
    block_ids,
    expert_ids,
    out_grad,
):
    tok, g_own = tokens[0], out_grad[0]
    rows = tok.shape[0]
    places = np.arange(2 * rows)[:, None]
    frequency = rope_base ** (-np.arange(64) / 64.0)
    cosine, sine = np.cos(places * frequency), np.sin(places * frequency)
    cs = np.concatenate([cosine, cosine], axis=1).astype(np.float32)
    sn = np.concatenate([-sine, sine], axis=1).astype(np.float32)

    def vm(*shape, kind=bf16):
        return pltpu.VMEM(shape, kind)

    def o(*shape, kind=bf16, at=A):
        return (shape, kind, at)

    w_q = w_qkv.transpose(1, 0, 2).reshape(768, 512)
    b = call(
        layer_kernel,
        0,
        dict(
            tok_in=(tok, A),
            g_in=(g_own, A),
            bias=(b_qkv, V),
            cs_in=(cs, A),
            sn_in=(sn, A),
            blocks=(block_ids, V),
            ids_own=(expert_ids[0].T, V),
            gain_one=(norm1_gain, V),
            gain_two=(norm2_gain, V),
            gate_vector=(shared_gate, V),
            router=(w_router.T, V),
            w_q=(w_q, A),
            w_o=(w_out, A),
            w_si=(w_shared_in, A),
            w_sd=(w_shared_out, A),
            w_ei=(w_expert_in[0], A),
            w_ed=(w_expert_out[0], A),
        ),
        dict(
            output=o(64, 2048, at=V),
            grad_tokens=o(64, 2048, at=V),
            keep_v=o(16, 512),
            keep_q=o(256, 512),
            keep_kv=o(512, 512),
            keep_o=o(512, 256),
            d_si=o(256, 2, 1408),
            d_sd=o(1408, 256),
            d_ei=o(512, 2, 1408),
            d_ed=o(1408, 512),
            split_si=o(2, 256, 1408),
            split_ei=o(2, 512, 1408),
            s_q=o(8, 768, 512),
            s_o=o(8, 512, 256),
            s_sg=o(8, 256, 1408),
            s_su=o(8, 256, 1408),
            s_sd=o(8, 1408, 256),
            s_eg=o(4, 512, 1408),
            s_eu=o(4, 512, 1408),
            s_ed=o(4, 1408, 512),
            ex_up=o(3, 512, 1408),
            ex_up_x=o(3, 512, 1408),
            ex_keep=o(1024, 1024),
            ex_x=o(1024, 1024),
            sh_up=o(3, 256, 1408),
            sh_up_x=o(3, 256, 1408),
            sh_keep=o(256, 1024),
            sh_x=o(256, 1024),
            k_eg=o(512, 1408),
            k_eu=o(512, 1408),
            k_ed=o(1408, 512),
            t_eg=o(512, 1408),
            t_eu=o(512, 1408),
            t_ed=o(1408, 512),
            y_ga=o(2, 128, 1408),
            y_gb=o(2, 128, 1408),
            y_su=o(2, 256, 1408),
            y_sd=o(2, 1408, 256),
            y_q=o(2, 256, 512),
            y_kv=o(2, 512, 512),
            y_o=o(2, 512, 256),
            y_v=o(2, 16, 512),
            x_ga=o(128, 1408),
            x_gb=o(128, 1408),
            x_su=o(256, 1408),
            x_sd=o(1408, 256),
            x_q=o(256, 512),
            x_kv=o(512, 512),
            x_o=o(512, 256),
            x_v=o(16, 512),
            x_eg=o(512, 1408),
            x_eu=o(512, 1408),
            x_ed=o(1408, 512),
            n_x=o(256, 1024),
            low_x=o(256, 512),
            h_x=o(256, 1024),
            lin_x=o(768, 512),
            e_out_z=o(3, 64, 2048),
            s_out_z=o(3, 64, 2048),
        ),
        dict(
            s_v=vm(8, 16, 256),
            tok=vm(256, 2048),
            g_own=vm(256, 2048),
            cs_all=vm(512, 128, kind=f32),
            sn_all=vm(512, 128, kind=f32),
            w_v=vm(16, 256),
            col=vm(512, 128, kind=f32),
            ids_q=vm(256, 128, kind=f32),
            ids_near=vm(8, 256, kind=f32),
            ids_far=vm(8, 256, kind=f32),
            cs=vm(256, 128, kind=f32),
            sn=vm(256, 128, kind=f32),
            ids=vm(4, 128, 128, kind=f32),
            ids_y=vm(64, 128, kind=f32),
            g_oth=vm(256, 2048),
            q=vm(256, 512),
            kv=vm(512, 512),
            kv_oth=vm(512, 512),
            low=vm(256, 512),
            n_keep=vm(256, 1024),
            n_send=vm(256, 1024),
            small=vm(16, 2048),
            inv1=vm(256, 1, kind=f32),
            k_sd=vm(2, 1408, 256),
            t_sd=vm(2, 1408, 256),
            att=vm(3, 64, 2048),
            att_send=vm(4, 64, 2048),
            hidden=vm(64, 2048, kind=f32),
            rows=vm(512, 2048),
            out_sum=vm(256, 2048, kind=f32),
            grad_sum=vm(256, 2048, kind=f32),
            extras=vm(256, 128, kind=f32),
            e_out=vm(4, 64, 2048),
            e_grad=vm(4, 64, 2176),
            e_grad_z=vm(3, 64, 2176),
            s_out=vm(4, 64, 2048),
            s_grad=vm(4, 64, 2176),
            s_grad_z=vm(3, 64, 2176),
            g_send=vm(64, 2176),
            g_y=vm(64, 2176),
            o_send=vm(64, 2048),
            o_y=vm(64, 2048),
            gh=vm(4, 64, 2048),
            gkv_y=vm(512, 512),
            gn_z=vm(3, 64, 2048),
            vec_x=vm(16, 2048, kind=f32),
            vec_z=vm(3, 16, 2048, kind=f32),
            vec_sum=vm(16, 2048, kind=f32),
            send_sems=dma(144),
            recv_sems=dma(144),
            load_sems=dma(224),
        ),
        63,
        4 * 10**10,
        2 * 10**8,
    )
    c = call(
        close_kernel,
        None,
        dict(
            output=(b.output, A),
            grad_tokens=(b.grad_tokens, A),
            keep_v=(b.keep_v, V),
            y_v=(b.y_v, V),
            x_v=(b.x_v, V),
            keep_q=(b.keep_q, A),
            y_q=(b.y_q, A),
            x_q=(b.x_q, A),
            keep_kv=(b.keep_kv, A),
            y_kv=(b.y_kv, A),
            x_kv=(b.x_kv, A),
            keep_o=(b.keep_o, A),
            y_o=(b.y_o, A),
            x_o=(b.x_o, A),
            d_si=(b.d_si, A),
            d_sd=(b.d_sd, A),
            d_ei=(b.d_ei, A),
            d_ed=(b.d_ed, A),
        ),
        dict(
            c_out=o(64, 2048),
            c_tok=o(64, 2048),
            c_one=o(256, at=V),
            c_two=o(256, at=V),
            c_gate=o(256, at=V),
            c_router=o(8, 256, at=V),
            c_bias=o(3, 4, 16, at=V),
            c_q=o(768, 512),
            c_o=o(512, 256),
            c_si=o(256, 2, 1408),
            c_sd=o(1408, 256),
            c_ei=o(512, 2, 1408),
            c_ed=o(1408, 512),
        ),
        dict(
            b_out=vm(64, 2048),
            b_tok=vm(64, 2048),
            b_q=vm(3, 256, 512),
            b_kv=vm(3, 512, 512),
            b_o=vm(3, 512, 256),
            b_si=vm(256, 2, 1408),
            b_sd=vm(1408, 256),
            b_ei=vm(512, 2, 1408),
            b_ed=vm(1408, 512),
            load_sems=dma(32),
        ),
        63,
        10**6,
        2 * 10**7,
    )
    return (
        c.c_out[None],
        c.c_tok[None],
        c.c_one,
        c.c_q.reshape(3, 256, 512).transpose(1, 0, 2),
        c.c_bias,
        c.c_o,
        c.c_two,
        c.c_router.T,
        c.c_gate,
        c.c_si,
        c.c_sd,
        c.c_ei[None],
        c.c_ed[None],
    )


def solution(mesh):
    placed = (
        P(DP, CTX, None),
        P(PLANE),
        P(PLANE, None, EXP),
        P(None, EXP, None),
        P(EXP, PLANE),
        P(PLANE),
        P(PLANE, None),
        P(PLANE),
        P(PLANE, None, EXP),
        P(EXP, PLANE),
        P(GROUP, DP, None, None),
        P(GROUP, None, DP),
        P(DP, None),
        P(DP, GROUP, None),
        P(DP, CTX, None),
    )
    fixed = tuple(mesh.shape[a] for a in (DP, CTX, EXP)) == (4, 2, 4)
    return jax.shard_map(
        fixed_body if fixed else general_body,
        mesh=mesh,
        in_specs=placed,
        out_specs=(
            P(DP, GROUP, None),
            P(DP, GROUP, None),
            P(PLANE),
            P(PLANE, None, EXP),
            P(None, EXP, PLANE),
            P(EXP, PLANE),
            P(PLANE),
            P(PLANE, None),
            P(PLANE),
            P(PLANE, None, EXP),
            P(EXP, PLANE),
            P(GROUP, DP, None, None),
            P(GROUP, None, DP),
        ),
        check_vma=False,
    )
```

```python
from types import SimpleNamespace

import jax
import jax.numpy as jnp
import numpy as np
from jax import lax
from jax.experimental import pallas as pl
from jax.experimental.pallas import tpu as pltpu
from jax.sharding import PartitionSpec as P

highest = lax.Precision.HIGHEST
epsilon = 1e-06
rope_base = 1000000.0
f32 = jnp.float32
bf16 = jnp.bfloat16
DP, CTX, EXP = "dp", "context", "expert"
PLANE, GROUP = (DP, CTX), (CTX, EXP)


def rotary_tables(first_row, row_count, head_size):
    exponent = jnp.arange(head_size // 2).astype(jnp.float32) * (2.0 / head_size)
    frequency = rope_base ** (-exponent)
    positions = (first_row + jnp.arange(row_count, dtype=jnp.int32)).astype(jnp.float32)
    angles = positions[:, None] * frequency[None, :]
    return (jnp.cos(angles)[:, None, :], jnp.sin(angles)[:, None, :])


def rotate(values, cosine, sine_table):
    half_size = values.shape[-1] // 2
    first_half = values[..., :half_size]
    second_half = values[..., half_size:]
    return jnp.concatenate(
        [
            first_half * cosine - second_half * sine_table,
            second_half * cosine + first_half * sine_table,
        ],
        axis=-1,
    )


def rotate_back(grad_values, cosine, sine_table):
    half_size = grad_values.shape[-1] // 2
    first_half = grad_values[..., :half_size]
    second_half = grad_values[..., half_size:]
    return jnp.concatenate(
        [
            first_half * cosine + second_half * sine_table,
            second_half * cosine - first_half * sine_table,
        ],
        axis=-1,
    )


def gated_grads(gate_part, up_part, grad_act):
    sigmoid_gate = jax.nn.sigmoid(gate_part)
    grad_gate = grad_act * up_part * sigmoid_gate * (1.0 + gate_part * (1.0 - sigmoid_gate))
    grad_up = grad_act * gate_part * sigmoid_gate
    return (grad_gate, grad_up)


def masked_scores(queries, all_keys, allowed, score_scale):
    scores = (
        jnp.einsum("qhd,khd->hqk", queries, all_keys, preferred_element_type=jnp.float32)
        * score_scale
    )
    return jnp.where(allowed[None], scores, -1e30)


def fetch_dense(
    norm1_gain, w_qkv, w_out, norm2_gain, w_router, shared_gate, w_shared_in, w_shared_out
):
    return (
        lax.all_gather(norm1_gain, PLANE, axis=0, tiled=True),
        lax.all_gather(w_qkv, PLANE, axis=0, tiled=True),
        lax.all_gather(w_out, PLANE, axis=1, tiled=True),
        lax.all_gather(norm2_gain, PLANE, axis=0, tiled=True),
        lax.all_gather(w_router, PLANE, axis=0, tiled=True),
        lax.all_gather(shared_gate, PLANE, axis=0, tiled=True),
        lax.all_gather(w_shared_in, PLANE, axis=0, tiled=True),
        lax.all_gather(w_shared_out, PLANE, axis=1, tiled=True),
    )


def fetch_experts(w_expert_in, w_expert_out):
    return (
        lax.all_gather(w_expert_in, DP, axis=1, tiled=True),
        lax.all_gather(w_expert_out, DP, axis=2, tiled=True),
    )


def fetch_keys(key_rows, value_rows):
    return (
        lax.all_gather(key_rows, CTX, axis=0, tiled=True),
        lax.all_gather(value_rows, CTX, axis=0, tiled=True),
    )


def general_body(
    tokens,
    norm1_gain,
    w_qkv,
    b_qkv,
    w_out,
    norm2_gain,
    w_router,
    shared_gate,
    w_shared_in,
    w_shared_out,
    w_expert_in,
    w_expert_out,
    block_ids,
    expert_ids,
    out_grad,
):
    token_rows = tokens[0]
    rows_local, model_width = token_rows.shape
    lane_count = lax.axis_size(EXP)
    quarter = rows_local // lane_count
    first_row = lax.axis_index(CTX) * rows_local
    own_row = lax.axis_index(EXP) * quarter
    sequence_ids = block_ids[0]
    chosen = expert_ids[0]
    top_count = chosen.shape[1]
    heads_local = b_qkv.shape[1]
    head_size = b_qkv.shape[2]
    dense_full = fetch_dense(
        norm1_gain, w_qkv, w_out, norm2_gain, w_router, shared_gate, w_shared_in, w_shared_out
    )
    (
        gain_one,
        qkv_weight,
        out_weight,
        gain_two,
        router_weight,
        gate_vector,
        shared_in,
        shared_out,
    ) = dense_full
    expert_pair = fetch_experts(w_expert_in, w_expert_out)
    expert_in = expert_pair[0][0]
    expert_back = expert_pair[1][0]
    ffe_width = expert_in.shape[2]
    experts = router_weight.shape[1]
    capacity = max(2, 3 * quarter * top_count // (2 * experts))
    tokens_wide = token_rows.astype(jnp.float32)
    inverse_one = lax.rsqrt(jnp.mean(tokens_wide * tokens_wide, axis=-1, keepdims=True) + epsilon)
    normed = (tokens_wide * inverse_one * gain_one.astype(jnp.float32)).astype(jnp.bfloat16)
    linear = jnp.dot(
        normed, qkv_weight.reshape(model_width, -1), preferred_element_type=jnp.float32
    )
    linear = linear.reshape(rows_local, 3, heads_local, head_size) + b_qkv.astype(jnp.float32)[None]
    cosine, sine_table = rotary_tables(first_row, rows_local, head_size)
    queries = rotate(linear[:, 0], cosine, sine_table).astype(jnp.bfloat16)
    key_rows = rotate(linear[:, 1], cosine, sine_table).astype(jnp.bfloat16)
    value_rows = linear[:, 2].astype(jnp.bfloat16)
    all_keys, all_values = fetch_keys(key_rows, value_rows)
    query_ids = lax.dynamic_slice_in_dim(sequence_ids, first_row, rows_local)
    allowed = sequence_ids[None, :] <= query_ids[:, None]
    score_scale = head_size ** (-0.5)
    scores = masked_scores(queries, all_keys, allowed, score_scale)
    row_peak = jnp.max(scores, axis=-1, keepdims=True)
    log_total = row_peak + jnp.log(jnp.sum(jnp.exp(scores - row_peak), axis=-1, keepdims=True))
    weights = jnp.exp(scores - log_total).astype(jnp.bfloat16)
    attended = jnp.einsum("hqk,khd->qhd", weights, all_values, preferred_element_type=jnp.float32)
    attended_low = attended.astype(jnp.bfloat16).reshape(rows_local, heads_local * head_size)
    attention = lax.psum(
        jnp.dot(attended_low, out_weight, preferred_element_type=jnp.float32).astype(jnp.bfloat16),
        EXP,
    ).astype(jnp.float32)
    hidden = tokens_wide + attention
    inverse_two = lax.rsqrt(jnp.mean(hidden * hidden, axis=-1, keepdims=True) + epsilon)
    routed = (hidden * inverse_two * gain_two.astype(jnp.float32)).astype(jnp.bfloat16)
    shared_up = jnp.dot(
        routed, shared_in.reshape(model_width, -1), preferred_element_type=jnp.float32
    )
    shared_up = shared_up.reshape(rows_local, 2, -1)
    shared_act = (jax.nn.silu(shared_up[:, 0]) * shared_up[:, 1]).astype(jnp.bfloat16)
    shared_part = jnp.dot(shared_act, shared_out, preferred_element_type=jnp.float32)
    shared_rows = lax.psum_scatter(
        shared_part.astype(jnp.bfloat16), EXP, scatter_dimension=0, tiled=True
    ).astype(jnp.float32)
    shared_weight = jax.nn.sigmoid(jnp.dot(routed, gate_vector, preferred_element_type=jnp.float32))
    routed_own = lax.dynamic_slice_in_dim(routed, own_row, quarter)
    hidden_own = lax.dynamic_slice_in_dim(hidden, own_row, quarter)
    weight_own = lax.dynamic_slice_in_dim(shared_weight, own_row, quarter)
    logits = jnp.dot(routed_own, router_weight, preferred_element_type=jnp.float32)
    probability = jax.nn.softmax(logits, axis=-1)
    expert_match = (chosen[..., None] == jnp.arange(experts, dtype=jnp.int32)).astype(jnp.float32)
    gate_values = jnp.sum(probability[:, None, :] * expert_match, axis=-1)
    flat_ids = chosen.reshape(-1)
    onehot = (flat_ids[:, None] == jnp.arange(experts, dtype=jnp.int32)).astype(jnp.int32)
    slot_rank = jnp.sum((jnp.cumsum(onehot, axis=0) - onehot) * onehot, axis=-1)
    slot_index = flat_ids * capacity + slot_rank
    placement = (slot_index[:, None] == jnp.arange(experts * capacity, dtype=jnp.int32)).astype(
        jnp.bfloat16
    )
    repeated = jnp.repeat(routed_own, top_count, axis=0)
    outgoing = jnp.einsum("sr,sd->rd", placement, repeated, preferred_element_type=jnp.float32)
    outgoing = outgoing.astype(jnp.bfloat16).reshape(experts, capacity, model_width)
    incoming = lax.all_to_all(
        outgoing, GROUP, split_axis=0, concat_axis=0, tiled=True
    )
    flat_rows = incoming.reshape(-1, model_width)
    gate_up = jnp.dot(
        flat_rows, expert_in.reshape(model_width, -1), preferred_element_type=jnp.float32
    ).reshape(-1, 2, ffe_width)
    activated = (jax.nn.silu(gate_up[:, 0]) * gate_up[:, 1]).astype(jnp.bfloat16)
    result = jnp.dot(activated, expert_back, preferred_element_type=jnp.float32).astype(
        jnp.bfloat16
    )
    expert_result = result.reshape(incoming.shape)
    returned = lax.all_to_all(
        expert_result, GROUP, split_axis=0, concat_axis=0, tiled=True
    )
    picked = jnp.dot(
        placement, returned.reshape(-1, model_width), preferred_element_type=jnp.float32
    )
    picked = picked.reshape(quarter, top_count, model_width)
    combined = jnp.sum(gate_values[..., None] * picked, axis=1)
    result_rows = hidden_own + combined + weight_own[:, None] * shared_rows
    output = result_rows.astype(jnp.bfloat16)[None]
    (
        gain_one_b,
        qkv_weight_b,
        out_weight_b,
        gain_two_b,
        router_weight_b,
        gate_vector_b,
        shared_in_b,
        shared_out_b,
    ) = dense_full
    expert_in_b = expert_pair[0][0]
    expert_back_b = expert_pair[1][0]
    grad_full = out_grad[0].astype(jnp.float32)
    grad_own = lax.dynamic_slice_in_dim(grad_full, own_row, quarter)
    shared_grad = (shared_weight[:, None] * grad_full).astype(jnp.bfloat16)
    grad_shared_out = jnp.einsum(
        "tf,td->fd", shared_act, shared_grad, preferred_element_type=jnp.float32
    )
    grad_shared_act = jnp.einsum(
        "td,fd->tf", shared_grad, shared_out_b, preferred_element_type=jnp.float32
    )
    shared_gate_grad, shared_up_grad = gated_grads(
        shared_up[:, 0], shared_up[:, 1], grad_shared_act
    )
    grad_shared_up = jnp.stack([shared_gate_grad, shared_up_grad], axis=1).astype(jnp.bfloat16)
    grad_shared_in = jnp.einsum(
        "td,tkf->dkf", routed, grad_shared_up, preferred_element_type=jnp.float32
    )
    grad_routed = jnp.einsum(
        "tkf,dkf->td", grad_shared_up, shared_in_b, preferred_element_type=jnp.float32
    )
    gate_slope = jnp.sum(grad_own * shared_rows, axis=-1) * weight_own * (1.0 - weight_own)
    grad_gate_vector = jnp.dot(gate_slope, routed_own.astype(jnp.float32), precision=highest)
    grad_own_routed = gate_slope[:, None] * gate_vector_b.astype(jnp.float32)[None]
    grad_gates = jnp.sum(grad_own[:, None, :] * picked, axis=-1)
    grad_slots = (
        (gate_values[..., None] * grad_own[:, None, :])
        .astype(jnp.bfloat16)
        .reshape(-1, model_width)
    )
    grad_send = jnp.einsum("sr,sd->rd", placement, grad_slots, preferred_element_type=jnp.float32)
    grad_send = grad_send.astype(jnp.bfloat16).reshape(experts, capacity, model_width)
    grad_arrived = lax.all_to_all(
        grad_send, GROUP, split_axis=0, concat_axis=0, tiled=True
    )
    arrived_rows = incoming.reshape(-1, model_width)
    arrived_grad = grad_arrived.reshape(-1, model_width)
    expert_up = jnp.dot(
        arrived_rows, expert_in_b.reshape(model_width, -1), preferred_element_type=jnp.float32
    ).reshape(-1, 2, ffe_width)
    expert_act = (jax.nn.silu(expert_up[:, 0]) * expert_up[:, 1]).astype(jnp.bfloat16)
    grad_expert_back = jnp.einsum(
        "rf,rd->fd", expert_act, arrived_grad, preferred_element_type=jnp.float32
    )
    grad_expert_act = jnp.einsum(
        "rd,fd->rf", arrived_grad, expert_back_b, preferred_element_type=jnp.float32
    )
    expert_gate_grad, expert_up_grad = gated_grads(
        expert_up[:, 0], expert_up[:, 1], grad_expert_act
    )
    grad_expert_up = jnp.stack([expert_gate_grad, expert_up_grad], axis=1).astype(jnp.bfloat16)
    grad_expert_in = jnp.einsum(
        "rd,rkf->dkf", arrived_rows, grad_expert_up, preferred_element_type=jnp.float32
    )
    grad_arrived_rows = jnp.einsum(
        "rkf,dkf->rd", grad_expert_up, expert_in_b, preferred_element_type=jnp.float32
    )
    grad_arrived_rows = grad_arrived_rows.astype(jnp.bfloat16).reshape(
        experts, capacity, model_width
    )
    grad_returned = lax.all_to_all(
        grad_arrived_rows, GROUP, split_axis=0, concat_axis=0, tiled=True
    )
    grad_copies = jnp.dot(
        placement, grad_returned.reshape(-1, model_width), preferred_element_type=jnp.float32
    )
    grad_own_routed = grad_own_routed + jnp.sum(
        grad_copies.reshape(quarter, top_count, model_width), axis=1
    )
    grad_probability = jnp.sum(grad_gates[..., None] * expert_match, axis=1)
    grad_logits = probability * (
        grad_probability - jnp.sum(probability * grad_probability, axis=-1, keepdims=True)
    )
    grad_router = jnp.dot(routed_own.astype(jnp.float32).T, grad_logits, precision=highest)
    grad_own_routed = grad_own_routed + jnp.dot(
        grad_logits, router_weight_b.astype(jnp.float32).T, precision=highest
    )
    own_part = lax.dynamic_slice_in_dim(grad_routed, own_row, quarter) + grad_own_routed
    grad_routed = lax.dynamic_update_slice_in_dim(grad_routed, own_part, own_row, 0)
    grad_routed, grad_router, grad_gate_vector = (
        lax.psum(grad_routed.astype(jnp.bfloat16), EXP).astype(jnp.float32),
        lax.psum(grad_router.astype(jnp.bfloat16), EXP).astype(jnp.float32),
        lax.psum(grad_gate_vector.astype(jnp.bfloat16), EXP).astype(jnp.float32),
    )
    scaled_two = grad_routed * gain_two_b.astype(jnp.float32)
    grad_gain_two = jnp.sum(grad_routed * hidden * inverse_two, axis=0)
    grad_hidden = (
        grad_full
        + inverse_two * scaled_two
        - hidden * inverse_two**3 * jnp.mean(scaled_two * hidden, axis=-1, keepdims=True)
    )
    grad_hidden_low = grad_hidden.astype(jnp.bfloat16)
    grad_out_weight = jnp.einsum(
        "tn,td->nd", attended_low, grad_hidden_low, preferred_element_type=jnp.float32
    )
    grad_attended = jnp.einsum(
        "td,nd->tn", grad_hidden_low, out_weight_b, preferred_element_type=jnp.float32
    )
    grad_attended = grad_attended.astype(jnp.bfloat16).reshape(rows_local, heads_local, head_size)
    back_keys, back_values = (all_keys, all_values)
    scores_again = masked_scores(queries, back_keys, allowed, score_scale)
    weights_wide = jnp.exp(scores_again - log_total)
    row_delta = jnp.sum(grad_attended.astype(jnp.float32) * attended, axis=-1).T
    grad_weights = jnp.einsum(
        "qhd,khd->hqk", grad_attended, back_values, preferred_element_type=jnp.float32
    )
    grad_scores = (weights_wide * (grad_weights - row_delta[..., None])).astype(jnp.bfloat16)
    grad_queries = (
        jnp.einsum("hqk,khd->qhd", grad_scores, back_keys, preferred_element_type=jnp.float32)
        * score_scale
    )
    grad_keys = (
        jnp.einsum("hqk,qhd->khd", grad_scores, queries, preferred_element_type=jnp.float32)
        * score_scale
    )
    grad_values = jnp.einsum(
        "hqk,qhd->khd",
        weights_wide.astype(jnp.bfloat16),
        grad_attended,
        preferred_element_type=jnp.float32,
    )
    grad_keys, grad_values = (
        lax.psum_scatter(
            grad_keys.astype(jnp.bfloat16), CTX, scatter_dimension=0, tiled=True
        ).astype(jnp.float32),
        lax.psum_scatter(
            grad_values.astype(jnp.bfloat16), CTX, scatter_dimension=0, tiled=True
        ).astype(jnp.float32),
    )
    grad_linear = jnp.stack(
        [
            rotate_back(grad_queries, cosine, sine_table),
            rotate_back(grad_keys, cosine, sine_table),
            grad_values,
        ],
        axis=1,
    )
    grad_linear = grad_linear.astype(jnp.bfloat16)
    grad_bias = jnp.sum(grad_linear.astype(jnp.float32), axis=0)
    grad_flat = grad_linear.reshape(rows_local, -1)
    grad_qkv = jnp.einsum(
        "td,tn->dn", normed, grad_flat, preferred_element_type=jnp.float32
    ).reshape(qkv_weight_b.shape)
    grad_normed = jnp.einsum(
        "tn,dn->td",
        grad_flat,
        qkv_weight_b.reshape(model_width, -1),
        preferred_element_type=jnp.float32,
    )
    grad_normed = lax.psum(grad_normed.astype(jnp.bfloat16), EXP).astype(jnp.float32)
    scaled_one = grad_normed * gain_one_b.astype(jnp.float32)
    grad_gain_one = jnp.sum(grad_normed * tokens_wide * inverse_one, axis=0)
    grad_tokens = (
        grad_hidden
        + inverse_one * scaled_one
        - tokens_wide * inverse_one**3 * jnp.mean(scaled_one * tokens_wide, axis=-1, keepdims=True)
    )
    grad_tokens_own = lax.dynamic_slice_in_dim(grad_tokens, own_row, quarter).astype(jnp.bfloat16)[
        None
    ]
    dense_sums = (
        lax.psum_scatter(
            grad_gain_one.astype(jnp.bfloat16), PLANE, scatter_dimension=0, tiled=True
        ).astype(jnp.float32),
        lax.psum_scatter(
            grad_qkv.astype(jnp.bfloat16), PLANE, scatter_dimension=0, tiled=True
        ).astype(jnp.float32),
        lax.psum_scatter(
            grad_bias.astype(jnp.bfloat16), PLANE, scatter_dimension=2, tiled=True
        ).astype(jnp.float32),
        lax.psum_scatter(
            grad_out_weight.astype(jnp.bfloat16), PLANE, scatter_dimension=1, tiled=True
        ).astype(jnp.float32),
        lax.psum_scatter(
            grad_gain_two.astype(jnp.bfloat16), PLANE, scatter_dimension=0, tiled=True
        ).astype(jnp.float32),
        lax.psum_scatter(
            grad_router.astype(jnp.bfloat16), PLANE, scatter_dimension=0, tiled=True
        ).astype(jnp.float32),
        lax.psum_scatter(
            grad_gate_vector.astype(jnp.bfloat16),
            PLANE,
            scatter_dimension=0,
            tiled=True,
        ).astype(jnp.float32),
        lax.psum_scatter(
            grad_shared_in.astype(jnp.bfloat16), PLANE, scatter_dimension=0, tiled=True
        ).astype(jnp.float32),
        lax.psum_scatter(
            grad_shared_out.astype(jnp.bfloat16), PLANE, scatter_dimension=1, tiled=True
        ).astype(jnp.float32),
    )
    expert_sums = (
        lax.psum_scatter(
            grad_expert_in[None].astype(jnp.bfloat16), DP, scatter_dimension=1, tiled=True
        ).astype(jnp.float32),
        lax.psum_scatter(
            grad_expert_back[None].astype(jnp.bfloat16), DP, scatter_dimension=2, tiled=True
        ).astype(jnp.float32),
    )
    return (
        output,
        grad_tokens_own,
        dense_sums[0].astype(jnp.bfloat16),
        dense_sums[1].astype(jnp.bfloat16),
        dense_sums[2].astype(jnp.bfloat16),
        dense_sums[3].astype(jnp.bfloat16),
        dense_sums[4].astype(jnp.bfloat16),
        dense_sums[5].astype(jnp.bfloat16),
        dense_sums[6].astype(jnp.bfloat16),
        dense_sums[7].astype(jnp.bfloat16),
        dense_sums[8].astype(jnp.bfloat16),
        expert_sums[0].astype(jnp.bfloat16),
        expert_sums[1].astype(jnp.bfloat16),
    )


MIB = 1 << 20
CUT = 192
MESH = pl.DeviceIdType.MESH


def dot_nn(a, b):
    return lax.dot_general(a, b, (((1,), (0,)), ((), ())), preferred_element_type=f32)


def dot_nt(a, b):
    return lax.dot_general(a, b, (((1,), (1,)), ((), ())), preferred_element_type=f32)


def dot_tn(a, b):
    return lax.dot_general(a, b, (((0,), (0,)), ((), ())), preferred_element_type=f32)


def place():
    i = lax.axis_index(DP)
    return i // 2, i % 2, lax.axis_index(CTX), lax.axis_index(EXP)


def owner_dense(r):
    x, c, y, _ = place()
    return (((x + r % 2) % 2) * 2 + (c + r // 4) % 2) * 2 + (y + (r // 2) % 2) % 2


def owner_expert(r):
    x, c, _, _ = place()
    return ((x + r % 2) % 2) * 2 + (c + r // 2) % 2


def near(d):
    z = lax.axis_index(EXP)
    return ((z // 2 + d // 2) % 2) * 2 + (z % 2 + d % 2) % 2


def peers():
    x, c, y, _ = place()
    far = [{EXP: near(d)} for d in (1, 2, 3)]
    return {DP: ((x + 1) % 2) * 2 + c}, {CTX: 1 - y}, {DP: x * 2 + (c + 1) % 2}, far


def greet(devices):
    barrier = pltpu.get_barrier_semaphore()
    for device in devices:
        pl.semaphore_signal(barrier, 1, device_id=device, device_id_type=MESH)
    pl.semaphore_wait(barrier, len(devices))


class Wire:
    def __init__(self, wires, ends, device):
        self.ends, self.device, self.sent = ends, device, False
        self.send, self.recv, self.k = wires.send, wires.recv, len(wires.copies)
        wires.copies.append(self)

    def copy(self):
        source, target = self.ends()
        return pltpu.make_async_remote_copy(
            src_ref=source,
            dst_ref=target,
            send_sem=self.send.at[self.k],
            recv_sem=self.recv.at[self.k],
            device_id=self.device,
            device_id_type=MESH,
        )

    def start(self):
        self.copy().start()
        return self

    def wait_recv(self):
        self.copy().wait_recv()

    def wait_send(self):
        self.copy().wait_send()
        self.sent = True


class Wires:
    def __init__(self, send, recv):
        self.send, self.recv, self.copies = send, recv, []

    def add(self, ends, device):
        return Wire(self, ends, device)

    def go(self, ends, device):
        return Wire(self, ends, device).start()

    def drain(self):
        for wire in self.copies:
            if not wire.sent:
                wire.wait_send()


class Loads:
    def __init__(self, sems):
        self.sems, self.count = sems, 0

    def go(self, source, target):
        copy = pltpu.make_async_copy(source, target, self.sems.at[self.count])
        self.count += 1
        copy.start()
        return copy


def cols(ref, block, width):
    return ref[:, pl.ds(pl.multiple_of(block * width, width), width)]


def piece(ref, d, rows):
    return ref[pl.ds(pl.multiple_of(near(d) * rows, rows), rows), :]


def turn(values, cosine, sine):
    return values * cosine + pltpu.roll(values, 64, 1) * sine


def turn_back(values, cosine, sine):
    return values * cosine - pltpu.roll(values, 64, 1) * sine


def gated(gate, up, grad_act):
    s = jax.nn.sigmoid(gate)
    act = gate * s
    return act * up, grad_act * up * s * (1.0 + gate * (1.0 - s)), grad_act * act


def softmax_parts(q, k_own, k_oth, mask_own, mask_oth):
    scale = 128 ** (-0.5)
    s_own = jnp.where(mask_own, dot_nt(q, k_own) * scale, -1e30)
    s_oth = jnp.where(mask_oth, dot_nt(q, k_oth) * scale, -1e30)
    peak = jnp.maximum(
        jnp.max(s_own, axis=-1, keepdims=True), jnp.max(s_oth, axis=-1, keepdims=True)
    )
    e_own = jnp.exp(s_own - peak)
    e_oth = jnp.exp(s_oth - peak)
    total = jnp.sum(e_own, axis=-1, keepdims=True) + jnp.sum(e_oth, axis=-1, keepdims=True)
    back = 1.0 / total
    return e_own * back, e_oth * back


def split3(v):
    high = v.astype(bf16).astype(f32)
    mid = (v - high).astype(bf16).astype(f32)
    return high, mid, v - high - mid


def probabilities(rows, small):
    logits = dot_nt(rows, small[...])
    lane = lax.broadcasted_iota(jnp.int32, logits.shape, 1)
    logits = jnp.where((lane >= 3) & (lane < 11), logits, -1e30)
    e = jnp.exp(logits - jnp.max(logits, axis=-1, keepdims=True))
    return e / jnp.sum(e, axis=-1, keepdims=True), lane


ARRIVAL = (0, 4, 1, 5, 2, 6, 3, 7)


class Spread:
    def __init__(self, wires, own, slots, dense):
        x, y, core, _ = peers()
        self.slots, self.own, self.copies = slots, own, {}

        def ends(r, target):
            return lambda: (self.block(r), slots.at[target])

        self.copies[1] = wires.add(ends(0, 1), x)
        if dense:
            self.copies[2] = wires.add(ends(0, 2), y)
            self.copies[3] = wires.add(ends(1, 3), y)
        side = 4 if dense else 2
        for r in range(side):
            self.copies[side + r] = wires.add(ends(r, side + r), core)

    def block(self, r):
        return self.own() if r == 0 else self.slots.at[r]

    def start(self, r):
        self.copies[r].start()

    def wait(self, r):
        self.copies[r].wait_recv()


V, A = "vmem", "any"


def call(kernel, number, ins, outs, scratch, vmem, flops, traffic):
    def spec(kind):
        return pl.BlockSpec(memory_space=pl.ANY if kind == A else pltpu.VMEM)

    names = list(ins) + list(outs) + list(scratch)

    def run(*refs):
        kernel(SimpleNamespace(**dict(zip(names, refs))))

    made = pl.pallas_call(
        run,
        out_shape=tuple(jax.ShapeDtypeStruct(o[0], o[1]) for o in outs.values()),
        in_specs=[spec(i[1]) for i in ins.values()],
        out_specs=tuple(spec(o[2]) for o in outs.values()),
        scratch_shapes=list(scratch.values()),
        compiler_params=pltpu.CompilerParams(
            vmem_limit_bytes=vmem * MIB, collective_id=number, has_side_effects=number is not None
        ),
        cost_estimate=pl.CostEstimate(flops=flops, bytes_accessed=traffic, transcendentals=0),
    )(*[i[0] for i in ins.values()])
    return SimpleNamespace(**dict(zip(outs, made)))


def own_rows(total, hidden, routed, g, small, high_o, low_o, vec_o):
    extra = total[:, 2048:2176]
    wide = routed.astype(f32)
    prob, _ = probabilities(routed, small)
    sw = jax.nn.sigmoid(jnp.sum(wide * small[2:3, :].astype(f32), axis=-1, keepdims=True))
    slope = jnp.sum(extra[:, 48:96], axis=-1, keepdims=True) * sw * (1.0 - sw)
    dgate = [
        extra[:, e : e + 1] + extra[:, 16 + e : 17 + e] + extra[:, 32 + e : 33 + e]
        for e in range(8)
    ]
    probs = [prob[:, 3 + e : 4 + e] for e in range(8)]
    mean = sum(p * d for p, d in zip(probs, dgate))
    grad = total[:, 0:2048] + slope * small[2:3, :].astype(f32)
    vec_o[...] = jnp.zeros_like(vec_o)
    vec_o[2:3, :] = jnp.sum(slope * wide, axis=0, keepdims=True)
    for e in range(8):
        dlogit = probs[e] * (dgate[e] - mean)
        grad += dlogit * small[3 + e : 4 + e, :].astype(f32)
        vec_o[3 + e : 4 + e, :] = jnp.sum(dlogit * wide, axis=0, keepdims=True)
    inv = lax.rsqrt(jnp.mean(hidden * hidden, axis=-1, keepdims=True) + epsilon)
    vec_o[1:2, :] = jnp.sum(grad * hidden * inv, axis=0, keepdims=True)
    scaled = grad * small[1:2, :].astype(f32)
    mean = jnp.mean(scaled * hidden, axis=-1, keepdims=True)
    high = g.astype(f32) + inv * scaled - hidden * (inv * inv * inv * mean)
    high_o[...] = high
    low_o[...] = high.astype(bf16)


def layer_kernel(k):
    x_dev, y_dev, core_dev, z_dev = peers()
    wires, loads = Wires(k.send_sems, k.recv_sems), Loads(k.load_sems)
    inputs = [
        loads.go(a, b)
        for a, b in (
            (k.tok_in, k.tok),
            (k.cs_in, k.cs_all),
            (k.sn_in, k.sn_all),
            (k.g_in, k.g_own),
        )
    ]
    greet([x_dev, y_dev, core_dev] + z_dev)
    y = lax.axis_index(CTX)
    mine = y * 4 + lax.axis_index(EXP)

    def to_z(make):
        return [wires.go(make(d), z_dev[d - 1]) for d in (1, 2, 3)]

    class Collect:
        def __init__(self, slot):
            self.slot = slot
            self.one = wires.go(lambda: (slot(0), slot(1)), z_dev[0])
            self.three = wires.go(lambda: (slot(0), slot(3)), z_dev[2])

        def hand_on(self):
            self.three.wait_recv()
            self.two = wires.go(lambda: (self.slot(3), self.slot(2)), z_dev[0])

        def wait(self):
            self.one.wait_recv()
            self.two.wait_recv()

    vec = Spread(wires, lambda: k.w_v, k.s_v, True)
    qkv = Spread(wires, lambda: k.w_q, k.s_q, True)
    out = Spread(wires, lambda: k.w_o, k.s_o, True)
    eg = Spread(wires, lambda: k.split_ei.at[0], k.s_eg, False)
    eu = Spread(wires, lambda: k.split_ei.at[1], k.s_eu, False)
    ed = Spread(wires, lambda: k.w_ed, k.s_ed, False)
    sg = Spread(wires, lambda: k.split_si.at[0], k.s_sg, True)
    su = Spread(wires, lambda: k.split_si.at[1], k.s_su, True)
    sd = Spread(wires, lambda: k.w_sd, k.s_sd, True)
    first, expert, shared = (vec, qkv), (eg, eu, ed), (sg, su, sd)
    qkv.start(1)
    qkv.start(2)
    k.w_v[...] = jnp.zeros_like(k.w_v)
    for m, vector in enumerate((k.gain_one, k.gain_two, k.gate_vector)):
        k.w_v[m : m + 1, :] = vector[...].reshape(1, 256)
    k.w_v[3:11, :] = k.router[...]
    for s in (vec, out, ed):
        s.start(1)
    vec.start(2)
    for s in (qkv, out, vec):
        s.start(4)
    k.col[0:128, :] = jnp.full((128, 128), -1.0, f32)
    k.col[0:4, 0:64] = k.ids_own[...].astype(f32)
    k.ids[0, 0:64, :] = k.col[0:128, :].T[0:64, :]
    ids_y = wires.go(lambda: (k.ids.at[0, pl.ds(0, 64), :], k.ids_y), y_dev)
    k.s_v[0] = k.w_v[...]
    for copy in inputs:
        copy.wait()
    k.col[...] = jnp.broadcast_to(k.blocks[...].astype(f32), (128, 512)).T
    for target, half in ((k.ids_near, y), (k.ids_far, 1 - y)):
        for d in range(4):
            at = pl.ds(pl.multiple_of(half * 256 + near(d) * 64, 64), 64)
            k.ids_q[d * 64 : (d + 1) * 64, :] = k.col[at, :]
        target[...] = k.ids_q[...].T[0:8, :]
    for d in range(4):
        at = pl.ds(pl.multiple_of(y * 256 + near(d) * 64, 64), 64)
        to = slice(d * 64, (d + 1) * 64)
        k.ids_q[to, :] = k.col[at, :]
        k.cs[to, :] = k.cs_all[at, :]
        k.sn[to, :] = k.sn_all[at, :]
    later = []

    def attention_part(scaled, acc, w, low_w, mixed, apart):
        held, held_out = {}, []

        def bring(r):
            held[r] = loads.go(qkv.block(r), w.at[r])

        def bring_out(r):
            held_out.append(loads.go(out.block(r), low_w.at[r]))

        raw = [loads.go(k.w_ei.at[pl.ds(256 * m, 256)], mixed.at[m]) for m in range(2)]
        raw.append(loads.go(k.w_si, mixed.at[2]))
        bring(0)
        for d in range(4):
            t = piece(k.tok, d, 64).astype(f32)
            inv = lax.rsqrt(jnp.mean(t * t, axis=-1, keepdims=True) + epsilon)
            scaled[d * 64 : (d + 1) * 64, :] = t * inv
            k.inv1[d * 64 : (d + 1) * 64, :] = inv
        for m in range(3):
            for h in range(4):
                at = slice(h * 128, (h + 1) * 128)
                line = k.bias[m, h : h + 1, :].astype(f32)
                acc[m, :, at] = jnp.broadcast_to(line, (256, 128))

        def take_apart(m):
            raw[m].wait()
            target = k.split_si if m == 2 else k.split_ei
            to = pl.ds(0 if m == 2 else 256 * m, 256)
            done = []
            for n in range(2):
                apart[m, n] = mixed[m, :, n, :]
                done.append(loads.go(apart.at[m, n], target.at[n, to, :]))
            return done

        done = take_apart(0) + take_apart(1)
        for copy in done:
            copy.wait()
        for s in (eg, eu):
            s.start(1)
        for s in expert:
            s.start(2)

        def block(r):
            held[r].wait()
            o = owner_dense(r)
            vectors = k.s_v[r]
            k.small[:, pl.ds(pl.multiple_of(o * 256, 256), 256)] = vectors
            normed = (cols(scaled, o, 256) * vectors[0:1, :].astype(f32)).astype(bf16)
            target = k.n_keep if r < 4 else k.n_send
            target[:, (r % 4) * 256 : (r % 4 + 1) * 256] = normed
            for m in range(3):
                acc[m] += dot_nn(normed, w[r, m * 256 : (m + 1) * 256, :])

        def arrived(r, onward=()):
            for s in first:
                s.wait(r)
                for t in onward:
                    s.start(t)
            bring(r)

        arrived(4)
        block(0)
        block(4)
        arrived(1, (3, 5))
        out.start(2)
        arrived(2, (6,))
        block(1)
        arrived(5)
        block(5)
        arrived(6)
        block(2)
        block(6)
        for copy in take_apart(2):
            copy.wait()
        for s in shared:
            s.start(1)
        for s in shared:
            s.start(4)
        ids_y.wait_recv()
        k.ids[0, 64:128, :] = k.ids_y[...]
        later.extend(to_z(lambda d: lambda: (k.ids.at[0], k.ids.at[d])))
        bring_out(0)
        out.wait(4)
        bring_out(4)
        out.wait(1)
        out.start(5)
        bring_out(1)
        arrived(3, (7,))
        block(3)
        arrived(7)
        block(7)
        for h in range(4):
            at = slice(h * 128, (h + 1) * 128)
            k.kv[0:256, at] = turn(acc[1, :, at], k.cs[...], k.sn[...]).astype(bf16)
        k.kv[256:512, :] = acc[2].astype(bf16)
        kv_y = wires.go(lambda: (k.kv, k.kv_oth), y_dev)
        out.start(3)
        sg.start(2)
        su.start(2)
        for h in range(4):
            at = slice(h * 128, (h + 1) * 128)
            k.q[:, at] = turn(acc[0, :, at], k.cs[...], k.sn[...]).astype(bf16)
        out.wait(5)
        bring_out(5)
        out.wait(2)
        out.start(6)
        bring_out(2)
        kv_y.wait_recv()
        mask_own = k.ids_near[0:1, :] <= k.ids_q[:, 0:1]
        mask_oth = k.ids_far[0:1, :] <= k.ids_q[:, 0:1]
        for h in range(4):
            at = slice(h * 128, (h + 1) * 128)
            w_own, w_oth = softmax_parts(
                k.q[:, at], k.kv[0:256, at], k.kv_oth[0:256, at], mask_own, mask_oth
            )
            value = dot_nn(w_own.astype(bf16), k.kv[256:512, at])
            value += dot_nn(w_oth.astype(bf16), k.kv_oth[256:512, at])
            k.low[:, at] = value.astype(bf16)
        out.wait(6)
        bring_out(6)
        out.wait(3)
        out.start(7)
        bring_out(3)
        out.wait(7)
        bring_out(7)
        for copy in held_out:
            copy.wait()
        for r in range(8):
            part = dot_nn(k.low[...], low_w[r]).astype(bf16)
            at = pl.ds(pl.multiple_of(owner_dense(r) * 256, 256), 256)
            for d in range(4):
                k.att_send[d, :, at] = part[d * 64 : (d + 1) * 64, :]

    pl.run_scoped(
        attention_part,
        pltpu.VMEM((256, 2048), f32),
        pltpu.VMEM((3, 256, 512), f32),
        pltpu.VMEM((8, 768, 512), bf16),
        pltpu.VMEM((8, 512, 256), bf16),
        pltpu.VMEM((3, 256, 2, 1408), bf16),
        pltpu.VMEM((3, 2, 256, 1408), bf16),
    )
    att_two = wires.go(lambda: (k.att_send.at[2], k.att.at[1]), z_dev[0])
    att_one = wires.go(lambda: (k.att_send.at[1], k.att.at[0]), z_dev[0])
    swap_n = wires.go(lambda: (k.n_send, k.n_x), core_dev)
    swap_low = wires.go(lambda: (k.low, k.low_x), core_dev)
    parts = SimpleNamespace(started=False)

    def expert_part(wg, wu, wd, slopes, acc, up, keep, send):
        group = []

        def gather(s, w):
            group.append(loads.go(s.block(0), w.at[0]))
            s.wait(2)
            group.append(loads.go(s.block(2), w.at[2]))
            s.wait(1)
            s.start(3)
            group.append(loads.go(s.block(1), w.at[1]))

        def gather_last(s, w):
            s.wait(3)
            group.append(loads.go(s.block(3), w.at[3]))

        gather(ed, wd)
        att_two.wait_recv()
        pair = k.att_send[3].astype(f32) + k.att[1].astype(f32)
        k.att_pair[...] = pair.astype(bf16)
        att_three = wires.go(lambda: (k.att_pair, k.att.at[2]), z_dev[2])
        att_one.wait_recv()
        value = k.att_send[0].astype(f32) + k.att[0].astype(f32)
        att_three.wait_recv()
        value += piece(k.tok, 0, 64).astype(f32) + k.att[2].astype(f32)
        inv = lax.rsqrt(jnp.mean(value * value, axis=-1, keepdims=True) + epsilon)
        k.hidden[...] = value
        k.rows[0:64, :] = (value * inv * k.small[1:2, :].astype(f32)).astype(bf16)
        own_y = wires.go(
            lambda: (k.rows.at[pl.ds(0, 64), :], k.rows.at[pl.ds(256, 64), :]), y_dev
        )
        g_y = wires.go(lambda: (k.g_own, k.g_oth), y_dev)
        sd.start(2)
        own_z = Collect(lambda d: k.rows.at[pl.ds(64 * d, 64), :])
        gather_last(ed, wd)
        gather(eg, wg)
        gather_last(eg, wg)
        for s in (sg, su):
            s.wait(2)
            s.start(6)
        own_z.hand_on()
        for copy in later:
            copy.wait_recv()
        own_y.wait_recv()
        own_z.wait()
        oth_z = Collect(lambda d: k.rows.at[pl.ds(256 + 64 * d, 64), :])

        def g_piece(half, d, at):
            g = k.g_oth if half else k.g_own
            return g[pl.ds(pl.multiple_of(near(d) * 64, 64), 64), at].astype(f32)

        def route(half):
            chosen = []
            for d in range(4):
                named = (k.ids[d, half * 64 : (half + 1) * 64, :] == mine.astype(f32)).astype(f32)
                chosen.append(jnp.sum(named, axis=-1, keepdims=True))
            chosen = jnp.concatenate(chosen, axis=0)
            prob, lane = probabilities(k.rows[half * 256 : (half + 1) * 256, :], k.small)
            here = jnp.sum(jnp.where(lane == mine + 3, prob, 0.0), axis=-1, keepdims=True)
            gate = here * chosen
            for d in range(4):
                at = slice(half * 256 + d * 64, half * 256 + (d + 1) * 64)
                value = gate[d * 64 : (d + 1) * 64, :] * g_piece(half, d, slice(None))
                slopes[at, :] = value.astype(bf16)
            return gate, chosen

        def gate_part(half):
            rows_at = slice(half * 256, (half + 1) * 256)

            def one(r, _):
                at = pl.ds(pl.multiple_of(owner_expert(r) * 512, 512), 512)
                acc[0] += dot_nn(k.rows[rows_at, at], wg[r])
                acc[2] += dot_nt(slopes[rows_at, at], wd[r])
                return 0

            acc[...] = jnp.zeros_like(acc)
            lax.fori_loop(0, 4, one, 0)

        def phase_one(half):
            rows_at = slice(half * 256, (half + 1) * 256)

            def one(r, _):
                at = pl.ds(pl.multiple_of(owner_expert(r) * 512, 512), 512)
                acc[1] += dot_nn(k.rows[rows_at, at], wu[r])
                return 0

            lax.fori_loop(0, 4, one, 0)
            for d in range(4):
                at, to = slice(d * 64, (d + 1) * 64), slice(half * 256 + d * 64, half * 256 + (d + 1) * 64)
                act, gate_grad, up_grad = gated(acc[0, at, :], acc[1, at, :], acc[2, at, :])
                up[0, to, :] = act.astype(bf16)
                up[1, to, :] = gate_grad.astype(bf16)
                up[2, to, :] = up_grad.astype(bf16)

        lanes = lax.broadcasted_iota(jnp.int32, (64, 128), 1)

        def phase_two(half, gate, chosen):
            rows_at = slice(half * 256, (half + 1) * 256)

            def two(r, dgate):
                at = pl.ds(pl.multiple_of(owner_expert(r) * 512, 512), 512)
                result = dot_nn(up[0, rows_at, :], wd[r]).astype(bf16).astype(f32)
                grad = dot_nt(up[1, rows_at, :], wg[r]) + dot_nt(up[2, rows_at, :], wu[r])
                sums = []
                for d in range(4):
                    here = slice(d * 64, (d + 1) * 64)
                    g_rows = g_piece(half, d, at)
                    sums.append(jnp.sum(g_rows * result[here, :], axis=-1, keepdims=True))
                    part = gate[here, :] * result[here, :]
                    if half == 0:
                        k.out_sum[here, at] = part
                        k.grad_sum[here, at] = grad[here, :]
                    else:
                        k.e_out[d, :, at] = part.astype(bf16)
                        k.e_grad[d, :, at] = grad[here, :].astype(bf16)
                return dgate + jnp.concatenate(sums, axis=0)

            dgate = lax.fori_loop(0, 4, two, jnp.zeros((256, 1), f32)) * chosen
            for d in range(4):
                extra = jnp.zeros((64, 128), f32)
                for m, part in enumerate(split3(dgate[d * 64 : (d + 1) * 64, :])):
                    extra = jnp.where(lanes == mine + 16 * m, part, extra)
                if half == 0:
                    k.extras[d * 64 : (d + 1) * 64, :] = extra
                else:
                    k.e_grad[d, :, 2048:2176] = extra.astype(bf16)

        gate, chosen = route(0)
        for copy in group:
            copy.wait()
        group.clear()
        gate_part(0)
        gather(eu, wu)
        gather_last(eu, wu)
        for copy in group:
            copy.wait()
        phase_one(0)
        oth_z.hand_on()
        phase_two(0, gate, chosen)
        sg.wait(1)
        sg.start(3)
        sg.start(5)
        oth_z.wait()
        g_y.wait_recv()
        gate, chosen = route(1)
        gate_part(1)
        phase_one(1)
        saved = [loads.go(up, k.ex_up)]
        for r in range(4):
            to = slice(r * 256, (r + 1) * 256)
            for target, m in ((keep, r), (send, r + 4)):
                at = pl.ds(pl.multiple_of(owner_dense(m) * 256, 256), 256)
                target[0:512, to] = slopes[:, at]
                target[512:1024, to] = k.rows[:, at]
        saved.append(loads.go(keep, k.ex_keep))
        swap_ex = wires.go(lambda: (send, k.ex_x), core_dev)
        sd.wait(2)
        sd.start(6)
        phase_two(1, gate, chosen)
        su.wait(1)
        su.start(3)
        su.start(5)
        for copy in saved:
            copy.wait()
        swap_ex.wait_send()
        swap_ex.ends = lambda: (k.ex_keep, k.ex_x)
        parts.swap_ex = swap_ex

    pl.run_scoped(
        expert_part,
        pltpu.VMEM((4, 512, 1408), bf16),
        pltpu.VMEM((4, 512, 1408), bf16),
        pltpu.VMEM((4, 1408, 512), bf16),
        pltpu.VMEM((512, 2048), bf16),
        pltpu.VMEM((3, 256, 1408), f32),
        pltpu.VMEM((3, 512, 1408), bf16),
        pltpu.VMEM((1024, 1024), bf16),
        pltpu.VMEM((1024, 1024), bf16),
    )
    swap_up = {}
    for m in (1, 2, 0):
        swap_up[m] = wires.go(lambda m=m: (k.ex_up.at[m], k.ex_up_x.at[m]), core_dev)
    e_grad_z = to_z(lambda d: lambda: (k.e_grad.at[d], k.e_grad_z.at[d - 1]))
    e_out_z = to_z(lambda d: lambda: (k.e_out.at[d], k.e_out_z.at[d - 1]))
    over_y, over_x = {}, {}

    def expert_grad(m, kept, sent, landed):
        parts.swap_ex_wait()
        swap_up[m].wait_recv()

        def inner(left, right, keep, send):
            start = pl.ds(0 if m == 0 else 512, 512)
            got = [
                loads.go(k.ex_up.at[m], right.at[0]),
                loads.go(k.ex_up_x.at[m], right.at[1]),
                loads.go(k.ex_keep.at[start, :], left.at[0]),
                loads.go(k.ex_x.at[start, :], left.at[1]),
            ]
            for copy in got:
                copy.wait()
            saved = []
            for r in (3, 1, 2, 0):
                target = send if r % 2 else keep
                at = slice(r * 256, (r + 1) * 256)
                to = pl.ds(pl.multiple_of(((y + r // 2) % 2) * 256, 256), 256)
                if m == 0:
                    total = dot_tn(right[0], left[0, :, at]) + dot_tn(right[1], left[1, :, at])
                    target[:, to] = total.astype(bf16)
                else:
                    total = dot_tn(left[0, :, at], right[0]) + dot_tn(left[1, :, at], right[1])
                    target[to, :] = total.astype(bf16)
                if r == 1:
                    saved.append(loads.go(send, sent))
                if r == 2:
                    saved[0].wait()
                    over_x[6 + m] = wires.go(lambda: (sent, landed), x_dev)
            loads.go(keep, kept).wait()

        shape = (1408, 512) if m == 0 else (512, 1408)
        pl.run_scoped(
            inner,
            pltpu.VMEM((2, 512, 1024), bf16),
            pltpu.VMEM((2, 512, 1408), bf16),
            pltpu.VMEM(shape, bf16),
            pltpu.VMEM(shape, bf16),
        )

    def set_out(name, n, source, target, device):
        over_y[name, n] = wires.go(lambda: (source.at[n], target.at[n]), device)

    def y_first(name, keep, send, landed):
        def store(r, total):
            (send if r >= 2 else keep)[r % 2] = total
            if r == 3:
                set_out(name, 1, send, landed, y_dev)

        return store

    def shared_grad(m, store):
        def inner(left, right):
            if m == 0:
                got = [loads.go(k.sh_keep, left.at[0]), loads.go(k.sh_x, left.at[1])]
            else:
                start = pl.ds(512, 256)
                got = [
                    loads.go(k.ex_keep.at[start, :], left.at[0]),
                    loads.go(k.ex_x.at[start, :], left.at[1]),
                ]
            got.append(loads.go(k.sh_up.at[m], right.at[0]))
            got.append(loads.go(k.sh_up_x.at[m], right.at[1]))
            for copy in got:
                copy.wait()
            for r in (3, 1, 2, 0):
                at = slice(r * 256, (r + 1) * 256)
                if m == 0:
                    total = dot_tn(right[0], left[0, :, at]) + dot_tn(right[1], left[1, :, at])
                else:
                    total = dot_tn(left[0, :, at], right[0]) + dot_tn(left[1, :, at], right[1])
                store(r, total.astype(bf16))

        pl.run_scoped(
            inner, pltpu.VMEM((2, 256, 1024), bf16), pltpu.VMEM((2, 256, 1408), bf16)
        )

    def swap_ex_wait():
        if not parts.started:
            parts.swap_ex.wait_recv()
            parts.started = True

    parts.swap_ex_wait = swap_ex_wait

    def shared_part(wg, wu, wd, slopes, acc, up, keep, send):
        routed = k.rows.at[pl.ds(0, 256), :]
        held = []

        def bring(r, group):
            for s in group:
                held.append(loads.go(s.block(r), {sg: wg, su: wu, sd: wd}[s].at[r]))

        def arrived(r, group, onward=()):
            for s in group:
                s.wait(r)
                for t in onward:
                    s.start(t)
            bring(r, group)

        def settle():
            for copy in held:
                copy.wait()
            held.clear()

        pair, last = (sg, su), (sd,)
        for r in (0, 1, 2):
            bring(r, pair)
        for r in (4, 6):
            arrived(r, pair)
        expert_grad(1, k.k_eg, k.t_eg, k.x_eg)
        arrived(5, pair)
        sd.wait(1)
        sd.start(3)
        sd.start(5)
        bring(0, last)
        bring(1, last)
        bring(2, last)
        arrived(4, last)
        arrived(6, last)
        arrived(5, last)
        wide = routed[...].astype(f32) * k.small[2:3, :].astype(f32)
        sw = jax.nn.sigmoid(jnp.sum(wide, axis=-1, keepdims=True))
        for d in range(4):
            at = slice(d * 64, (d + 1) * 64)
            slopes[at, :] = (sw[at, :] * piece(k.g_own, d, 64).astype(f32)).astype(bf16)
        for r in range(4):
            to = slice(r * 256, (r + 1) * 256)
            keep[:, to] = cols(slopes, owner_dense(r), 256)
            send[:, to] = cols(slopes, owner_dense(r + 4), 256)
        saved = [loads.go(keep, k.sh_keep)]
        acc[...] = jnp.zeros_like(acc)

        def one(j, _):
            r = j // 2 + (j % 2) * 4
            row = cols(routed, owner_dense(r), 256)
            acc[0] += dot_nn(row, wg[r])
            acc[1] += dot_nn(row, wu[r])
            return 0

        def back(j, _):
            r = j // 2 + (j % 2) * 4
            acc[2] += dot_nt(cols(slopes, owner_dense(r), 256), wd[r])
            return 0

        settle()
        lax.fori_loop(0, 6, one, 0)
        arrived(3, pair, (7,))
        arrived(7, pair)
        settle()
        lax.fori_loop(6, 8, one, 0)
        for d in range(4):
            at = slice(d * 64, (d + 1) * 64)
            up[0, at, :] = (jax.nn.silu(acc[0, at, :]) * acc[1, at, :]).astype(bf16)
        swaps = [
            wires.go(lambda: (up.at[0], k.sh_up_x.at[0]), core_dev),
            wires.go(lambda: (send, k.sh_x), core_dev),
        ]
        saved.append(loads.go(up.at[0], k.sh_up.at[0]))
        for copy in saved:
            copy.wait()
        lax.fori_loop(0, 6, back, 0)
        for copy in swaps:
            copy.wait_recv()
            copy.wait_send()
        shared_grad(0, y_first(2, k.k_sd, k.t_sd, k.y_sd))
        for copy in e_grad_z:
            copy.wait_recv()
        oth = k.e_grad[0].astype(f32)
        for d in range(3):
            oth += k.e_grad_z[d].astype(f32)
        k.g_send[...] = oth.astype(bf16)
        parts.grad_y = wires.go(lambda: (k.g_send, k.g_y), y_dev)
        set_out(2, 0, k.t_sd, k.y_sd, y_dev)
        expert_grad(2, k.k_eu, k.t_eu, k.x_eu)
        arrived(3, last, (7,))
        arrived(7, last)
        settle()
        lax.fori_loop(6, 8, back, 0)
        for d in range(4):
            at = slice(d * 64, (d + 1) * 64)
            _, gate_grad, up_grad = gated(acc[0, at, :], acc[1, at, :], acc[2, at, :])
            up[1, at, :] = gate_grad.astype(bf16)
            up[2, at, :] = up_grad.astype(bf16)
        saved = [loads.go(up.at[m], k.sh_up.at[m]) for m in (1, 2)]

        def two(r, slope):
            at = pl.ds(pl.multiple_of(owner_dense(r) * 256, 256), 256)
            part = dot_nn(up[0], wd[r])
            total = sw * part + k.out_sum[:, at]
            back = dot_nt(up[1], wg[r]) + dot_nt(up[2], wu[r]) + k.grad_sum[:, at]
            sums = []
            for d in range(4):
                rows_at = slice(d * 64, (d + 1) * 64)
                g_rows = k.g_own[pl.ds(pl.multiple_of(near(d) * 64, 64), 64), at].astype(f32)
                sums.append(jnp.sum(g_rows * part[rows_at, :], axis=-1, keepdims=True))
                k.s_out[d, :, at] = total[rows_at, :].astype(bf16)
                k.s_grad[d, :, at] = back[rows_at, :].astype(bf16)
            return slope + jnp.concatenate(sums, axis=0)

        slope = lax.fori_loop(0, 8, two, jnp.zeros((256, 1), f32))
        lanes = lax.broadcasted_iota(jnp.int32, (64, 128), 1)
        for d in range(4):
            rows_at = slice(d * 64, (d + 1) * 64)
            extra = k.extras[rows_at, :]
            for m, part in enumerate(split3(slope[rows_at, :])):
                extra = jnp.where(lanes == mine + 48 + 16 * m, part, extra)
            k.s_grad[d, :, 2048:2176] = extra.astype(bf16)
        for copy in saved:
            copy.wait()

    pl.run_scoped(
        shared_part,
        pltpu.VMEM((8, 256, 1408), bf16),
        pltpu.VMEM((8, 256, 1408), bf16),
        pltpu.VMEM((8, 1408, 256), bf16),
        pltpu.VMEM((256, 2048), bf16),
        pltpu.VMEM((3, 256, 1408), f32),
        pltpu.VMEM((3, 256, 1408), bf16),
        pltpu.VMEM((256, 1024), bf16),
        pltpu.VMEM((256, 1024), bf16),
    )
    swap_sh = [
        wires.go(lambda m=m: (k.sh_up.at[m], k.sh_up_x.at[m]), core_dev) for m in (1, 2)
    ]
    s_grad_z = to_z(lambda d: lambda: (k.s_grad.at[d], k.s_grad_z.at[d - 1]))

    def back_part(*refs):
        k_ga, k_gb, k_su, k_q, k_kv, k_o, k_v = refs[:7]
        t_ga, t_gb, t_su, t_q, t_kv, t_o, t_v = refs[7:14]
        f_ga, f_gb, f_su, f_q, f_kv, f_o, f_v, f_sd = refs[14:22]
        h_keep, h_send, h_x, lin, lin_x, vec, high, gkv, gkv_send, gn = refs[22:]
        k_sd, t_sd = k.k_sd, k.t_sd

        def fold(name, keep, landed, send, target, device=x_dev):
            over_y[name, 1].wait_recv()

            def inner(buffer):
                loads.go(landed.at[1], buffer).wait()
                send[...] = (keep[1].astype(f32) + buffer[...].astype(f32)).astype(bf16)

            pl.run_scoped(inner, pltpu.VMEM(tuple(keep.shape[1:]), bf16))
            over_x[name] = wires.go(lambda: (send, target), device)

        def finish_pair():
            for name in (0, 9, 1):
                over_y[name, 0].wait_recv()
                over_x[name].wait_recv()

            def inner(left, right, total):
                first, last, whole = pl.ds(0, CUT), pl.ds(CUT, 256 - CUT), slice(0, 256)
                got = [
                    loads.go(k.y_ga.at[0], left.at[0, first, :]),
                    loads.go(k.x_ga, right.at[0, first, :]),
                    loads.go(k.y_gb.at[0], left.at[0, last, :]),
                    loads.go(k.x_gb, right.at[0, last, :]),
                    loads.go(k.y_su.at[0], left.at[1]),
                    loads.go(k.x_su, right.at[1]),
                ]
                for copy in got:
                    copy.wait()
                for n, keep, at in (
                    (0, k_ga, slice(0, CUT)),
                    (0, k_gb, slice(CUT, 256)),
                    (1, k_su, whole),
                ):
                    value = keep[0].astype(f32) + left[n, at, :].astype(f32)
                    value += right[n, at, :].astype(f32)
                    total[at, n, :] = value.astype(bf16)
                loads.go(total, k.d_si).wait()

            pair = pltpu.VMEM((2, 256, 1408), bf16)
            pl.run_scoped(inner, pair, pair, pltpu.VMEM((256, 2, 1408), bf16))

        def finish(name, keep, landed, target, result):
            over_y[name, 0].wait_recv()

            def inner(left, right, total):
                got = loads.go(landed.at[0], left)
                over_x[name].wait_recv()
                more = loads.go(target, right)
                got.wait()
                more.wait()
                value = keep[0].astype(f32) + left[...].astype(f32) + right[...].astype(f32)
                total[...] = value.astype(total.dtype)
                loads.go(total, result).wait()

            shape = tuple(keep.shape[1:])
            pl.run_scoped(
                inner,
                pltpu.VMEM(shape, bf16),
                pltpu.VMEM(shape, bf16),
                pltpu.VMEM(shape, result.dtype),
            )

        swap_sh[0].wait_recv()

        def gate_store(r, total):
            (t_ga if r >= 2 else k_ga)[r % 2] = total[0:CUT, :]
            (t_gb if r % 2 else k_gb)[r // 2] = total[CUT:256, :]
            if r == 3:
                set_out(0, 1, t_ga, k.y_ga, y_dev)
                set_out(9, 1, t_gb, k.y_gb, x_dev)

        shared_grad(1, gate_store)
        set_out(9, 0, t_gb, k.y_gb, x_dev)
        swap_sh[1].wait_recv()
        shared_grad(2, y_first(1, k_su, t_su, k.y_su))
        expert_grad(0, k.k_ed, k.t_ed, k.x_ed)
        fold(2, k_sd, k.y_sd, f_sd, k.x_sd)

        def other_rows(buffer):
            for copy in e_out_z:
                copy.wait_recv()
            loads.go(k.e_out_z, buffer).wait()
            oth = k.e_out[0].astype(f32)
            for d in range(3):
                oth += buffer[d].astype(f32)
            k.o_send[...] = oth.astype(bf16)

        pl.run_scoped(other_rows, pltpu.VMEM((3, 64, 2048), bf16))
        for copy in s_grad_z:
            copy.wait_recv()
        parts.grad_y.wait_recv()
        total = k.s_grad[0].astype(f32) + k.g_y[...].astype(f32)
        for d in range(3):
            total += k.s_grad_z[d].astype(f32)
        own_rows(
            total,
            k.hidden[...],
            k.rows[0:64, :],
            piece(k.g_own, 0, 64),
            k.small,
            high,
            k.gh.at[0],
            vec,
        )
        gh_z = Collect(lambda d: k.gh.at[d])
        out_y = wires.go(lambda: (k.o_send, k.o_y), y_dev)
        set_out(0, 0, t_ga, k.y_ga, y_dev)
        fold(0, k_ga, k.y_ga, f_ga, k.x_ga)
        fold(9, k_gb, k.y_gb, f_gb, k.x_gb, y_dev)
        gn_z, s_out_z, vec_z = [], [], []

        def attention_back(w, o_w, acc, low_g, n_x, low_x):
            got, more = [loads.go(k.w_o, o_w.at[0])], [loads.go(k.w_q, w.at[0])]
            for r in range(1, 8):
                got.append(loads.go(k.s_o.at[r], o_w.at[r]))
                more.append(loads.go(k.s_q.at[r], w.at[r]))
            gh_z.hand_on()
            gh_z.wait()
            s_out_z.extend(to_z(lambda d: lambda: (k.s_out.at[d], k.s_out_z.at[d - 1])))
            for copy in got:
                copy.wait()
            acc[...] = jnp.zeros_like(acc)
            for r in range(8):
                at = pl.ds(pl.multiple_of(owner_dense(r) * 256, 256), 256)
                row = jnp.concatenate([k.gh[d, :, at] for d in range(4)], axis=0)
                target = h_keep if r < 4 else h_send
                target[:, (r % 4) * 256 : (r % 4 + 1) * 256] = row
                acc[...] += dot_nt(row, o_w[r])
            swap_h = wires.go(lambda: (h_send, k.h_x), core_dev)
            low_g[...] = acc[...].astype(bf16)
            mask_own = k.ids_near[0:1, :] <= k.ids_q[:, 0:1]
            mask_oth = k.ids_far[0:1, :] <= k.ids_q[:, 0:1]
            scale = 128 ** (-0.5)
            for h in range(4):
                at = slice(h * 128, (h + 1) * 128)
                w_own, w_oth = softmax_parts(
                    k.q[:, at], k.kv[0:256, at], k.kv_oth[0:256, at], mask_own, mask_oth
                )
                dw_own = dot_nt(low_g[:, at], k.kv[256:512, at])
                dw_oth = dot_nt(low_g[:, at], k.kv_oth[256:512, at])
                mean = jnp.sum(w_own * dw_own, axis=-1, keepdims=True)
                mean += jnp.sum(w_oth * dw_oth, axis=-1, keepdims=True)
                ds_own = (w_own * (dw_own - mean)).astype(bf16)
                ds_oth = (w_oth * (dw_oth - mean)).astype(bf16)
                gq = dot_nn(ds_own, k.kv[0:256, at]) + dot_nn(ds_oth, k.kv_oth[0:256, at])
                lin[0:256, at] = turn_back(gq * scale, k.cs[...], k.sn[...]).astype(bf16)
                gkv[0:256, at] = dot_tn(ds_own, k.q[:, at]) * scale
                gkv[256:512, at] = dot_tn(w_own.astype(bf16), low_g[:, at])
                gkv_send[0:256, at] = (dot_tn(ds_oth, k.q[:, at]) * scale).astype(bf16)
                gkv_send[256:512, at] = dot_tn(w_oth.astype(bf16), low_g[:, at]).astype(bf16)
            gkv_y = wires.go(lambda: (gkv_send, k.gkv_y), y_dev)
            swap_q = wires.go(
                lambda: (lin.at[pl.ds(0, 256), :], k.lin_x.at[pl.ds(0, 256), :]), core_dev
            )
            fold(1, k_su, k.y_su, f_su, k.x_su)
            for copy in (swap_h, swap_n, swap_low, swap_q):
                copy.wait_recv()
            got = [
                loads.go(k.n_x, n_x),
                loads.go(k.low_x, low_x),
                loads.go(k.h_x, h_x),
                loads.go(k.lin_x.at[pl.ds(0, 256), :], lin_x.at[pl.ds(0, 256), :]),
            ]
            for copy in got:
                copy.wait()

            def projection(r, m):
                at, rows_at = slice(r * 256, (r + 1) * 256), slice(m * 256, (m + 1) * 256)
                total = dot_tn(k.n_keep[:, at], lin[rows_at, :])
                return (total + dot_tn(n_x[:, at], lin_x[rows_at, :])).astype(bf16)

            for r in (3, 1, 2, 0):
                at = slice(r * 256, (r + 1) * 256)
                total = dot_tn(k.low[...], h_keep[:, at]) + dot_tn(low_x[...], h_x[:, at])
                (t_o if r % 2 else k_o)[r // 2] = total.astype(bf16)
                if r % 2:
                    set_out(4, r // 2, t_o, k.y_o, x_dev)
                (t_q if r >= 2 else k_q)[r % 2] = projection(r, 0)
                if r == 3:
                    set_out(3, 1, t_q, k.y_q, y_dev)
            for copy in more:
                copy.wait()
            gkv_y.wait_recv()
            for h in range(4):
                at = slice(h * 128, (h + 1) * 128)
                gk = gkv[0:256, at] + k.gkv_y[0:256, at].astype(f32)
                lin[256:512, at] = turn_back(gk, k.cs[...], k.sn[...]).astype(bf16)
            lin[512:768, :] = (gkv[256:512, :] + k.gkv_y[256:512, :].astype(f32)).astype(bf16)
            swap_kv = wires.go(
                lambda: (lin.at[pl.ds(256, 512), :], k.lin_x.at[pl.ds(256, 512), :]), core_dev
            )
            for m in range(3):
                part = lin[m * 256 : (m + 1) * 256, :].astype(f32)
                vec[11 + m : 12 + m, 0:512] = jnp.sum(part, axis=0, keepdims=True)
            swap_kv.wait_recv()
            loads.go(k.lin_x.at[pl.ds(256, 512), :], lin_x.at[pl.ds(256, 512), :]).wait()
            for r in (3, 2, 1, 0):
                target = t_kv if r >= 2 else k_kv
                for m in (1, 2):
                    target[r % 2, (m - 1) * 256 : m * 256, :] = projection(r, m)
                if r == 3:
                    set_out(10, 1, t_kv, k.y_kv, y_dev)
                    set_out(1, 0, t_su, k.y_su, y_dev)
            for r in range(8):
                at = pl.ds(pl.multiple_of(owner_dense(r) * 256, 256), 256)
                back = dot_nt(lin[0:256, :], w[r, 0:256, :])
                back += dot_nt(lin[256:512, :], w[r, 256:512, :])
                back += dot_nt(lin[512:768, :], w[r, 512:768, :])
                gain = jnp.zeros((1, 256), f32)
                for d in range(4):
                    rows_at = slice(d * 64, (d + 1) * 64)
                    t = k.tok[pl.ds(pl.multiple_of(near(d) * 64, 64), 64), at].astype(f32)
                    gain += jnp.sum(
                        back[rows_at, :] * t * k.inv1[rows_at, :], axis=0, keepdims=True
                    )
                    gn[d, :, at] = back[rows_at, :].astype(bf16)
                vec[0:1, at] = gain
            vec_z.extend(to_z(lambda d: lambda: (vec, k.vec_z.at[d - 1])))
            gn_z.extend(to_z(lambda d: lambda: (gn.at[d], k.gn_z.at[d - 1])))

        pl.run_scoped(
            attention_back,
            pltpu.VMEM((8, 768, 512), bf16),
            pltpu.VMEM((8, 512, 256), bf16),
            pltpu.VMEM((256, 512), f32),
            pltpu.VMEM((256, 512), bf16),
            pltpu.VMEM((256, 1024), bf16),
            pltpu.VMEM((256, 512), bf16),
        )
        kept = [loads.go(k_q.at[0], k.keep_q), loads.go(k_kv.at[0], k.keep_kv)]
        kept.append(loads.go(k_o.at[0], k.keep_o))
        def expert_finish(m, kept, landed, result):
            def inner(left, right):
                got = loads.go(kept, left)
                over_x[6 + m].wait_recv()
                more = loads.go(landed, right)
                got.wait()
                more.wait()
                left[...] = (left[...].astype(f32) + right[...].astype(f32)).astype(bf16)
                loads.go(left, result).wait()

            shape = pltpu.VMEM(tuple(result.shape), bf16)
            pl.run_scoped(inner, shape, shape)

        def expert_pair():
            for m in (1, 2):
                over_x[6 + m].wait_recv()

            def inner(left, right, total):
                for half in range(2):
                    at = pl.ds(256 * half, 256)
                    got = []
                    for n, (kept, landed) in enumerate(((k.k_eg, k.x_eg), (k.k_eu, k.x_eu))):
                        got.append(loads.go(kept.at[at, :], left.at[n]))
                        got.append(loads.go(landed.at[at, :], right.at[n]))
                    for copy in got:
                        copy.wait()
                    for n in range(2):
                        value = left[n].astype(f32) + right[n].astype(f32)
                        total[:, n, :] = value.astype(bf16)
                    loads.go(total, k.d_ei.at[at]).wait()

            pair = pltpu.VMEM((2, 256, 1408), bf16)
            pl.run_scoped(inner, pair, pair, pltpu.VMEM((256, 2, 1408), bf16))

        expert_pair()
        for copy in vec_z:
            copy.wait_recv()
        line = lax.broadcasted_iota(jnp.int32, (16, 2048), 0)
        over_z = k.vec_z[0] + k.vec_z[1] + k.vec_z[2]
        k.vec_sum[...] = vec[...] + jnp.where(line < 11, over_z, 0.0)
        swap_vec = wires.go(lambda: (k.vec_sum, k.vec_x), core_dev)
        swap_vec.wait_recv()
        k.vec_x[...] += k.vec_sum[...]
        line = lax.broadcasted_iota(jnp.int32, (16, 512), 0)
        for r in (3, 2, 1, 0):
            here = cols(k.vec_x, owner_dense(r), 256)
            here = jnp.concatenate([here, jnp.zeros((16, 256), f32)], axis=1)
            here = jnp.where(line < 11, here, k.vec_x[:, 0:512]).astype(bf16)
            (t_v if r >= 2 else k_v)[r % 2] = here
            if r >= 2:
                set_out(5, r % 2, t_v, k.y_v, y_dev)
        kept.append(loads.go(k_v.at[0], k.keep_v))
        set_out(3, 0, t_q, k.y_q, y_dev)
        set_out(10, 0, t_kv, k.y_kv, y_dev)

        def outputs(s_z):
            for copy in s_out_z:
                copy.wait_recv()
            got = loads.go(k.s_out_z, s_z)
            for copy in gn_z:
                copy.wait_recv()
            grad = gn[0].astype(f32)
            for d in range(3):
                grad += k.gn_z[d].astype(f32)
            t = piece(k.tok, 0, 64).astype(f32)
            i = k.inv1[0:64, :]
            scaled = grad * k.small[0:1, :].astype(f32)
            mean = jnp.mean(scaled * t, axis=-1, keepdims=True)
            grad = high[...] + i * scaled - t * (i * i * i * mean)
            k.grad_tokens[...] = grad.astype(bf16)
            got.wait()
            total = k.hidden[...] + k.s_out[0].astype(f32)
            for d in range(3):
                total += s_z[d].astype(f32)
            out_y.wait_recv()
            k.output[...] = (total + k.o_y[...].astype(f32)).astype(bf16)

        expert_finish(0, k.k_ed, k.x_ed, k.d_ed)
        finish(2, k_sd, k.y_sd, k.x_sd, k.d_sd)
        fold(3, k_q, k.y_q, f_q, k.x_q)
        fold(10, k_kv, k.y_kv, f_kv, k.x_kv)
        fold(5, k_v, k.y_v, f_v, k.x_v)
        fold(4, k_o, k.y_o, f_o, k.x_o, y_dev)
        pl.run_scoped(outputs, pltpu.VMEM((3, 64, 2048), bf16))
        finish_pair()
        for name in (3, 10, 4, 5):
            over_y[name, 0].wait_recv()
            over_x[name].wait_recv()
        for copy in kept:
            copy.wait()
        wires.drain()

    shapes = [(CUT, 1408), (256 - CUT, 1408), (256, 1408)]
    shapes += [(256, 512), (512, 512), (512, 256), (16, 512)]

    def buffers(lead):
        return tuple(
            pltpu.VMEM(lead + shape, bf16)
            for shape in shapes
        )

    pl.run_scoped(
        back_part,
        *buffers((2,)),
        *buffers((2,)),
        *buffers(()),
        pltpu.VMEM((1408, 256), bf16),
        pltpu.VMEM((256, 1024), bf16),
        pltpu.VMEM((256, 1024), bf16),
        pltpu.VMEM((256, 1024), bf16),
        pltpu.VMEM((768, 512), bf16),
        pltpu.VMEM((768, 512), bf16),
        pltpu.VMEM((16, 2048), f32),
        pltpu.VMEM((64, 2048), f32),
        pltpu.VMEM((512, 512), f32),
        pltpu.VMEM((512, 512), bf16),
        pltpu.VMEM((4, 64, 2048), bf16),
    )


def close_kernel(k):
    loads = Loads(k.load_sems)
    sums = (
        (k.keep_q, k.y_q, k.x_q, k.b_q, k.c_q.at[pl.ds(0, 256), :]),
        (k.keep_kv, k.y_kv, k.x_kv, k.b_kv, k.c_q.at[pl.ds(256, 512), :]),
        (k.keep_o, k.y_o, k.x_o, k.b_o, k.c_o),
    )
    parts = []
    for keep, y, x, buffer, _ in sums:
        parts.append([loads.go(a, buffer.at[n]) for n, a in enumerate((keep, y.at[0], x))])
    passed = (
        (k.d_ei, k.b_ei, k.c_ei),
        (k.d_ed, k.b_ed, k.c_ed),
        (k.d_si, k.b_si, k.c_si),
        (k.d_sd, k.b_sd, k.c_sd),
        (k.output, k.b_out, k.c_out),
        (k.grad_tokens, k.b_tok, k.c_tok),
    )
    got = [loads.go(source, buffer) for source, buffer, _ in passed]
    total = k.keep_v[...].astype(f32) + k.y_v[0].astype(f32) + k.x_v[...].astype(f32)
    low = total.astype(bf16)
    for m, target in enumerate((k.c_one, k.c_two, k.c_gate)):
        target[...] = low[m : m + 1, 0:256].reshape(256)
    k.c_router[...] = low[3:11, 0:256]
    for h in range(4):
        here = pltpu.roll(
            total[:, h * 128 : (h + 1) * 128], (128 - owner_dense(0) * 16) % 128, 1
        )
        for m in range(3):
            k.c_bias[m, h : h + 1, :] = here[11 + m : 12 + m, 0:16].astype(bf16)
    done = []
    for copies, (_, _, _, buffer, target) in zip(parts, sums):
        for copy in copies:
            copy.wait()
        total = buffer[0].astype(f32) + buffer[1].astype(f32) + buffer[2].astype(f32)
        buffer[0] = total.astype(bf16)
        done.append(loads.go(buffer.at[0], target))
    for copy, (_, buffer, target) in zip(got, passed):
        copy.wait()
        done.append(loads.go(buffer, target))
    for copy in done:
        copy.wait()


def dma(n):
    return pltpu.SemaphoreType.DMA((n,))


def fixed_body(
    tokens,
    norm1_gain,
    w_qkv,
    b_qkv,
    w_out,
    norm2_gain,
    w_router,
    shared_gate,
    w_shared_in,
    w_shared_out,
    w_expert_in,
    w_expert_out,
    block_ids,
    expert_ids,
    out_grad,
):
    tok, g_own = tokens[0], out_grad[0]
    rows = tok.shape[0]
    places = np.arange(2 * rows)[:, None]
    frequency = rope_base ** (-np.arange(64) / 64.0)
    cosine, sine = np.cos(places * frequency), np.sin(places * frequency)
    cs = np.concatenate([cosine, cosine], axis=1).astype(np.float32)
    sn = np.concatenate([-sine, sine], axis=1).astype(np.float32)

    def vm(*shape, kind=bf16):
        return pltpu.VMEM(shape, kind)

    def o(*shape, kind=bf16, at=A):
        return (shape, kind, at)

    w_q = w_qkv.transpose(1, 0, 2).reshape(768, 512)
    b = call(
        layer_kernel,
        0,
        dict(
            tok_in=(tok, A),
            g_in=(g_own, A),
            bias=(b_qkv, V),
            cs_in=(cs, A),
            sn_in=(sn, A),
            blocks=(block_ids, V),
            ids_own=(expert_ids[0].T, V),
            gain_one=(norm1_gain, V),
            gain_two=(norm2_gain, V),
            gate_vector=(shared_gate, V),
            router=(w_router.T, V),
            w_q=(w_q, A),
            w_o=(w_out, A),
            w_si=(w_shared_in, A),
            w_sd=(w_shared_out, A),
            w_ei=(w_expert_in[0], A),
            w_ed=(w_expert_out[0], A),
        ),
        dict(
            output=o(64, 2048, at=V),
            grad_tokens=o(64, 2048, at=V),
            keep_v=o(16, 512),
            keep_q=o(256, 512),
            keep_kv=o(512, 512),
            keep_o=o(512, 256),
            d_si=o(256, 2, 1408),
            d_sd=o(1408, 256),
            d_ei=o(512, 2, 1408),
            d_ed=o(1408, 512),
            split_si=o(2, 256, 1408),
            split_ei=o(2, 512, 1408),
            s_q=o(8, 768, 512),
            s_o=o(8, 512, 256),
            s_sg=o(8, 256, 1408),
            s_su=o(8, 256, 1408),
            s_sd=o(8, 1408, 256),
            s_eg=o(4, 512, 1408),
            s_eu=o(4, 512, 1408),
            s_ed=o(4, 1408, 512),
            ex_up=o(3, 512, 1408),
            ex_up_x=o(3, 512, 1408),
            ex_keep=o(1024, 1024),
            ex_x=o(1024, 1024),
            sh_up=o(3, 256, 1408),
            sh_up_x=o(3, 256, 1408),
            sh_keep=o(256, 1024),
            sh_x=o(256, 1024),
            k_eg=o(512, 1408),
            k_eu=o(512, 1408),
            k_ed=o(1408, 512),
            t_eg=o(512, 1408),
            t_eu=o(512, 1408),
            t_ed=o(1408, 512),
            y_ga=o(2, CUT, 1408),
            y_gb=o(2, 256 - CUT, 1408),
            y_su=o(2, 256, 1408),
            y_sd=o(2, 1408, 256),
            y_q=o(2, 256, 512),
            y_kv=o(2, 512, 512),
            y_o=o(2, 512, 256),
            y_v=o(2, 16, 512),
            x_ga=o(CUT, 1408),
            x_gb=o(256 - CUT, 1408),
            x_su=o(256, 1408),
            x_sd=o(1408, 256),
            x_q=o(256, 512),
            x_kv=o(512, 512),
            x_o=o(512, 256),
            x_v=o(16, 512),
            x_eg=o(512, 1408),
            x_eu=o(512, 1408),
            x_ed=o(1408, 512),
            n_x=o(256, 1024),
            low_x=o(256, 512),
            h_x=o(256, 1024),
            lin_x=o(768, 512),
            e_out_z=o(3, 64, 2048),
            s_out_z=o(3, 64, 2048),
        ),
        dict(
            s_v=vm(8, 16, 256),
            tok=vm(256, 2048),
            g_own=vm(256, 2048),
            cs_all=vm(512, 128, kind=f32),
            sn_all=vm(512, 128, kind=f32),
            w_v=vm(16, 256),
            col=vm(512, 128, kind=f32),
            ids_q=vm(256, 128, kind=f32),
            ids_near=vm(8, 256, kind=f32),
            ids_far=vm(8, 256, kind=f32),
            cs=vm(256, 128, kind=f32),
            sn=vm(256, 128, kind=f32),
            ids=vm(4, 128, 128, kind=f32),
            ids_y=vm(64, 128, kind=f32),
            g_oth=vm(256, 2048),
            q=vm(256, 512),
            kv=vm(512, 512),
            kv_oth=vm(512, 512),
            low=vm(256, 512),
            n_keep=vm(256, 1024),
            n_send=vm(256, 1024),
            small=vm(16, 2048),
            inv1=vm(256, 1, kind=f32),
            k_sd=vm(2, 1408, 256),
            t_sd=vm(2, 1408, 256),
            att=vm(3, 64, 2048),
            att_send=vm(4, 64, 2048),
            att_pair=vm(64, 2048),
            hidden=vm(64, 2048, kind=f32),
            rows=vm(512, 2048),
            out_sum=vm(256, 2048, kind=f32),
            grad_sum=vm(256, 2048, kind=f32),
            extras=vm(256, 128, kind=f32),
            e_out=vm(4, 64, 2048),
            e_grad=vm(4, 64, 2176),
            e_grad_z=vm(3, 64, 2176),
            s_out=vm(4, 64, 2048),
            s_grad=vm(4, 64, 2176),
            s_grad_z=vm(3, 64, 2176),
            g_send=vm(64, 2176),
            g_y=vm(64, 2176),
            o_send=vm(64, 2048),
            o_y=vm(64, 2048),
            gh=vm(4, 64, 2048),
            gkv_y=vm(512, 512),
            gn_z=vm(3, 64, 2048),
            vec_x=vm(16, 2048, kind=f32),
            vec_z=vm(3, 16, 2048, kind=f32),
            vec_sum=vm(16, 2048, kind=f32),
            send_sems=dma(144),
            recv_sems=dma(144),
            load_sems=dma(224),
        ),
        63,
        4 * 10**10,
        2 * 10**8,
    )
    c = call(
        close_kernel,
        None,
        dict(
            output=(b.output, A),
            grad_tokens=(b.grad_tokens, A),
            keep_v=(b.keep_v, V),
            y_v=(b.y_v, V),
            x_v=(b.x_v, V),
            keep_q=(b.keep_q, A),
            y_q=(b.y_q, A),
            x_q=(b.x_q, A),
            keep_kv=(b.keep_kv, A),
            y_kv=(b.y_kv, A),
            x_kv=(b.x_kv, A),
            keep_o=(b.keep_o, A),
            y_o=(b.y_o, A),
            x_o=(b.x_o, A),
            d_si=(b.d_si, A),
            d_sd=(b.d_sd, A),
            d_ei=(b.d_ei, A),
            d_ed=(b.d_ed, A),
        ),
        dict(
            c_out=o(64, 2048),
            c_tok=o(64, 2048),
            c_one=o(256, at=V),
            c_two=o(256, at=V),
            c_gate=o(256, at=V),
            c_router=o(8, 256, at=V),
            c_bias=o(3, 4, 16, at=V),
            c_q=o(768, 512),
            c_o=o(512, 256),
            c_si=o(256, 2, 1408),
            c_sd=o(1408, 256),
            c_ei=o(512, 2, 1408),
            c_ed=o(1408, 512),
        ),
        dict(
            b_out=vm(64, 2048),
            b_tok=vm(64, 2048),
            b_q=vm(3, 256, 512),
            b_kv=vm(3, 512, 512),
            b_o=vm(3, 512, 256),
            b_si=vm(256, 2, 1408),
            b_sd=vm(1408, 256),
            b_ei=vm(512, 2, 1408),
            b_ed=vm(1408, 512),
            load_sems=dma(32),
        ),
        63,
        10**6,
        2 * 10**7,
    )
    return (
        c.c_out[None],
        c.c_tok[None],
        c.c_one,
        c.c_q.reshape(3, 256, 512).transpose(1, 0, 2),
        c.c_bias,
        c.c_o,
        c.c_two,
        c.c_router.T,
        c.c_gate,
        c.c_si,
        c.c_sd,
        c.c_ei[None],
        c.c_ed[None],
    )


def solution(mesh):
    placed = (
        P(DP, CTX, None),
        P(PLANE),
        P(PLANE, None, EXP),
        P(None, EXP, None),
        P(EXP, PLANE),
        P(PLANE),
        P(PLANE, None),
        P(PLANE),
        P(PLANE, None, EXP),
        P(EXP, PLANE),
        P(GROUP, DP, None, None),
        P(GROUP, None, DP),
        P(DP, None),
        P(DP, GROUP, None),
        P(DP, CTX, None),
    )
    fixed = tuple(mesh.shape[a] for a in (DP, CTX, EXP)) == (4, 2, 4)
    return jax.shard_map(
        fixed_body if fixed else general_body,
        mesh=mesh,
        in_specs=placed,
        out_specs=(
            P(DP, GROUP, None),
            P(DP, GROUP, None),
            P(PLANE),
            P(PLANE, None, EXP),
            P(None, EXP, PLANE),
            P(EXP, PLANE),
            P(PLANE),
            P(PLANE, None),
            P(PLANE),
            P(PLANE, None, EXP),
            P(EXP, PLANE),
            P(GROUP, DP, None, None),
            P(GROUP, None, DP),
        ),
        check_vma=False,
    )
```

```python
from types import SimpleNamespace

import jax
import jax.numpy as jnp
import numpy as np
from jax import lax
from jax.experimental import pallas as pl
from jax.experimental.pallas import tpu as pltpu
from jax.sharding import PartitionSpec as P

highest = lax.Precision.HIGHEST
epsilon = 1e-06
rope_base = 1000000.0
f32 = jnp.float32
bf16 = jnp.bfloat16
DP, CTX, EXP = "dp", "context", "expert"
PLANE, GROUP = (DP, CTX), (CTX, EXP)


def rotary_tables(first_row, row_count, head_size):
    exponent = jnp.arange(head_size // 2).astype(jnp.float32) * (2.0 / head_size)
    frequency = rope_base ** (-exponent)
    positions = (first_row + jnp.arange(row_count, dtype=jnp.int32)).astype(jnp.float32)
    angles = positions[:, None] * frequency[None, :]
    return (jnp.cos(angles)[:, None, :], jnp.sin(angles)[:, None, :])


def rotate(values, cosine, sine_table):
    half_size = values.shape[-1] // 2
    first_half = values[..., :half_size]
    second_half = values[..., half_size:]
    return jnp.concatenate(
        [
            first_half * cosine - second_half * sine_table,
            second_half * cosine + first_half * sine_table,
        ],
        axis=-1,
    )


def rotate_back(grad_values, cosine, sine_table):
    half_size = grad_values.shape[-1] // 2
    first_half = grad_values[..., :half_size]
    second_half = grad_values[..., half_size:]
    return jnp.concatenate(
        [
            first_half * cosine + second_half * sine_table,
            second_half * cosine - first_half * sine_table,
        ],
        axis=-1,
    )


def gated_grads(gate_part, up_part, grad_act):
    sigmoid_gate = jax.nn.sigmoid(gate_part)
    grad_gate = grad_act * up_part * sigmoid_gate * (1.0 + gate_part * (1.0 - sigmoid_gate))
    grad_up = grad_act * gate_part * sigmoid_gate
    return (grad_gate, grad_up)


def masked_scores(queries, all_keys, allowed, score_scale):
    scores = (
        jnp.einsum("qhd,khd->hqk", queries, all_keys, preferred_element_type=jnp.float32)
        * score_scale
    )
    return jnp.where(allowed[None], scores, -1e30)


def fetch_dense(
    norm1_gain, w_qkv, w_out, norm2_gain, w_router, shared_gate, w_shared_in, w_shared_out
):
    return (
        lax.all_gather(norm1_gain, PLANE, axis=0, tiled=True),
        lax.all_gather(w_qkv, PLANE, axis=0, tiled=True),
        lax.all_gather(w_out, PLANE, axis=1, tiled=True),
        lax.all_gather(norm2_gain, PLANE, axis=0, tiled=True),
        lax.all_gather(w_router, PLANE, axis=0, tiled=True),
        lax.all_gather(shared_gate, PLANE, axis=0, tiled=True),
        lax.all_gather(w_shared_in, PLANE, axis=0, tiled=True),
        lax.all_gather(w_shared_out, PLANE, axis=1, tiled=True),
    )


def fetch_experts(w_expert_in, w_expert_out):
    return (
        lax.all_gather(w_expert_in, DP, axis=1, tiled=True),
        lax.all_gather(w_expert_out, DP, axis=2, tiled=True),
    )


def fetch_keys(key_rows, value_rows):
    return (
        lax.all_gather(key_rows, CTX, axis=0, tiled=True),
        lax.all_gather(value_rows, CTX, axis=0, tiled=True),
    )


def general_body(
    tokens,
    norm1_gain,
    w_qkv,
    b_qkv,
    w_out,
    norm2_gain,
    w_router,
    shared_gate,
    w_shared_in,
    w_shared_out,
    w_expert_in,
    w_expert_out,
    block_ids,
    expert_ids,
    out_grad,
):
    token_rows = tokens[0]
    rows_local, model_width = token_rows.shape
    lane_count = lax.axis_size(EXP)
    quarter = rows_local // lane_count
    first_row = lax.axis_index(CTX) * rows_local
    own_row = lax.axis_index(EXP) * quarter
    sequence_ids = block_ids[0]
    chosen = expert_ids[0]
    top_count = chosen.shape[1]
    heads_local = b_qkv.shape[1]
    head_size = b_qkv.shape[2]
    dense_full = fetch_dense(
        norm1_gain, w_qkv, w_out, norm2_gain, w_router, shared_gate, w_shared_in, w_shared_out
    )
    (
        gain_one,
        qkv_weight,
        out_weight,
        gain_two,
        router_weight,
        gate_vector,
        shared_in,
        shared_out,
    ) = dense_full
    expert_pair = fetch_experts(w_expert_in, w_expert_out)
    expert_in = expert_pair[0][0]
    expert_back = expert_pair[1][0]
    ffe_width = expert_in.shape[2]
    experts = router_weight.shape[1]
    capacity = max(2, 3 * quarter * top_count // (2 * experts))
    tokens_wide = token_rows.astype(jnp.float32)
    inverse_one = lax.rsqrt(jnp.mean(tokens_wide * tokens_wide, axis=-1, keepdims=True) + epsilon)
    normed = (tokens_wide * inverse_one * gain_one.astype(jnp.float32)).astype(jnp.bfloat16)
    linear = jnp.dot(
        normed, qkv_weight.reshape(model_width, -1), preferred_element_type=jnp.float32
    )
    linear = linear.reshape(rows_local, 3, heads_local, head_size) + b_qkv.astype(jnp.float32)[None]
    cosine, sine_table = rotary_tables(first_row, rows_local, head_size)
    queries = rotate(linear[:, 0], cosine, sine_table).astype(jnp.bfloat16)
    key_rows = rotate(linear[:, 1], cosine, sine_table).astype(jnp.bfloat16)
    value_rows = linear[:, 2].astype(jnp.bfloat16)
    all_keys, all_values = fetch_keys(key_rows, value_rows)
    query_ids = lax.dynamic_slice_in_dim(sequence_ids, first_row, rows_local)
    allowed = sequence_ids[None, :] <= query_ids[:, None]
    score_scale = head_size ** (-0.5)
    scores = masked_scores(queries, all_keys, allowed, score_scale)
    row_peak = jnp.max(scores, axis=-1, keepdims=True)
    log_total = row_peak + jnp.log(jnp.sum(jnp.exp(scores - row_peak), axis=-1, keepdims=True))
    weights = jnp.exp(scores - log_total).astype(jnp.bfloat16)
    attended = jnp.einsum("hqk,khd->qhd", weights, all_values, preferred_element_type=jnp.float32)
    attended_low = attended.astype(jnp.bfloat16).reshape(rows_local, heads_local * head_size)
    attention = lax.psum(
        jnp.dot(attended_low, out_weight, preferred_element_type=jnp.float32).astype(jnp.bfloat16),
        EXP,
    ).astype(jnp.float32)
    hidden = tokens_wide + attention
    inverse_two = lax.rsqrt(jnp.mean(hidden * hidden, axis=-1, keepdims=True) + epsilon)
    routed = (hidden * inverse_two * gain_two.astype(jnp.float32)).astype(jnp.bfloat16)
    shared_up = jnp.dot(
        routed, shared_in.reshape(model_width, -1), preferred_element_type=jnp.float32
    )
    shared_up = shared_up.reshape(rows_local, 2, -1)
    shared_act = (jax.nn.silu(shared_up[:, 0]) * shared_up[:, 1]).astype(jnp.bfloat16)
    shared_part = jnp.dot(shared_act, shared_out, preferred_element_type=jnp.float32)
    shared_rows = lax.psum_scatter(
        shared_part.astype(jnp.bfloat16), EXP, scatter_dimension=0, tiled=True
    ).astype(jnp.float32)
    shared_weight = jax.nn.sigmoid(jnp.dot(routed, gate_vector, preferred_element_type=jnp.float32))
    routed_own = lax.dynamic_slice_in_dim(routed, own_row, quarter)
    hidden_own = lax.dynamic_slice_in_dim(hidden, own_row, quarter)
    weight_own = lax.dynamic_slice_in_dim(shared_weight, own_row, quarter)
    logits = jnp.dot(routed_own, router_weight, preferred_element_type=jnp.float32)
    probability = jax.nn.softmax(logits, axis=-1)
    expert_match = (chosen[..., None] == jnp.arange(experts, dtype=jnp.int32)).astype(jnp.float32)
    gate_values = jnp.sum(probability[:, None, :] * expert_match, axis=-1)
    flat_ids = chosen.reshape(-1)
    onehot = (flat_ids[:, None] == jnp.arange(experts, dtype=jnp.int32)).astype(jnp.int32)
    slot_rank = jnp.sum((jnp.cumsum(onehot, axis=0) - onehot) * onehot, axis=-1)
    slot_index = flat_ids * capacity + slot_rank
    placement = (slot_index[:, None] == jnp.arange(experts * capacity, dtype=jnp.int32)).astype(
        jnp.bfloat16
    )
    repeated = jnp.repeat(routed_own, top_count, axis=0)
    outgoing = jnp.einsum("sr,sd->rd", placement, repeated, preferred_element_type=jnp.float32)
    outgoing = outgoing.astype(jnp.bfloat16).reshape(experts, capacity, model_width)
    incoming = lax.all_to_all(
        outgoing, GROUP, split_axis=0, concat_axis=0, tiled=True
    )
    flat_rows = incoming.reshape(-1, model_width)
    gate_up = jnp.dot(
        flat_rows, expert_in.reshape(model_width, -1), preferred_element_type=jnp.float32
    ).reshape(-1, 2, ffe_width)
    activated = (jax.nn.silu(gate_up[:, 0]) * gate_up[:, 1]).astype(jnp.bfloat16)
    result = jnp.dot(activated, expert_back, preferred_element_type=jnp.float32).astype(
        jnp.bfloat16
    )
    expert_result = result.reshape(incoming.shape)
    returned = lax.all_to_all(
        expert_result, GROUP, split_axis=0, concat_axis=0, tiled=True
    )
    picked = jnp.dot(
        placement, returned.reshape(-1, model_width), preferred_element_type=jnp.float32
    )
    picked = picked.reshape(quarter, top_count, model_width)
    combined = jnp.sum(gate_values[..., None] * picked, axis=1)
    result_rows = hidden_own + combined + weight_own[:, None] * shared_rows
    output = result_rows.astype(jnp.bfloat16)[None]
    (
        gain_one_b,
        qkv_weight_b,
        out_weight_b,
        gain_two_b,
        router_weight_b,
        gate_vector_b,
        shared_in_b,
        shared_out_b,
    ) = dense_full
    expert_in_b = expert_pair[0][0]
    expert_back_b = expert_pair[1][0]
    grad_full = out_grad[0].astype(jnp.float32)
    grad_own = lax.dynamic_slice_in_dim(grad_full, own_row, quarter)
    shared_grad = (shared_weight[:, None] * grad_full).astype(jnp.bfloat16)
    grad_shared_out = jnp.einsum(
        "tf,td->fd", shared_act, shared_grad, preferred_element_type=jnp.float32
    )
    grad_shared_act = jnp.einsum(
        "td,fd->tf", shared_grad, shared_out_b, preferred_element_type=jnp.float32
    )
    shared_gate_grad, shared_up_grad = gated_grads(
        shared_up[:, 0], shared_up[:, 1], grad_shared_act
    )
    grad_shared_up = jnp.stack([shared_gate_grad, shared_up_grad], axis=1).astype(jnp.bfloat16)
    grad_shared_in = jnp.einsum(
        "td,tkf->dkf", routed, grad_shared_up, preferred_element_type=jnp.float32
    )
    grad_routed = jnp.einsum(
        "tkf,dkf->td", grad_shared_up, shared_in_b, preferred_element_type=jnp.float32
    )
    gate_slope = jnp.sum(grad_own * shared_rows, axis=-1) * weight_own * (1.0 - weight_own)
    grad_gate_vector = jnp.dot(gate_slope, routed_own.astype(jnp.float32), precision=highest)
    grad_own_routed = gate_slope[:, None] * gate_vector_b.astype(jnp.float32)[None]
    grad_gates = jnp.sum(grad_own[:, None, :] * picked, axis=-1)
    grad_slots = (
        (gate_values[..., None] * grad_own[:, None, :])
        .astype(jnp.bfloat16)
        .reshape(-1, model_width)
    )
    grad_send = jnp.einsum("sr,sd->rd", placement, grad_slots, preferred_element_type=jnp.float32)
    grad_send = grad_send.astype(jnp.bfloat16).reshape(experts, capacity, model_width)
    grad_arrived = lax.all_to_all(
        grad_send, GROUP, split_axis=0, concat_axis=0, tiled=True
    )
    arrived_rows = incoming.reshape(-1, model_width)
    arrived_grad = grad_arrived.reshape(-1, model_width)
    expert_up = jnp.dot(
        arrived_rows, expert_in_b.reshape(model_width, -1), preferred_element_type=jnp.float32
    ).reshape(-1, 2, ffe_width)
    expert_act = (jax.nn.silu(expert_up[:, 0]) * expert_up[:, 1]).astype(jnp.bfloat16)
    grad_expert_back = jnp.einsum(
        "rf,rd->fd", expert_act, arrived_grad, preferred_element_type=jnp.float32
    )
    grad_expert_act = jnp.einsum(
        "rd,fd->rf", arrived_grad, expert_back_b, preferred_element_type=jnp.float32
    )
    expert_gate_grad, expert_up_grad = gated_grads(
        expert_up[:, 0], expert_up[:, 1], grad_expert_act
    )
    grad_expert_up = jnp.stack([expert_gate_grad, expert_up_grad], axis=1).astype(jnp.bfloat16)
    grad_expert_in = jnp.einsum(
        "rd,rkf->dkf", arrived_rows, grad_expert_up, preferred_element_type=jnp.float32
    )
    grad_arrived_rows = jnp.einsum(
        "rkf,dkf->rd", grad_expert_up, expert_in_b, preferred_element_type=jnp.float32
    )
    grad_arrived_rows = grad_arrived_rows.astype(jnp.bfloat16).reshape(
        experts, capacity, model_width
    )
    grad_returned = lax.all_to_all(
        grad_arrived_rows, GROUP, split_axis=0, concat_axis=0, tiled=True
    )
    grad_copies = jnp.dot(
        placement, grad_returned.reshape(-1, model_width), preferred_element_type=jnp.float32
    )
    grad_own_routed = grad_own_routed + jnp.sum(
        grad_copies.reshape(quarter, top_count, model_width), axis=1
    )
    grad_probability = jnp.sum(grad_gates[..., None] * expert_match, axis=1)
    grad_logits = probability * (
        grad_probability - jnp.sum(probability * grad_probability, axis=-1, keepdims=True)
    )
    grad_router = jnp.dot(routed_own.astype(jnp.float32).T, grad_logits, precision=highest)
    grad_own_routed = grad_own_routed + jnp.dot(
        grad_logits, router_weight_b.astype(jnp.float32).T, precision=highest
    )
    own_part = lax.dynamic_slice_in_dim(grad_routed, own_row, quarter) + grad_own_routed
    grad_routed = lax.dynamic_update_slice_in_dim(grad_routed, own_part, own_row, 0)
    grad_routed, grad_router, grad_gate_vector = (
        lax.psum(grad_routed.astype(jnp.bfloat16), EXP).astype(jnp.float32),
        lax.psum(grad_router.astype(jnp.bfloat16), EXP).astype(jnp.float32),
        lax.psum(grad_gate_vector.astype(jnp.bfloat16), EXP).astype(jnp.float32),
    )
    scaled_two = grad_routed * gain_two_b.astype(jnp.float32)
    grad_gain_two = jnp.sum(grad_routed * hidden * inverse_two, axis=0)
    grad_hidden = (
        grad_full
        + inverse_two * scaled_two
        - hidden * inverse_two**3 * jnp.mean(scaled_two * hidden, axis=-1, keepdims=True)
    )
    grad_hidden_low = grad_hidden.astype(jnp.bfloat16)
    grad_out_weight = jnp.einsum(
        "tn,td->nd", attended_low, grad_hidden_low, preferred_element_type=jnp.float32
    )
    grad_attended = jnp.einsum(
        "td,nd->tn", grad_hidden_low, out_weight_b, preferred_element_type=jnp.float32
    )
    grad_attended = grad_attended.astype(jnp.bfloat16).reshape(rows_local, heads_local, head_size)
    back_keys, back_values = (all_keys, all_values)
    scores_again = masked_scores(queries, back_keys, allowed, score_scale)
    weights_wide = jnp.exp(scores_again - log_total)
    row_delta = jnp.sum(grad_attended.astype(jnp.float32) * attended, axis=-1).T
    grad_weights = jnp.einsum(
        "qhd,khd->hqk", grad_attended, back_values, preferred_element_type=jnp.float32
    )
    grad_scores = (weights_wide * (grad_weights - row_delta[..., None])).astype(jnp.bfloat16)
    grad_queries = (
        jnp.einsum("hqk,khd->qhd", grad_scores, back_keys, preferred_element_type=jnp.float32)
        * score_scale
    )
    grad_keys = (
        jnp.einsum("hqk,qhd->khd", grad_scores, queries, preferred_element_type=jnp.float32)
        * score_scale
    )
    grad_values = jnp.einsum(
        "hqk,qhd->khd",
        weights_wide.astype(jnp.bfloat16),
        grad_attended,
        preferred_element_type=jnp.float32,
    )
    grad_keys, grad_values = (
        lax.psum_scatter(
            grad_keys.astype(jnp.bfloat16), CTX, scatter_dimension=0, tiled=True
        ).astype(jnp.float32),
        lax.psum_scatter(
            grad_values.astype(jnp.bfloat16), CTX, scatter_dimension=0, tiled=True
        ).astype(jnp.float32),
    )
    grad_linear = jnp.stack(
        [
            rotate_back(grad_queries, cosine, sine_table),
            rotate_back(grad_keys, cosine, sine_table),
            grad_values,
        ],
        axis=1,
    )
    grad_linear = grad_linear.astype(jnp.bfloat16)
    grad_bias = jnp.sum(grad_linear.astype(jnp.float32), axis=0)
    grad_flat = grad_linear.reshape(rows_local, -1)
    grad_qkv = jnp.einsum(
        "td,tn->dn", normed, grad_flat, preferred_element_type=jnp.float32
    ).reshape(qkv_weight_b.shape)
    grad_normed = jnp.einsum(
        "tn,dn->td",
        grad_flat,
        qkv_weight_b.reshape(model_width, -1),
        preferred_element_type=jnp.float32,
    )
    grad_normed = lax.psum(grad_normed.astype(jnp.bfloat16), EXP).astype(jnp.float32)
    scaled_one = grad_normed * gain_one_b.astype(jnp.float32)
    grad_gain_one = jnp.sum(grad_normed * tokens_wide * inverse_one, axis=0)
    grad_tokens = (
        grad_hidden
        + inverse_one * scaled_one
        - tokens_wide * inverse_one**3 * jnp.mean(scaled_one * tokens_wide, axis=-1, keepdims=True)
    )
    grad_tokens_own = lax.dynamic_slice_in_dim(grad_tokens, own_row, quarter).astype(jnp.bfloat16)[
        None
    ]
    dense_sums = (
        lax.psum_scatter(
            grad_gain_one.astype(jnp.bfloat16), PLANE, scatter_dimension=0, tiled=True
        ).astype(jnp.float32),
        lax.psum_scatter(
            grad_qkv.astype(jnp.bfloat16), PLANE, scatter_dimension=0, tiled=True
        ).astype(jnp.float32),
        lax.psum_scatter(
            grad_bias.astype(jnp.bfloat16), PLANE, scatter_dimension=2, tiled=True
        ).astype(jnp.float32),
        lax.psum_scatter(
            grad_out_weight.astype(jnp.bfloat16), PLANE, scatter_dimension=1, tiled=True
        ).astype(jnp.float32),
        lax.psum_scatter(
            grad_gain_two.astype(jnp.bfloat16), PLANE, scatter_dimension=0, tiled=True
        ).astype(jnp.float32),
        lax.psum_scatter(
            grad_router.astype(jnp.bfloat16), PLANE, scatter_dimension=0, tiled=True
        ).astype(jnp.float32),
        lax.psum_scatter(
            grad_gate_vector.astype(jnp.bfloat16),
            PLANE,
            scatter_dimension=0,
            tiled=True,
        ).astype(jnp.float32),
        lax.psum_scatter(
            grad_shared_in.astype(jnp.bfloat16), PLANE, scatter_dimension=0, tiled=True
        ).astype(jnp.float32),
        lax.psum_scatter(
            grad_shared_out.astype(jnp.bfloat16), PLANE, scatter_dimension=1, tiled=True
        ).astype(jnp.float32),
    )
    expert_sums = (
        lax.psum_scatter(
            grad_expert_in[None].astype(jnp.bfloat16), DP, scatter_dimension=1, tiled=True
        ).astype(jnp.float32),
        lax.psum_scatter(
            grad_expert_back[None].astype(jnp.bfloat16), DP, scatter_dimension=2, tiled=True
        ).astype(jnp.float32),
    )
    return (
        output,
        grad_tokens_own,
        dense_sums[0].astype(jnp.bfloat16),
        dense_sums[1].astype(jnp.bfloat16),
        dense_sums[2].astype(jnp.bfloat16),
        dense_sums[3].astype(jnp.bfloat16),
        dense_sums[4].astype(jnp.bfloat16),
        dense_sums[5].astype(jnp.bfloat16),
        dense_sums[6].astype(jnp.bfloat16),
        dense_sums[7].astype(jnp.bfloat16),
        dense_sums[8].astype(jnp.bfloat16),
        expert_sums[0].astype(jnp.bfloat16),
        expert_sums[1].astype(jnp.bfloat16),
    )


MIB = 1 << 20
CUT = 192
MESH = pl.DeviceIdType.MESH


def dot_nn(a, b):
    return lax.dot_general(a, b, (((1,), (0,)), ((), ())), preferred_element_type=f32)


def dot_nt(a, b):
    return lax.dot_general(a, b, (((1,), (1,)), ((), ())), preferred_element_type=f32)


def dot_tn(a, b):
    return lax.dot_general(a, b, (((0,), (0,)), ((), ())), preferred_element_type=f32)


def place():
    i = lax.axis_index(DP)
    return i // 2, i % 2, lax.axis_index(CTX), lax.axis_index(EXP)


def owner_dense(r):
    x, c, y, _ = place()
    return (((x + r % 2) % 2) * 2 + (c + r // 4) % 2) * 2 + (y + (r // 2) % 2) % 2


def owner_expert(r):
    x, c, _, _ = place()
    return ((x + r % 2) % 2) * 2 + (c + r // 2) % 2


def near(d):
    z = lax.axis_index(EXP)
    return ((z // 2 + d // 2) % 2) * 2 + (z % 2 + d % 2) % 2


def peers():
    x, c, y, _ = place()
    far = [{EXP: near(d)} for d in (1, 2, 3)]
    return {DP: ((x + 1) % 2) * 2 + c}, {CTX: 1 - y}, {DP: x * 2 + (c + 1) % 2}, far


def greet(devices):
    barrier = pltpu.get_barrier_semaphore()
    for device in devices:
        pl.semaphore_signal(barrier, 1, device_id=device, device_id_type=MESH)
    pl.semaphore_wait(barrier, len(devices))


class Wire:
    def __init__(self, wires, ends, device):
        self.ends, self.device, self.sent = ends, device, False
        self.send, self.recv, self.k = wires.send, wires.recv, len(wires.copies)
        wires.copies.append(self)

    def copy(self):
        source, target = self.ends()
        return pltpu.make_async_remote_copy(
            src_ref=source,
            dst_ref=target,
            send_sem=self.send.at[self.k],
            recv_sem=self.recv.at[self.k],
            device_id=self.device,
            device_id_type=MESH,
        )

    def start(self):
        self.copy().start()
        return self

    def wait_recv(self):
        self.copy().wait_recv()

    def wait_send(self):
        self.copy().wait_send()
        self.sent = True


class Wires:
    def __init__(self, send, recv):
        self.send, self.recv, self.copies = send, recv, []

    def add(self, ends, device):
        return Wire(self, ends, device)

    def go(self, ends, device):
        return Wire(self, ends, device).start()

    def drain(self):
        for wire in self.copies:
            if not wire.sent:
                wire.wait_send()


class Loads:
    def __init__(self, sems):
        self.sems, self.count = sems, 0

    def go(self, source, target):
        copy = pltpu.make_async_copy(source, target, self.sems.at[self.count])
        self.count += 1
        copy.start()
        return copy


def cols(ref, block, width):
    return ref[:, pl.ds(pl.multiple_of(block * width, width), width)]


def piece(ref, d, rows):
    return ref[pl.ds(pl.multiple_of(near(d) * rows, rows), rows), :]


def turn(values, cosine, sine):
    return values * cosine + pltpu.roll(values, 64, 1) * sine


def turn_back(values, cosine, sine):
    return values * cosine - pltpu.roll(values, 64, 1) * sine


def gated(gate, up, grad_act):
    s = jax.nn.sigmoid(gate)
    act = gate * s
    return act * up, grad_act * up * s * (1.0 + gate * (1.0 - s)), grad_act * act


def softmax_parts(q, k_own, k_oth, mask_own, mask_oth):
    scale = 128 ** (-0.5)
    s_own = jnp.where(mask_own, dot_nt(q, k_own) * scale, -1e30)
    s_oth = jnp.where(mask_oth, dot_nt(q, k_oth) * scale, -1e30)
    peak = jnp.maximum(
        jnp.max(s_own, axis=-1, keepdims=True), jnp.max(s_oth, axis=-1, keepdims=True)
    )
    e_own = jnp.exp(s_own - peak)
    e_oth = jnp.exp(s_oth - peak)
    total = jnp.sum(e_own, axis=-1, keepdims=True) + jnp.sum(e_oth, axis=-1, keepdims=True)
    back = 1.0 / total
    return e_own * back, e_oth * back


def split3(v):
    high = v.astype(bf16).astype(f32)
    mid = (v - high).astype(bf16).astype(f32)
    return high, mid, v - high - mid


def probabilities(rows, small):
    logits = dot_nt(rows, small[...])
    lane = lax.broadcasted_iota(jnp.int32, logits.shape, 1)
    logits = jnp.where((lane >= 3) & (lane < 11), logits, -1e30)
    e = jnp.exp(logits - jnp.max(logits, axis=-1, keepdims=True))
    return e / jnp.sum(e, axis=-1, keepdims=True), lane


ARRIVAL = (0, 4, 1, 5, 2, 6, 3, 7)


class Spread:
    def __init__(self, wires, own, slots, dense):
        x, y, core, _ = peers()
        self.slots, self.own, self.copies = slots, own, {}

        def ends(r, target):
            return lambda: (self.block(r), slots.at[target])

        self.copies[1] = wires.add(ends(0, 1), x)
        if dense:
            self.copies[2] = wires.add(ends(0, 2), y)
            self.copies[3] = wires.add(ends(1, 3), y)
        side = 4 if dense else 2
        for r in range(side):
            self.copies[side + r] = wires.add(ends(r, side + r), core)

    def block(self, r):
        return self.own() if r == 0 else self.slots.at[r]

    def start(self, r):
        self.copies[r].start()

    def wait(self, r):
        self.copies[r].wait_recv()


V, A = "vmem", "any"


def call(kernel, number, ins, outs, scratch, vmem, flops, traffic):
    def spec(kind):
        return pl.BlockSpec(memory_space=pl.ANY if kind == A else pltpu.VMEM)

    names = list(ins) + list(outs) + list(scratch)

    def run(*refs):
        kernel(SimpleNamespace(**dict(zip(names, refs))))

    made = pl.pallas_call(
        run,
        out_shape=tuple(jax.ShapeDtypeStruct(o[0], o[1]) for o in outs.values()),
        in_specs=[spec(i[1]) for i in ins.values()],
        out_specs=tuple(spec(o[2]) for o in outs.values()),
        scratch_shapes=list(scratch.values()),
        compiler_params=pltpu.CompilerParams(
            vmem_limit_bytes=vmem * MIB, collective_id=number, has_side_effects=number is not None
        ),
        cost_estimate=pl.CostEstimate(flops=flops, bytes_accessed=traffic, transcendentals=0),
    )(*[i[0] for i in ins.values()])
    return SimpleNamespace(**dict(zip(outs, made)))


def own_rows(total, hidden, routed, g, small, high_o, low_o, vec_o):
    extra = total[:, 2048:2176]
    wide = routed.astype(f32)
    prob, _ = probabilities(routed, small)
    sw = jax.nn.sigmoid(jnp.sum(wide * small[2:3, :].astype(f32), axis=-1, keepdims=True))
    slope = jnp.sum(extra[:, 48:96], axis=-1, keepdims=True) * sw * (1.0 - sw)
    dgate = [
        extra[:, e : e + 1] + extra[:, 16 + e : 17 + e] + extra[:, 32 + e : 33 + e]
        for e in range(8)
    ]
    probs = [prob[:, 3 + e : 4 + e] for e in range(8)]
    mean = sum(p * d for p, d in zip(probs, dgate))
    grad = total[:, 0:2048] + slope * small[2:3, :].astype(f32)
    vec_o[...] = jnp.zeros_like(vec_o)
    vec_o[2:3, :] = jnp.sum(slope * wide, axis=0, keepdims=True)
    for e in range(8):
        dlogit = probs[e] * (dgate[e] - mean)
        grad += dlogit * small[3 + e : 4 + e, :].astype(f32)
        vec_o[3 + e : 4 + e, :] = jnp.sum(dlogit * wide, axis=0, keepdims=True)
    inv = lax.rsqrt(jnp.mean(hidden * hidden, axis=-1, keepdims=True) + epsilon)
    vec_o[1:2, :] = jnp.sum(grad * hidden * inv, axis=0, keepdims=True)
    scaled = grad * small[1:2, :].astype(f32)
    mean = jnp.mean(scaled * hidden, axis=-1, keepdims=True)
    high = g.astype(f32) + inv * scaled - hidden * (inv * inv * inv * mean)
    high_o[...] = high
    low_o[...] = high.astype(bf16)


def layer_kernel(k):
    x_dev, y_dev, core_dev, z_dev = peers()
    wires, loads = Wires(k.send_sems, k.recv_sems), Loads(k.load_sems)
    inputs = [
        loads.go(a, b)
        for a, b in (
            (k.one_in, k.gain_one),
            (k.two_in, k.gain_two),
            (k.gate_in, k.gate_vector),
            (k.router_in, k.router),
            (k.ids_in, k.ids_own),
            (k.blocks_in, k.blocks),
            (k.tok_in, k.tok),
            (k.bias_in, k.bias),
            (k.cs_in, k.cs_all),
            (k.sn_in, k.sn_all),
            (k.g_in, k.g_own),
        )
    ]
    greet([x_dev, y_dev, core_dev] + z_dev)
    y = lax.axis_index(CTX)
    mine = y * 4 + lax.axis_index(EXP)

    def to_z(make):
        return [wires.go(make(d), z_dev[d - 1]) for d in (1, 2, 3)]

    class Collect:
        def __init__(self, slot):
            self.slot = slot
            self.one = wires.go(lambda: (slot(0), slot(1)), z_dev[0])
            self.three = wires.go(lambda: (slot(0), slot(3)), z_dev[2])

        def hand_on(self):
            self.three.wait_recv()
            self.two = wires.go(lambda: (self.slot(3), self.slot(2)), z_dev[0])

        def wait(self):
            self.one.wait_recv()
            self.two.wait_recv()

    vec = Spread(wires, lambda: k.w_v, k.s_v, True)
    qkv = Spread(wires, lambda: k.w_q, k.s_q, True)
    out = Spread(wires, lambda: k.w_o, k.s_o, True)
    eg = Spread(wires, lambda: k.split_ei.at[0], k.s_eg, False)
    eu = Spread(wires, lambda: k.split_ei.at[1], k.s_eu, False)
    ed = Spread(wires, lambda: k.w_ed, k.s_ed, False)
    sg = Spread(wires, lambda: k.split_si.at[0], k.s_sg, True)
    su = Spread(wires, lambda: k.split_si.at[1], k.s_su, True)
    sd = Spread(wires, lambda: k.w_sd, k.s_sd, True)
    first, expert, shared = (vec, qkv), (eg, eu, ed), (sg, su, sd)
    qkv.start(1)
    qkv.start(2)
    k.w_v[...] = jnp.zeros_like(k.w_v)
    for copy in inputs[:6]:
        copy.wait()
    for m, vector in enumerate((k.gain_one, k.gain_two, k.gate_vector)):
        k.w_v[m : m + 1, :] = vector[...].reshape(1, 256)
    k.w_v[3:11, :] = k.router[...]
    for s in (vec, out, ed):
        s.start(1)
    vec.start(2)
    for s in (qkv, out, vec):
        s.start(4)
    k.col[0:128, :] = jnp.full((128, 128), -1.0, f32)
    k.col[0:4, 0:64] = k.ids_own[...].astype(f32)
    k.ids[0, 0:64, :] = k.col[0:128, :].T[0:64, :]
    ids_y = wires.go(lambda: (k.ids.at[0, pl.ds(0, 64), :], k.ids_y), y_dev)
    k.s_v[0] = k.w_v[...]
    for copy in inputs[6:]:
        copy.wait()
    k.col[...] = jnp.broadcast_to(k.blocks[...].astype(f32), (128, 512)).T
    for target, half in ((k.ids_near, y), (k.ids_far, 1 - y)):
        for d in range(4):
            at = pl.ds(pl.multiple_of(half * 256 + near(d) * 64, 64), 64)
            k.ids_q[d * 64 : (d + 1) * 64, :] = k.col[at, :]
        target[...] = k.ids_q[...].T[0:8, :]
    for d in range(4):
        at = pl.ds(pl.multiple_of(y * 256 + near(d) * 64, 64), 64)
        to = slice(d * 64, (d + 1) * 64)
        k.ids_q[to, :] = k.col[at, :]
        k.cs[to, :] = k.cs_all[at, :]
        k.sn[to, :] = k.sn_all[at, :]
    later = []

    def attention_part(scaled, acc, w, low_w, mixed, apart):
        held, held_out = {}, []

        def bring(r):
            held[r] = loads.go(qkv.block(r), w.at[r])

        def bring_out(r):
            held_out.append(loads.go(out.block(r), low_w.at[r]))

        raw = [loads.go(k.w_ei.at[pl.ds(256 * m, 256)], mixed.at[m]) for m in range(2)]
        raw.append(loads.go(k.w_si, mixed.at[2]))
        bring(0)
        for d in range(4):
            t = piece(k.tok, d, 64).astype(f32)
            inv = lax.rsqrt(jnp.mean(t * t, axis=-1, keepdims=True) + epsilon)
            scaled[d * 64 : (d + 1) * 64, :] = t * inv
            k.inv1[d * 64 : (d + 1) * 64, :] = inv
        for m in range(3):
            for h in range(4):
                at = slice(h * 128, (h + 1) * 128)
                line = k.bias[m, h : h + 1, :].astype(f32)
                acc[m, :, at] = jnp.broadcast_to(line, (256, 128))

        def take_apart(m):
            raw[m].wait()
            target = k.split_si if m == 2 else k.split_ei
            to = pl.ds(0 if m == 2 else 256 * m, 256)
            done = []
            for n in range(2):
                apart[m, n] = mixed[m, :, n, :]
                done.append(loads.go(apart.at[m, n], target.at[n, to, :]))
            return done

        done = take_apart(0) + take_apart(1)
        for copy in done:
            copy.wait()
        for s in (eg, eu):
            s.start(1)
        for s in expert:
            s.start(2)

        def block(r):
            held[r].wait()
            o = owner_dense(r)
            vectors = k.s_v[r]
            k.small[:, pl.ds(pl.multiple_of(o * 256, 256), 256)] = vectors
            normed = (cols(scaled, o, 256) * vectors[0:1, :].astype(f32)).astype(bf16)
            target = k.n_keep if r < 4 else k.n_send
            target[:, (r % 4) * 256 : (r % 4 + 1) * 256] = normed
            for m in range(3):
                acc[m] += dot_nn(normed, w[r, m * 256 : (m + 1) * 256, :])

        def arrived(r, onward=()):
            for s in first:
                s.wait(r)
                for t in onward:
                    s.start(t)
            bring(r)

        arrived(4)
        block(0)
        block(4)
        arrived(1, (3, 5))
        out.start(2)
        arrived(2, (6,))
        block(1)
        arrived(5)
        block(5)
        arrived(6)
        block(2)
        block(6)
        for copy in take_apart(2):
            copy.wait()
        for s in shared:
            s.start(1)
        for s in shared:
            s.start(4)
        ids_y.wait_recv()
        k.ids[0, 64:128, :] = k.ids_y[...]
        later.extend(to_z(lambda d: lambda: (k.ids.at[0], k.ids.at[d])))
        bring_out(0)
        out.wait(4)
        bring_out(4)
        out.wait(1)
        out.start(5)
        bring_out(1)
        arrived(3, (7,))
        block(3)
        arrived(7)
        block(7)
        for h in range(4):
            at = slice(h * 128, (h + 1) * 128)
            k.kv[0:256, at] = turn(acc[1, :, at], k.cs[...], k.sn[...]).astype(bf16)
        k.kv[256:512, :] = acc[2].astype(bf16)
        kv_y = wires.go(lambda: (k.kv, k.kv_oth), y_dev)
        out.start(3)
        sg.start(2)
        su.start(2)
        for h in range(4):
            at = slice(h * 128, (h + 1) * 128)
            k.q[:, at] = turn(acc[0, :, at], k.cs[...], k.sn[...]).astype(bf16)
        out.wait(5)
        bring_out(5)
        out.wait(2)
        out.start(6)
        bring_out(2)
        kv_y.wait_recv()
        mask_own = k.ids_near[0:1, :] <= k.ids_q[:, 0:1]
        mask_oth = k.ids_far[0:1, :] <= k.ids_q[:, 0:1]
        for h in range(4):
            at = slice(h * 128, (h + 1) * 128)
            w_own, w_oth = softmax_parts(
                k.q[:, at], k.kv[0:256, at], k.kv_oth[0:256, at], mask_own, mask_oth
            )
            value = dot_nn(w_own.astype(bf16), k.kv[256:512, at])
            value += dot_nn(w_oth.astype(bf16), k.kv_oth[256:512, at])
            k.low[:, at] = value.astype(bf16)
        out.wait(6)
        bring_out(6)
        out.wait(3)
        out.start(7)
        bring_out(3)
        out.wait(7)
        bring_out(7)
        for copy in held_out:
            copy.wait()
        for r in range(8):
            part = dot_nn(k.low[...], low_w[r]).astype(bf16)
            at = pl.ds(pl.multiple_of(owner_dense(r) * 256, 256), 256)
            for d in range(4):
                k.att_send[d, :, at] = part[d * 64 : (d + 1) * 64, :]

    pl.run_scoped(
        attention_part,
        pltpu.VMEM((256, 2048), f32),
        pltpu.VMEM((3, 256, 512), f32),
        pltpu.VMEM((8, 768, 512), bf16),
        pltpu.VMEM((8, 512, 256), bf16),
        pltpu.VMEM((3, 256, 2, 1408), bf16),
        pltpu.VMEM((3, 2, 256, 1408), bf16),
    )
    att_two = wires.go(lambda: (k.att_send.at[2], k.att.at[1]), z_dev[0])
    att_one = wires.go(lambda: (k.att_send.at[1], k.att.at[0]), z_dev[0])
    swap_n = wires.go(lambda: (k.n_send, k.n_x), core_dev)
    swap_low = wires.go(lambda: (k.low, k.low_x), core_dev)
    parts = SimpleNamespace(started=False)

    def expert_part(wg, wu, wd, slopes, acc, up, keep, send):
        group = []

        def gather(s, w):
            group.append(loads.go(s.block(0), w.at[0]))
            s.wait(2)
            group.append(loads.go(s.block(2), w.at[2]))
            s.wait(1)
            s.start(3)
            group.append(loads.go(s.block(1), w.at[1]))

        def gather_last(s, w):
            s.wait(3)
            group.append(loads.go(s.block(3), w.at[3]))

        gather(ed, wd)
        att_two.wait_recv()
        pair = k.att_send[3].astype(f32) + k.att[1].astype(f32)
        k.att_pair[...] = pair.astype(bf16)
        att_three = wires.go(lambda: (k.att_pair, k.att.at[2]), z_dev[2])
        att_one.wait_recv()
        value = k.att_send[0].astype(f32) + k.att[0].astype(f32)
        att_three.wait_recv()
        value += piece(k.tok, 0, 64).astype(f32) + k.att[2].astype(f32)
        inv = lax.rsqrt(jnp.mean(value * value, axis=-1, keepdims=True) + epsilon)
        k.hidden[...] = value
        k.rows[0:64, :] = (value * inv * k.small[1:2, :].astype(f32)).astype(bf16)
        own_y = wires.go(
            lambda: (k.rows.at[pl.ds(0, 64), :], k.rows.at[pl.ds(256, 64), :]), y_dev
        )
        g_y = wires.go(lambda: (k.g_own, k.g_oth), y_dev)
        sd.start(2)
        own_z = Collect(lambda d: k.rows.at[pl.ds(64 * d, 64), :])
        gather_last(ed, wd)
        gather(eg, wg)
        gather_last(eg, wg)
        for s in (sg, su):
            s.wait(2)
            s.start(6)
        own_z.hand_on()
        for copy in later:
            copy.wait_recv()
        own_y.wait_recv()
        own_z.wait()
        oth_z = Collect(lambda d: k.rows.at[pl.ds(256 + 64 * d, 64), :])

        def g_piece(half, d, at):
            g = k.g_oth if half else k.g_own
            return g[pl.ds(pl.multiple_of(near(d) * 64, 64), 64), at].astype(f32)

        def route(half):
            chosen = []
            for d in range(4):
                named = (k.ids[d, half * 64 : (half + 1) * 64, :] == mine.astype(f32)).astype(f32)
                chosen.append(jnp.sum(named, axis=-1, keepdims=True))
            chosen = jnp.concatenate(chosen, axis=0)
            prob, lane = probabilities(k.rows[half * 256 : (half + 1) * 256, :], k.small)
            here = jnp.sum(jnp.where(lane == mine + 3, prob, 0.0), axis=-1, keepdims=True)
            gate = here * chosen
            for d in range(4):
                at = slice(half * 256 + d * 64, half * 256 + (d + 1) * 64)
                value = gate[d * 64 : (d + 1) * 64, :] * g_piece(half, d, slice(None))
                slopes[at, :] = value.astype(bf16)
            return gate, chosen

        def gate_part(half):
            rows_at = slice(half * 256, (half + 1) * 256)

            def one(r, _):
                at = pl.ds(pl.multiple_of(owner_expert(r) * 512, 512), 512)
                acc[0] += dot_nn(k.rows[rows_at, at], wg[r])
                acc[2] += dot_nt(slopes[rows_at, at], wd[r])
                return 0

            acc[...] = jnp.zeros_like(acc)
            lax.fori_loop(0, 4, one, 0)

        def phase_one(half):
            rows_at = slice(half * 256, (half + 1) * 256)

            def one(r, _):
                at = pl.ds(pl.multiple_of(owner_expert(r) * 512, 512), 512)
                acc[1] += dot_nn(k.rows[rows_at, at], wu[r])
                return 0

            lax.fori_loop(0, 4, one, 0)
            for d in range(4):
                at, to = slice(d * 64, (d + 1) * 64), slice(half * 256 + d * 64, half * 256 + (d + 1) * 64)
                act, gate_grad, up_grad = gated(acc[0, at, :], acc[1, at, :], acc[2, at, :])
                up[0, to, :] = act.astype(bf16)
                up[1, to, :] = gate_grad.astype(bf16)
                up[2, to, :] = up_grad.astype(bf16)

        lanes = lax.broadcasted_iota(jnp.int32, (64, 128), 1)

        def phase_two(half, gate, chosen):
            rows_at = slice(half * 256, (half + 1) * 256)

            def two(r, dgate):
                at = pl.ds(pl.multiple_of(owner_expert(r) * 512, 512), 512)
                result = dot_nn(up[0, rows_at, :], wd[r]).astype(bf16).astype(f32)
                grad = dot_nt(up[1, rows_at, :], wg[r]) + dot_nt(up[2, rows_at, :], wu[r])
                sums = []
                for d in range(4):
                    here = slice(d * 64, (d + 1) * 64)
                    g_rows = g_piece(half, d, at)
                    sums.append(jnp.sum(g_rows * result[here, :], axis=-1, keepdims=True))
                    part = gate[here, :] * result[here, :]
                    if half == 0:
                        k.out_sum[here, at] = part
                        k.grad_sum[here, at] = grad[here, :]
                    else:
                        k.e_out[d, :, at] = part.astype(bf16)
                        k.e_grad[d, :, at] = grad[here, :].astype(bf16)
                return dgate + jnp.concatenate(sums, axis=0)

            dgate = lax.fori_loop(0, 4, two, jnp.zeros((256, 1), f32)) * chosen
            for d in range(4):
                extra = jnp.zeros((64, 128), f32)
                for m, part in enumerate(split3(dgate[d * 64 : (d + 1) * 64, :])):
                    extra = jnp.where(lanes == mine + 16 * m, part, extra)
                if half == 0:
                    k.extras[d * 64 : (d + 1) * 64, :] = extra
                else:
                    k.e_grad[d, :, 2048:2176] = extra.astype(bf16)

        gate, chosen = route(0)
        for copy in group:
            copy.wait()
        group.clear()
        gate_part(0)
        gather(eu, wu)
        gather_last(eu, wu)
        for copy in group:
            copy.wait()
        phase_one(0)
        oth_z.hand_on()
        phase_two(0, gate, chosen)
        sg.wait(1)
        sg.start(3)
        sg.start(5)
        oth_z.wait()
        g_y.wait_recv()
        gate, chosen = route(1)
        gate_part(1)
        phase_one(1)
        saved = [loads.go(up, k.ex_up)]
        for r in range(4):
            to = slice(r * 256, (r + 1) * 256)
            for target, m in ((keep, r), (send, r + 4)):
                at = pl.ds(pl.multiple_of(owner_dense(m) * 256, 256), 256)
                target[0:512, to] = slopes[:, at]
                target[512:1024, to] = k.rows[:, at]
        saved.append(loads.go(keep, k.ex_keep))
        swap_ex = wires.go(lambda: (send, k.ex_x), core_dev)
        sd.wait(2)
        sd.start(6)
        phase_two(1, gate, chosen)
        su.wait(1)
        su.start(3)
        su.start(5)
        for copy in saved:
            copy.wait()
        swap_ex.wait_send()
        swap_ex.ends = lambda: (k.ex_keep, k.ex_x)
        parts.swap_ex = swap_ex

    pl.run_scoped(
        expert_part,
        pltpu.VMEM((4, 512, 1408), bf16),
        pltpu.VMEM((4, 512, 1408), bf16),
        pltpu.VMEM((4, 1408, 512), bf16),
        pltpu.VMEM((512, 2048), bf16),
        pltpu.VMEM((3, 256, 1408), f32),
        pltpu.VMEM((3, 512, 1408), bf16),
        pltpu.VMEM((1024, 1024), bf16),
        pltpu.VMEM((1024, 1024), bf16),
    )
    swap_up = {}
    for m in (1, 2, 0):
        swap_up[m] = wires.go(lambda m=m: (k.ex_up.at[m], k.ex_up_x.at[m]), core_dev)
    e_grad_z = to_z(lambda d: lambda: (k.e_grad.at[d], k.e_grad_z.at[d - 1]))
    e_out_z = to_z(lambda d: lambda: (k.e_out.at[d], k.e_out_z.at[d - 1]))
    over_y, over_x = {}, {}

    def expert_grad(m, kept, sent, landed):
        parts.swap_ex_wait()
        swap_up[m].wait_recv()

        def inner(left, right, keep, send):
            start = pl.ds(0 if m == 0 else 512, 512)
            got = [
                loads.go(k.ex_up.at[m], right.at[0]),
                loads.go(k.ex_up_x.at[m], right.at[1]),
                loads.go(k.ex_keep.at[start, :], left.at[0]),
                loads.go(k.ex_x.at[start, :], left.at[1]),
            ]
            for copy in got:
                copy.wait()
            saved = []
            for r in (3, 1, 2, 0):
                target = send if r % 2 else keep
                at = slice(r * 256, (r + 1) * 256)
                to = pl.ds(pl.multiple_of(((y + r // 2) % 2) * 256, 256), 256)
                if m == 0:
                    total = dot_tn(right[0], left[0, :, at]) + dot_tn(right[1], left[1, :, at])
                    target[:, to] = total.astype(bf16)
                else:
                    total = dot_tn(left[0, :, at], right[0]) + dot_tn(left[1, :, at], right[1])
                    target[to, :] = total.astype(bf16)
                if r == 1:
                    saved.append(loads.go(send, sent))
                if r == 2:
                    saved[0].wait()
                    over_x[6 + m] = wires.go(lambda: (sent, landed), x_dev)
            loads.go(keep, kept).wait()

        shape = (1408, 512) if m == 0 else (512, 1408)
        pl.run_scoped(
            inner,
            pltpu.VMEM((2, 512, 1024), bf16),
            pltpu.VMEM((2, 512, 1408), bf16),
            pltpu.VMEM(shape, bf16),
            pltpu.VMEM(shape, bf16),
        )

    def set_out(name, n, source, target, device):
        over_y[name, n] = wires.go(lambda: (source.at[n], target.at[n]), device)

    def y_first(name, keep, send, landed):
        def store(r, total):
            (send if r >= 2 else keep)[r % 2] = total
            if r == 3:
                set_out(name, 1, send, landed, y_dev)

        return store

    def shared_grad(m, store):
        def inner(left, right):
            if m == 0:
                got = [loads.go(k.sh_keep, left.at[0]), loads.go(k.sh_x, left.at[1])]
            else:
                start = pl.ds(512, 256)
                got = [
                    loads.go(k.ex_keep.at[start, :], left.at[0]),
                    loads.go(k.ex_x.at[start, :], left.at[1]),
                ]
            got.append(loads.go(k.sh_up.at[m], right.at[0]))
            got.append(loads.go(k.sh_up_x.at[m], right.at[1]))
            for copy in got:
                copy.wait()
            for r in (3, 1, 2, 0):
                at = slice(r * 256, (r + 1) * 256)
                if m == 0:
                    total = dot_tn(right[0], left[0, :, at]) + dot_tn(right[1], left[1, :, at])
                else:
                    total = dot_tn(left[0, :, at], right[0]) + dot_tn(left[1, :, at], right[1])
                store(r, total.astype(bf16))

        pl.run_scoped(
            inner, pltpu.VMEM((2, 256, 1024), bf16), pltpu.VMEM((2, 256, 1408), bf16)
        )

    def swap_ex_wait():
        if not parts.started:
            parts.swap_ex.wait_recv()
            parts.started = True

    parts.swap_ex_wait = swap_ex_wait

    def shared_part(wg, wu, wd, slopes, acc, up, keep, send):
        routed = k.rows.at[pl.ds(0, 256), :]
        held = []

        def bring(r, group):
            for s in group:
                held.append(loads.go(s.block(r), {sg: wg, su: wu, sd: wd}[s].at[r]))

        def arrived(r, group, onward=()):
            for s in group:
                s.wait(r)
                for t in onward:
                    s.start(t)
            bring(r, group)

        def settle():
            for copy in held:
                copy.wait()
            held.clear()

        pair, last = (sg, su), (sd,)
        for r in (0, 1, 2):
            bring(r, pair)
        for r in (4, 6):
            arrived(r, pair)
        expert_grad(1, k.k_eg, k.t_eg, k.x_eg)
        arrived(5, pair)
        sd.wait(1)
        sd.start(3)
        sd.start(5)
        bring(0, last)
        bring(1, last)
        bring(2, last)
        arrived(4, last)
        arrived(6, last)
        arrived(5, last)
        wide = routed[...].astype(f32) * k.small[2:3, :].astype(f32)
        sw = jax.nn.sigmoid(jnp.sum(wide, axis=-1, keepdims=True))
        for d in range(4):
            at = slice(d * 64, (d + 1) * 64)
            slopes[at, :] = (sw[at, :] * piece(k.g_own, d, 64).astype(f32)).astype(bf16)
        for r in range(4):
            to = slice(r * 256, (r + 1) * 256)
            keep[:, to] = cols(slopes, owner_dense(r), 256)
            send[:, to] = cols(slopes, owner_dense(r + 4), 256)
        saved = [loads.go(keep, k.sh_keep)]
        acc[...] = jnp.zeros_like(acc)

        def one(j, _):
            r = j // 2 + (j % 2) * 4
            row = cols(routed, owner_dense(r), 256)
            acc[0] += dot_nn(row, wg[r])
            acc[1] += dot_nn(row, wu[r])
            return 0

        def back(j, _):
            r = j // 2 + (j % 2) * 4
            acc[2] += dot_nt(cols(slopes, owner_dense(r), 256), wd[r])
            return 0

        settle()
        lax.fori_loop(0, 6, one, 0)
        arrived(3, pair, (7,))
        arrived(7, pair)
        settle()
        lax.fori_loop(6, 8, one, 0)
        for d in range(4):
            at = slice(d * 64, (d + 1) * 64)
            up[0, at, :] = (jax.nn.silu(acc[0, at, :]) * acc[1, at, :]).astype(bf16)
        swaps = [
            wires.go(lambda: (up.at[0], k.sh_up_x.at[0]), core_dev),
            wires.go(lambda: (send, k.sh_x), core_dev),
        ]
        saved.append(loads.go(up.at[0], k.sh_up.at[0]))
        for copy in saved:
            copy.wait()
        lax.fori_loop(0, 6, back, 0)
        for copy in swaps:
            copy.wait_recv()
            copy.wait_send()
        shared_grad(0, y_first(2, k.k_sd, k.t_sd, k.y_sd))
        for copy in e_grad_z:
            copy.wait_recv()
        oth = k.e_grad[0].astype(f32)
        for d in range(3):
            oth += k.e_grad_z[d].astype(f32)
        k.g_send[...] = oth.astype(bf16)
        parts.grad_y = wires.go(lambda: (k.g_send, k.g_y), y_dev)
        set_out(2, 0, k.t_sd, k.y_sd, y_dev)
        expert_grad(2, k.k_eu, k.t_eu, k.x_eu)
        arrived(3, last, (7,))
        arrived(7, last)
        settle()
        lax.fori_loop(6, 8, back, 0)
        for d in range(4):
            at = slice(d * 64, (d + 1) * 64)
            _, gate_grad, up_grad = gated(acc[0, at, :], acc[1, at, :], acc[2, at, :])
            up[1, at, :] = gate_grad.astype(bf16)
            up[2, at, :] = up_grad.astype(bf16)
        saved = [loads.go(up.at[m], k.sh_up.at[m]) for m in (1, 2)]

        def two(r, slope):
            at = pl.ds(pl.multiple_of(owner_dense(r) * 256, 256), 256)
            part = dot_nn(up[0], wd[r])
            total = sw * part + k.out_sum[:, at]
            back = dot_nt(up[1], wg[r]) + dot_nt(up[2], wu[r]) + k.grad_sum[:, at]
            sums = []
            for d in range(4):
                rows_at = slice(d * 64, (d + 1) * 64)
                g_rows = k.g_own[pl.ds(pl.multiple_of(near(d) * 64, 64), 64), at].astype(f32)
                sums.append(jnp.sum(g_rows * part[rows_at, :], axis=-1, keepdims=True))
                k.s_out[d, :, at] = total[rows_at, :].astype(bf16)
                k.s_grad[d, :, at] = back[rows_at, :].astype(bf16)
            return slope + jnp.concatenate(sums, axis=0)

        slope = lax.fori_loop(0, 8, two, jnp.zeros((256, 1), f32))
        lanes = lax.broadcasted_iota(jnp.int32, (64, 128), 1)
        for d in range(4):
            rows_at = slice(d * 64, (d + 1) * 64)
            extra = k.extras[rows_at, :]
            for m, part in enumerate(split3(slope[rows_at, :])):
                extra = jnp.where(lanes == mine + 48 + 16 * m, part, extra)
            k.s_grad[d, :, 2048:2176] = extra.astype(bf16)
        for copy in saved:
            copy.wait()

    pl.run_scoped(
        shared_part,
        pltpu.VMEM((8, 256, 1408), bf16),
        pltpu.VMEM((8, 256, 1408), bf16),
        pltpu.VMEM((8, 1408, 256), bf16),
        pltpu.VMEM((256, 2048), bf16),
        pltpu.VMEM((3, 256, 1408), f32),
        pltpu.VMEM((3, 256, 1408), bf16),
        pltpu.VMEM((256, 1024), bf16),
        pltpu.VMEM((256, 1024), bf16),
    )
    swap_sh = [
        wires.go(lambda m=m: (k.sh_up.at[m], k.sh_up_x.at[m]), core_dev) for m in (1, 2)
    ]
    s_grad_z = to_z(lambda d: lambda: (k.s_grad.at[d], k.s_grad_z.at[d - 1]))

    def back_part(*refs):
        k_ga, k_gb, k_su, k_q, k_kv, k_o, k_v = refs[:7]
        t_ga, t_gb, t_su, t_q, t_kv, t_o, t_v = refs[7:14]
        f_ga, f_gb, f_su, f_q, f_kv, f_o, f_v, f_sd = refs[14:22]
        h_keep, h_send, h_x, lin, lin_x, vec, high, gkv, gkv_send, gn = refs[22:]
        k_sd, t_sd = k.k_sd, k.t_sd

        def fold(name, keep, landed, send, target, device=x_dev):
            over_y[name, 1].wait_recv()

            def inner(buffer):
                loads.go(landed.at[1], buffer).wait()
                send[...] = (keep[1].astype(f32) + buffer[...].astype(f32)).astype(bf16)

            pl.run_scoped(inner, pltpu.VMEM(tuple(keep.shape[1:]), bf16))
            over_x[name] = wires.go(lambda: (send, target), device)

        def finish_pair():
            for name in (0, 9, 1):
                over_y[name, 0].wait_recv()
                over_x[name].wait_recv()

            def inner(left, right, total):
                first, last, whole = pl.ds(0, CUT), pl.ds(CUT, 256 - CUT), slice(0, 256)
                got = [
                    loads.go(k.y_ga.at[0], left.at[0, first, :]),
                    loads.go(k.x_ga, right.at[0, first, :]),
                    loads.go(k.y_gb.at[0], left.at[0, last, :]),
                    loads.go(k.x_gb, right.at[0, last, :]),
                    loads.go(k.y_su.at[0], left.at[1]),
                    loads.go(k.x_su, right.at[1]),
                ]
                for copy in got:
                    copy.wait()
                for n, keep, at in (
                    (0, k_ga, slice(0, CUT)),
                    (0, k_gb, slice(CUT, 256)),
                    (1, k_su, whole),
                ):
                    value = keep[0].astype(f32) + left[n, at, :].astype(f32)
                    value += right[n, at, :].astype(f32)
                    total[at, n, :] = value.astype(bf16)
                loads.go(total, k.d_si).wait()

            pair = pltpu.VMEM((2, 256, 1408), bf16)
            pl.run_scoped(inner, pair, pair, pltpu.VMEM((256, 2, 1408), bf16))

        def finish(name, keep, landed, target, result):
            over_y[name, 0].wait_recv()

            def inner(left, right, total):
                got = loads.go(landed.at[0], left)
                over_x[name].wait_recv()
                more = loads.go(target, right)
                got.wait()
                more.wait()
                value = keep[0].astype(f32) + left[...].astype(f32) + right[...].astype(f32)
                total[...] = value.astype(total.dtype)
                loads.go(total, result).wait()

            shape = tuple(keep.shape[1:])
            pl.run_scoped(
                inner,
                pltpu.VMEM(shape, bf16),
                pltpu.VMEM(shape, bf16),
                pltpu.VMEM(shape, result.dtype),
            )

        swap_sh[0].wait_recv()

        def gate_store(r, total):
            (t_ga if r >= 2 else k_ga)[r % 2] = total[0:CUT, :]
            (t_gb if r % 2 else k_gb)[r // 2] = total[CUT:256, :]
            if r == 3:
                set_out(0, 1, t_ga, k.y_ga, y_dev)
                set_out(9, 1, t_gb, k.y_gb, x_dev)

        shared_grad(1, gate_store)
        set_out(9, 0, t_gb, k.y_gb, x_dev)
        swap_sh[1].wait_recv()
        shared_grad(2, y_first(1, k_su, t_su, k.y_su))
        expert_grad(0, k.k_ed, k.t_ed, k.x_ed)
        fold(2, k_sd, k.y_sd, f_sd, k.x_sd)

        def other_rows(buffer):
            for copy in e_out_z:
                copy.wait_recv()
            loads.go(k.e_out_z, buffer).wait()
            oth = k.e_out[0].astype(f32)
            for d in range(3):
                oth += buffer[d].astype(f32)
            k.o_send[...] = oth.astype(bf16)

        pl.run_scoped(other_rows, pltpu.VMEM((3, 64, 2048), bf16))
        for copy in s_grad_z:
            copy.wait_recv()
        parts.grad_y.wait_recv()
        total = k.s_grad[0].astype(f32) + k.g_y[...].astype(f32)
        for d in range(3):
            total += k.s_grad_z[d].astype(f32)
        own_rows(
            total,
            k.hidden[...],
            k.rows[0:64, :],
            piece(k.g_own, 0, 64),
            k.small,
            high,
            k.gh.at[0],
            vec,
        )
        gh_z = Collect(lambda d: k.gh.at[d])
        out_y = wires.go(lambda: (k.o_send, k.o_y), y_dev)
        set_out(0, 0, t_ga, k.y_ga, y_dev)
        fold(0, k_ga, k.y_ga, f_ga, k.x_ga)
        fold(9, k_gb, k.y_gb, f_gb, k.x_gb, y_dev)
        gn_z, s_out_z, vec_z = [], [], []

        def attention_back(w, o_w, acc, low_g, n_x, low_x):
            got, more = [loads.go(k.w_o, o_w.at[0])], [loads.go(k.w_q, w.at[0])]
            for r in range(1, 8):
                got.append(loads.go(k.s_o.at[r], o_w.at[r]))
                more.append(loads.go(k.s_q.at[r], w.at[r]))
            gh_z.hand_on()
            gh_z.wait()
            s_out_z.extend(to_z(lambda d: lambda: (k.s_out.at[d], k.s_out_z.at[d - 1])))
            for copy in got:
                copy.wait()
            acc[...] = jnp.zeros_like(acc)
            for r in range(8):
                at = pl.ds(pl.multiple_of(owner_dense(r) * 256, 256), 256)
                row = jnp.concatenate([k.gh[d, :, at] for d in range(4)], axis=0)
                target = h_keep if r < 4 else h_send
                target[:, (r % 4) * 256 : (r % 4 + 1) * 256] = row
                acc[...] += dot_nt(row, o_w[r])
            swap_h = wires.go(lambda: (h_send, k.h_x), core_dev)
            low_g[...] = acc[...].astype(bf16)
            mask_own = k.ids_near[0:1, :] <= k.ids_q[:, 0:1]
            mask_oth = k.ids_far[0:1, :] <= k.ids_q[:, 0:1]
            scale = 128 ** (-0.5)
            for h in range(4):
                at = slice(h * 128, (h + 1) * 128)
                w_own, w_oth = softmax_parts(
                    k.q[:, at], k.kv[0:256, at], k.kv_oth[0:256, at], mask_own, mask_oth
                )
                dw_own = dot_nt(low_g[:, at], k.kv[256:512, at])
                dw_oth = dot_nt(low_g[:, at], k.kv_oth[256:512, at])
                mean = jnp.sum(w_own * dw_own, axis=-1, keepdims=True)
                mean += jnp.sum(w_oth * dw_oth, axis=-1, keepdims=True)
                ds_own = (w_own * (dw_own - mean)).astype(bf16)
                ds_oth = (w_oth * (dw_oth - mean)).astype(bf16)
                gq = dot_nn(ds_own, k.kv[0:256, at]) + dot_nn(ds_oth, k.kv_oth[0:256, at])
                lin[0:256, at] = turn_back(gq * scale, k.cs[...], k.sn[...]).astype(bf16)
                gkv[0:256, at] = dot_tn(ds_own, k.q[:, at]) * scale
                gkv[256:512, at] = dot_tn(w_own.astype(bf16), low_g[:, at])
                gkv_send[0:256, at] = (dot_tn(ds_oth, k.q[:, at]) * scale).astype(bf16)
                gkv_send[256:512, at] = dot_tn(w_oth.astype(bf16), low_g[:, at]).astype(bf16)
            gkv_y = wires.go(lambda: (gkv_send, k.gkv_y), y_dev)
            swap_q = wires.go(
                lambda: (lin.at[pl.ds(0, 256), :], k.lin_x.at[pl.ds(0, 256), :]), core_dev
            )
            fold(1, k_su, k.y_su, f_su, k.x_su)
            for copy in (swap_h, swap_n, swap_low, swap_q):
                copy.wait_recv()
            got = [
                loads.go(k.n_x, n_x),
                loads.go(k.low_x, low_x),
                loads.go(k.h_x, h_x),
                loads.go(k.lin_x.at[pl.ds(0, 256), :], lin_x.at[pl.ds(0, 256), :]),
            ]
            for copy in got:
                copy.wait()

            def projection(r, m):
                at, rows_at = slice(r * 256, (r + 1) * 256), slice(m * 256, (m + 1) * 256)
                total = dot_tn(k.n_keep[:, at], lin[rows_at, :])
                return (total + dot_tn(n_x[:, at], lin_x[rows_at, :])).astype(bf16)

            for r in (3, 1, 2, 0):
                at = slice(r * 256, (r + 1) * 256)
                total = dot_tn(k.low[...], h_keep[:, at]) + dot_tn(low_x[...], h_x[:, at])
                (t_o if r % 2 else k_o)[r // 2] = total.astype(bf16)
                if r % 2:
                    set_out(4, r // 2, t_o, k.y_o, x_dev)
                (t_q if r >= 2 else k_q)[r % 2] = projection(r, 0)
                if r == 3:
                    set_out(3, 1, t_q, k.y_q, y_dev)
            for copy in more:
                copy.wait()
            gkv_y.wait_recv()
            for h in range(4):
                at = slice(h * 128, (h + 1) * 128)
                gk = gkv[0:256, at] + k.gkv_y[0:256, at].astype(f32)
                lin[256:512, at] = turn_back(gk, k.cs[...], k.sn[...]).astype(bf16)
            lin[512:768, :] = (gkv[256:512, :] + k.gkv_y[256:512, :].astype(f32)).astype(bf16)
            swap_kv = wires.go(
                lambda: (lin.at[pl.ds(256, 512), :], k.lin_x.at[pl.ds(256, 512), :]), core_dev
            )
            for m in range(3):
                part = lin[m * 256 : (m + 1) * 256, :].astype(f32)
                vec[11 + m : 12 + m, 0:512] = jnp.sum(part, axis=0, keepdims=True)
            swap_kv.wait_recv()
            loads.go(k.lin_x.at[pl.ds(256, 512), :], lin_x.at[pl.ds(256, 512), :]).wait()
            for r in (3, 2, 1, 0):
                target = t_kv if r >= 2 else k_kv
                for m in (1, 2):
                    target[r % 2, (m - 1) * 256 : m * 256, :] = projection(r, m)
                if r == 3:
                    set_out(10, 1, t_kv, k.y_kv, y_dev)
                    set_out(1, 0, t_su, k.y_su, y_dev)
            for r in range(8):
                at = pl.ds(pl.multiple_of(owner_dense(r) * 256, 256), 256)
                back = dot_nt(lin[0:256, :], w[r, 0:256, :])
                back += dot_nt(lin[256:512, :], w[r, 256:512, :])
                back += dot_nt(lin[512:768, :], w[r, 512:768, :])
                gain = jnp.zeros((1, 256), f32)
                for d in range(4):
                    rows_at = slice(d * 64, (d + 1) * 64)
                    t = k.tok[pl.ds(pl.multiple_of(near(d) * 64, 64), 64), at].astype(f32)
                    gain += jnp.sum(
                        back[rows_at, :] * t * k.inv1[rows_at, :], axis=0, keepdims=True
                    )
                    gn[d, :, at] = back[rows_at, :].astype(bf16)
                vec[0:1, at] = gain
            vec_z.extend(to_z(lambda d: lambda: (vec, k.vec_z.at[d - 1])))
            gn_z.extend(to_z(lambda d: lambda: (gn.at[d], k.gn_z.at[d - 1])))

        pl.run_scoped(
            attention_back,
            pltpu.VMEM((8, 768, 512), bf16),
            pltpu.VMEM((8, 512, 256), bf16),
            pltpu.VMEM((256, 512), f32),
            pltpu.VMEM((256, 512), bf16),
            pltpu.VMEM((256, 1024), bf16),
            pltpu.VMEM((256, 512), bf16),
        )
        kept = [loads.go(k_q.at[0], k.keep_q), loads.go(k_kv.at[0], k.keep_kv)]
        kept.append(loads.go(k_o.at[0], k.keep_o))
        def expert_finish(m, kept, landed, result):
            def inner(left, right):
                got = loads.go(kept, left)
                over_x[6 + m].wait_recv()
                more = loads.go(landed, right)
                got.wait()
                more.wait()
                left[...] = (left[...].astype(f32) + right[...].astype(f32)).astype(bf16)
                loads.go(left, result).wait()

            shape = pltpu.VMEM(tuple(result.shape), bf16)
            pl.run_scoped(inner, shape, shape)

        def expert_pair():
            for m in (1, 2):
                over_x[6 + m].wait_recv()

            def inner(left, right, total):
                for half in range(2):
                    at = pl.ds(256 * half, 256)
                    got = []
                    for n, (kept, landed) in enumerate(((k.k_eg, k.x_eg), (k.k_eu, k.x_eu))):
                        got.append(loads.go(kept.at[at, :], left.at[n]))
                        got.append(loads.go(landed.at[at, :], right.at[n]))
                    for copy in got:
                        copy.wait()
                    for n in range(2):
                        value = left[n].astype(f32) + right[n].astype(f32)
                        total[:, n, :] = value.astype(bf16)
                    loads.go(total, k.d_ei.at[at]).wait()

            pair = pltpu.VMEM((2, 256, 1408), bf16)
            pl.run_scoped(inner, pair, pair, pltpu.VMEM((256, 2, 1408), bf16))

        expert_pair()
        for copy in vec_z:
            copy.wait_recv()
        line = lax.broadcasted_iota(jnp.int32, (16, 2048), 0)
        over_z = k.vec_z[0] + k.vec_z[1] + k.vec_z[2]
        k.vec_sum[...] = vec[...] + jnp.where(line < 11, over_z, 0.0)
        swap_vec = wires.go(lambda: (k.vec_sum, k.vec_x), core_dev)
        swap_vec.wait_recv()
        k.vec_x[...] += k.vec_sum[...]
        line = lax.broadcasted_iota(jnp.int32, (16, 512), 0)
        for r in (3, 2, 1, 0):
            here = cols(k.vec_x, owner_dense(r), 256)
            here = jnp.concatenate([here, jnp.zeros((16, 256), f32)], axis=1)
            here = jnp.where(line < 11, here, k.vec_x[:, 0:512]).astype(bf16)
            (t_v if r >= 2 else k_v)[r % 2] = here
            if r >= 2:
                set_out(5, r % 2, t_v, k.y_v, y_dev)
        kept.append(loads.go(k_v.at[0], k.keep_v))
        set_out(3, 0, t_q, k.y_q, y_dev)
        set_out(10, 0, t_kv, k.y_kv, y_dev)

        def outputs(s_z):
            for copy in s_out_z:
                copy.wait_recv()
            got = loads.go(k.s_out_z, s_z)
            for copy in gn_z:
                copy.wait_recv()
            grad = gn[0].astype(f32)
            for d in range(3):
                grad += k.gn_z[d].astype(f32)
            t = piece(k.tok, 0, 64).astype(f32)
            i = k.inv1[0:64, :]
            scaled = grad * k.small[0:1, :].astype(f32)
            mean = jnp.mean(scaled * t, axis=-1, keepdims=True)
            grad = high[...] + i * scaled - t * (i * i * i * mean)
            k.tok_low[...] = grad.astype(bf16)
            wrote = [loads.go(k.tok_low, k.grad_tokens)]
            got.wait()
            total = k.hidden[...] + k.s_out[0].astype(f32)
            for d in range(3):
                total += s_z[d].astype(f32)
            out_y.wait_recv()
            k.out_low[...] = (total + k.o_y[...].astype(f32)).astype(bf16)
            wrote.append(loads.go(k.out_low, k.output))
            for copy in wrote:
                copy.wait()

        expert_finish(0, k.k_ed, k.x_ed, k.d_ed)
        finish(2, k_sd, k.y_sd, k.x_sd, k.d_sd)
        fold(3, k_q, k.y_q, f_q, k.x_q)
        fold(10, k_kv, k.y_kv, f_kv, k.x_kv)
        fold(5, k_v, k.y_v, f_v, k.x_v)
        fold(4, k_o, k.y_o, f_o, k.x_o, y_dev)
        pl.run_scoped(outputs, pltpu.VMEM((3, 64, 2048), bf16))
        finish_pair()
        for name in (3, 10, 4, 5):
            over_y[name, 0].wait_recv()
            over_x[name].wait_recv()
        for copy in kept:
            copy.wait()
        wires.drain()

    shapes = [(CUT, 1408), (256 - CUT, 1408), (256, 1408)]
    shapes += [(256, 512), (512, 512), (512, 256), (16, 512)]

    def buffers(lead):
        return tuple(
            pltpu.VMEM(lead + shape, bf16)
            for shape in shapes
        )

    pl.run_scoped(
        back_part,
        *buffers((2,)),
        *buffers((2,)),
        *buffers(()),
        pltpu.VMEM((1408, 256), bf16),
        pltpu.VMEM((256, 1024), bf16),
        pltpu.VMEM((256, 1024), bf16),
        pltpu.VMEM((256, 1024), bf16),
        pltpu.VMEM((768, 512), bf16),
        pltpu.VMEM((768, 512), bf16),
        pltpu.VMEM((16, 2048), f32),
        pltpu.VMEM((64, 2048), f32),
        pltpu.VMEM((512, 512), f32),
        pltpu.VMEM((512, 512), bf16),
        pltpu.VMEM((4, 64, 2048), bf16),
    )


def close_kernel(k):
    loads = Loads(k.load_sems)
    sums = (
        (k.keep_q, k.y_q, k.x_q, k.b_q, k.c_q.at[pl.ds(0, 256), :]),
        (k.keep_kv, k.y_kv, k.x_kv, k.b_kv, k.c_q.at[pl.ds(256, 512), :]),
        (k.keep_o, k.y_o, k.x_o, k.b_o, k.c_o),
    )
    parts = []
    for keep, y, x, buffer, _ in sums:
        parts.append([loads.go(a, buffer.at[n]) for n, a in enumerate((keep, y.at[0], x))])
    passed = (
        (k.d_ei, k.b_ei, k.c_ei),
        (k.d_ed, k.b_ed, k.c_ed),
        (k.d_si, k.b_si, k.c_si),
        (k.d_sd, k.b_sd, k.c_sd),
        (k.output, k.b_out, k.c_out),
        (k.grad_tokens, k.b_tok, k.c_tok),
    )
    vectors = [loads.go(a, k.b_v.at[n]) for n, a in enumerate((k.keep_v, k.y_v.at[0], k.x_v))]
    got = [loads.go(source, buffer) for source, buffer, _ in passed]
    for copy in vectors:
        copy.wait()
    total = k.b_v[0].astype(f32) + k.b_v[1].astype(f32) + k.b_v[2].astype(f32)
    low = total.astype(bf16)
    for m, target in enumerate((k.c_one, k.c_two, k.c_gate)):
        target[...] = low[m : m + 1, 0:256].reshape(256)
    k.c_router[...] = low[3:11, 0:256]
    for h in range(4):
        here = pltpu.roll(
            total[:, h * 128 : (h + 1) * 128], (128 - owner_dense(0) * 16) % 128, 1
        )
        for m in range(3):
            k.c_bias[m, h : h + 1, :] = here[11 + m : 12 + m, 0:16].astype(bf16)
    done = []
    for copies, (_, _, _, buffer, target) in zip(parts, sums):
        for copy in copies:
            copy.wait()
        total = buffer[0].astype(f32) + buffer[1].astype(f32) + buffer[2].astype(f32)
        buffer[0] = total.astype(bf16)
        done.append(loads.go(buffer.at[0], target))
    for copy, (_, buffer, target) in zip(got, passed):
        copy.wait()
        done.append(loads.go(buffer, target))
    for copy in done:
        copy.wait()


def dma(n):
    return pltpu.SemaphoreType.DMA((n,))


def fixed_body(
    tokens,
    norm1_gain,
    w_qkv,
    b_qkv,
    w_out,
    norm2_gain,
    w_router,
    shared_gate,
    w_shared_in,
    w_shared_out,
    w_expert_in,
    w_expert_out,
    block_ids,
    expert_ids,
    out_grad,
):
    tok, g_own = tokens[0], out_grad[0]
    rows = tok.shape[0]
    places = np.arange(2 * rows)[:, None]
    frequency = rope_base ** (-np.arange(64) / 64.0)
    cosine, sine = np.cos(places * frequency), np.sin(places * frequency)
    cs = np.concatenate([cosine, cosine], axis=1).astype(np.float32)
    sn = np.concatenate([-sine, sine], axis=1).astype(np.float32)

    def vm(*shape, kind=bf16):
        return pltpu.VMEM(shape, kind)

    def o(*shape, kind=bf16, at=A):
        return (shape, kind, at)

    w_q = w_qkv.transpose(1, 0, 2).reshape(768, 512)
    b = call(
        layer_kernel,
        0,
        dict(
            tok_in=(tok, A),
            g_in=(g_own, A),
            bias_in=(b_qkv, A),
            cs_in=(cs, A),
            sn_in=(sn, A),
            blocks_in=(block_ids, A),
            ids_in=(expert_ids[0].T, A),
            one_in=(norm1_gain, A),
            two_in=(norm2_gain, A),
            gate_in=(shared_gate, A),
            router_in=(w_router.T, A),
            w_q=(w_q, A),
            w_o=(w_out, A),
            w_si=(w_shared_in, A),
            w_sd=(w_shared_out, A),
            w_ei=(w_expert_in[0], A),
            w_ed=(w_expert_out[0], A),
        ),
        dict(
            output=o(64, 2048),
            grad_tokens=o(64, 2048),
            keep_v=o(16, 512),
            keep_q=o(256, 512),
            keep_kv=o(512, 512),
            keep_o=o(512, 256),
            d_si=o(256, 2, 1408),
            d_sd=o(1408, 256),
            d_ei=o(512, 2, 1408),
            d_ed=o(1408, 512),
            split_si=o(2, 256, 1408),
            split_ei=o(2, 512, 1408),
            s_q=o(8, 768, 512),
            s_o=o(8, 512, 256),
            s_sg=o(8, 256, 1408),
            s_su=o(8, 256, 1408),
            s_sd=o(8, 1408, 256),
            s_eg=o(4, 512, 1408),
            s_eu=o(4, 512, 1408),
            s_ed=o(4, 1408, 512),
            ex_up=o(3, 512, 1408),
            ex_up_x=o(3, 512, 1408),
            ex_keep=o(1024, 1024),
            ex_x=o(1024, 1024),
            sh_up=o(3, 256, 1408),
            sh_up_x=o(3, 256, 1408),
            sh_keep=o(256, 1024),
            sh_x=o(256, 1024),
            k_eg=o(512, 1408),
            k_eu=o(512, 1408),
            k_ed=o(1408, 512),
            t_eg=o(512, 1408),
            t_eu=o(512, 1408),
            t_ed=o(1408, 512),
            y_ga=o(2, CUT, 1408),
            y_gb=o(2, 256 - CUT, 1408),
            y_su=o(2, 256, 1408),
            y_sd=o(2, 1408, 256),
            y_q=o(2, 256, 512),
            y_kv=o(2, 512, 512),
            y_o=o(2, 512, 256),
            y_v=o(2, 16, 512),
            x_ga=o(CUT, 1408),
            x_gb=o(256 - CUT, 1408),
            x_su=o(256, 1408),
            x_sd=o(1408, 256),
            x_q=o(256, 512),
            x_kv=o(512, 512),
            x_o=o(512, 256),
            x_v=o(16, 512),
            x_eg=o(512, 1408),
            x_eu=o(512, 1408),
            x_ed=o(1408, 512),
            n_x=o(256, 1024),
            low_x=o(256, 512),
            h_x=o(256, 1024),
            lin_x=o(768, 512),
            e_out_z=o(3, 64, 2048),
            s_out_z=o(3, 64, 2048),
        ),
        dict(
            s_v=vm(8, 16, 256),
            tok=vm(256, 2048),
            g_own=vm(256, 2048),
            bias=vm(3, 4, 128),
            blocks=vm(1, 512, kind=jnp.int32),
            ids_own=vm(4, 64, kind=jnp.int32),
            gain_one=vm(256),
            gain_two=vm(256),
            gate_vector=vm(256),
            router=vm(8, 256),
            cs_all=vm(512, 128, kind=f32),
            sn_all=vm(512, 128, kind=f32),
            w_v=vm(16, 256),
            col=vm(512, 128, kind=f32),
            ids_q=vm(256, 128, kind=f32),
            ids_near=vm(8, 256, kind=f32),
            ids_far=vm(8, 256, kind=f32),
            cs=vm(256, 128, kind=f32),
            sn=vm(256, 128, kind=f32),
            ids=vm(4, 128, 128, kind=f32),
            ids_y=vm(64, 128, kind=f32),
            g_oth=vm(256, 2048),
            q=vm(256, 512),
            kv=vm(512, 512),
            kv_oth=vm(512, 512),
            low=vm(256, 512),
            n_keep=vm(256, 1024),
            n_send=vm(256, 1024),
            small=vm(16, 2048),
            inv1=vm(256, 1, kind=f32),
            k_sd=vm(2, 1408, 256),
            t_sd=vm(2, 1408, 256),
            att=vm(3, 64, 2048),
            att_send=vm(4, 64, 2048),
            att_pair=vm(64, 2048),
            hidden=vm(64, 2048, kind=f32),
            rows=vm(512, 2048),
            out_sum=vm(256, 2048, kind=f32),
            grad_sum=vm(256, 2048, kind=f32),
            extras=vm(256, 128, kind=f32),
            e_out=vm(4, 64, 2048),
            e_grad=vm(4, 64, 2176),
            e_grad_z=vm(3, 64, 2176),
            s_out=vm(4, 64, 2048),
            s_grad=vm(4, 64, 2176),
            s_grad_z=vm(3, 64, 2176),
            g_send=vm(64, 2176),
            g_y=vm(64, 2176),
            o_send=vm(64, 2048),
            o_y=vm(64, 2048),
            out_low=vm(64, 2048),
            tok_low=vm(64, 2048),
            gh=vm(4, 64, 2048),
            gkv_y=vm(512, 512),
            gn_z=vm(3, 64, 2048),
            vec_x=vm(16, 2048, kind=f32),
            vec_z=vm(3, 16, 2048, kind=f32),
            vec_sum=vm(16, 2048, kind=f32),
            send_sems=dma(144),
            recv_sems=dma(144),
            load_sems=dma(224),
        ),
        63,
        4 * 10**10,
        2 * 10**8,
    )
    c = call(
        close_kernel,
        None,
        dict(
            output=(b.output, A),
            grad_tokens=(b.grad_tokens, A),
            keep_v=(b.keep_v, A),
            y_v=(b.y_v, A),
            x_v=(b.x_v, A),
            keep_q=(b.keep_q, A),
            y_q=(b.y_q, A),
            x_q=(b.x_q, A),
            keep_kv=(b.keep_kv, A),
            y_kv=(b.y_kv, A),
            x_kv=(b.x_kv, A),
            keep_o=(b.keep_o, A),
            y_o=(b.y_o, A),
            x_o=(b.x_o, A),
            d_si=(b.d_si, A),
            d_sd=(b.d_sd, A),
            d_ei=(b.d_ei, A),
            d_ed=(b.d_ed, A),
        ),
        dict(
            c_out=o(64, 2048),
            c_tok=o(64, 2048),
            c_one=o(256, at=V),
            c_two=o(256, at=V),
            c_gate=o(256, at=V),
            c_router=o(8, 256, at=V),
            c_bias=o(3, 4, 16, at=V),
            c_q=o(768, 512),
            c_o=o(512, 256),
            c_si=o(256, 2, 1408),
            c_sd=o(1408, 256),
            c_ei=o(512, 2, 1408),
            c_ed=o(1408, 512),
        ),
        dict(
            b_v=vm(3, 16, 512),
            b_out=vm(64, 2048),
            b_tok=vm(64, 2048),
            b_q=vm(3, 256, 512),
            b_kv=vm(3, 512, 512),
            b_o=vm(3, 512, 256),
            b_si=vm(256, 2, 1408),
            b_sd=vm(1408, 256),
            b_ei=vm(512, 2, 1408),
            b_ed=vm(1408, 512),
            load_sems=dma(32),
        ),
        63,
        10**6,
        2 * 10**7,
    )
    return (
        c.c_out[None],
        c.c_tok[None],
        c.c_one,
        c.c_q.reshape(3, 256, 512).transpose(1, 0, 2),
        c.c_bias,
        c.c_o,
        c.c_two,
        c.c_router.T,
        c.c_gate,
        c.c_si,
        c.c_sd,
        c.c_ei[None],
        c.c_ed[None],
    )


def solution(mesh):
    placed = (
        P(DP, CTX, None),
        P(PLANE),
        P(PLANE, None, EXP),
        P(None, EXP, None),
        P(EXP, PLANE),
        P(PLANE),
        P(PLANE, None),
        P(PLANE),
        P(PLANE, None, EXP),
        P(EXP, PLANE),
        P(GROUP, DP, None, None),
        P(GROUP, None, DP),
        P(DP, None),
        P(DP, GROUP, None),
        P(DP, CTX, None),
    )
    fixed = tuple(mesh.shape[a] for a in (DP, CTX, EXP)) == (4, 2, 4)
    return jax.shard_map(
        fixed_body if fixed else general_body,
        mesh=mesh,
        in_specs=placed,
        out_specs=(
            P(DP, GROUP, None),
            P(DP, GROUP, None),
            P(PLANE),
            P(PLANE, None, EXP),
            P(None, EXP, PLANE),
            P(EXP, PLANE),
            P(PLANE),
            P(PLANE, None),
            P(PLANE),
            P(PLANE, None, EXP),
            P(EXP, PLANE),
            P(GROUP, DP, None, None),
            P(GROUP, None, DP),
        ),
        check_vma=False,
    )
```

```python
from types import SimpleNamespace

import jax
import jax.numpy as jnp
import numpy as np
from jax import lax
from jax.experimental import pallas as pl
from jax.experimental.pallas import tpu as pltpu
from jax.sharding import PartitionSpec as P

highest = lax.Precision.HIGHEST
epsilon = 1e-06
rope_base = 1000000.0
f32 = jnp.float32
bf16 = jnp.bfloat16
DP, CTX, EXP = "dp", "context", "expert"
PLANE, GROUP = (DP, CTX), (CTX, EXP)


def rotary_tables(first_row, row_count, head_size):
    exponent = jnp.arange(head_size // 2).astype(jnp.float32) * (2.0 / head_size)
    frequency = rope_base ** (-exponent)
    positions = (first_row + jnp.arange(row_count, dtype=jnp.int32)).astype(jnp.float32)
    angles = positions[:, None] * frequency[None, :]
    return (jnp.cos(angles)[:, None, :], jnp.sin(angles)[:, None, :])


def rotate(values, cosine, sine_table):
    half_size = values.shape[-1] // 2
    first_half = values[..., :half_size]
    second_half = values[..., half_size:]
    return jnp.concatenate(
        [
            first_half * cosine - second_half * sine_table,
            second_half * cosine + first_half * sine_table,
        ],
        axis=-1,
    )


def rotate_back(grad_values, cosine, sine_table):
    half_size = grad_values.shape[-1] // 2
    first_half = grad_values[..., :half_size]
    second_half = grad_values[..., half_size:]
    return jnp.concatenate(
        [
            first_half * cosine + second_half * sine_table,
            second_half * cosine - first_half * sine_table,
        ],
        axis=-1,
    )


def gated_grads(gate_part, up_part, grad_act):
    sigmoid_gate = jax.nn.sigmoid(gate_part)
    grad_gate = grad_act * up_part * sigmoid_gate * (1.0 + gate_part * (1.0 - sigmoid_gate))
    grad_up = grad_act * gate_part * sigmoid_gate
    return (grad_gate, grad_up)


def masked_scores(queries, all_keys, allowed, score_scale):
    scores = (
        jnp.einsum("qhd,khd->hqk", queries, all_keys, preferred_element_type=jnp.float32)
        * score_scale
    )
    return jnp.where(allowed[None], scores, -1e30)


def fetch_dense(
    norm1_gain, w_qkv, w_out, norm2_gain, w_router, shared_gate, w_shared_in, w_shared_out
):
    return (
        lax.all_gather(norm1_gain, PLANE, axis=0, tiled=True),
        lax.all_gather(w_qkv, PLANE, axis=0, tiled=True),
        lax.all_gather(w_out, PLANE, axis=1, tiled=True),
        lax.all_gather(norm2_gain, PLANE, axis=0, tiled=True),
        lax.all_gather(w_router, PLANE, axis=0, tiled=True),
        lax.all_gather(shared_gate, PLANE, axis=0, tiled=True),
        lax.all_gather(w_shared_in, PLANE, axis=0, tiled=True),
        lax.all_gather(w_shared_out, PLANE, axis=1, tiled=True),
    )


def fetch_experts(w_expert_in, w_expert_out):
    return (
        lax.all_gather(w_expert_in, DP, axis=1, tiled=True),
        lax.all_gather(w_expert_out, DP, axis=2, tiled=True),
    )


def fetch_keys(key_rows, value_rows):
    return (
        lax.all_gather(key_rows, CTX, axis=0, tiled=True),
        lax.all_gather(value_rows, CTX, axis=0, tiled=True),
    )


def general_body(
    tokens,
    norm1_gain,
    w_qkv,
    b_qkv,
    w_out,
    norm2_gain,
    w_router,
    shared_gate,
    w_shared_in,
    w_shared_out,
    w_expert_in,
    w_expert_out,
    block_ids,
    expert_ids,
    out_grad,
):
    token_rows = tokens[0]
    rows_local, model_width = token_rows.shape
    lane_count = lax.axis_size(EXP)
    quarter = rows_local // lane_count
    first_row = lax.axis_index(CTX) * rows_local
    own_row = lax.axis_index(EXP) * quarter
    sequence_ids = block_ids[0]
    chosen = expert_ids[0]
    top_count = chosen.shape[1]
    heads_local = b_qkv.shape[1]
    head_size = b_qkv.shape[2]
    dense_full = fetch_dense(
        norm1_gain, w_qkv, w_out, norm2_gain, w_router, shared_gate, w_shared_in, w_shared_out
    )
    (
        gain_one,
        qkv_weight,
        out_weight,
        gain_two,
        router_weight,
        gate_vector,
        shared_in,
        shared_out,
    ) = dense_full
    expert_pair = fetch_experts(w_expert_in, w_expert_out)
    expert_in = expert_pair[0][0]
    expert_back = expert_pair[1][0]
    ffe_width = expert_in.shape[2]
    experts = router_weight.shape[1]
    capacity = max(2, 3 * quarter * top_count // (2 * experts))
    tokens_wide = token_rows.astype(jnp.float32)
    inverse_one = lax.rsqrt(jnp.mean(tokens_wide * tokens_wide, axis=-1, keepdims=True) + epsilon)
    normed = (tokens_wide * inverse_one * gain_one.astype(jnp.float32)).astype(jnp.bfloat16)
    linear = jnp.dot(
        normed, qkv_weight.reshape(model_width, -1), preferred_element_type=jnp.float32
    )
    linear = linear.reshape(rows_local, 3, heads_local, head_size) + b_qkv.astype(jnp.float32)[None]
    cosine, sine_table = rotary_tables(first_row, rows_local, head_size)
    queries = rotate(linear[:, 0], cosine, sine_table).astype(jnp.bfloat16)
    key_rows = rotate(linear[:, 1], cosine, sine_table).astype(jnp.bfloat16)
    value_rows = linear[:, 2].astype(jnp.bfloat16)
    all_keys, all_values = fetch_keys(key_rows, value_rows)
    query_ids = lax.dynamic_slice_in_dim(sequence_ids, first_row, rows_local)
    allowed = sequence_ids[None, :] <= query_ids[:, None]
    score_scale = head_size ** (-0.5)
    scores = masked_scores(queries, all_keys, allowed, score_scale)
    row_peak = jnp.max(scores, axis=-1, keepdims=True)
    log_total = row_peak + jnp.log(jnp.sum(jnp.exp(scores - row_peak), axis=-1, keepdims=True))
    weights = jnp.exp(scores - log_total).astype(jnp.bfloat16)
    attended = jnp.einsum("hqk,khd->qhd", weights, all_values, preferred_element_type=jnp.float32)
    attended_low = attended.astype(jnp.bfloat16).reshape(rows_local, heads_local * head_size)
    attention = lax.psum(
        jnp.dot(attended_low, out_weight, preferred_element_type=jnp.float32).astype(jnp.bfloat16),
        EXP,
    ).astype(jnp.float32)
    hidden = tokens_wide + attention
    inverse_two = lax.rsqrt(jnp.mean(hidden * hidden, axis=-1, keepdims=True) + epsilon)
    routed = (hidden * inverse_two * gain_two.astype(jnp.float32)).astype(jnp.bfloat16)
    shared_up = jnp.dot(
        routed, shared_in.reshape(model_width, -1), preferred_element_type=jnp.float32
    )
    shared_up = shared_up.reshape(rows_local, 2, -1)
    shared_act = (jax.nn.silu(shared_up[:, 0]) * shared_up[:, 1]).astype(jnp.bfloat16)
    shared_part = jnp.dot(shared_act, shared_out, preferred_element_type=jnp.float32)
    shared_rows = lax.psum_scatter(
        shared_part.astype(jnp.bfloat16), EXP, scatter_dimension=0, tiled=True
    ).astype(jnp.float32)
    shared_weight = jax.nn.sigmoid(jnp.dot(routed, gate_vector, preferred_element_type=jnp.float32))
    routed_own = lax.dynamic_slice_in_dim(routed, own_row, quarter)
    hidden_own = lax.dynamic_slice_in_dim(hidden, own_row, quarter)
    weight_own = lax.dynamic_slice_in_dim(shared_weight, own_row, quarter)
    logits = jnp.dot(routed_own, router_weight, preferred_element_type=jnp.float32)
    probability = jax.nn.softmax(logits, axis=-1)
    expert_match = (chosen[..., None] == jnp.arange(experts, dtype=jnp.int32)).astype(jnp.float32)
    gate_values = jnp.sum(probability[:, None, :] * expert_match, axis=-1)
    flat_ids = chosen.reshape(-1)
    onehot = (flat_ids[:, None] == jnp.arange(experts, dtype=jnp.int32)).astype(jnp.int32)
    slot_rank = jnp.sum((jnp.cumsum(onehot, axis=0) - onehot) * onehot, axis=-1)
    slot_index = flat_ids * capacity + slot_rank
    placement = (slot_index[:, None] == jnp.arange(experts * capacity, dtype=jnp.int32)).astype(
        jnp.bfloat16
    )
    repeated = jnp.repeat(routed_own, top_count, axis=0)
    outgoing = jnp.einsum("sr,sd->rd", placement, repeated, preferred_element_type=jnp.float32)
    outgoing = outgoing.astype(jnp.bfloat16).reshape(experts, capacity, model_width)
    incoming = lax.all_to_all(
        outgoing, GROUP, split_axis=0, concat_axis=0, tiled=True
    )
    flat_rows = incoming.reshape(-1, model_width)
    gate_up = jnp.dot(
        flat_rows, expert_in.reshape(model_width, -1), preferred_element_type=jnp.float32
    ).reshape(-1, 2, ffe_width)
    activated = (jax.nn.silu(gate_up[:, 0]) * gate_up[:, 1]).astype(jnp.bfloat16)
    result = jnp.dot(activated, expert_back, preferred_element_type=jnp.float32).astype(
        jnp.bfloat16
    )
    expert_result = result.reshape(incoming.shape)
    returned = lax.all_to_all(
        expert_result, GROUP, split_axis=0, concat_axis=0, tiled=True
    )
    picked = jnp.dot(
        placement, returned.reshape(-1, model_width), preferred_element_type=jnp.float32
    )
    picked = picked.reshape(quarter, top_count, model_width)
    combined = jnp.sum(gate_values[..., None] * picked, axis=1)
    result_rows = hidden_own + combined + weight_own[:, None] * shared_rows
    output = result_rows.astype(jnp.bfloat16)[None]
    (
        gain_one_b,
        qkv_weight_b,
        out_weight_b,
        gain_two_b,
        router_weight_b,
        gate_vector_b,
        shared_in_b,
        shared_out_b,
    ) = dense_full
    expert_in_b = expert_pair[0][0]
    expert_back_b = expert_pair[1][0]
    grad_full = out_grad[0].astype(jnp.float32)
    grad_own = lax.dynamic_slice_in_dim(grad_full, own_row, quarter)
    shared_grad = (shared_weight[:, None] * grad_full).astype(jnp.bfloat16)
    grad_shared_out = jnp.einsum(
        "tf,td->fd", shared_act, shared_grad, preferred_element_type=jnp.float32
    )
    grad_shared_act = jnp.einsum(
        "td,fd->tf", shared_grad, shared_out_b, preferred_element_type=jnp.float32
    )
    shared_gate_grad, shared_up_grad = gated_grads(
        shared_up[:, 0], shared_up[:, 1], grad_shared_act
    )
    grad_shared_up = jnp.stack([shared_gate_grad, shared_up_grad], axis=1).astype(jnp.bfloat16)
    grad_shared_in = jnp.einsum(
        "td,tkf->dkf", routed, grad_shared_up, preferred_element_type=jnp.float32
    )
    grad_routed = jnp.einsum(
        "tkf,dkf->td", grad_shared_up, shared_in_b, preferred_element_type=jnp.float32
    )
    gate_slope = jnp.sum(grad_own * shared_rows, axis=-1) * weight_own * (1.0 - weight_own)
    grad_gate_vector = jnp.dot(gate_slope, routed_own.astype(jnp.float32), precision=highest)
    grad_own_routed = gate_slope[:, None] * gate_vector_b.astype(jnp.float32)[None]
    grad_gates = jnp.sum(grad_own[:, None, :] * picked, axis=-1)
    grad_slots = (
        (gate_values[..., None] * grad_own[:, None, :])
        .astype(jnp.bfloat16)
        .reshape(-1, model_width)
    )
    grad_send = jnp.einsum("sr,sd->rd", placement, grad_slots, preferred_element_type=jnp.float32)
    grad_send = grad_send.astype(jnp.bfloat16).reshape(experts, capacity, model_width)
    grad_arrived = lax.all_to_all(
        grad_send, GROUP, split_axis=0, concat_axis=0, tiled=True
    )
    arrived_rows = incoming.reshape(-1, model_width)
    arrived_grad = grad_arrived.reshape(-1, model_width)
    expert_up = jnp.dot(
        arrived_rows, expert_in_b.reshape(model_width, -1), preferred_element_type=jnp.float32
    ).reshape(-1, 2, ffe_width)
    expert_act = (jax.nn.silu(expert_up[:, 0]) * expert_up[:, 1]).astype(jnp.bfloat16)
    grad_expert_back = jnp.einsum(
        "rf,rd->fd", expert_act, arrived_grad, preferred_element_type=jnp.float32
    )
    grad_expert_act = jnp.einsum(
        "rd,fd->rf", arrived_grad, expert_back_b, preferred_element_type=jnp.float32
    )
    expert_gate_grad, expert_up_grad = gated_grads(
        expert_up[:, 0], expert_up[:, 1], grad_expert_act
    )
    grad_expert_up = jnp.stack([expert_gate_grad, expert_up_grad], axis=1).astype(jnp.bfloat16)
    grad_expert_in = jnp.einsum(
        "rd,rkf->dkf", arrived_rows, grad_expert_up, preferred_element_type=jnp.float32
    )
    grad_arrived_rows = jnp.einsum(
        "rkf,dkf->rd", grad_expert_up, expert_in_b, preferred_element_type=jnp.float32
    )
    grad_arrived_rows = grad_arrived_rows.astype(jnp.bfloat16).reshape(
        experts, capacity, model_width
    )
    grad_returned = lax.all_to_all(
        grad_arrived_rows, GROUP, split_axis=0, concat_axis=0, tiled=True
    )
    grad_copies = jnp.dot(
        placement, grad_returned.reshape(-1, model_width), preferred_element_type=jnp.float32
    )
    grad_own_routed = grad_own_routed + jnp.sum(
        grad_copies.reshape(quarter, top_count, model_width), axis=1
    )
    grad_probability = jnp.sum(grad_gates[..., None] * expert_match, axis=1)
    grad_logits = probability * (
        grad_probability - jnp.sum(probability * grad_probability, axis=-1, keepdims=True)
    )
    grad_router = jnp.dot(routed_own.astype(jnp.float32).T, grad_logits, precision=highest)
    grad_own_routed = grad_own_routed + jnp.dot(
        grad_logits, router_weight_b.astype(jnp.float32).T, precision=highest
    )
    own_part = lax.dynamic_slice_in_dim(grad_routed, own_row, quarter) + grad_own_routed
    grad_routed = lax.dynamic_update_slice_in_dim(grad_routed, own_part, own_row, 0)
    grad_routed, grad_router, grad_gate_vector = (
        lax.psum(grad_routed.astype(jnp.bfloat16), EXP).astype(jnp.float32),
        lax.psum(grad_router.astype(jnp.bfloat16), EXP).astype(jnp.float32),
        lax.psum(grad_gate_vector.astype(jnp.bfloat16), EXP).astype(jnp.float32),
    )
    scaled_two = grad_routed * gain_two_b.astype(jnp.float32)
    grad_gain_two = jnp.sum(grad_routed * hidden * inverse_two, axis=0)
    grad_hidden = (
        grad_full
        + inverse_two * scaled_two
        - hidden * inverse_two**3 * jnp.mean(scaled_two * hidden, axis=-1, keepdims=True)
    )
    grad_hidden_low = grad_hidden.astype(jnp.bfloat16)
    grad_out_weight = jnp.einsum(
        "tn,td->nd", attended_low, grad_hidden_low, preferred_element_type=jnp.float32
    )
    grad_attended = jnp.einsum(
        "td,nd->tn", grad_hidden_low, out_weight_b, preferred_element_type=jnp.float32
    )
    grad_attended = grad_attended.astype(jnp.bfloat16).reshape(rows_local, heads_local, head_size)
    back_keys, back_values = (all_keys, all_values)
    scores_again = masked_scores(queries, back_keys, allowed, score_scale)
    weights_wide = jnp.exp(scores_again - log_total)
    row_delta = jnp.sum(grad_attended.astype(jnp.float32) * attended, axis=-1).T
    grad_weights = jnp.einsum(
        "qhd,khd->hqk", grad_attended, back_values, preferred_element_type=jnp.float32
    )
    grad_scores = (weights_wide * (grad_weights - row_delta[..., None])).astype(jnp.bfloat16)
    grad_queries = (
        jnp.einsum("hqk,khd->qhd", grad_scores, back_keys, preferred_element_type=jnp.float32)
        * score_scale
    )
    grad_keys = (
        jnp.einsum("hqk,qhd->khd", grad_scores, queries, preferred_element_type=jnp.float32)
        * score_scale
    )
    grad_values = jnp.einsum(
        "hqk,qhd->khd",
        weights_wide.astype(jnp.bfloat16),
        grad_attended,
        preferred_element_type=jnp.float32,
    )
    grad_keys, grad_values = (
        lax.psum_scatter(
            grad_keys.astype(jnp.bfloat16), CTX, scatter_dimension=0, tiled=True
        ).astype(jnp.float32),
        lax.psum_scatter(
            grad_values.astype(jnp.bfloat16), CTX, scatter_dimension=0, tiled=True
        ).astype(jnp.float32),
    )
    grad_linear = jnp.stack(
        [
            rotate_back(grad_queries, cosine, sine_table),
            rotate_back(grad_keys, cosine, sine_table),
            grad_values,
        ],
        axis=1,
    )
    grad_linear = grad_linear.astype(jnp.bfloat16)
    grad_bias = jnp.sum(grad_linear.astype(jnp.float32), axis=0)
    grad_flat = grad_linear.reshape(rows_local, -1)
    grad_qkv = jnp.einsum(
        "td,tn->dn", normed, grad_flat, preferred_element_type=jnp.float32
    ).reshape(qkv_weight_b.shape)
    grad_normed = jnp.einsum(
        "tn,dn->td",
        grad_flat,
        qkv_weight_b.reshape(model_width, -1),
        preferred_element_type=jnp.float32,
    )
    grad_normed = lax.psum(grad_normed.astype(jnp.bfloat16), EXP).astype(jnp.float32)
    scaled_one = grad_normed * gain_one_b.astype(jnp.float32)
    grad_gain_one = jnp.sum(grad_normed * tokens_wide * inverse_one, axis=0)
    grad_tokens = (
        grad_hidden
        + inverse_one * scaled_one
        - tokens_wide * inverse_one**3 * jnp.mean(scaled_one * tokens_wide, axis=-1, keepdims=True)
    )
    grad_tokens_own = lax.dynamic_slice_in_dim(grad_tokens, own_row, quarter).astype(jnp.bfloat16)[
        None
    ]
    dense_sums = (
        lax.psum_scatter(
            grad_gain_one.astype(jnp.bfloat16), PLANE, scatter_dimension=0, tiled=True
        ).astype(jnp.float32),
        lax.psum_scatter(
            grad_qkv.astype(jnp.bfloat16), PLANE, scatter_dimension=0, tiled=True
        ).astype(jnp.float32),
        lax.psum_scatter(
            grad_bias.astype(jnp.bfloat16), PLANE, scatter_dimension=2, tiled=True
        ).astype(jnp.float32),
        lax.psum_scatter(
            grad_out_weight.astype(jnp.bfloat16), PLANE, scatter_dimension=1, tiled=True
        ).astype(jnp.float32),
        lax.psum_scatter(
            grad_gain_two.astype(jnp.bfloat16), PLANE, scatter_dimension=0, tiled=True
        ).astype(jnp.float32),
        lax.psum_scatter(
            grad_router.astype(jnp.bfloat16), PLANE, scatter_dimension=0, tiled=True
        ).astype(jnp.float32),
        lax.psum_scatter(
            grad_gate_vector.astype(jnp.bfloat16),
            PLANE,
            scatter_dimension=0,
            tiled=True,
        ).astype(jnp.float32),
        lax.psum_scatter(
            grad_shared_in.astype(jnp.bfloat16), PLANE, scatter_dimension=0, tiled=True
        ).astype(jnp.float32),
        lax.psum_scatter(
            grad_shared_out.astype(jnp.bfloat16), PLANE, scatter_dimension=1, tiled=True
        ).astype(jnp.float32),
    )
    expert_sums = (
        lax.psum_scatter(
            grad_expert_in[None].astype(jnp.bfloat16), DP, scatter_dimension=1, tiled=True
        ).astype(jnp.float32),
        lax.psum_scatter(
            grad_expert_back[None].astype(jnp.bfloat16), DP, scatter_dimension=2, tiled=True
        ).astype(jnp.float32),
    )
    return (
        output,
        grad_tokens_own,
        dense_sums[0].astype(jnp.bfloat16),
        dense_sums[1].astype(jnp.bfloat16),
        dense_sums[2].astype(jnp.bfloat16),
        dense_sums[3].astype(jnp.bfloat16),
        dense_sums[4].astype(jnp.bfloat16),
        dense_sums[5].astype(jnp.bfloat16),
        dense_sums[6].astype(jnp.bfloat16),
        dense_sums[7].astype(jnp.bfloat16),
        dense_sums[8].astype(jnp.bfloat16),
        expert_sums[0].astype(jnp.bfloat16),
        expert_sums[1].astype(jnp.bfloat16),
    )


MIB = 1 << 20
CUT = 192
MESH = pl.DeviceIdType.MESH


def dot_nn(a, b):
    return lax.dot_general(a, b, (((1,), (0,)), ((), ())), preferred_element_type=f32)


def dot_nt(a, b):
    return lax.dot_general(a, b, (((1,), (1,)), ((), ())), preferred_element_type=f32)


def dot_tn(a, b):
    return lax.dot_general(a, b, (((0,), (0,)), ((), ())), preferred_element_type=f32)


def place():
    i = lax.axis_index(DP)
    return i // 2, i % 2, lax.axis_index(CTX), lax.axis_index(EXP)


def owner_dense(r):
    x, c, y, _ = place()
    return (((x + r % 2) % 2) * 2 + (c + r // 4) % 2) * 2 + (y + (r // 2) % 2) % 2


def owner_expert(r):
    x, c, _, _ = place()
    return ((x + r % 2) % 2) * 2 + (c + r // 2) % 2


def near(d):
    z = lax.axis_index(EXP)
    return ((z // 2 + d // 2) % 2) * 2 + (z % 2 + d % 2) % 2


def peers():
    x, c, y, _ = place()
    far = [{EXP: near(d)} for d in (1, 2, 3)]
    return {DP: ((x + 1) % 2) * 2 + c}, {CTX: 1 - y}, {DP: x * 2 + (c + 1) % 2}, far


def greet(devices, meanwhile):
    barrier = pltpu.get_barrier_semaphore()
    for device in devices:
        pl.semaphore_signal(barrier, 1, device_id=device, device_id_type=MESH)
    result = meanwhile()
    pl.semaphore_wait(barrier, len(devices))
    return result


class Wire:
    def __init__(self, wires, ends, device):
        self.ends, self.device, self.sent = ends, device, False
        self.send, self.recv, self.k = wires.send, wires.recv, len(wires.copies)
        wires.copies.append(self)

    def copy(self):
        source, target = self.ends()
        return pltpu.make_async_remote_copy(
            src_ref=source,
            dst_ref=target,
            send_sem=self.send.at[self.k],
            recv_sem=self.recv.at[self.k],
            device_id=self.device,
            device_id_type=MESH,
        )

    def start(self):
        self.copy().start()
        return self

    def wait_recv(self):
        self.copy().wait_recv()

    def wait_send(self):
        self.copy().wait_send()
        self.sent = True


class Wires:
    def __init__(self, send, recv):
        self.send, self.recv, self.copies = send, recv, []

    def add(self, ends, device):
        return Wire(self, ends, device)

    def go(self, ends, device):
        return Wire(self, ends, device).start()

    def drain(self):
        for wire in self.copies:
            if not wire.sent:
                wire.wait_send()


class Loads:
    def __init__(self, sems):
        self.sems, self.count = sems, 0

    def go(self, source, target):
        copy = pltpu.make_async_copy(source, target, self.sems.at[self.count])
        self.count += 1
        copy.start()
        return copy


def cols(ref, block, width):
    return ref[:, pl.ds(pl.multiple_of(block * width, width), width)]


def piece(ref, d, rows):
    return ref[pl.ds(pl.multiple_of(near(d) * rows, rows), rows), :]


def turn(values, cosine, sine):
    return values * cosine + pltpu.roll(values, 64, 1) * sine


def turn_back(values, cosine, sine):
    return values * cosine - pltpu.roll(values, 64, 1) * sine


def gated(gate, up, grad_act):
    s = jax.nn.sigmoid(gate)
    act = gate * s
    return act * up, grad_act * up * s * (1.0 + gate * (1.0 - s)), grad_act * act


def softmax_parts(q, k_own, k_oth, mask_own, mask_oth):
    scale = 128 ** (-0.5)
    s_own = jnp.where(mask_own, dot_nt(q, k_own) * scale, -1e30)
    s_oth = jnp.where(mask_oth, dot_nt(q, k_oth) * scale, -1e30)
    peak = jnp.maximum(
        jnp.max(s_own, axis=-1, keepdims=True), jnp.max(s_oth, axis=-1, keepdims=True)
    )
    e_own = jnp.exp(s_own - peak)
    e_oth = jnp.exp(s_oth - peak)
    total = jnp.sum(e_own, axis=-1, keepdims=True) + jnp.sum(e_oth, axis=-1, keepdims=True)
    back = 1.0 / total
    return e_own * back, e_oth * back


def split3(v):
    high = v.astype(bf16).astype(f32)
    mid = (v - high).astype(bf16).astype(f32)
    return high, mid, v - high - mid


def probabilities(rows, small):
    logits = dot_nt(rows, small[...])
    lane = lax.broadcasted_iota(jnp.int32, logits.shape, 1)
    logits = jnp.where((lane >= 3) & (lane < 11), logits, -1e30)
    e = jnp.exp(logits - jnp.max(logits, axis=-1, keepdims=True))
    return e / jnp.sum(e, axis=-1, keepdims=True), lane


ARRIVAL = (0, 4, 1, 5, 2, 6, 3, 7)


class Spread:
    def __init__(self, wires, own, slots, dense):
        x, y, core, _ = peers()
        self.slots, self.own, self.copies = slots, own, {}

        def ends(r, target):
            return lambda: (self.block(r), slots.at[target])

        self.copies[1] = wires.add(ends(0, 1), x)
        if dense:
            self.copies[2] = wires.add(ends(0, 2), y)
            self.copies[3] = wires.add(ends(1, 3), y)
        side = 4 if dense else 2
        for r in range(side):
            self.copies[side + r] = wires.add(ends(r, side + r), core)

    def block(self, r):
        return self.own() if r == 0 else self.slots.at[r]

    def start(self, r):
        self.copies[r].start()

    def wait(self, r):
        self.copies[r].wait_recv()


V, A = "vmem", "any"


def call(kernel, number, ins, outs, scratch, vmem, flops, traffic):
    def spec(kind):
        return pl.BlockSpec(memory_space=pl.ANY if kind == A else pltpu.VMEM)

    names = list(ins) + list(outs) + list(scratch)

    def run(*refs):
        kernel(SimpleNamespace(**dict(zip(names, refs))))

    made = pl.pallas_call(
        run,
        out_shape=tuple(jax.ShapeDtypeStruct(o[0], o[1]) for o in outs.values()),
        in_specs=[spec(i[1]) for i in ins.values()],
        out_specs=tuple(spec(o[2]) for o in outs.values()),
        scratch_shapes=list(scratch.values()),
        compiler_params=pltpu.CompilerParams(
            vmem_limit_bytes=vmem * MIB, collective_id=number, has_side_effects=number is not None
        ),
        cost_estimate=pl.CostEstimate(flops=flops, bytes_accessed=traffic, transcendentals=0),
    )(*[i[0] for i in ins.values()])
    return SimpleNamespace(**dict(zip(outs, made)))


def own_rows(total, hidden, routed, g, small, high_o, low_o, vec_o):
    extra = total[:, 2048:2176]
    wide = routed.astype(f32)
    prob, _ = probabilities(routed, small)
    sw = jax.nn.sigmoid(jnp.sum(wide * small[2:3, :].astype(f32), axis=-1, keepdims=True))
    slope = jnp.sum(extra[:, 48:96], axis=-1, keepdims=True) * sw * (1.0 - sw)
    dgate = [
        extra[:, e : e + 1] + extra[:, 16 + e : 17 + e] + extra[:, 32 + e : 33 + e]
        for e in range(8)
    ]
    probs = [prob[:, 3 + e : 4 + e] for e in range(8)]
    mean = sum(p * d for p, d in zip(probs, dgate))
    grad = total[:, 0:2048] + slope * small[2:3, :].astype(f32)
    vec_o[...] = jnp.zeros_like(vec_o)
    vec_o[2:3, :] = jnp.sum(slope * wide, axis=0, keepdims=True)
    for e in range(8):
        dlogit = probs[e] * (dgate[e] - mean)
        grad += dlogit * small[3 + e : 4 + e, :].astype(f32)
        vec_o[3 + e : 4 + e, :] = jnp.sum(dlogit * wide, axis=0, keepdims=True)
    inv = lax.rsqrt(jnp.mean(hidden * hidden, axis=-1, keepdims=True) + epsilon)
    vec_o[1:2, :] = jnp.sum(grad * hidden * inv, axis=0, keepdims=True)
    scaled = grad * small[1:2, :].astype(f32)
    mean = jnp.mean(scaled * hidden, axis=-1, keepdims=True)
    high = g.astype(f32) + inv * scaled - hidden * (inv * inv * inv * mean)
    high_o[...] = high
    low_o[...] = high.astype(bf16)


def layer_kernel(k):
    x_dev, y_dev, core_dev, z_dev = peers()
    wires, loads = Wires(k.send_sems, k.recv_sems), Loads(k.load_sems)
    def bring_inputs():
        return [
            loads.go(a, b)
            for a, b in (
                (k.one_in, k.gain_one),
                (k.two_in, k.gain_two),
                (k.gate_in, k.gate_vector),
                (k.router_in, k.router),
                (k.ids_in, k.ids_own),
                (k.blocks_in, k.blocks),
                (k.tok_in, k.tok),
                (k.bias_in, k.bias),
                (k.cs_in, k.cs_all),
                (k.sn_in, k.sn_all),
                (k.g_in, k.g_own),
            )
        ]

    inputs = greet([x_dev, y_dev, core_dev] + z_dev, bring_inputs)
    y = lax.axis_index(CTX)
    mine = y * 4 + lax.axis_index(EXP)

    def to_z(make):
        return [wires.go(make(d), z_dev[d - 1]) for d in (1, 2, 3)]

    class Collect:
        def __init__(self, slot):
            self.slot = slot
            self.one = wires.go(lambda: (slot(0), slot(1)), z_dev[0])
            self.three = wires.go(lambda: (slot(0), slot(3)), z_dev[2])

        def hand_on(self):
            self.three.wait_recv()
            self.two = wires.go(lambda: (self.slot(3), self.slot(2)), z_dev[0])

        def wait(self):
            self.one.wait_recv()
            self.two.wait_recv()

    vec = Spread(wires, lambda: k.w_v, k.s_v, True)
    qkv = Spread(wires, lambda: k.w_q, k.s_q, True)
    out = Spread(wires, lambda: k.w_o, k.s_o, True)
    eg = Spread(wires, lambda: k.split_ei.at[0], k.s_eg, False)
    eu = Spread(wires, lambda: k.split_ei.at[1], k.s_eu, False)
    ed = Spread(wires, lambda: k.w_ed, k.s_ed, False)
    sg = Spread(wires, lambda: k.split_si.at[0], k.s_sg, True)
    su = Spread(wires, lambda: k.split_si.at[1], k.s_su, True)
    sd = Spread(wires, lambda: k.w_sd, k.s_sd, True)
    first, expert, shared = (vec, qkv), (eg, eu, ed), (sg, su, sd)
    qkv.start(1)
    qkv.start(2)
    k.w_v[...] = jnp.zeros_like(k.w_v)
    for copy in inputs[:6]:
        copy.wait()
    for m, vector in enumerate((k.gain_one, k.gain_two, k.gate_vector)):
        k.w_v[m : m + 1, :] = vector[...].reshape(1, 256)
    k.w_v[3:11, :] = k.router[...]
    for s in (vec, out, ed):
        s.start(1)
    vec.start(2)
    for s in (qkv, out, vec):
        s.start(4)
    k.col[0:128, :] = jnp.full((128, 128), -1.0, f32)
    k.col[0:4, 0:64] = k.ids_own[...].astype(f32)
    k.ids[0, 0:64, :] = k.col[0:128, :].T[0:64, :]
    ids_y = wires.go(lambda: (k.ids.at[0, pl.ds(0, 64), :], k.ids_y), y_dev)
    k.s_v[0] = k.w_v[...]
    for copy in inputs[6:]:
        copy.wait()
    k.col[...] = jnp.broadcast_to(k.blocks[...].astype(f32), (128, 512)).T
    for target, half in ((k.ids_near, y), (k.ids_far, 1 - y)):
        for d in range(4):
            at = pl.ds(pl.multiple_of(half * 256 + near(d) * 64, 64), 64)
            k.ids_q[d * 64 : (d + 1) * 64, :] = k.col[at, :]
        target[...] = k.ids_q[...].T[0:8, :]
    for d in range(4):
        at = pl.ds(pl.multiple_of(y * 256 + near(d) * 64, 64), 64)
        to = slice(d * 64, (d + 1) * 64)
        k.ids_q[to, :] = k.col[at, :]
        k.cs[to, :] = k.cs_all[at, :]
        k.sn[to, :] = k.sn_all[at, :]
    later = []

    def attention_part(scaled, acc, w, low_w, mixed, apart):
        held, held_out = {}, []

        def bring(r):
            held[r] = loads.go(qkv.block(r), w.at[r])

        def bring_out(r):
            held_out.append(loads.go(out.block(r), low_w.at[r]))

        raw = [loads.go(k.w_ei.at[pl.ds(256 * m, 256)], mixed.at[m]) for m in range(2)]
        raw.append(loads.go(k.w_si, mixed.at[2]))
        bring(0)
        for d in range(4):
            t = piece(k.tok, d, 64).astype(f32)
            inv = lax.rsqrt(jnp.mean(t * t, axis=-1, keepdims=True) + epsilon)
            scaled[d * 64 : (d + 1) * 64, :] = t * inv
            k.inv1[d * 64 : (d + 1) * 64, :] = inv
        for m in range(3):
            for h in range(4):
                at = slice(h * 128, (h + 1) * 128)
                line = k.bias[m, h : h + 1, :].astype(f32)
                acc[m, :, at] = jnp.broadcast_to(line, (256, 128))

        def take_apart(m):
            raw[m].wait()
            target = k.split_si if m == 2 else k.split_ei
            to = pl.ds(0 if m == 2 else 256 * m, 256)
            done = []
            for n in range(2):
                apart[m, n] = mixed[m, :, n, :]
                done.append(loads.go(apart.at[m, n], target.at[n, to, :]))
            return done

        done = take_apart(0) + take_apart(1)
        for copy in done:
            copy.wait()
        for s in (eg, eu):
            s.start(1)
        for s in expert:
            s.start(2)

        def block(r):
            held[r].wait()
            o = owner_dense(r)
            vectors = k.s_v[r]
            k.small[:, pl.ds(pl.multiple_of(o * 256, 256), 256)] = vectors
            normed = (cols(scaled, o, 256) * vectors[0:1, :].astype(f32)).astype(bf16)
            target = k.n_keep if r < 4 else k.n_send
            target[:, (r % 4) * 256 : (r % 4 + 1) * 256] = normed
            for m in range(3):
                acc[m] += dot_nn(normed, w[r, m * 256 : (m + 1) * 256, :])

        def arrived(r, onward=()):
            for s in first:
                s.wait(r)
                for t in onward:
                    s.start(t)
            bring(r)

        arrived(4)
        block(0)
        block(4)
        arrived(1, (3, 5))
        out.start(2)
        arrived(2, (6,))
        block(1)
        arrived(5)
        block(5)
        arrived(6)
        block(2)
        block(6)
        for copy in take_apart(2):
            copy.wait()
        for s in shared:
            s.start(1)
        for s in shared:
            s.start(4)
        ids_y.wait_recv()
        k.ids[0, 64:128, :] = k.ids_y[...]
        later.extend(to_z(lambda d: lambda: (k.ids.at[0], k.ids.at[d])))
        bring_out(0)
        out.wait(4)
        bring_out(4)
        out.wait(1)
        out.start(5)
        bring_out(1)
        arrived(3, (7,))
        block(3)
        arrived(7)
        block(7)
        for h in range(4):
            at = slice(h * 128, (h + 1) * 128)
            k.kv[0:256, at] = turn(acc[1, :, at], k.cs[...], k.sn[...]).astype(bf16)
        k.kv[256:512, :] = acc[2].astype(bf16)
        kv_y = wires.go(lambda: (k.kv, k.kv_oth), y_dev)
        out.start(3)
        sg.start(2)
        su.start(2)
        for h in range(4):
            at = slice(h * 128, (h + 1) * 128)
            k.q[:, at] = turn(acc[0, :, at], k.cs[...], k.sn[...]).astype(bf16)
        out.wait(5)
        bring_out(5)
        out.wait(2)
        out.start(6)
        bring_out(2)
        kv_y.wait_recv()
        mask_own = k.ids_near[0:1, :] <= k.ids_q[:, 0:1]
        mask_oth = k.ids_far[0:1, :] <= k.ids_q[:, 0:1]
        for h in range(4):
            at = slice(h * 128, (h + 1) * 128)
            w_own, w_oth = softmax_parts(
                k.q[:, at], k.kv[0:256, at], k.kv_oth[0:256, at], mask_own, mask_oth
            )
            value = dot_nn(w_own.astype(bf16), k.kv[256:512, at])
            value += dot_nn(w_oth.astype(bf16), k.kv_oth[256:512, at])
            k.low[:, at] = value.astype(bf16)
        out.wait(6)
        bring_out(6)
        out.wait(3)
        out.start(7)
        bring_out(3)
        out.wait(7)
        bring_out(7)
        for copy in held_out:
            copy.wait()
        for r in range(8):
            part = dot_nn(k.low[...], low_w[r]).astype(bf16)
            at = pl.ds(pl.multiple_of(owner_dense(r) * 256, 256), 256)
            for d in range(4):
                k.att_send[d, :, at] = part[d * 64 : (d + 1) * 64, :]

    pl.run_scoped(
        attention_part,
        pltpu.VMEM((256, 2048), f32),
        pltpu.VMEM((3, 256, 512), f32),
        pltpu.VMEM((8, 768, 512), bf16),
        pltpu.VMEM((8, 512, 256), bf16),
        pltpu.VMEM((3, 256, 2, 1408), bf16),
        pltpu.VMEM((3, 2, 256, 1408), bf16),
    )
    att_two = wires.go(lambda: (k.att_send.at[2], k.att.at[1]), z_dev[0])
    att_one = wires.go(lambda: (k.att_send.at[1], k.att.at[0]), z_dev[0])
    swap_n = wires.go(lambda: (k.n_send, k.n_x), core_dev)
    swap_low = wires.go(lambda: (k.low, k.low_x), core_dev)
    parts = SimpleNamespace(started=False)

    def expert_part(wg, wu, wd, slopes, acc, up, keep, send):
        group = []

        def gather(s, w):
            group.append(loads.go(s.block(0), w.at[0]))
            s.wait(2)
            group.append(loads.go(s.block(2), w.at[2]))
            s.wait(1)
            s.start(3)
            group.append(loads.go(s.block(1), w.at[1]))

        def gather_last(s, w):
            s.wait(3)
            group.append(loads.go(s.block(3), w.at[3]))

        gather(ed, wd)
        att_two.wait_recv()
        pair = k.att_send[3].astype(f32) + k.att[1].astype(f32)
        k.att_pair[...] = pair.astype(bf16)
        att_three = wires.go(lambda: (k.att_pair, k.att.at[2]), z_dev[2])
        att_one.wait_recv()
        value = k.att_send[0].astype(f32) + k.att[0].astype(f32)
        att_three.wait_recv()
        value += piece(k.tok, 0, 64).astype(f32) + k.att[2].astype(f32)
        inv = lax.rsqrt(jnp.mean(value * value, axis=-1, keepdims=True) + epsilon)
        k.hidden[...] = value
        k.rows[0:64, :] = (value * inv * k.small[1:2, :].astype(f32)).astype(bf16)
        own_y = wires.go(
            lambda: (k.rows.at[pl.ds(0, 64), :], k.rows.at[pl.ds(256, 64), :]), y_dev
        )
        g_y = wires.go(lambda: (k.g_own, k.g_oth), y_dev)
        sd.start(2)
        own_z = Collect(lambda d: k.rows.at[pl.ds(64 * d, 64), :])
        gather_last(ed, wd)
        gather(eg, wg)
        gather_last(eg, wg)
        for s in (sg, su):
            s.wait(2)
            s.start(6)
        own_z.hand_on()
        for copy in later:
            copy.wait_recv()
        own_y.wait_recv()
        own_z.wait()
        oth_z = Collect(lambda d: k.rows.at[pl.ds(256 + 64 * d, 64), :])

        def g_piece(half, d, at):
            g = k.g_oth if half else k.g_own
            return g[pl.ds(pl.multiple_of(near(d) * 64, 64), 64), at].astype(f32)

        def route(half):
            chosen = []
            for d in range(4):
                named = (k.ids[d, half * 64 : (half + 1) * 64, :] == mine.astype(f32)).astype(f32)
                chosen.append(jnp.sum(named, axis=-1, keepdims=True))
            chosen = jnp.concatenate(chosen, axis=0)
            prob, lane = probabilities(k.rows[half * 256 : (half + 1) * 256, :], k.small)
            here = jnp.sum(jnp.where(lane == mine + 3, prob, 0.0), axis=-1, keepdims=True)
            gate = here * chosen
            for d in range(4):
                at = slice(half * 256 + d * 64, half * 256 + (d + 1) * 64)
                value = gate[d * 64 : (d + 1) * 64, :] * g_piece(half, d, slice(None))
                slopes[at, :] = value.astype(bf16)
            return gate, chosen

        def gate_part(half):
            rows_at = slice(half * 256, (half + 1) * 256)

            def one(r, _):
                at = pl.ds(pl.multiple_of(owner_expert(r) * 512, 512), 512)
                acc[0] += dot_nn(k.rows[rows_at, at], wg[r])
                acc[2] += dot_nt(slopes[rows_at, at], wd[r])
                return 0

            acc[...] = jnp.zeros_like(acc)
            lax.fori_loop(0, 4, one, 0)

        def phase_one(half):
            rows_at = slice(half * 256, (half + 1) * 256)

            def one(r, _):
                at = pl.ds(pl.multiple_of(owner_expert(r) * 512, 512), 512)
                acc[1] += dot_nn(k.rows[rows_at, at], wu[r])
                return 0

            lax.fori_loop(0, 4, one, 0)
            for d in range(4):
                at, to = slice(d * 64, (d + 1) * 64), slice(half * 256 + d * 64, half * 256 + (d + 1) * 64)
                act, gate_grad, up_grad = gated(acc[0, at, :], acc[1, at, :], acc[2, at, :])
                up[0, to, :] = act.astype(bf16)
                up[1, to, :] = gate_grad.astype(bf16)
                up[2, to, :] = up_grad.astype(bf16)

        lanes = lax.broadcasted_iota(jnp.int32, (64, 128), 1)

        def phase_two(half, gate, chosen):
            rows_at = slice(half * 256, (half + 1) * 256)

            def two(r, dgate):
                at = pl.ds(pl.multiple_of(owner_expert(r) * 512, 512), 512)
                result = dot_nn(up[0, rows_at, :], wd[r]).astype(bf16).astype(f32)
                grad = dot_nt(up[1, rows_at, :], wg[r]) + dot_nt(up[2, rows_at, :], wu[r])
                sums = []
                for d in range(4):
                    here = slice(d * 64, (d + 1) * 64)
                    g_rows = g_piece(half, d, at)
                    sums.append(jnp.sum(g_rows * result[here, :], axis=-1, keepdims=True))
                    part = gate[here, :] * result[here, :]
                    if half == 0:
                        k.out_sum[here, at] = part
                        k.grad_sum[here, at] = grad[here, :]
                    else:
                        k.e_out[d, :, at] = part.astype(bf16)
                        k.e_grad[d, :, at] = grad[here, :].astype(bf16)
                return dgate + jnp.concatenate(sums, axis=0)

            dgate = lax.fori_loop(0, 4, two, jnp.zeros((256, 1), f32)) * chosen
            for d in range(4):
                extra = jnp.zeros((64, 128), f32)
                for m, part in enumerate(split3(dgate[d * 64 : (d + 1) * 64, :])):
                    extra = jnp.where(lanes == mine + 16 * m, part, extra)
                if half == 0:
                    k.extras[d * 64 : (d + 1) * 64, :] = extra
                else:
                    k.e_grad[d, :, 2048:2176] = extra.astype(bf16)

        gate, chosen = route(0)
        for copy in group:
            copy.wait()
        group.clear()
        gate_part(0)
        gather(eu, wu)
        gather_last(eu, wu)
        for copy in group:
            copy.wait()
        phase_one(0)
        oth_z.hand_on()
        phase_two(0, gate, chosen)
        sg.wait(1)
        sg.start(3)
        sg.start(5)
        oth_z.wait()
        g_y.wait_recv()
        gate, chosen = route(1)
        gate_part(1)
        phase_one(1)
        saved = [loads.go(up, k.ex_up)]
        for r in range(4):
            to = slice(r * 256, (r + 1) * 256)
            for target, m in ((keep, r), (send, r + 4)):
                at = pl.ds(pl.multiple_of(owner_dense(m) * 256, 256), 256)
                target[0:512, to] = slopes[:, at]
                target[512:1024, to] = k.rows[:, at]
        saved.append(loads.go(keep, k.ex_keep))
        swap_ex = wires.go(lambda: (send, k.ex_x), core_dev)
        sd.wait(2)
        sd.start(6)
        phase_two(1, gate, chosen)
        su.wait(1)
        su.start(3)
        su.start(5)
        for copy in saved:
            copy.wait()
        swap_ex.wait_send()
        swap_ex.ends = lambda: (k.ex_keep, k.ex_x)
        parts.swap_ex = swap_ex

    pl.run_scoped(
        expert_part,
        pltpu.VMEM((4, 512, 1408), bf16),
        pltpu.VMEM((4, 512, 1408), bf16),
        pltpu.VMEM((4, 1408, 512), bf16),
        pltpu.VMEM((512, 2048), bf16),
        pltpu.VMEM((3, 256, 1408), f32),
        pltpu.VMEM((3, 512, 1408), bf16),
        pltpu.VMEM((1024, 1024), bf16),
        pltpu.VMEM((1024, 1024), bf16),
    )
    swap_up = {}
    for m in (1, 2, 0):
        swap_up[m] = wires.go(lambda m=m: (k.ex_up.at[m], k.ex_up_x.at[m]), core_dev)
    e_grad_z = to_z(lambda d: lambda: (k.e_grad.at[d], k.e_grad_z.at[d - 1]))
    e_out_z = to_z(lambda d: lambda: (k.e_out.at[d], k.e_out_z.at[d - 1]))
    over_y, over_x = {}, {}

    def expert_grad(m, kept, sent, landed):
        parts.swap_ex_wait()
        swap_up[m].wait_recv()

        def inner(left, right, keep, send):
            start = pl.ds(0 if m == 0 else 512, 512)
            got = [
                loads.go(k.ex_up.at[m], right.at[0]),
                loads.go(k.ex_up_x.at[m], right.at[1]),
                loads.go(k.ex_keep.at[start, :], left.at[0]),
                loads.go(k.ex_x.at[start, :], left.at[1]),
            ]
            for copy in got:
                copy.wait()
            saved = []
            for r in (3, 1, 2, 0):
                target = send if r % 2 else keep
                at = slice(r * 256, (r + 1) * 256)
                to = pl.ds(pl.multiple_of(((y + r // 2) % 2) * 256, 256), 256)
                if m == 0:
                    total = dot_tn(right[0], left[0, :, at]) + dot_tn(right[1], left[1, :, at])
                    target[:, to] = total.astype(bf16)
                else:
                    total = dot_tn(left[0, :, at], right[0]) + dot_tn(left[1, :, at], right[1])
                    target[to, :] = total.astype(bf16)
                if r == 1:
                    saved.append(loads.go(send, sent))
                if r == 2:
                    saved[0].wait()
                    over_x[6 + m] = wires.go(lambda: (sent, landed), x_dev)
            loads.go(keep, kept).wait()

        shape = (1408, 512) if m == 0 else (512, 1408)
        pl.run_scoped(
            inner,
            pltpu.VMEM((2, 512, 1024), bf16),
            pltpu.VMEM((2, 512, 1408), bf16),
            pltpu.VMEM(shape, bf16),
            pltpu.VMEM(shape, bf16),
        )

    def set_out(name, n, source, target, device):
        over_y[name, n] = wires.go(lambda: (source.at[n], target.at[n]), device)

    def y_first(name, keep, send, landed):
        def store(r, total):
            (send if r >= 2 else keep)[r % 2] = total
            if r == 3:
                set_out(name, 1, send, landed, y_dev)

        return store

    def shared_grad(m, store):
        def inner(left, right):
            if m == 0:
                got = [loads.go(k.sh_keep, left.at[0]), loads.go(k.sh_x, left.at[1])]
            else:
                start = pl.ds(512, 256)
                got = [
                    loads.go(k.ex_keep.at[start, :], left.at[0]),
                    loads.go(k.ex_x.at[start, :], left.at[1]),
                ]
            got.append(loads.go(k.sh_up.at[m], right.at[0]))
            got.append(loads.go(k.sh_up_x.at[m], right.at[1]))
            for copy in got:
                copy.wait()
            for r in (3, 1, 2, 0):
                at = slice(r * 256, (r + 1) * 256)
                if m == 0:
                    total = dot_tn(right[0], left[0, :, at]) + dot_tn(right[1], left[1, :, at])
                else:
                    total = dot_tn(left[0, :, at], right[0]) + dot_tn(left[1, :, at], right[1])
                store(r, total.astype(bf16))

        pl.run_scoped(
            inner, pltpu.VMEM((2, 256, 1024), bf16), pltpu.VMEM((2, 256, 1408), bf16)
        )

    def swap_ex_wait():
        if not parts.started:
            parts.swap_ex.wait_recv()
            parts.started = True

    parts.swap_ex_wait = swap_ex_wait

    def shared_part(wg, wu, wd, slopes, acc, up, keep, send):
        routed = k.rows.at[pl.ds(0, 256), :]
        held = []

        def bring(r, group):
            for s in group:
                held.append(loads.go(s.block(r), {sg: wg, su: wu, sd: wd}[s].at[r]))

        def arrived(r, group, onward=()):
            for s in group:
                s.wait(r)
                for t in onward:
                    s.start(t)
            bring(r, group)

        def settle():
            for copy in held:
                copy.wait()
            held.clear()

        pair, last = (sg, su), (sd,)
        for r in (0, 1, 2):
            bring(r, pair)
        for r in (4, 6):
            arrived(r, pair)
        expert_grad(1, k.k_eg, k.t_eg, k.x_eg)
        arrived(5, pair)
        sd.wait(1)
        sd.start(3)
        sd.start(5)
        bring(0, last)
        bring(1, last)
        bring(2, last)
        arrived(4, last)
        arrived(6, last)
        arrived(5, last)
        wide = routed[...].astype(f32) * k.small[2:3, :].astype(f32)
        sw = jax.nn.sigmoid(jnp.sum(wide, axis=-1, keepdims=True))
        for d in range(4):
            at = slice(d * 64, (d + 1) * 64)
            slopes[at, :] = (sw[at, :] * piece(k.g_own, d, 64).astype(f32)).astype(bf16)
        for r in range(4):
            to = slice(r * 256, (r + 1) * 256)
            keep[:, to] = cols(slopes, owner_dense(r), 256)
            send[:, to] = cols(slopes, owner_dense(r + 4), 256)
        saved = [loads.go(keep, k.sh_keep)]
        acc[...] = jnp.zeros_like(acc)

        def one(j, _):
            r = j // 2 + (j % 2) * 4
            row = cols(routed, owner_dense(r), 256)
            acc[0] += dot_nn(row, wg[r])
            acc[1] += dot_nn(row, wu[r])
            return 0

        def back(j, _):
            r = j // 2 + (j % 2) * 4
            acc[2] += dot_nt(cols(slopes, owner_dense(r), 256), wd[r])
            return 0

        settle()
        lax.fori_loop(0, 6, one, 0)
        arrived(3, pair, (7,))
        arrived(7, pair)
        settle()
        lax.fori_loop(6, 8, one, 0)
        for d in range(4):
            at = slice(d * 64, (d + 1) * 64)
            up[0, at, :] = (jax.nn.silu(acc[0, at, :]) * acc[1, at, :]).astype(bf16)
        swaps = [
            wires.go(lambda: (up.at[0], k.sh_up_x.at[0]), core_dev),
            wires.go(lambda: (send, k.sh_x), core_dev),
        ]
        saved.append(loads.go(up.at[0], k.sh_up.at[0]))
        for copy in saved:
            copy.wait()
        lax.fori_loop(0, 6, back, 0)
        for copy in swaps:
            copy.wait_recv()
            copy.wait_send()
        shared_grad(0, y_first(2, k.k_sd, k.t_sd, k.y_sd))
        for copy in e_grad_z:
            copy.wait_recv()
        oth = k.e_grad[0].astype(f32)
        for d in range(3):
            oth += k.e_grad_z[d].astype(f32)
        k.g_send[...] = oth.astype(bf16)
        parts.grad_y = wires.go(lambda: (k.g_send, k.g_y), y_dev)
        set_out(2, 0, k.t_sd, k.y_sd, y_dev)
        expert_grad(2, k.k_eu, k.t_eu, k.x_eu)
        arrived(3, last, (7,))
        arrived(7, last)
        settle()
        lax.fori_loop(6, 8, back, 0)
        for d in range(4):
            at = slice(d * 64, (d + 1) * 64)
            _, gate_grad, up_grad = gated(acc[0, at, :], acc[1, at, :], acc[2, at, :])
            up[1, at, :] = gate_grad.astype(bf16)
            up[2, at, :] = up_grad.astype(bf16)
        saved = [loads.go(up.at[m], k.sh_up.at[m]) for m in (1, 2)]

        def two(r, slope):
            at = pl.ds(pl.multiple_of(owner_dense(r) * 256, 256), 256)
            part = dot_nn(up[0], wd[r])
            total = sw * part + k.out_sum[:, at]
            back = dot_nt(up[1], wg[r]) + dot_nt(up[2], wu[r]) + k.grad_sum[:, at]
            sums = []
            for d in range(4):
                rows_at = slice(d * 64, (d + 1) * 64)
                g_rows = k.g_own[pl.ds(pl.multiple_of(near(d) * 64, 64), 64), at].astype(f32)
                sums.append(jnp.sum(g_rows * part[rows_at, :], axis=-1, keepdims=True))
                k.s_out[d, :, at] = total[rows_at, :].astype(bf16)
                k.s_grad[d, :, at] = back[rows_at, :].astype(bf16)
            return slope + jnp.concatenate(sums, axis=0)

        slope = lax.fori_loop(0, 8, two, jnp.zeros((256, 1), f32))
        lanes = lax.broadcasted_iota(jnp.int32, (64, 128), 1)
        for d in range(4):
            rows_at = slice(d * 64, (d + 1) * 64)
            extra = k.extras[rows_at, :]
            for m, part in enumerate(split3(slope[rows_at, :])):
                extra = jnp.where(lanes == mine + 48 + 16 * m, part, extra)
            k.s_grad[d, :, 2048:2176] = extra.astype(bf16)
        for copy in saved:
            copy.wait()

    pl.run_scoped(
        shared_part,
        pltpu.VMEM((8, 256, 1408), bf16),
        pltpu.VMEM((8, 256, 1408), bf16),
        pltpu.VMEM((8, 1408, 256), bf16),
        pltpu.VMEM((256, 2048), bf16),
        pltpu.VMEM((3, 256, 1408), f32),
        pltpu.VMEM((3, 256, 1408), bf16),
        pltpu.VMEM((256, 1024), bf16),
        pltpu.VMEM((256, 1024), bf16),
    )
    swap_sh = [
        wires.go(lambda m=m: (k.sh_up.at[m], k.sh_up_x.at[m]), core_dev) for m in (1, 2)
    ]
    s_grad_z = to_z(lambda d: lambda: (k.s_grad.at[d], k.s_grad_z.at[d - 1]))

    def back_part(*refs):
        k_ga, k_gb, k_su, k_q, k_kv, k_o, k_v = refs[:7]
        t_ga, t_gb, t_su, t_q, t_kv, t_o, t_v = refs[7:14]
        f_ga, f_gb, f_su, f_q, f_kv, f_o, f_v, f_sd = refs[14:22]
        h_keep, h_send, h_x, lin, lin_x, vec, high, gkv, gkv_send, gn = refs[22:]
        k_sd, t_sd = k.k_sd, k.t_sd

        def fold(name, keep, landed, send, target, device=x_dev):
            over_y[name, 1].wait_recv()

            def inner(buffer):
                loads.go(landed.at[1], buffer).wait()
                send[...] = (keep[1].astype(f32) + buffer[...].astype(f32)).astype(bf16)

            pl.run_scoped(inner, pltpu.VMEM(tuple(keep.shape[1:]), bf16))
            over_x[name] = wires.go(lambda: (send, target), device)

        def finish_pair():
            for name in (0, 9, 1):
                over_y[name, 0].wait_recv()
                over_x[name].wait_recv()

            def inner(left, right, total):
                first, last, whole = pl.ds(0, CUT), pl.ds(CUT, 256 - CUT), slice(0, 256)
                got = [
                    loads.go(k.y_ga.at[0], left.at[0, first, :]),
                    loads.go(k.x_ga, right.at[0, first, :]),
                    loads.go(k.y_gb.at[0], left.at[0, last, :]),
                    loads.go(k.x_gb, right.at[0, last, :]),
                    loads.go(k.y_su.at[0], left.at[1]),
                    loads.go(k.x_su, right.at[1]),
                ]
                for copy in got:
                    copy.wait()
                for n, keep, at in (
                    (0, k_ga, slice(0, CUT)),
                    (0, k_gb, slice(CUT, 256)),
                    (1, k_su, whole),
                ):
                    value = keep[0].astype(f32) + left[n, at, :].astype(f32)
                    value += right[n, at, :].astype(f32)
                    total[at, n, :] = value.astype(bf16)
                loads.go(total, k.d_si).wait()

            pair = pltpu.VMEM((2, 256, 1408), bf16)
            pl.run_scoped(inner, pair, pair, pltpu.VMEM((256, 2, 1408), bf16))

        def finish(name, keep, landed, target, result):
            over_y[name, 0].wait_recv()

            def inner(left, right, total):
                got = loads.go(landed.at[0], left)
                over_x[name].wait_recv()
                more = loads.go(target, right)
                got.wait()
                more.wait()
                value = keep[0].astype(f32) + left[...].astype(f32) + right[...].astype(f32)
                total[...] = value.astype(total.dtype)
                loads.go(total, result).wait()

            shape = tuple(keep.shape[1:])
            pl.run_scoped(
                inner,
                pltpu.VMEM(shape, bf16),
                pltpu.VMEM(shape, bf16),
                pltpu.VMEM(shape, result.dtype),
            )

        swap_sh[0].wait_recv()

        def gate_store(r, total):
            (t_ga if r >= 2 else k_ga)[r % 2] = total[0:CUT, :]
            (t_gb if r % 2 else k_gb)[r // 2] = total[CUT:256, :]
            if r == 3:
                set_out(0, 1, t_ga, k.y_ga, y_dev)
                set_out(9, 1, t_gb, k.y_gb, x_dev)

        shared_grad(1, gate_store)
        set_out(9, 0, t_gb, k.y_gb, x_dev)
        swap_sh[1].wait_recv()
        shared_grad(2, y_first(1, k_su, t_su, k.y_su))
        expert_grad(0, k.k_ed, k.t_ed, k.x_ed)
        fold(2, k_sd, k.y_sd, f_sd, k.x_sd)

        def other_rows(buffer):
            for copy in e_out_z:
                copy.wait_recv()
            loads.go(k.e_out_z, buffer).wait()
            oth = k.e_out[0].astype(f32)
            for d in range(3):
                oth += buffer[d].astype(f32)
            k.o_send[...] = oth.astype(bf16)

        pl.run_scoped(other_rows, pltpu.VMEM((3, 64, 2048), bf16))
        for copy in s_grad_z:
            copy.wait_recv()
        parts.grad_y.wait_recv()
        total = k.s_grad[0].astype(f32) + k.g_y[...].astype(f32)
        for d in range(3):
            total += k.s_grad_z[d].astype(f32)
        own_rows(
            total,
            k.hidden[...],
            k.rows[0:64, :],
            piece(k.g_own, 0, 64),
            k.small,
            high,
            k.gh.at[0],
            vec,
        )
        gh_z = Collect(lambda d: k.gh.at[d])
        out_y = wires.go(lambda: (k.o_send, k.o_y), y_dev)
        set_out(0, 0, t_ga, k.y_ga, y_dev)
        fold(0, k_ga, k.y_ga, f_ga, k.x_ga)
        fold(9, k_gb, k.y_gb, f_gb, k.x_gb, y_dev)
        gn_z, s_out_z, vec_z = [], [], []

        def attention_back(w, o_w, acc, low_g, n_x, low_x):
            got, more = [loads.go(k.w_o, o_w.at[0])], [loads.go(k.w_q, w.at[0])]
            for r in range(1, 8):
                got.append(loads.go(k.s_o.at[r], o_w.at[r]))
                more.append(loads.go(k.s_q.at[r], w.at[r]))
            gh_z.hand_on()
            gh_z.wait()
            s_out_z.extend(to_z(lambda d: lambda: (k.s_out.at[d], k.s_out_z.at[d - 1])))
            for copy in got:
                copy.wait()
            acc[...] = jnp.zeros_like(acc)
            for r in range(8):
                at = pl.ds(pl.multiple_of(owner_dense(r) * 256, 256), 256)
                row = jnp.concatenate([k.gh[d, :, at] for d in range(4)], axis=0)
                target = h_keep if r < 4 else h_send
                target[:, (r % 4) * 256 : (r % 4 + 1) * 256] = row
                acc[...] += dot_nt(row, o_w[r])
            swap_h = wires.go(lambda: (h_send, k.h_x), core_dev)
            low_g[...] = acc[...].astype(bf16)
            mask_own = k.ids_near[0:1, :] <= k.ids_q[:, 0:1]
            mask_oth = k.ids_far[0:1, :] <= k.ids_q[:, 0:1]
            scale = 128 ** (-0.5)
            for h in range(4):
                at = slice(h * 128, (h + 1) * 128)
                w_own, w_oth = softmax_parts(
                    k.q[:, at], k.kv[0:256, at], k.kv_oth[0:256, at], mask_own, mask_oth
                )
                dw_own = dot_nt(low_g[:, at], k.kv[256:512, at])
                dw_oth = dot_nt(low_g[:, at], k.kv_oth[256:512, at])
                mean = jnp.sum(w_own * dw_own, axis=-1, keepdims=True)
                mean += jnp.sum(w_oth * dw_oth, axis=-1, keepdims=True)
                ds_own = (w_own * (dw_own - mean)).astype(bf16)
                ds_oth = (w_oth * (dw_oth - mean)).astype(bf16)
                gq = dot_nn(ds_own, k.kv[0:256, at]) + dot_nn(ds_oth, k.kv_oth[0:256, at])
                lin[0:256, at] = turn_back(gq * scale, k.cs[...], k.sn[...]).astype(bf16)
                gkv[0:256, at] = dot_tn(ds_own, k.q[:, at]) * scale
                gkv[256:512, at] = dot_tn(w_own.astype(bf16), low_g[:, at])
                gkv_send[0:256, at] = (dot_tn(ds_oth, k.q[:, at]) * scale).astype(bf16)
                gkv_send[256:512, at] = dot_tn(w_oth.astype(bf16), low_g[:, at]).astype(bf16)
            gkv_y = wires.go(lambda: (gkv_send, k.gkv_y), y_dev)
            swap_q = wires.go(
                lambda: (lin.at[pl.ds(0, 256), :], k.lin_x.at[pl.ds(0, 256), :]), core_dev
            )
            fold(1, k_su, k.y_su, f_su, k.x_su)
            for copy in (swap_h, swap_n, swap_low, swap_q):
                copy.wait_recv()
            got = [
                loads.go(k.n_x, n_x),
                loads.go(k.low_x, low_x),
                loads.go(k.h_x, h_x),
                loads.go(k.lin_x.at[pl.ds(0, 256), :], lin_x.at[pl.ds(0, 256), :]),
            ]
            for copy in got:
                copy.wait()

            def projection(r, m):
                at, rows_at = slice(r * 256, (r + 1) * 256), slice(m * 256, (m + 1) * 256)
                total = dot_tn(k.n_keep[:, at], lin[rows_at, :])
                return (total + dot_tn(n_x[:, at], lin_x[rows_at, :])).astype(bf16)

            for r in (3, 1, 2, 0):
                at = slice(r * 256, (r + 1) * 256)
                total = dot_tn(k.low[...], h_keep[:, at]) + dot_tn(low_x[...], h_x[:, at])
                (t_o if r % 2 else k_o)[r // 2] = total.astype(bf16)
                if r % 2:
                    set_out(4, r // 2, t_o, k.y_o, x_dev)
                (t_q if r >= 2 else k_q)[r % 2] = projection(r, 0)
                if r == 3:
                    set_out(3, 1, t_q, k.y_q, y_dev)
            for copy in more:
                copy.wait()
            gkv_y.wait_recv()
            for h in range(4):
                at = slice(h * 128, (h + 1) * 128)
                gk = gkv[0:256, at] + k.gkv_y[0:256, at].astype(f32)
                lin[256:512, at] = turn_back(gk, k.cs[...], k.sn[...]).astype(bf16)
            lin[512:768, :] = (gkv[256:512, :] + k.gkv_y[256:512, :].astype(f32)).astype(bf16)
            swap_kv = wires.go(
                lambda: (lin.at[pl.ds(256, 512), :], k.lin_x.at[pl.ds(256, 512), :]), core_dev
            )
            for m in range(3):
                part = lin[m * 256 : (m + 1) * 256, :].astype(f32)
                vec[11 + m : 12 + m, 0:512] = jnp.sum(part, axis=0, keepdims=True)
            swap_kv.wait_recv()
            loads.go(k.lin_x.at[pl.ds(256, 512), :], lin_x.at[pl.ds(256, 512), :]).wait()
            for r in (3, 2, 1, 0):
                target = t_kv if r >= 2 else k_kv
                for m in (1, 2):
                    target[r % 2, (m - 1) * 256 : m * 256, :] = projection(r, m)
                if r == 3:
                    set_out(10, 1, t_kv, k.y_kv, y_dev)
                    set_out(1, 0, t_su, k.y_su, y_dev)
            for r in range(8):
                at = pl.ds(pl.multiple_of(owner_dense(r) * 256, 256), 256)
                back = dot_nt(lin[0:256, :], w[r, 0:256, :])
                back += dot_nt(lin[256:512, :], w[r, 256:512, :])
                back += dot_nt(lin[512:768, :], w[r, 512:768, :])
                gain = jnp.zeros((1, 256), f32)
                for d in range(4):
                    rows_at = slice(d * 64, (d + 1) * 64)
                    t = k.tok[pl.ds(pl.multiple_of(near(d) * 64, 64), 64), at].astype(f32)
                    gain += jnp.sum(
                        back[rows_at, :] * t * k.inv1[rows_at, :], axis=0, keepdims=True
                    )
                    gn[d, :, at] = back[rows_at, :].astype(bf16)
                vec[0:1, at] = gain
            vec_z.extend(to_z(lambda d: lambda: (vec, k.vec_z.at[d - 1])))
            gn_z.extend(to_z(lambda d: lambda: (gn.at[d], k.gn_z.at[d - 1])))

        pl.run_scoped(
            attention_back,
            pltpu.VMEM((8, 768, 512), bf16),
            pltpu.VMEM((8, 512, 256), bf16),
            pltpu.VMEM((256, 512), f32),
            pltpu.VMEM((256, 512), bf16),
            pltpu.VMEM((256, 1024), bf16),
            pltpu.VMEM((256, 512), bf16),
        )
        kept = [loads.go(k_q.at[0], k.keep_q), loads.go(k_kv.at[0], k.keep_kv)]
        kept.append(loads.go(k_o.at[0], k.keep_o))
        def expert_finish(m, kept, landed, result):
            def inner(left, right):
                got = loads.go(kept, left)
                over_x[6 + m].wait_recv()
                more = loads.go(landed, right)
                got.wait()
                more.wait()
                left[...] = (left[...].astype(f32) + right[...].astype(f32)).astype(bf16)
                loads.go(left, result).wait()

            shape = pltpu.VMEM(tuple(result.shape), bf16)
            pl.run_scoped(inner, shape, shape)

        def expert_pair():
            for m in (1, 2):
                over_x[6 + m].wait_recv()

            def inner(left, right, total):
                for half in range(2):
                    at = pl.ds(256 * half, 256)
                    got = []
                    for n, (kept, landed) in enumerate(((k.k_eg, k.x_eg), (k.k_eu, k.x_eu))):
                        got.append(loads.go(kept.at[at, :], left.at[n]))
                        got.append(loads.go(landed.at[at, :], right.at[n]))
                    for copy in got:
                        copy.wait()
                    for n in range(2):
                        value = left[n].astype(f32) + right[n].astype(f32)
                        total[:, n, :] = value.astype(bf16)
                    loads.go(total, k.d_ei.at[at]).wait()

            pair = pltpu.VMEM((2, 256, 1408), bf16)
            pl.run_scoped(inner, pair, pair, pltpu.VMEM((256, 2, 1408), bf16))

        expert_pair()
        for copy in vec_z:
            copy.wait_recv()
        line = lax.broadcasted_iota(jnp.int32, (16, 2048), 0)
        over_z = k.vec_z[0] + k.vec_z[1] + k.vec_z[2]
        k.vec_sum[...] = vec[...] + jnp.where(line < 11, over_z, 0.0)
        swap_vec = wires.go(lambda: (k.vec_sum, k.vec_x), core_dev)
        swap_vec.wait_recv()
        k.vec_x[...] += k.vec_sum[...]
        line = lax.broadcasted_iota(jnp.int32, (16, 512), 0)
        for r in (3, 2, 1, 0):
            here = cols(k.vec_x, owner_dense(r), 256)
            here = jnp.concatenate([here, jnp.zeros((16, 256), f32)], axis=1)
            here = jnp.where(line < 11, here, k.vec_x[:, 0:512]).astype(bf16)
            (t_v if r >= 2 else k_v)[r % 2] = here
            if r >= 2:
                set_out(5, r % 2, t_v, k.y_v, y_dev)
        kept.append(loads.go(k_v.at[0], k.keep_v))
        set_out(3, 0, t_q, k.y_q, y_dev)
        set_out(10, 0, t_kv, k.y_kv, y_dev)

        def outputs(s_z):
            for copy in s_out_z:
                copy.wait_recv()
            got = loads.go(k.s_out_z, s_z)
            for copy in gn_z:
                copy.wait_recv()
            grad = gn[0].astype(f32)
            for d in range(3):
                grad += k.gn_z[d].astype(f32)
            t = piece(k.tok, 0, 64).astype(f32)
            i = k.inv1[0:64, :]
            scaled = grad * k.small[0:1, :].astype(f32)
            mean = jnp.mean(scaled * t, axis=-1, keepdims=True)
            grad = high[...] + i * scaled - t * (i * i * i * mean)
            k.tok_low[...] = grad.astype(bf16)
            wrote = [loads.go(k.tok_low, k.grad_tokens)]
            got.wait()
            total = k.hidden[...] + k.s_out[0].astype(f32)
            for d in range(3):
                total += s_z[d].astype(f32)
            out_y.wait_recv()
            k.out_low[...] = (total + k.o_y[...].astype(f32)).astype(bf16)
            wrote.append(loads.go(k.out_low, k.output))
            for copy in wrote:
                copy.wait()

        expert_finish(0, k.k_ed, k.x_ed, k.d_ed)
        finish(2, k_sd, k.y_sd, k.x_sd, k.d_sd)
        fold(3, k_q, k.y_q, f_q, k.x_q)
        fold(10, k_kv, k.y_kv, f_kv, k.x_kv)
        fold(5, k_v, k.y_v, f_v, k.x_v)
        fold(4, k_o, k.y_o, f_o, k.x_o, y_dev)
        pl.run_scoped(outputs, pltpu.VMEM((3, 64, 2048), bf16))
        finish_pair()
        for name in (3, 10, 4, 5):
            over_y[name, 0].wait_recv()
            over_x[name].wait_recv()
        for copy in kept:
            copy.wait()
        wires.drain()

    shapes = [(CUT, 1408), (256 - CUT, 1408), (256, 1408)]
    shapes += [(256, 512), (512, 512), (512, 256), (16, 512)]

    def buffers(lead):
        return tuple(
            pltpu.VMEM(lead + shape, bf16)
            for shape in shapes
        )

    pl.run_scoped(
        back_part,
        *buffers((2,)),
        *buffers((2,)),
        *buffers(()),
        pltpu.VMEM((1408, 256), bf16),
        pltpu.VMEM((256, 1024), bf16),
        pltpu.VMEM((256, 1024), bf16),
        pltpu.VMEM((256, 1024), bf16),
        pltpu.VMEM((768, 512), bf16),
        pltpu.VMEM((768, 512), bf16),
        pltpu.VMEM((16, 2048), f32),
        pltpu.VMEM((64, 2048), f32),
        pltpu.VMEM((512, 512), f32),
        pltpu.VMEM((512, 512), bf16),
        pltpu.VMEM((4, 64, 2048), bf16),
    )


def close_kernel(k):
    loads = Loads(k.load_sems)
    sums = (
        (k.keep_q, k.y_q, k.x_q, k.b_q, k.c_q.at[pl.ds(0, 256), :]),
        (k.keep_kv, k.y_kv, k.x_kv, k.b_kv, k.c_q.at[pl.ds(256, 512), :]),
        (k.keep_o, k.y_o, k.x_o, k.b_o, k.c_o),
    )
    parts = []
    for keep, y, x, buffer, _ in sums:
        parts.append([loads.go(a, buffer.at[n]) for n, a in enumerate((keep, y.at[0], x))])
    passed = (
        (k.d_ei, k.b_ei, k.c_ei),
        (k.d_ed, k.b_ed, k.c_ed),
        (k.d_si, k.b_si, k.c_si),
        (k.d_sd, k.b_sd, k.c_sd),
        (k.output, k.b_out, k.c_out),
        (k.grad_tokens, k.b_tok, k.c_tok),
    )
    vectors = [loads.go(a, k.b_v.at[n]) for n, a in enumerate((k.keep_v, k.y_v.at[0], k.x_v))]
    got = [loads.go(source, buffer) for source, buffer, _ in passed]
    for copy in vectors:
        copy.wait()
    total = k.b_v[0].astype(f32) + k.b_v[1].astype(f32) + k.b_v[2].astype(f32)
    low = total.astype(bf16)
    for m, target in enumerate((k.c_one, k.c_two, k.c_gate)):
        target[...] = low[m : m + 1, 0:256].reshape(256)
    k.c_router[...] = low[3:11, 0:256]
    for h in range(4):
        here = pltpu.roll(
            total[:, h * 128 : (h + 1) * 128], (128 - owner_dense(0) * 16) % 128, 1
        )
        for m in range(3):
            k.c_bias[m, h : h + 1, :] = here[11 + m : 12 + m, 0:16].astype(bf16)
    done = []
    for copies, (_, _, _, buffer, target) in zip(parts, sums):
        for copy in copies:
            copy.wait()
        total = buffer[0].astype(f32) + buffer[1].astype(f32) + buffer[2].astype(f32)
        buffer[0] = total.astype(bf16)
        done.append(loads.go(buffer.at[0], target))
    for copy, (_, buffer, target) in zip(got, passed):
        copy.wait()
        done.append(loads.go(buffer, target))
    for copy in done:
        copy.wait()


def dma(n):
    return pltpu.SemaphoreType.DMA((n,))


def fixed_body(
    tokens,
    norm1_gain,
    w_qkv,
    b_qkv,
    w_out,
    norm2_gain,
    w_router,
    shared_gate,
    w_shared_in,
    w_shared_out,
    w_expert_in,
    w_expert_out,
    block_ids,
    expert_ids,
    out_grad,
):
    tok, g_own = tokens[0], out_grad[0]
    rows = tok.shape[0]
    places = np.arange(2 * rows)[:, None]
    frequency = rope_base ** (-np.arange(64) / 64.0)
    cosine, sine = np.cos(places * frequency), np.sin(places * frequency)
    cs = np.concatenate([cosine, cosine], axis=1).astype(np.float32)
    sn = np.concatenate([-sine, sine], axis=1).astype(np.float32)

    def vm(*shape, kind=bf16):
        return pltpu.VMEM(shape, kind)

    def o(*shape, kind=bf16, at=A):
        return (shape, kind, at)

    w_q = w_qkv.transpose(1, 0, 2).reshape(768, 512)
    b = call(
        layer_kernel,
        0,
        dict(
            tok_in=(tok, A),
            g_in=(g_own, A),
            bias_in=(b_qkv, A),
            cs_in=(cs, A),
            sn_in=(sn, A),
            blocks_in=(block_ids, A),
            ids_in=(expert_ids[0].T, A),
            one_in=(norm1_gain, A),
            two_in=(norm2_gain, A),
            gate_in=(shared_gate, A),
            router_in=(w_router.T, A),
            w_q=(w_q, A),
            w_o=(w_out, A),
            w_si=(w_shared_in, A),
            w_sd=(w_shared_out, A),
            w_ei=(w_expert_in[0], A),
            w_ed=(w_expert_out[0], A),
        ),
        dict(
            output=o(64, 2048),
            grad_tokens=o(64, 2048),
            keep_v=o(16, 512),
            keep_q=o(256, 512),
            keep_kv=o(512, 512),
            keep_o=o(512, 256),
            d_si=o(256, 2, 1408),
            d_sd=o(1408, 256),
            d_ei=o(512, 2, 1408),
            d_ed=o(1408, 512),
            split_si=o(2, 256, 1408),
            split_ei=o(2, 512, 1408),
            s_q=o(8, 768, 512),
            s_o=o(8, 512, 256),
            s_sg=o(8, 256, 1408),
            s_su=o(8, 256, 1408),
            s_sd=o(8, 1408, 256),
            s_eg=o(4, 512, 1408),
            s_eu=o(4, 512, 1408),
            s_ed=o(4, 1408, 512),
            ex_up=o(3, 512, 1408),
            ex_up_x=o(3, 512, 1408),
            ex_keep=o(1024, 1024),
            ex_x=o(1024, 1024),
            sh_up=o(3, 256, 1408),
            sh_up_x=o(3, 256, 1408),
            sh_keep=o(256, 1024),
            sh_x=o(256, 1024),
            k_eg=o(512, 1408),
            k_eu=o(512, 1408),
            k_ed=o(1408, 512),
            t_eg=o(512, 1408),
            t_eu=o(512, 1408),
            t_ed=o(1408, 512),
            y_ga=o(2, CUT, 1408),
            y_gb=o(2, 256 - CUT, 1408),
            y_su=o(2, 256, 1408),
            y_sd=o(2, 1408, 256),
            y_q=o(2, 256, 512),
            y_kv=o(2, 512, 512),
            y_o=o(2, 512, 256),
            y_v=o(2, 16, 512),
            x_ga=o(CUT, 1408),
            x_gb=o(256 - CUT, 1408),
            x_su=o(256, 1408),
            x_sd=o(1408, 256),
            x_q=o(256, 512),
            x_kv=o(512, 512),
            x_o=o(512, 256),
            x_v=o(16, 512),
            x_eg=o(512, 1408),
            x_eu=o(512, 1408),
            x_ed=o(1408, 512),
            n_x=o(256, 1024),
            low_x=o(256, 512),
            h_x=o(256, 1024),
            lin_x=o(768, 512),
            e_out_z=o(3, 64, 2048),
            s_out_z=o(3, 64, 2048),
        ),
        dict(
            s_v=vm(8, 16, 256),
            tok=vm(256, 2048),
            g_own=vm(256, 2048),
            bias=vm(3, 4, 128),
            blocks=vm(1, 512, kind=jnp.int32),
            ids_own=vm(4, 64, kind=jnp.int32),
            gain_one=vm(256),
            gain_two=vm(256),
            gate_vector=vm(256),
            router=vm(8, 256),
            cs_all=vm(512, 128, kind=f32),
            sn_all=vm(512, 128, kind=f32),
            w_v=vm(16, 256),
            col=vm(512, 128, kind=f32),
            ids_q=vm(256, 128, kind=f32),
            ids_near=vm(8, 256, kind=f32),
            ids_far=vm(8, 256, kind=f32),
            cs=vm(256, 128, kind=f32),
            sn=vm(256, 128, kind=f32),
            ids=vm(4, 128, 128, kind=f32),
            ids_y=vm(64, 128, kind=f32),
            g_oth=vm(256, 2048),
            q=vm(256, 512),
            kv=vm(512, 512),
            kv_oth=vm(512, 512),
            low=vm(256, 512),
            n_keep=vm(256, 1024),
            n_send=vm(256, 1024),
            small=vm(16, 2048),
            inv1=vm(256, 1, kind=f32),
            k_sd=vm(2, 1408, 256),
            t_sd=vm(2, 1408, 256),
            att=vm(3, 64, 2048),
            att_send=vm(4, 64, 2048),
            att_pair=vm(64, 2048),
            hidden=vm(64, 2048, kind=f32),
            rows=vm(512, 2048),
            out_sum=vm(256, 2048, kind=f32),
            grad_sum=vm(256, 2048, kind=f32),
            extras=vm(256, 128, kind=f32),
            e_out=vm(4, 64, 2048),
            e_grad=vm(4, 64, 2176),
            e_grad_z=vm(3, 64, 2176),
            s_out=vm(4, 64, 2048),
            s_grad=vm(4, 64, 2176),
            s_grad_z=vm(3, 64, 2176),
            g_send=vm(64, 2176),
            g_y=vm(64, 2176),
            o_send=vm(64, 2048),
            o_y=vm(64, 2048),
            out_low=vm(64, 2048),
            tok_low=vm(64, 2048),
            gh=vm(4, 64, 2048),
            gkv_y=vm(512, 512),
            gn_z=vm(3, 64, 2048),
            vec_x=vm(16, 2048, kind=f32),
            vec_z=vm(3, 16, 2048, kind=f32),
            vec_sum=vm(16, 2048, kind=f32),
            send_sems=dma(144),
            recv_sems=dma(144),
            load_sems=dma(224),
        ),
        63,
        4 * 10**10,
        2 * 10**8,
    )
    c = call(
        close_kernel,
        None,
        dict(
            output=(b.output, A),
            grad_tokens=(b.grad_tokens, A),
            keep_v=(b.keep_v, A),
            y_v=(b.y_v, A),
            x_v=(b.x_v, A),
            keep_q=(b.keep_q, A),
            y_q=(b.y_q, A),
            x_q=(b.x_q, A),
            keep_kv=(b.keep_kv, A),
            y_kv=(b.y_kv, A),
            x_kv=(b.x_kv, A),
            keep_o=(b.keep_o, A),
            y_o=(b.y_o, A),
            x_o=(b.x_o, A),
            d_si=(b.d_si, A),
            d_sd=(b.d_sd, A),
            d_ei=(b.d_ei, A),
            d_ed=(b.d_ed, A),
        ),
        dict(
            c_out=o(64, 2048),
            c_tok=o(64, 2048),
            c_one=o(256, at=V),
            c_two=o(256, at=V),
            c_gate=o(256, at=V),
            c_router=o(8, 256, at=V),
            c_bias=o(3, 4, 16, at=V),
            c_q=o(768, 512),
            c_o=o(512, 256),
            c_si=o(256, 2, 1408),
            c_sd=o(1408, 256),
            c_ei=o(512, 2, 1408),
            c_ed=o(1408, 512),
        ),
        dict(
            b_v=vm(3, 16, 512),
            b_out=vm(64, 2048),
            b_tok=vm(64, 2048),
            b_q=vm(3, 256, 512),
            b_kv=vm(3, 512, 512),
            b_o=vm(3, 512, 256),
            b_si=vm(256, 2, 1408),
            b_sd=vm(1408, 256),
            b_ei=vm(512, 2, 1408),
            b_ed=vm(1408, 512),
            load_sems=dma(32),
        ),
        63,
        10**6,
        2 * 10**7,
    )
    return (
        c.c_out[None],
        c.c_tok[None],
        c.c_one,
        c.c_q.reshape(3, 256, 512).transpose(1, 0, 2),
        c.c_bias,
        c.c_o,
        c.c_two,
        c.c_router.T,
        c.c_gate,
        c.c_si,
        c.c_sd,
        c.c_ei[None],
        c.c_ed[None],
    )


def solution(mesh):
    placed = (
        P(DP, CTX, None),
        P(PLANE),
        P(PLANE, None, EXP),
        P(None, EXP, None),
        P(EXP, PLANE),
        P(PLANE),
        P(PLANE, None),
        P(PLANE),
        P(PLANE, None, EXP),
        P(EXP, PLANE),
        P(GROUP, DP, None, None),
        P(GROUP, None, DP),
        P(DP, None),
        P(DP, GROUP, None),
        P(DP, CTX, None),
    )
    fixed = tuple(mesh.shape[a] for a in (DP, CTX, EXP)) == (4, 2, 4)
    return jax.shard_map(
        fixed_body if fixed else general_body,
        mesh=mesh,
        in_specs=placed,
        out_specs=(
            P(DP, GROUP, None),
            P(DP, GROUP, None),
            P(PLANE),
            P(PLANE, None, EXP),
            P(None, EXP, PLANE),
            P(EXP, PLANE),
            P(PLANE),
            P(PLANE, None),
            P(PLANE),
            P(PLANE, None, EXP),
            P(EXP, PLANE),
            P(GROUP, DP, None, None),
            P(GROUP, None, DP),
        ),
        check_vma=False,
    )
```
